32 devices in a mesh: req: 8 (over z, x), row: 2 (over core), col: 2 (over y).
Axes of the slice: x: 2, y: 2, z: 4, core: 2. Of those that a mesh axis runs over, the one named last changes fastest.
Arguments:
- image_qkv: bfloat16 [192, 24, 3, 1280], P(('req', 'row'), 'col'), parts along dimension 0, may hold values from -6 to 6
- text_kv: bfloat16 [768, 2, 1280], P(('req', 'row'), None, 'col'), parts along dimension 0, may hold values from -6 to 6
- gain_query: float32 [64], replicated, may hold values from 1 to 3
- gain_key: float32 [64], replicated, may hold values from 1 to 3
- gain_text: float32 [64], replicated, may hold values from 1 to 3
- out_weight: bfloat16 [1280, 2432], P('col', 'row'), may hold values from -0.15625 to 0.15625
- final_weight: bfloat16 [64, 2432], P(None, 'row'), may hold values from -0.125 to 0.125
- hidden: bfloat16 [192, 24, 2432], P(('req', 'row'), 'col'), parts along dimension 0, may hold values from -6 to 6
- modulation: float32 [24, 2432], P('req'), parts along dimension 0, may hold values from -3 to 3
- latent: float32 [384, 768], P(('req', 'row'), 'col'), parts along dimension 0, may hold values from -6 to 6
- step_index: int32 [8], P('req'), parts along dimension 0, may hold values from 0 to 20
- step_count: int32 [8], P('req'), parts along dimension 0, may hold values from 1 to 5
Outputs:
- velocity: float32 [384, 768], P(('req', 'row'), 'col'), parts along dimension 0
- latent_next: float32 [384, 768], P(('req', 'row'), 'col'), parts along dimension 0
The draws below stay inside these ranges and needn't reach their ends.
There are 8 independent parts, one for each index of `req`. The reference program is written for one: setup_inputs(seed, part) draws one part's arguments, and reference() takes and returns one part's arrays. A program takes and returns all parts, laid end to end along the dimension named above; an argument that names none is the same for every part. Nothing has to cross between parts.
All inputs are finite; a program needn't handle non-finite values.
Results may differ from the reference program's by a relative error of at most 0.009.
Values may be sent and summed in bfloat16 or wider, within the bound.
No kernel may reach another device: no remote copies, remote signals or barrier semaphores. Data moves between devices by JAX's collectives and lax.ppermute only.
A program may use at most 128 MiB of HBM per device.

```python
import math
import jax
import jax.numpy as jnp
from jax import lax

D = 2432
HEAD = 64
HEADS = 20
CH = 16
PATCH = 2
GRID = 24
TXT = 96
STEPS = 28
HW = 1280
LAT = 48
PATCHC = 64
N_COL = 2


def level_of(key, dims, cuts, low, largest):
    loudness, own = 1.0, jax.random.fold_in(key, 6)
    for axis_at, blocks in cuts:
        steps = jnp.exp(jax.random.uniform(jax.random.fold_in(own, axis_at), (blocks,), jnp.float32, low / len(cuts), largest / len(cuts)))
        loudness = loudness * jnp.repeat(steps, dims[axis_at] // blocks).reshape([-1 if axis == axis_at else 1 for axis in range(len(dims))])
    return loudness


def normal_values(stream_key, shape, scale, most, split=(), held_as=jnp.bfloat16):
    values = jax.random.normal(stream_key, shape, jnp.float32) * scale
    if len(split) > 0:
        values = level_of(stream_key, shape, split, -0.22, 0.18) * values
    return jnp.clip(values, min=-most, max=most).astype(held_as)


def setup_inputs(seed: int = 0, part: int = 0) -> dict:
    streams_of = jax.random.split(jax.random.key(seed), 13)
    part_keys = jax.random.split(jax.random.fold_in(streams_of[12], part), 13)
    return {
        "image_qkv": normal_values(part_keys[0], (GRID, GRID, 3, HW), 1.0, 6.0, ((0, 2), (1, 2))),
        "text_kv": normal_values(part_keys[1], (TXT, 2, HW), 1.0, 6.0, ((0, 2), (2, 2))),
        "gain_query": jnp.clip(jnp.exp(jax.random.uniform(streams_of[2], (HEAD,), jnp.float32, math.log(1.0), math.log(3.0))), 1.0, 3.0),
        "gain_key": jnp.clip(jnp.exp(jax.random.uniform(streams_of[3], (HEAD,), jnp.float32, math.log(1.0), math.log(3.0))), 1.0, 3.0),
        "gain_text": jnp.clip(jnp.exp(jax.random.uniform(streams_of[4], (HEAD,), jnp.float32, math.log(1.0), math.log(3.0))), 1.0, 3.0),
        "out_weight": normal_values(streams_of[5], (HW, D), HW ** -0.5, 0.15625, ((0, 2), (1, 2))),
        "final_weight": normal_values(streams_of[6], (PATCHC, D), D ** -0.5, 0.125, ((1, 2),)),
        "hidden": normal_values(part_keys[7], (GRID, GRID, D), 1.0, 6.0, ((0, 2), (1, 2))),
        "modulation": normal_values(part_keys[8], (3, D), 0.5, 3.0, (), jnp.float32),
        "latent": normal_values(part_keys[9], (LAT, LAT * CH), 1.0, 6.0, ((0, 2), (1, 2)), jnp.float32),
        "step_index": jax.random.randint(part_keys[10], (1,), 0, 21).astype(jnp.int32),
        "step_count": jax.random.randint(part_keys[11], (1,), 1, 6).astype(jnp.int32),
    }


SHIFT_FACTOR = 3.0

def head_rmsnorm(head_block, gain_vector):
    block_shape = head_block.shape
    width_head = gain_vector.shape[0]
    split_heads = head_block.astype(jnp.float32).reshape(block_shape[:-1] + (block_shape[-1] // width_head, width_head))
    inverse = lax.rsqrt(lax.optimization_barrier(jnp.mean(split_heads * split_heads, axis=-1, keepdims=True)) + 1e-06)
    return (split_heads * inverse * gain_vector).reshape(block_shape).astype(jnp.bfloat16)

def noise_level(step_number):
    fraction = 1.0 - step_number.astype(jnp.float32) / STEPS
    return SHIFT_FACTOR * fraction / (1.0 + (SHIFT_FACTOR - 1.0) * fraction)

def reference(image_qkv, text_kv, gain_query, gain_key, gain_text, out_weight, final_weight, hidden, modulation, latent, step_index, step_count):
    tokens_all = GRID * GRID
    queries = head_rmsnorm(image_qkv[:, :, 0], gain_query).reshape(tokens_all, HEADS, HEAD)
    key_rows = jnp.concatenate([head_rmsnorm(image_qkv[:, :, 1], gain_key).reshape(tokens_all, HEADS, HEAD), head_rmsnorm(text_kv[:, 0], gain_text).reshape(TXT, HEADS, HEAD)], axis=0)
    value_rows = jnp.concatenate([image_qkv[:, :, 2].reshape(tokens_all, HEADS, HEAD), text_kv[:, 1].reshape(TXT, HEADS, HEAD)], axis=0)
    score_scale = 1.0 / math.sqrt(HEAD)

    def single_head(operands):
        query_head, key_head, value_head = operands
        scores = jnp.dot(query_head, key_head.T, preferred_element_type=jnp.float32) * score_scale
        weights = jnp.exp(scores).astype(jnp.bfloat16)
        weighted = jnp.dot(weights, value_head, preferred_element_type=jnp.float32)
        totals = lax.optimization_barrier(jnp.sum(weights.astype(jnp.float32), axis=-1, keepdims=True))
        return (weighted / totals).astype(jnp.bfloat16)
    attended = lax.map(single_head, (queries.transpose(1, 0, 2), key_rows.transpose(1, 0, 2), value_rows.transpose(1, 0, 2)))
    attended = attended.transpose(1, 0, 2).reshape(tokens_all, HEADS * HEAD)
    group_width = HEADS * HEAD // N_COL
    projected = jnp.zeros((tokens_all, D), jnp.float32)
    for member in range(N_COL):
        product = jnp.dot(attended[:, member * group_width:(member + 1) * group_width], out_weight[member * group_width:(member + 1) * group_width], preferred_element_type=jnp.float32)
        projected = projected + lax.optimization_barrier(product.astype(jnp.bfloat16)).astype(jnp.float32)
    mixed = hidden.reshape(tokens_all, D).astype(jnp.float32) + modulation[2] * projected
    row_mean = lax.optimization_barrier(jnp.mean(mixed, axis=-1, keepdims=True))
    centered = mixed - row_mean
    row_var = lax.optimization_barrier(jnp.mean(centered * centered, axis=-1, keepdims=True))
    normed = (centered * lax.rsqrt(row_var + 1e-06) * (1.0 + modulation[1]) + modulation[0]).astype(jnp.bfloat16)
    velocity = jnp.dot(normed, final_weight.T, preferred_element_type=jnp.float32)
    velocity = velocity.reshape(GRID, GRID, PATCH, PATCH, CH).transpose(0, 2, 1, 3, 4).reshape(GRID * PATCH, GRID * PATCH * CH)
    euler_step = noise_level(step_index[0] + step_count[0]) - noise_level(step_index[0])
    return (velocity, latent + euler_step * velocity)
```

```python
import functools
import math

import jax
import jax.numpy as jnp
from jax import lax
from jax.experimental import pallas as pl
from jax.experimental.pallas import tpu as pltpu
from jax.sharding import PartitionSpec as P

HEAD = 64
CH = 16
PATCH = 2
STEPS = 28
SHIFT_FACTOR = 3.0
LANES = 128
EPS = 1e-06
VMEM_LIMIT = 48 * 1024 * 1024
SWAP = [(0, 1), (1, 0)]


def noise_level(step_number):
    fraction = 1.0 - step_number.astype(jnp.float32) / STEPS
    return SHIFT_FACTOR * fraction / (1.0 + (SHIFT_FACTOR - 1.0) * fraction)


def same_head(width):
    row = lax.broadcasted_iota(jnp.int32, (width, width), 0) // HEAD
    col = lax.broadcasted_iota(jnp.int32, (width, width), 1) // HEAD
    return (row == col).astype(jnp.bfloat16)


def head_norm(x, gain):
    square = x * x
    high = square.astype(jnp.bfloat16)
    low = (square - high.astype(jnp.float32)).astype(jnp.bfloat16)
    ones = same_head(LANES)
    pieces = []
    for at in range(0, x.shape[1], LANES):
        total = jnp.dot(high[:, at : at + LANES], ones, preferred_element_type=jnp.float32)
        total += jnp.dot(low[:, at : at + LANES], ones, preferred_element_type=jnp.float32)
        inverse = lax.rsqrt(total * (1.0 / HEAD) + EPS)
        pieces.append((x[:, at : at + LANES] * inverse * gain).astype(jnp.bfloat16))
    return jnp.concatenate(pieces, axis=1)


def prep_other_kernel(x_ref, gains_ref, kv_ref, q_ref, held, sem):
    tokens, _, width = held.shape
    at = pl.multiple_of((1 - lax.axis_index("col")) * width, LANES)
    copy = pltpu.make_async_copy(x_ref.at[:, :, pl.ds(at, width)], held, sem)
    copy.start()
    copy.wait()
    x = held[...].astype(jnp.float32)
    kv_ref[:tokens] = head_norm(x[:, 1], gains_ref[1:2])
    kv_ref[tokens:] = x[:, 2].astype(jnp.bfloat16)
    q_ref[...] = head_norm(x[:, 0], gains_ref[0:1])


def prep_own_kernel(x_ref, text_ref, gains_ref, kvt_ref, q_ref, held, sem):
    tokens, _, width = held.shape
    words = text_ref.shape[0]
    keys = tokens + words
    at = pl.multiple_of(lax.axis_index("col") * width, LANES)
    copy = pltpu.make_async_copy(x_ref.at[:, :, pl.ds(at, width)], held, sem)
    copy.start()
    text = text_ref[...].astype(jnp.float32)
    kvt_ref[tokens:keys] = head_norm(text[:, 0], gains_ref[2:3])
    kvt_ref[keys + tokens :] = text[:, 1].astype(jnp.bfloat16)
    copy.wait()
    x = held[...].astype(jnp.float32)
    kvt_ref[:tokens] = head_norm(x[:, 1], gains_ref[1:2])
    kvt_ref[keys : keys + tokens] = x[:, 2].astype(jnp.bfloat16)
    q_ref[...] = head_norm(x[:, 0], gains_ref[0:1])


def attend(q, key_refs, attended_ref):
    tokens, width = q.shape
    first = lax.broadcasted_iota(jnp.int32, (tokens, LANES), 1) < HEAD
    scale = math.log2(math.e) / math.sqrt(HEAD)
    zero = jnp.zeros((tokens, LANES), jnp.bfloat16)
    total_keys = sum(ref.shape[0] // 2 for ref in key_refs)
    ones = jnp.ones((total_keys, LANES), jnp.bfloat16)
    for at in range(0, width, LANES):
        lanes = slice(at, at + LANES)
        keys = jnp.concatenate([ref[: ref.shape[0] // 2, lanes] for ref in key_refs], axis=0)
        values = jnp.concatenate([ref[ref.shape[0] // 2 :, lanes] for ref in key_refs], axis=0)
        block = q[:, lanes]
        both = jnp.concatenate(
            [jnp.where(first, block, zero), jnp.where(first, zero, block)], axis=0
        )
        scores = lax.dot_general(
            both, keys, (((1,), (1,)), ((), ())), preferred_element_type=jnp.float32
        )
        weights = jnp.exp2(scores * scale).astype(jnp.bfloat16)
        out = jnp.dot(
            weights,
            jnp.concatenate([values, ones], axis=1),
            preferred_element_type=jnp.float32,
        )
        ratio = out[:, :LANES] / out[:, LANES:]
        attended_ref[:, lanes] = jnp.where(first, ratio[:tokens], ratio[tokens:]).astype(
            jnp.bfloat16
        )


def project(attended, weight_ref, store, step):
    features = weight_ref.shape[0]
    for at in range(0, features, step):
        upto = min(at + step, features)
        product = lax.dot_general(
            attended,
            weight_ref[at:upto],
            (((1,), (1,)), ((), ())),
            preferred_element_type=jnp.float32,
        )
        store(at, upto, product.astype(jnp.bfloat16))


def group_kernel(q_ref, a_ref, b_ref, c_ref, d_ref, w_ref, out_ref, weight, attended, sem):
    copy = pltpu.make_async_copy(w_ref, weight, sem)
    copy.start()
    attend(q_ref[...], [a_ref, b_ref, c_ref, d_ref], attended)
    copy.wait()

    def store(at, upto, product):
        out_ref[:, at:upto] = product

    project(attended[...], weight, store, 640)


def own_kernel(
    q_ref, a_ref, b_ref, c_ref, d_ref, w_ref, hidden_ref, mod_ref, out_ref, weight, attended, sem
):
    copy = pltpu.make_async_copy(w_ref, weight, sem)
    copy.start()
    attend(q_ref[...], [a_ref, b_ref, c_ref, d_ref], attended)
    copy.wait()
    tile_rows, tile_cols, _ = hidden_ref.shape

    def store(at, upto, product):
        part = mod_ref[2:3, at:upto] * product.astype(jnp.float32)
        held = jnp.concatenate(
            [hidden_ref[row, :, at:upto].astype(jnp.float32) for row in range(tile_rows)], axis=0
        )
        out_ref[:, at:upto] = held + part

    project(attended[...], weight, store, 640)


def final_kernel(mixed_ref, got_ref, mod_ref, final_ref, out_ref):
    mixed = mixed_ref[...] + mod_ref[2:3] * got_ref[...].astype(jnp.float32)
    mean = jnp.mean(mixed, axis=-1, keepdims=True)
    centered = mixed - mean
    var = jnp.mean(centered * centered, axis=-1, keepdims=True)
    normed = (
        centered * lax.rsqrt(var + EPS) * (1.0 + mod_ref[1:2]) + mod_ref[0:1]
    ).astype(jnp.bfloat16)
    out_ref[...] = lax.dot_general(
        normed, final_ref[...], (((1,), (1,)), ((), ())), preferred_element_type=jnp.float32
    )


def params():
    return pltpu.CompilerParams(vmem_limit_bytes=VMEM_LIMIT)


def shape(dims, dtype=jnp.bfloat16):
    return jax.ShapeDtypeStruct(dims, dtype)


VMEM = pl.BlockSpec(memory_space=pltpu.VMEM)
ANY = pl.BlockSpec(memory_space=pl.ANY)


def on_device(
    image_qkv,
    text_kv,
    gain_query,
    gain_key,
    gain_text,
    out_weight,
    final_weight,
    hidden,
    modulation,
    latent,
    step_index,
    step_count,
):
    tile_rows, tile_cols, _, all_width = image_qkv.shape
    tokens = tile_rows * tile_cols
    words = text_kv.shape[0]
    width = all_width // lax.axis_size("col")
    weight = lax.all_gather(out_weight.T, "row", axis=0, tiled=True)
    finals = lax.all_gather(final_weight, "row", axis=1, tiled=True)
    features = weight.shape[0]
    gains = jnp.stack([gain_query, gain_key, gain_text])
    gains = jnp.concatenate([gains, gains], axis=1)
    x = image_qkv.reshape(tokens, 3, all_width)

    kv_sent, q_sent = pl.pallas_call(
        prep_other_kernel,
        out_shape=(shape((2 * tokens, width)), shape((tokens, width))),
        in_specs=[ANY, VMEM],
        out_specs=(VMEM, VMEM),
        scratch_shapes=[pltpu.VMEM((tokens, 3, width), jnp.bfloat16), pltpu.SemaphoreType.DMA],
        compiler_params=params(),
        name="prep_other",
    )(x, gains)
    kv_got = lax.ppermute(kv_sent, "col", SWAP)
    q_got = lax.ppermute(q_sent, "col", SWAP)
    kvt, q_own = pl.pallas_call(
        prep_own_kernel,
        out_shape=(shape((2 * (tokens + words), width)), shape((tokens, width))),
        in_specs=[ANY, VMEM, VMEM],
        out_specs=(VMEM, VMEM),
        scratch_shapes=[pltpu.VMEM((tokens, 3, width), jnp.bfloat16), pltpu.SemaphoreType.DMA],
        compiler_params=params(),
        name="prep_own",
    )(x, text_kv, gains)
    kvt_row = lax.ppermute(kvt, "row", SWAP)
    kv_got_row = lax.ppermute(kv_got, "row", SWAP)

    flops = 2 * tokens * width * (2 * 2 * (tokens * 4 + words * 2) + features)
    scratch = [
        pltpu.VMEM((features, width), jnp.bfloat16),
        pltpu.VMEM((tokens, width), jnp.bfloat16),
        pltpu.SemaphoreType.DMA,
    ]
    estimate = pl.CostEstimate(
        flops=flops, bytes_accessed=features * width * 2, transcendentals=0
    )
    group = pl.pallas_call(
        group_kernel,
        out_shape=shape((tokens, features)),
        in_specs=[VMEM] * 5 + [ANY],
        out_specs=VMEM,
        scratch_shapes=scratch,
        compiler_params=params(),
        cost_estimate=estimate,
        name="group",
    )(q_got, kvt, kvt_row, kv_got, kv_got_row, weight)
    group_got = lax.ppermute(group, "col", SWAP)
    mixed = pl.pallas_call(
        own_kernel,
        out_shape=shape((tokens, features), jnp.float32),
        in_specs=[VMEM] * 5 + [ANY, VMEM, VMEM],
        out_specs=VMEM,
        scratch_shapes=scratch,
        compiler_params=params(),
        cost_estimate=estimate,
        name="own",
    )(q_own, kvt, kvt_row, kv_got, kv_got_row, weight, hidden, modulation)
    velocity = pl.pallas_call(
        final_kernel,
        out_shape=shape((tokens, PATCH * PATCH * CH), jnp.float32),
        in_specs=[VMEM] * 4,
        out_specs=VMEM,
        compiler_params=params(),
        name="final",
    )(mixed, group_got, modulation, finals)
    velocity = (
        velocity.reshape(tile_rows, tile_cols, PATCH, PATCH, CH)
        .transpose(0, 2, 1, 3, 4)
        .reshape(tile_rows * PATCH, tile_cols * PATCH * CH)
    )
    euler_step = noise_level(step_index[0] + step_count[0]) - noise_level(step_index[0])
    return (velocity, latent + euler_step * velocity)


def solution(mesh):
    placed = (
        P(("req", "row"), "col", None, None),
        P(("req", "row"), None, "col"),
        P(),
        P(),
        P(),
        P("col", "row"),
        P(None, "row"),
        P(("req", "row"), "col", None),
        P("req", None),
        P(("req", "row"), "col"),
        P("req"),
        P("req"),
    )
    return jax.shard_map(
        on_device,
        mesh=mesh,
        in_specs=placed,
        out_specs=(P(("req", "row"), "col"), P(("req", "row"), "col")),
        check_vma=False,
    )
```

```python
import functools
import math

import jax
import jax.numpy as jnp
from jax import lax
from jax.experimental import pallas as pl
from jax.experimental.pallas import tpu as pltpu
from jax.sharding import PartitionSpec as P

HEAD = 64
CH = 16
PATCH = 2
STEPS = 28
SHIFT_FACTOR = 3.0
LANES = 128
EPS = 1e-06
VMEM_LIMIT = 16 * 1024 * 1024
SWAP = [(0, 1), (1, 0)]


def noise_level(step_number):
    fraction = 1.0 - step_number.astype(jnp.float32) / STEPS
    return SHIFT_FACTOR * fraction / (1.0 + (SHIFT_FACTOR - 1.0) * fraction)


def same_head(width):
    row = lax.broadcasted_iota(jnp.int32, (width, width), 0) // HEAD
    col = lax.broadcasted_iota(jnp.int32, (width, width), 1) // HEAD
    return (row == col).astype(jnp.bfloat16)


def head_norm(x, gain):
    square = x * x
    high = square.astype(jnp.bfloat16)
    low = (square - high.astype(jnp.float32)).astype(jnp.bfloat16)
    ones = same_head(LANES)
    pieces = []
    for at in range(0, x.shape[1], LANES):
        total = jnp.dot(high[:, at : at + LANES], ones, preferred_element_type=jnp.float32)
        total += jnp.dot(low[:, at : at + LANES], ones, preferred_element_type=jnp.float32)
        inverse = lax.rsqrt(total * (1.0 / HEAD) + EPS)
        pieces.append((x[:, at : at + LANES] * inverse * gain).astype(jnp.bfloat16))
    return jnp.concatenate(pieces, axis=1)


def prep_other_kernel(x_ref, gains_ref, out_ref, held, sem):
    tokens, _, width = held.shape
    at = pl.multiple_of((1 - lax.axis_index("col")) * width, LANES)
    copy = pltpu.make_async_copy(x_ref.at[:, :, pl.ds(at, width)], held, sem)
    copy.start()
    copy.wait()
    x = held[...].astype(jnp.float32)
    out_ref[:tokens] = head_norm(x[:, 1], gains_ref[1:2])
    out_ref[tokens : 2 * tokens] = x[:, 2].astype(jnp.bfloat16)
    out_ref[2 * tokens :] = head_norm(x[:, 0], gains_ref[0:1])


def prep_own_kernel(
    x_ref, text_ref, gains_ref, mine_ref, theirs_ref, kvt_ref, q_ref, weight_ref, held, sems
):
    tokens, _, width = held.shape
    words = text_ref.shape[0]
    keys = tokens + words
    at = pl.multiple_of(lax.axis_index("col") * width, LANES)
    copy = pltpu.make_async_copy(x_ref.at[:, :, pl.ds(at, width)], held, sems.at[0])
    copy.start()
    rows = mine_ref.shape[0]
    row = lax.axis_index("row")
    stacks = [
        pltpu.make_async_copy(
            ref, weight_ref.at[pl.ds(pl.multiple_of(place * rows, 16), rows)], sems.at[1 + at]
        )
        for at, (ref, place) in enumerate(((mine_ref, row), (theirs_ref, 1 - row)))
    ]
    for stack in stacks:
        stack.start()
    text = text_ref[...].astype(jnp.float32)
    kvt_ref[tokens:keys] = head_norm(text[:, 0], gains_ref[2:3])
    kvt_ref[keys + tokens :] = text[:, 1].astype(jnp.bfloat16)
    copy.wait()
    x = held[...].astype(jnp.float32)
    kvt_ref[:tokens] = head_norm(x[:, 1], gains_ref[1:2])
    kvt_ref[keys : keys + tokens] = x[:, 2].astype(jnp.bfloat16)
    q_ref[...] = head_norm(x[:, 0], gains_ref[0:1])
    for stack in stacks:
        stack.wait()


def attend(q, key_pairs, store):
    tokens, width = q.shape
    first = lax.broadcasted_iota(jnp.int32, (tokens, LANES), 1) < HEAD
    scale = math.log2(math.e) / math.sqrt(HEAD)
    zero = jnp.zeros((tokens, LANES), jnp.bfloat16)
    total_keys = sum(keys.shape[0] for keys, _ in key_pairs)
    ones = jnp.ones((total_keys, LANES), jnp.bfloat16)
    for at in range(0, width, LANES):
        lanes = slice(at, at + LANES)
        keys = jnp.concatenate([pair[0][:, lanes] for pair in key_pairs], axis=0)
        values = jnp.concatenate([pair[1][:, lanes] for pair in key_pairs], axis=0)
        block = q[:, lanes]
        both = jnp.concatenate(
            [jnp.where(first, block, zero), jnp.where(first, zero, block)], axis=0
        )
        scores = lax.dot_general(
            both, keys, (((1,), (1,)), ((), ())), preferred_element_type=jnp.float32
        )
        weights = jnp.exp2(scores * scale).astype(jnp.bfloat16)
        out = jnp.dot(
            weights,
            jnp.concatenate([values, ones], axis=1),
            preferred_element_type=jnp.float32,
        )
        store(
            lanes,
            jnp.where(first, out[:tokens, :LANES], out[tokens:, :LANES]),
            jnp.where(first, out[:tokens, LANES:], out[tokens:, LANES:]),
        )


def halves(ref):
    keys = ref.shape[0] // 2
    return ref.at[:keys], ref.at[keys:]


def project(attended, weight_ref, store, step):
    features = weight_ref.shape[0]
    for at in range(0, features, step):
        upto = min(at + step, features)
        product = lax.dot_general(
            attended,
            weight_ref[at:upto],
            (((1,), (1,)), ((), ())),
            preferred_element_type=jnp.float32,
        )
        store(at, upto, product.astype(jnp.bfloat16))


def partial_kernel(got_ref, a_ref, b_ref, sum_ref, total_ref):
    tokens = got_ref.shape[0] // 3

    def store(lanes, weighted, total):
        sum_ref[:, lanes] = weighted
        total_ref[:, lanes] = total

    pairs = [halves(a_ref), halves(b_ref), (got_ref.at[:tokens], got_ref.at[tokens : 2 * tokens])]
    attend(got_ref[2 * tokens :], pairs, store)


def group_kernel(start, upto, got_ref, d_ref, sum_ref, total_ref, w_ref, out_ref, attended):
    tokens = got_ref.shape[0] // 3

    def store(lanes, weighted, total):
        attended[:, lanes] = (
            (weighted + sum_ref[start:upto, lanes]) / (total + total_ref[start:upto, lanes])
        ).astype(jnp.bfloat16)

    attend(got_ref[2 * tokens + start : 2 * tokens + upto], [halves(d_ref)], store)

    def keep(at, upto, product):
        out_ref[:, at:upto] = product

    project(attended[...], w_ref, keep, 640)


def own_kernel(
    q_ref, a_ref, b_ref, c_ref, d_ref, w_ref, hidden_ref, mod_ref, out_ref, attended
):
    tokens = q_ref.shape[0]

    def store(lanes, weighted, total):
        attended[:, lanes] = (weighted / total).astype(jnp.bfloat16)

    pairs = [
        halves(a_ref),
        halves(b_ref),
        (c_ref.at[:tokens], c_ref.at[tokens : 2 * tokens]),
        halves(d_ref),
    ]
    attend(q_ref[...], pairs, store)
    tile_rows, tile_cols, _ = hidden_ref.shape

    def keep(at, upto, product):
        part = mod_ref[2:3, at:upto] * product.astype(jnp.float32)
        held = jnp.concatenate(
            [hidden_ref[row, :, at:upto].astype(jnp.float32) for row in range(tile_rows)], axis=0
        )
        out_ref[:, at:upto] = held + part

    project(attended[...], w_ref, keep, 640)


def final_kernel(start, mixed_ref, got_ref, mod_ref, final_ref, out_ref):
    upto = start + got_ref.shape[0]
    mixed = mixed_ref[start:upto] + mod_ref[2:3] * got_ref[...].astype(jnp.float32)
    mean = jnp.mean(mixed, axis=-1, keepdims=True)
    centered = mixed - mean
    var = jnp.mean(centered * centered, axis=-1, keepdims=True)
    normed = (
        centered * lax.rsqrt(var + EPS) * (1.0 + mod_ref[1:2]) + mod_ref[0:1]
    ).astype(jnp.bfloat16)
    out_ref[...] = lax.dot_general(
        normed, final_ref[...], (((1,), (1,)), ((), ())), preferred_element_type=jnp.float32
    )


def params():
    return pltpu.CompilerParams(vmem_limit_bytes=VMEM_LIMIT)


def shape(dims, dtype=jnp.bfloat16):
    return jax.ShapeDtypeStruct(dims, dtype)


VMEM = pl.BlockSpec(memory_space=pltpu.VMEM)
ANY = pl.BlockSpec(memory_space=pl.ANY)


def on_device(
    image_qkv,
    text_kv,
    gain_query,
    gain_key,
    gain_text,
    out_weight,
    final_weight,
    hidden,
    modulation,
    latent,
    step_index,
    step_count,
):
    tile_rows, tile_cols, _, all_width = image_qkv.shape
    tokens = tile_rows * tile_cols
    words = text_kv.shape[0]
    width = all_width // lax.axis_size("col")
    features = hidden.shape[2]
    row_first = lax.axis_index("row") == 0
    gains = jnp.stack([gain_query, gain_key, gain_text])
    gains = jnp.concatenate([gains, gains], axis=1)
    x = image_qkv.reshape(tokens, 3, all_width)
    weight_half = out_weight.T
    held = pltpu.VMEM((tokens, 3, width), jnp.bfloat16)

    sent = pl.pallas_call(
        prep_other_kernel,
        out_shape=shape((3 * tokens, width)),
        in_specs=[ANY, VMEM],
        out_specs=VMEM,
        scratch_shapes=[held, pltpu.SemaphoreType.DMA],
        compiler_params=params(),
        name="prep_other",
    )(x, gains)
    got = lax.ppermute(sent, "col", SWAP)
    weight_got = lax.ppermute(weight_half, "row", SWAP)
    final_got = lax.ppermute(final_weight, "row", SWAP)
    finals = jnp.concatenate(
        [
            jnp.where(row_first, final_weight, final_got),
            jnp.where(row_first, final_got, final_weight),
        ],
        axis=1,
    )
    kvt, q_own, weight = pl.pallas_call(
        prep_own_kernel,
        out_shape=(
            shape((2 * (tokens + words), width)),
            shape((tokens, width)),
            shape((features, width)),
        ),
        in_specs=[ANY, VMEM, VMEM, ANY, ANY],
        out_specs=(VMEM, VMEM, VMEM),
        scratch_shapes=[held, pltpu.SemaphoreType.DMA((3,))],
        compiler_params=params(),
        name="prep_own",
    )(x, text_kv, gains, weight_half, weight_got)
    kvt_row = lax.ppermute(kvt, "row", SWAP)
    got_row = lax.ppermute(got[: 2 * tokens], "row", SWAP)

    def cost(queries, keys, projected):
        return pl.CostEstimate(
            flops=2 * queries * width * (4 * keys + (features if projected else 0)),
            bytes_accessed=features * width * 2,
            transcendentals=0,
        )

    sums, totals = pl.pallas_call(
        partial_kernel,
        out_shape=(shape((tokens, width), jnp.float32),) * 2,
        in_specs=[VMEM] * 3,
        out_specs=(VMEM, VMEM),
        compiler_params=params(),
        cost_estimate=cost(tokens, 3 * tokens + 2 * words, False),
        name="partial",
    )(got, kvt, kvt_row)
    cut = (tokens // 2 + 15) // 16 * 16
    chunks = ((0, cut), (cut, tokens))
    returned = []
    for start, upto in chunks:
        group = pl.pallas_call(
            functools.partial(group_kernel, start, upto),
            out_shape=shape((upto - start, features)),
            in_specs=[VMEM] * 5,
            out_specs=VMEM,
            scratch_shapes=[pltpu.VMEM((upto - start, width), jnp.bfloat16)],
            compiler_params=params(),
            cost_estimate=cost(upto - start, tokens, True),
            name="group",
        )(got, got_row, sums, totals, weight)
        returned.append(lax.ppermute(group, "col", SWAP))
    mixed = pl.pallas_call(
        own_kernel,
        out_shape=shape((tokens, features), jnp.float32),
        in_specs=[VMEM] * 8,
        out_specs=VMEM,
        scratch_shapes=[pltpu.VMEM((tokens, width), jnp.bfloat16)],
        compiler_params=params(),
        cost_estimate=cost(tokens, 4 * tokens + 2 * words, True),
        name="own",
    )(q_own, kvt, kvt_row, got, got_row, weight, hidden, modulation)
    velocity = jnp.concatenate(
        [
            pl.pallas_call(
                functools.partial(final_kernel, start),
                out_shape=shape((upto - start, PATCH * PATCH * CH), jnp.float32),
                in_specs=[VMEM] * 4,
                out_specs=VMEM,
                compiler_params=params(),
                name="final",
            )(mixed, part, modulation, finals)
            for (start, upto), part in zip(chunks, returned)
        ],
        axis=0,
    )
    velocity = (
        velocity.reshape(tile_rows, tile_cols, PATCH, PATCH, CH)
        .transpose(0, 2, 1, 3, 4)
        .reshape(tile_rows * PATCH, tile_cols * PATCH * CH)
    )
    euler_step = noise_level(step_index[0] + step_count[0]) - noise_level(step_index[0])
    return (velocity, latent + euler_step * velocity)


def solution(mesh):
    placed = (
        P(("req", "row"), "col", None, None),
        P(("req", "row"), None, "col"),
        P(),
        P(),
        P(),
        P("col", "row"),
        P(None, "row"),
        P(("req", "row"), "col", None),
        P("req", None),
        P(("req", "row"), "col"),
        P("req"),
        P("req"),
    )
    return jax.shard_map(
        on_device,
        mesh=mesh,
        in_specs=placed,
        out_specs=(P(("req", "row"), "col"), P(("req", "row"), "col")),
        check_vma=False,
    )
```

```python
import functools
import math

import jax
import jax.numpy as jnp
from jax import lax
from jax.experimental import pallas as pl
from jax.experimental.pallas import tpu as pltpu
from jax.sharding import PartitionSpec as P

HEAD = 64
CH = 16
PATCH = 2
STEPS = 28
SHIFT_FACTOR = 3.0
LANES = 128
EPS = 1e-06
VMEM_LIMIT = 16 * 1024 * 1024
VMEM_MOST = 60 * 1024 * 1024
LOADS = 3
FIRST = 1280
SWAP = [(0, 1), (1, 0)]


def noise_level(step_number):
    fraction = 1.0 - step_number.astype(jnp.float32) / STEPS
    return SHIFT_FACTOR * fraction / (1.0 + (SHIFT_FACTOR - 1.0) * fraction)


def same_head(width):
    row = lax.broadcasted_iota(jnp.int32, (width, width), 0) // HEAD
    col = lax.broadcasted_iota(jnp.int32, (width, width), 1) // HEAD
    return (row == col).astype(jnp.bfloat16)


def head_norm(x, gain):
    square = x * x
    high = square.astype(jnp.bfloat16)
    low = (square - high.astype(jnp.float32)).astype(jnp.bfloat16)
    ones = same_head(LANES)
    both = jnp.concatenate([ones, ones], axis=0)
    gain = jnp.concatenate([gain, gain], axis=1)
    pieces = []
    for at in range(0, x.shape[1], LANES):
        lanes = slice(at, at + LANES)
        total = jnp.dot(
            jnp.concatenate([high[:, lanes], low[:, lanes]], axis=1),
            both,
            preferred_element_type=jnp.float32,
        )
        inverse = lax.rsqrt(total * (1.0 / HEAD) + EPS)
        pieces.append((x[:, lanes] * inverse * gain).astype(jnp.bfloat16))
    return jnp.concatenate(pieces, axis=1)


def load_half(x_ref, held, sems, column):
    tokens, _, width = held.shape
    at = pl.multiple_of(column * width, LANES)
    step = tokens // sems.shape[0]
    copies = [
        pltpu.make_async_copy(
            x_ref.at[start : start + step, :, pl.ds(at, width)],
            held.at[start : start + step],
            sems.at[start // step],
        )
        for start in range(0, tokens, step)
    ]
    for copy in copies:
        copy.start()
    return [(slice(at * step, at * step + step), copy) for at, copy in enumerate(copies)]


def load_gains(refs, gains, sems):
    copies = [
        pltpu.make_async_copy(ref, gains.at[at : at + 1], sems.at[at])
        for at, ref in enumerate(refs)
    ]
    for copy in copies:
        copy.start()
    return copies


def prep_other_kernel(
    x_ref,
    gain_q_ref,
    gain_k_ref,
    gain_t_ref,
    k_ref,
    v_ref,
    q_ref,
    gains,
    held,
    wide,
    sems,
    gain_sems,
):
    blocks = load_half(x_ref, held, sems, 1 - lax.axis_index("col"))
    for copy in load_gains((gain_q_ref, gain_k_ref, gain_t_ref), gains, gain_sems):
        copy.wait()
    for rows, copy in blocks:
        copy.wait()
        wide[rows] = held[rows].astype(jnp.float32)
        k_ref[rows] = head_norm(wide[rows, 1], gains[1:2])
        v_ref[rows] = wide[rows, 2].astype(jnp.bfloat16)
        q_ref[rows] = head_norm(wide[rows, 0], gains[0:1])


def prep_own_kernel(
    x_ref,
    text_ref,
    gains,
    mine_ref,
    theirs_ref,
    k_ref,
    v_ref,
    q_ref,
    weight_ref,
    held,
    wide,
    sems,
    stack_sems,
):
    tokens = q_ref.shape[0]
    blocks = load_half(x_ref, held, sems, lax.axis_index("col"))
    rows = mine_ref.shape[0]
    row = lax.axis_index("row")
    stacks = [
        pltpu.make_async_copy(
            ref, weight_ref.at[pl.ds(pl.multiple_of(place * rows, 16), rows)], stack_sems.at[at]
        )
        for at, (ref, place) in enumerate(((mine_ref, row), (theirs_ref, 1 - row)))
    ]
    for stack in stacks:
        stack.start()
    text = text_ref[...].astype(jnp.float32)
    k_ref[tokens:] = head_norm(text[:, 0], gains[2:3])
    v_ref[tokens:] = text[:, 1].astype(jnp.bfloat16)
    for rows, copy in blocks:
        copy.wait()
        wide[rows] = held[rows].astype(jnp.float32)
        k_ref[rows] = head_norm(wide[rows, 1], gains[1:2])
        v_ref[rows] = wide[rows, 2].astype(jnp.bfloat16)
        q_ref[rows] = head_norm(wide[rows, 0], gains[0:1])
    for stack in stacks:
        stack.wait()


def attend(q, keys_refs, values_refs, attended_ref):
    tokens, width = q.shape
    first = lax.broadcasted_iota(jnp.int32, (tokens, LANES), 1) < HEAD
    scale = math.log2(math.e) / math.sqrt(HEAD)
    zero = jnp.zeros((tokens, LANES), jnp.bfloat16)
    ones = jnp.ones((sum(ref.shape[0] for ref in keys_refs), LANES), jnp.bfloat16)

    def scores_of(at):
        lanes = slice(at, at + LANES)
        keys = jnp.concatenate([ref[:, lanes] for ref in keys_refs], axis=0)
        block = q[:, lanes]
        both = jnp.concatenate(
            [jnp.where(first, block, zero), jnp.where(first, zero, block)], axis=0
        )
        return lax.dot_general(
            both, keys, (((1,), (1,)), ((), ())), preferred_element_type=jnp.float32
        )

    def finish(at, scores):
        lanes = slice(at, at + LANES)
        values = jnp.concatenate([ref[:, lanes] for ref in values_refs], axis=0)
        weights = jnp.exp2(scores * scale).astype(jnp.bfloat16)
        out = jnp.dot(
            weights,
            jnp.concatenate([values, ones], axis=1),
            preferred_element_type=jnp.float32,
        )
        weighted = jnp.where(first, out[:tokens, :LANES], out[tokens:, :LANES])
        total = jnp.where(first, out[:tokens, LANES:], out[tokens:, LANES:])
        attended_ref[:, lanes] = (weighted / total).astype(jnp.bfloat16)

    ahead = scores_of(0)
    for at in range(0, width, LANES):
        scores = ahead
        if at + LANES < width:
            ahead = scores_of(at + LANES)
        finish(at, scores)


def project(attended, weight_ref, start, upto, store, step):
    for at in range(start, upto, step):
        to = min(at + step, upto)
        product = lax.dot_general(
            attended,
            weight_ref[at:to],
            (((1,), (1,)), ((), ())),
            preferred_element_type=jnp.float32,
        )
        store(at, to, product.astype(jnp.bfloat16))


def group_first_kernel(*refs):
    q_ref, keys, values, (w_ref, out_ref, attended_ref) = refs[0], refs[1:5], refs[5:9], refs[9:]
    attend(q_ref[...], keys, values, attended_ref)

    def keep(at, to, product):
        out_ref[:, at:to] = product

    project(attended_ref[...], w_ref, 0, out_ref.shape[1], keep, 640)


def group_second_kernel(attended_ref, w_ref, out_ref):
    features = w_ref.shape[0]
    start = features - out_ref.shape[1]

    def keep(at, to, product):
        out_ref[:, at - start : to - start] = product

    project(attended_ref[...], w_ref, start, features, keep, 640)


def own_kernel(*refs):
    q_ref, keys, values = refs[0], refs[1:5], refs[5:9]
    w_ref, hidden_ref, mod_ref, mine_ref, theirs_ref, out_ref, finals_ref, attended = refs[9:]
    attend(q_ref[...], keys, values, attended)
    tile_rows = hidden_ref.shape[0]

    def keep(at, to, product):
        part = mod_ref[2:3, at:to] * product.astype(jnp.float32)
        held = jnp.concatenate(
            [hidden_ref[row, :, at:to].astype(jnp.float32) for row in range(tile_rows)], axis=0
        )
        out_ref[:, at:to] = held + part

    project(attended[...], w_ref, 0, w_ref.shape[0], keep, 640)
    is_first = lax.axis_index("row") == 0
    mine = mine_ref[...].astype(jnp.float32)
    theirs = theirs_ref[...].astype(jnp.float32)
    finals_ref[...] = jnp.concatenate(
        [jnp.where(is_first, mine, theirs), jnp.where(is_first, theirs, mine)], axis=1
    ).astype(jnp.bfloat16)


def one_hot(dims, condition):
    row = lax.broadcasted_iota(jnp.int32, dims, 0)
    col = lax.broadcasted_iota(jnp.int32, dims, 1)
    return jnp.where(condition(row, col), 1.0, 0.0).astype(jnp.bfloat16)


def to_pixels(velocity, tile_cols):
    tokens, values = velocity.shape
    side = values // PATCH
    out_rows, out_lanes = tokens // tile_cols * PATCH, tile_cols * side
    terms, rest = [], velocity
    for _ in range(3):
        term = rest.astype(jnp.bfloat16)
        rest = rest - term.astype(jnp.float32)
        terms.append(term)
    terms = jnp.concatenate(terms, axis=0)
    row = lax.broadcasted_iota(jnp.int32, (3 * tokens, out_lanes), 0)
    col = lax.broadcasted_iota(jnp.int32, (3 * tokens, out_lanes), 1)
    here = col // side == row % tile_cols
    total = jnp.zeros((out_rows, out_lanes), jnp.float32)
    for at in range(PATCH):
        spread = one_hot((values, out_lanes), lambda r, c: r == c % side + at * side)
        wide = jnp.dot(terms, spread, preferred_element_type=jnp.float32)
        wide = jnp.where(here, wide, 0.0).astype(jnp.bfloat16)
        pick = one_hot(
            (out_rows, 3 * tokens), lambda r, c: r == c % tokens // tile_cols * PATCH + at
        )
        total += jnp.dot(pick, wide, preferred_element_type=jnp.float32)
    return total


def final_kernel(
    index_ref,
    count_ref,
    mixed_ref,
    first_ref,
    second_ref,
    mod_ref,
    final_ref,
    latent_ref,
    velocity_ref,
    next_ref,
):
    tokens = mixed_ref.shape[0]
    step = tokens // 3
    parts = []
    for start in range(0, tokens, step):
        rows = slice(start, start + step)
        got = jnp.concatenate([first_ref[rows], second_ref[rows]], axis=1).astype(jnp.float32)
        mixed = mixed_ref[rows] + mod_ref[2:3] * got
        mean = jnp.mean(mixed, axis=-1, keepdims=True)
        centered = mixed - mean
        var = jnp.mean(centered * centered, axis=-1, keepdims=True)
        normed = (
            centered * lax.rsqrt(var + EPS) * (1.0 + mod_ref[1:2]) + mod_ref[0:1]
        ).astype(jnp.bfloat16)
        parts.append(
            lax.dot_general(
                normed,
                final_ref[...],
                (((1,), (1,)), ((), ())),
                preferred_element_type=jnp.float32,
            )
        )
    side = final_ref.shape[0] // PATCH
    velocity = to_pixels(jnp.concatenate(parts, axis=0), latent_ref.shape[1] // side)
    index = jnp.full(latent_ref.shape, index_ref[0], jnp.int32)
    count = jnp.full(latent_ref.shape, count_ref[0], jnp.int32)
    euler_step = noise_level(index + count) - noise_level(index)
    velocity_ref[...] = velocity
    next_ref[...] = latent_ref[...] + euler_step * velocity


def params(limit=VMEM_LIMIT):
    return pltpu.CompilerParams(vmem_limit_bytes=limit)


def shape(dims, dtype=jnp.bfloat16):
    return jax.ShapeDtypeStruct(dims, dtype)


VMEM = pl.BlockSpec(memory_space=pltpu.VMEM)
ANY = pl.BlockSpec(memory_space=pl.ANY)
HBM = pl.BlockSpec(memory_space=pltpu.HBM)
SMEM = pl.BlockSpec(memory_space=pltpu.SMEM)


def on_device(
    image_qkv,
    text_kv,
    gain_query,
    gain_key,
    gain_text,
    out_weight,
    final_weight,
    hidden,
    modulation,
    latent,
    step_index,
    step_count,
):
    tile_rows, tile_cols, _, all_width = image_qkv.shape
    tokens = tile_rows * tile_cols
    words = text_kv.shape[0]
    width = all_width // lax.axis_size("col")
    features = hidden.shape[2]
    gains = [gain.reshape(1, HEAD) for gain in (gain_query, gain_key, gain_text)]
    x = image_qkv.reshape(tokens, 3, all_width)
    weight_half = out_weight.T
    held = pltpu.VMEM((tokens, 3, width), jnp.bfloat16)
    wide = pltpu.VMEM((tokens, 3, width), jnp.float32)
    block = shape((tokens, width))

    scratch = [held, wide, pltpu.SemaphoreType.DMA((LOADS,))]
    k_sent, v_sent, q_sent, gains = pl.pallas_call(
        prep_other_kernel,
        out_shape=(block,) * 3 + (shape((len(gains), HEAD), jnp.float32),),
        in_specs=[HBM] * 4,
        out_specs=(VMEM,) * 4,
        scratch_shapes=scratch + [pltpu.SemaphoreType.DMA((len(gains),))],
        compiler_params=params(VMEM_MOST),
        name="prep_other",
    )(x, *gains)
    k_got = lax.ppermute(k_sent, "col", SWAP)
    v_got = lax.ppermute(v_sent, "col", SWAP)
    q_got = lax.ppermute(q_sent, "col", SWAP)
    weight_got = lax.ppermute(weight_half, "row", SWAP)
    final_got = lax.ppermute(final_weight, "row", SWAP)
    k_own, v_own, q_own, weight = pl.pallas_call(
        prep_own_kernel,
        out_shape=(
            shape((tokens + words, width)),
            shape((tokens + words, width)),
            block,
            shape((features, width)),
        ),
        in_specs=[HBM, VMEM, VMEM, ANY, ANY],
        out_specs=(VMEM,) * 4,
        scratch_shapes=scratch + [pltpu.SemaphoreType.DMA((2,))],
        compiler_params=params(),
        name="prep_own",
    )(x, text_kv, gains, weight_half, weight_got)
    keys = [k_own, lax.ppermute(k_own, "row", SWAP), k_got, lax.ppermute(k_got, "row", SWAP)]
    values = [v_own, lax.ppermute(v_own, "row", SWAP), v_got, lax.ppermute(v_got, "row", SWAP)]

    def cost(attended, projected):
        per_query = 4 * attended * (4 * tokens + 2 * words) + projected
        return pl.CostEstimate(
            flops=2 * tokens * width * per_query,
            bytes_accessed=projected * width * 2,
            transcendentals=0,
        )

    first, attended = pl.pallas_call(
        group_first_kernel,
        out_shape=(shape((tokens, FIRST)), block),
        in_specs=[VMEM] * 10,
        out_specs=(VMEM, VMEM),
        compiler_params=params(),
        cost_estimate=cost(1, FIRST),
        name="group_first",
    )(q_got, *keys, *values, weight)
    first_got = lax.ppermute(first, "col", SWAP)
    second = pl.pallas_call(
        group_second_kernel,
        out_shape=shape((tokens, features - FIRST)),
        in_specs=[VMEM] * 2,
        out_specs=VMEM,
        compiler_params=params(),
        cost_estimate=cost(0, features - FIRST),
        name="group_second",
    )(attended, weight)
    second_got = lax.ppermute(second, "col", SWAP)
    mixed, finals = pl.pallas_call(
        own_kernel,
        out_shape=(shape((tokens, features), jnp.float32), shape((final_weight.shape[0], features))),
        in_specs=[VMEM] * 14,
        out_specs=(VMEM, VMEM),
        scratch_shapes=[pltpu.VMEM((tokens, width), jnp.bfloat16)],
        compiler_params=params(),
        cost_estimate=cost(1, features),
        name="own",
    )(q_own, *keys, *values, weight, hidden, modulation, final_weight, final_got)
    return pl.pallas_call(
        final_kernel,
        out_shape=(shape(latent.shape, jnp.float32),) * 2,
        in_specs=[SMEM] * 2 + [VMEM] * 6,
        out_specs=(VMEM, VMEM),
        compiler_params=params(),
        name="final",
    )(step_index, step_count, mixed, first_got, second_got, modulation, finals, latent)


def solution(mesh):
    placed = (
        P(("req", "row"), "col", None, None),
        P(("req", "row"), None, "col"),
        P(),
        P(),
        P(),
        P("col", "row"),
        P(None, "row"),
        P(("req", "row"), "col", None),
        P("req", None),
        P(("req", "row"), "col"),
        P("req"),
        P("req"),
    )
    return jax.shard_map(
        on_device,
        mesh=mesh,
        in_specs=placed,
        out_specs=(P(("req", "row"), "col"), P(("req", "row"), "col")),
        check_vma=False,
    )
```

```python
import functools
import math

import jax
import jax.numpy as jnp
from jax import lax
from jax.experimental import pallas as pl
from jax.experimental.pallas import tpu as pltpu
from jax.sharding import PartitionSpec as P

HEAD = 64
CH = 16
PATCH = 2
STEPS = 28
SHIFT_FACTOR = 3.0
LANES = 128
EPS = 1e-06
VMEM_LIMIT = 16 * 1024 * 1024
VMEM_MOST = 60 * 1024 * 1024
LOADS = 3
SWAP = [(0, 1), (1, 0)]


def noise_level(step_number):
    fraction = 1.0 - step_number.astype(jnp.float32) / STEPS
    return SHIFT_FACTOR * fraction / (1.0 + (SHIFT_FACTOR - 1.0) * fraction)


def same_head(width):
    row = lax.broadcasted_iota(jnp.int32, (width, width), 0) // HEAD
    col = lax.broadcasted_iota(jnp.int32, (width, width), 1) // HEAD
    return (row == col).astype(jnp.bfloat16)


def head_norms(pairs):
    ones = same_head(LANES)
    squares = []
    for x, _ in pairs:
        for at in range(0, x.shape[1], LANES):
            square = x[:, at : at + LANES] * x[:, at : at + LANES]
            high = square.astype(jnp.bfloat16)
            low = (square - high.astype(jnp.float32)).astype(jnp.bfloat16)
            squares.append(jnp.concatenate([high, low], axis=1))
    totals = jnp.dot(
        jnp.concatenate(squares, axis=0),
        jnp.concatenate([ones, ones], axis=0),
        preferred_element_type=jnp.float32,
    )
    inverse = lax.rsqrt(totals * (1.0 / HEAD) + EPS)
    results, start = [], 0
    for x, gain in pairs:
        gain = jnp.concatenate([gain, gain], axis=1)
        pieces = []
        for at in range(0, x.shape[1], LANES):
            factor = inverse[start : start + x.shape[0]]
            pieces.append((x[:, at : at + LANES] * factor * gain).astype(jnp.bfloat16))
            start += x.shape[0]
        results.append(jnp.concatenate(pieces, axis=1))
    return results


def load_half(x_ref, held, sems, column):
    tokens, _, width = held.shape
    at = pl.multiple_of(column * width, LANES)
    step = tokens // sems.shape[0]
    copies = [
        pltpu.make_async_copy(
            x_ref.at[start : start + step, :, pl.ds(at, width)],
            held.at[start : start + step],
            sems.at[start // step],
        )
        for start in range(0, tokens, step)
    ]
    for copy in copies:
        copy.start()
    return [(slice(at * step, at * step + step), copy) for at, copy in enumerate(copies)]


def load_gains(refs, gains, sems):
    copies = [
        pltpu.make_async_copy(ref, gains.at[at : at + 1], sems.at[at])
        for at, ref in enumerate(refs)
    ]
    for copy in copies:
        copy.start()
    return copies


def prep_other_kernel(
    x_ref,
    gain_q_ref,
    gain_k_ref,
    gain_t_ref,
    k_ref,
    v_ref,
    q_ref,
    gains,
    held,
    wide,
    sems,
    gain_sems,
):
    tokens, kinds, width = held.shape
    blocks = load_half(x_ref, held, sems, 1 - lax.axis_index("col"))
    gain_copies = load_gains((gain_q_ref, gain_k_ref, gain_t_ref), gains, gain_sems)
    room = wide.shape[1] // tokens
    for rows, copy in blocks:
        copy.wait()
        for token in range(rows.start, rows.stop):
            x = held[token].astype(jnp.float32)
            for at in range(width // LANES):
                wide[at, room * token : room * token + kinds] = x[:, at * LANES : (at + 1) * LANES]

    def kind(which):
        return jnp.concatenate(
            [
                wide[at, pl.ds(which, tokens, stride=room), :]
                for at in range(width // LANES)
            ],
            axis=1,
        )

    v_ref[...] = kind(2).astype(jnp.bfloat16)
    for copy in gain_copies:
        copy.wait()
    k_ref[...], q_ref[...] = head_norms([(kind(1), gains[1:2]), (kind(0), gains[0:1])])


def prep_own_kernel(
    x_ref,
    text_ref,
    gains,
    mine_ref,
    theirs_ref,
    k_ref,
    v_ref,
    q_ref,
    weight_ref,
    held,
    sems,
    stack_sems,
):
    tokens = q_ref.shape[0]
    blocks = load_half(x_ref, held, sems, lax.axis_index("col"))
    rows = mine_ref.shape[0]
    row = lax.axis_index("row")
    stacks = [
        pltpu.make_async_copy(
            ref, weight_ref.at[pl.ds(pl.multiple_of(place * rows, 16), rows)], stack_sems.at[at]
        )
        for at, (ref, place) in enumerate(((mine_ref, row), (theirs_ref, 1 - row)))
    ]
    for stack in stacks:
        stack.start()
    text = text_ref[...].astype(jnp.float32).transpose(1, 0, 2)
    v_ref[tokens:] = text[1].astype(jnp.bfloat16)
    for _, copy in blocks:
        copy.wait()
    x = held[...].astype(jnp.float32).transpose(1, 0, 2)
    v_ref[:tokens] = x[2].astype(jnp.bfloat16)
    k_ref[:tokens], k_ref[tokens:], q_ref[...] = head_norms(
        [(x[1], gains[1:2]), (text[0], gains[2:3]), (x[0], gains[0:1])]
    )
    for stack in stacks:
        stack.wait()


def attend(q, keys_refs, values_refs, attended_ref):
    tokens, width = q.shape
    first = lax.broadcasted_iota(jnp.int32, (tokens, LANES), 1) < HEAD
    scale = math.log2(math.e) / math.sqrt(HEAD)
    zero = jnp.zeros((tokens, LANES), jnp.bfloat16)
    ones = jnp.ones((sum(ref.shape[0] for ref in keys_refs), LANES), jnp.bfloat16)

    def scores_of(at):
        lanes = slice(at, at + LANES)
        keys = jnp.concatenate([ref[:, lanes] for ref in keys_refs], axis=0)
        block = q[:, lanes]
        both = jnp.concatenate(
            [jnp.where(first, block, zero), jnp.where(first, zero, block)], axis=0
        )
        return lax.dot_general(
            both, keys, (((1,), (1,)), ((), ())), preferred_element_type=jnp.float32
        )

    def finish(at, scores):
        lanes = slice(at, at + LANES)
        values = jnp.concatenate([ref[:, lanes] for ref in values_refs], axis=0)
        weights = jnp.exp2(scores * scale).astype(jnp.bfloat16)
        out = jnp.dot(
            weights,
            jnp.concatenate([values, ones], axis=1),
            preferred_element_type=jnp.float32,
        )
        weighted = jnp.where(first, out[:tokens, :LANES], out[tokens:, :LANES])
        total = jnp.where(first, out[:tokens, LANES:], out[tokens:, LANES:])
        attended_ref[:, lanes] = (weighted / total).astype(jnp.bfloat16)

    ahead = scores_of(0)
    for at in range(0, width, LANES):
        scores = ahead
        if at + LANES < width:
            ahead = scores_of(at + LANES)
        finish(at, scores)


def project(attended, weight_ref, start, upto, store, step):
    for at in range(start, upto, step):
        to = min(at + step, upto)
        product = lax.dot_general(
            attended,
            weight_ref[at:to],
            (((1,), (1,)), ((), ())),
            preferred_element_type=jnp.float32,
        )
        store(at, to, product.astype(jnp.bfloat16))


def group_kernel(start, *refs):
    q_ref, keys, values, (w_ref, out_ref, attended) = refs[0], refs[1:5], refs[5:9], refs[9:]
    attend(q_ref[start : start + out_ref.shape[0]], keys, values, attended)

    def keep(at, to, product):
        out_ref[:, at:to] = product

    project(attended[...], w_ref, 0, w_ref.shape[0], keep, 640)


def own_kernel(*refs):
    q_ref, keys, values = refs[0], refs[1:5], refs[5:9]
    w_ref, hidden_ref, mod_ref, mine_ref, theirs_ref, out_ref, finals_ref, attended = refs[9:]
    attend(q_ref[...], keys, values, attended)
    tile_rows = hidden_ref.shape[0]

    def keep(at, to, product):
        part = mod_ref[2:3, at:to] * product.astype(jnp.float32)
        held = jnp.concatenate(
            [hidden_ref[row, :, at:to].astype(jnp.float32) for row in range(tile_rows)], axis=0
        )
        out_ref[:, at:to] = held + part

    project(attended[...], w_ref, 0, w_ref.shape[0], keep, 640)
    is_first = lax.axis_index("row") == 0
    mine = mine_ref[...].astype(jnp.float32)
    theirs = theirs_ref[...].astype(jnp.float32)
    finals_ref[...] = jnp.concatenate(
        [jnp.where(is_first, mine, theirs), jnp.where(is_first, theirs, mine)], axis=1
    ).astype(jnp.bfloat16)


def one_hot(dims, condition):
    row = lax.broadcasted_iota(jnp.int32, dims, 0)
    col = lax.broadcasted_iota(jnp.int32, dims, 1)
    return jnp.where(condition(row, col), 1.0, 0.0).astype(jnp.bfloat16)


def to_pixels(velocity, tile_cols):
    tokens, values = velocity.shape
    side = values // PATCH
    out_rows, out_lanes = tokens // tile_cols * PATCH, tile_cols * side
    terms, rest = [], velocity
    for _ in range(3):
        term = rest.astype(jnp.bfloat16)
        rest = rest - term.astype(jnp.float32)
        terms.append(term)
    terms = jnp.concatenate(terms, axis=0)
    row = lax.broadcasted_iota(jnp.int32, (3 * tokens, out_lanes), 0)
    col = lax.broadcasted_iota(jnp.int32, (3 * tokens, out_lanes), 1)
    here = col // side == row % tile_cols
    total = jnp.zeros((out_rows, out_lanes), jnp.float32)
    for at in range(PATCH):
        spread = one_hot((values, out_lanes), lambda r, c: r == c % side + at * side)
        wide = jnp.dot(terms, spread, preferred_element_type=jnp.float32)
        wide = jnp.where(here, wide, 0.0).astype(jnp.bfloat16)
        pick = one_hot(
            (out_rows, 3 * tokens), lambda r, c: r == c % tokens // tile_cols * PATCH + at
        )
        total += jnp.dot(pick, wide, preferred_element_type=jnp.float32)
    return total


def final_kernel(
    start,
    index_ref,
    count_ref,
    mixed_ref,
    got_ref,
    mod_ref,
    final_ref,
    latent_ref,
    *refs,
):
    velocity_ref, next_ref = refs[-2:]
    tokens = got_ref.shape[0]
    step = 48
    parts = []
    for at in range(0, tokens, step):
        got = got_ref[at : at + step].astype(jnp.float32)
        mixed = mixed_ref[start + at : start + at + step] + mod_ref[2:3] * got
        mean = jnp.mean(mixed, axis=-1, keepdims=True)
        centered = mixed - mean
        var = jnp.mean(centered * centered, axis=-1, keepdims=True)
        normed = (
            centered * lax.rsqrt(var + EPS) * (1.0 + mod_ref[1:2]) + mod_ref[0:1]
        ).astype(jnp.bfloat16)
        parts.append(
            lax.dot_general(
                normed,
                final_ref[...],
                (((1,), (1,)), ((), ())),
                preferred_element_type=jnp.float32,
            )
        )
    tile_cols = latent_ref.shape[1] // (final_ref.shape[0] // PATCH)
    velocity = to_pixels(jnp.concatenate(parts, axis=0), tile_cols)
    first = start // tile_cols * PATCH
    pixels = slice(first, first + velocity.shape[0])
    index = jnp.full(velocity.shape, index_ref[0], jnp.int32)
    count = jnp.full(velocity.shape, count_ref[0], jnp.int32)
    euler_step = noise_level(index + count) - noise_level(index)
    for before_ref, after_ref in zip(refs[:-2], refs[-2:]):
        after_ref[:first] = before_ref[:first]
    velocity_ref[pixels] = velocity
    next_ref[pixels] = latent_ref[pixels] + euler_step * velocity


def params(limit=VMEM_LIMIT):
    return pltpu.CompilerParams(vmem_limit_bytes=limit)


def shape(dims, dtype=jnp.bfloat16):
    return jax.ShapeDtypeStruct(dims, dtype)


VMEM = pl.BlockSpec(memory_space=pltpu.VMEM)
ANY = pl.BlockSpec(memory_space=pl.ANY)
HBM = pl.BlockSpec(memory_space=pltpu.HBM)
SMEM = pl.BlockSpec(memory_space=pltpu.SMEM)


def on_device(
    image_qkv,
    text_kv,
    gain_query,
    gain_key,
    gain_text,
    out_weight,
    final_weight,
    hidden,
    modulation,
    latent,
    step_index,
    step_count,
):
    tile_rows, tile_cols, _, all_width = image_qkv.shape
    tokens = tile_rows * tile_cols
    words = text_kv.shape[0]
    width = all_width // lax.axis_size("col")
    features = hidden.shape[2]
    gains = [gain.reshape(1, HEAD) for gain in (gain_query, gain_key, gain_text)]
    x = image_qkv.reshape(tokens, 3, all_width)
    weight_half = out_weight.T
    held = pltpu.VMEM((tokens, 3, width), jnp.bfloat16)
    wide = pltpu.VMEM((width // LANES, 4 * tokens, LANES), jnp.float32)
    block = shape((tokens, width))

    loads = pltpu.SemaphoreType.DMA((LOADS,))
    k_sent, v_sent, q_sent, gains = pl.pallas_call(
        prep_other_kernel,
        out_shape=(block,) * 3 + (shape((len(gains), HEAD), jnp.float32),),
        in_specs=[HBM] * 4,
        out_specs=(VMEM,) * 4,
        scratch_shapes=[held, wide, loads, pltpu.SemaphoreType.DMA((len(gains),))],
        compiler_params=params(VMEM_MOST),
        name="prep_other",
    )(x, *gains)
    k_got = lax.ppermute(k_sent, "col", SWAP)
    v_got = lax.ppermute(v_sent, "col", SWAP)
    q_got = lax.ppermute(q_sent, "col", SWAP)
    weight_got = lax.ppermute(weight_half, "row", SWAP)
    final_got = lax.ppermute(final_weight, "row", SWAP)
    k_own, v_own, q_own, weight = pl.pallas_call(
        prep_own_kernel,
        out_shape=(
            shape((tokens + words, width)),
            shape((tokens + words, width)),
            block,
            shape((features, width)),
        ),
        in_specs=[HBM, VMEM, VMEM, ANY, ANY],
        out_specs=(VMEM,) * 4,
        scratch_shapes=[held, loads, pltpu.SemaphoreType.DMA((2,))],
        compiler_params=params(),
        name="prep_own",
    )(x, text_kv, gains, weight_half, weight_got)
    keys = [k_own, lax.ppermute(k_own, "row", SWAP), k_got, lax.ppermute(k_got, "row", SWAP)]
    values = [v_own, lax.ppermute(v_own, "row", SWAP), v_got, lax.ppermute(v_got, "row", SWAP)]

    def cost(queries):
        return pl.CostEstimate(
            flops=2 * queries * width * (4 * (4 * tokens + 2 * words) + features),
            bytes_accessed=features * width * 2,
            transcendentals=0,
        )

    cut = tile_rows // 3 * 2 * tile_cols
    chunks = ((0, cut), (cut, tokens))
    returned = []
    for start, upto in chunks:
        product = pl.pallas_call(
            functools.partial(group_kernel, start),
            out_shape=shape((upto - start, features)),
            in_specs=[VMEM] * 10,
            out_specs=VMEM,
            scratch_shapes=[pltpu.VMEM((upto - start, width), jnp.bfloat16)],
            compiler_params=params(),
            cost_estimate=cost(upto - start),
            name="group",
        )(q_got, *keys, *values, weight)
        returned.append(lax.ppermute(product, "col", SWAP))
    mixed, finals = pl.pallas_call(
        own_kernel,
        out_shape=(shape((tokens, features), jnp.float32), shape((final_weight.shape[0], features))),
        in_specs=[VMEM] * 14,
        out_specs=(VMEM, VMEM),
        scratch_shapes=[pltpu.VMEM((tokens, width), jnp.bfloat16)],
        compiler_params=params(),
        cost_estimate=cost(tokens),
        name="own",
    )(q_own, *keys, *values, weight, hidden, modulation, final_weight, final_got)
    results = ()
    for (start, _), got in zip(chunks, returned):
        results = pl.pallas_call(
            functools.partial(final_kernel, start),
            out_shape=(shape(latent.shape, jnp.float32),) * 2,
            in_specs=[SMEM] * 2 + [VMEM] * (5 + len(results)),
            out_specs=(VMEM, VMEM),
            compiler_params=params(),
            cost_estimate=cost(0),
            name="final",
        )(step_index, step_count, mixed, got, modulation, finals, latent, *results)
    return results


def solution(mesh):
    placed = (
        P(("req", "row"), "col", None, None),
        P(("req", "row"), None, "col"),
        P(),
        P(),
        P(),
        P("col", "row"),
        P(None, "row"),
        P(("req", "row"), "col", None),
        P("req", None),
        P(("req", "row"), "col"),
        P("req"),
        P("req"),
    )
    return jax.shard_map(
        on_device,
        mesh=mesh,
        in_specs=placed,
        out_specs=(P(("req", "row"), "col"), P(("req", "row"), "col")),
        check_vma=False,
    )
```

```python
import functools
import math

import jax
import jax.numpy as jnp
from jax import lax
from jax.experimental import pallas as pl
from jax.experimental.pallas import tpu as pltpu
from jax.sharding import PartitionSpec as P

HEAD = 64
CH = 16
PATCH = 2
STEPS = 28
SHIFT_FACTOR = 3.0
LANES = 128
EPS = 1e-06
VMEM_LIMIT = 16 * 1024 * 1024
VMEM_MOST = 60 * 1024 * 1024
LOADS = 3
FIRST = 768
SWAP = [(0, 1), (1, 0)]


def noise_level(step_number):
    fraction = 1.0 - step_number.astype(jnp.float32) / STEPS
    return SHIFT_FACTOR * fraction / (1.0 + (SHIFT_FACTOR - 1.0) * fraction)


def same_head(width):
    row = lax.broadcasted_iota(jnp.int32, (width, width), 0) // HEAD
    col = lax.broadcasted_iota(jnp.int32, (width, width), 1) // HEAD
    return (row == col).astype(jnp.bfloat16)


def head_norms(pairs):
    ones = same_head(LANES)
    squares = []
    for x, _ in pairs:
        for at in range(0, x.shape[1], LANES):
            square = x[:, at : at + LANES] * x[:, at : at + LANES]
            high = square.astype(jnp.bfloat16)
            low = (square - high.astype(jnp.float32)).astype(jnp.bfloat16)
            squares.append(jnp.concatenate([high, low], axis=1))
    totals = jnp.dot(
        jnp.concatenate(squares, axis=0),
        jnp.concatenate([ones, ones], axis=0),
        preferred_element_type=jnp.float32,
    )
    inverse = lax.rsqrt(totals * (1.0 / HEAD) + EPS)
    results, start = [], 0
    for x, gain in pairs:
        gain = jnp.concatenate([gain, gain], axis=1)
        pieces = []
        for at in range(0, x.shape[1], LANES):
            factor = inverse[start : start + x.shape[0]]
            pieces.append((x[:, at : at + LANES] * factor * gain).astype(jnp.bfloat16))
            start += x.shape[0]
        results.append(jnp.concatenate(pieces, axis=1))
    return results


def load_half(x_ref, held, sems, column):
    tokens, _, width = held.shape
    at = pl.multiple_of(column * width, LANES)
    step = tokens // sems.shape[0]
    copies = [
        pltpu.make_async_copy(
            x_ref.at[start : start + step, :, pl.ds(at, width)],
            held.at[start : start + step],
            sems.at[start // step],
        )
        for start in range(0, tokens, step)
    ]
    for copy in copies:
        copy.start()
    return [(slice(at * step, at * step + step), copy) for at, copy in enumerate(copies)]


def prep_other_kernel(
    x_ref, gain_q_ref, gain_k_ref, gain_t_ref, k_ref, v_ref, q_ref, gains, held, sems, gain_sems
):
    blocks = load_half(x_ref, held, sems, 1 - lax.axis_index("col"))
    gain_copies = [
        pltpu.make_async_copy(ref, gains.at[at : at + 1], gain_sems.at[at])
        for at, ref in enumerate((gain_q_ref, gain_k_ref, gain_t_ref))
    ]
    for copy in gain_copies:
        copy.start()
    parts = []
    for rows, copy in blocks:
        copy.wait()
        parts.append(held[rows].astype(jnp.float32).transpose(1, 0, 2))
    for copy in gain_copies:
        copy.wait()
    q, k, v = (jnp.concatenate([part[kind] for part in parts], axis=0) for kind in range(3))
    v_ref[...] = v.astype(jnp.bfloat16)
    k_ref[...], q_ref[...] = head_norms([(k, gains[1:2]), (q, gains[0:1])])


def prep_own_kernel(
    x_ref,
    text_ref,
    gains,
    mine_ref,
    theirs_ref,
    k_ref,
    v_ref,
    q_ref,
    weight_ref,
    held,
    sems,
    stack_sems,
):
    tokens = q_ref.shape[0]
    blocks = load_half(x_ref, held, sems, lax.axis_index("col"))
    rows = mine_ref.shape[0]
    row = lax.axis_index("row")
    stacks = [
        pltpu.make_async_copy(
            ref, weight_ref.at[pl.ds(pl.multiple_of(place * rows, 16), rows)], stack_sems.at[at]
        )
        for at, (ref, place) in enumerate(((mine_ref, row), (theirs_ref, 1 - row)))
    ]
    for stack in stacks:
        stack.start()
    text = text_ref[...].astype(jnp.float32).transpose(1, 0, 2)
    v_ref[tokens:] = text[1].astype(jnp.bfloat16)
    for _, copy in blocks:
        copy.wait()
    x = held[...].astype(jnp.float32).transpose(1, 0, 2)
    v_ref[:tokens] = x[2].astype(jnp.bfloat16)
    k_ref[:tokens], k_ref[tokens:], q_ref[...] = head_norms(
        [(x[1], gains[1:2]), (text[0], gains[2:3]), (x[0], gains[0:1])]
    )
    for stack in stacks:
        stack.wait()


def attend(q, keys_refs, values_refs, attended_ref):
    tokens, width = q.shape
    first = lax.broadcasted_iota(jnp.int32, (tokens, LANES), 1) < HEAD
    scale = math.log2(math.e) / math.sqrt(HEAD)
    zero = jnp.zeros((tokens, LANES), jnp.bfloat16)
    ones = jnp.ones((sum(ref.shape[0] for ref in keys_refs), LANES), jnp.bfloat16)

    def scores_of(at):
        lanes = slice(at, at + LANES)
        keys = jnp.concatenate([ref[:, lanes] for ref in keys_refs], axis=0)
        block = q[:, lanes]
        both = jnp.concatenate(
            [jnp.where(first, block, zero), jnp.where(first, zero, block)], axis=0
        )
        return lax.dot_general(
            both, keys, (((1,), (1,)), ((), ())), preferred_element_type=jnp.float32
        )

    def finish(at, scores):
        lanes = slice(at, at + LANES)
        values = jnp.concatenate([ref[:, lanes] for ref in values_refs], axis=0)
        weights = jnp.exp2(scores * scale).astype(jnp.bfloat16)
        out = jnp.dot(
            weights,
            jnp.concatenate([values, ones], axis=1),
            preferred_element_type=jnp.float32,
        )
        weighted = jnp.where(first, out[:tokens, :LANES], out[tokens:, :LANES])
        total = jnp.where(first, out[:tokens, LANES:], out[tokens:, LANES:])
        attended_ref[:, lanes] = (weighted / total).astype(jnp.bfloat16)

    ahead = scores_of(0)
    for at in range(0, width, LANES):
        scores = ahead
        if at + LANES < width:
            ahead = scores_of(at + LANES)
        finish(at, scores)


def project(attended, weight_ref, start, upto, store, step):
    for at in range(start, upto, step):
        to = min(at + step, upto)
        product = lax.dot_general(
            attended,
            weight_ref[at:to],
            (((1,), (1,)), ((), ())),
            preferred_element_type=jnp.float32,
        )
        store(at, to, product.astype(jnp.bfloat16))


def attend_kernel(*refs):
    q_ref, keys, values, (w_ref, out_ref, attended) = refs[0], refs[1:5], refs[5:9], refs[9:]
    attend(q_ref[...], keys, values, attended)

    def keep(at, to, product):
        out_ref[:, at:to] = product

    project(attended[...], w_ref, 0, out_ref.shape[1], keep, out_ref.shape[1])


def rest_kernel(attended_ref, w_ref, *out_refs):
    features, start = w_ref.shape[0], w_ref.shape[0] - out_refs[0].shape[1]

    def keep(at, to, product):
        row = 0
        for ref in out_refs:
            ref[:, at - start : to - start] = product[row : row + ref.shape[0]]
            row += ref.shape[0]

    project(attended_ref[...], w_ref, start, features, keep, 640)


def own_kernel(*refs):
    q_ref, keys, values = refs[0], refs[1:5], refs[5:9]
    w_ref, hidden_ref, mod_ref, mine_ref, theirs_ref, out_ref, finals_ref, attended = refs[9:]
    attend(q_ref[...], keys, values, attended)
    tile_rows = hidden_ref.shape[0]

    def keep(at, to, product):
        part = mod_ref[2:3, at:to] * product.astype(jnp.float32)
        held = jnp.concatenate(
            [hidden_ref[row, :, at:to].astype(jnp.float32) for row in range(tile_rows)], axis=0
        )
        out_ref[:, at:to] = held + part

    project(attended[...], w_ref, 0, w_ref.shape[0], keep, 640)
    is_first = lax.axis_index("row") == 0
    mine = mine_ref[...].astype(jnp.float32)
    theirs = theirs_ref[...].astype(jnp.float32)
    finals_ref[...] = jnp.concatenate(
        [jnp.where(is_first, mine, theirs), jnp.where(is_first, theirs, mine)], axis=1
    ).astype(jnp.bfloat16)


def one_hot(dims, condition):
    row = lax.broadcasted_iota(jnp.int32, dims, 0)
    col = lax.broadcasted_iota(jnp.int32, dims, 1)
    return jnp.where(condition(row, col), 1.0, 0.0).astype(jnp.bfloat16)


def to_pixels(velocity, tile_cols):
    tokens, values = velocity.shape
    side = values // PATCH
    out_rows, out_lanes = tokens // tile_cols * PATCH, tile_cols * side
    terms, rest = [], velocity
    for _ in range(3):
        term = rest.astype(jnp.bfloat16)
        rest = rest - term.astype(jnp.float32)
        terms.append(term)
    terms = jnp.concatenate(terms, axis=0)
    row = lax.broadcasted_iota(jnp.int32, (3 * tokens, out_lanes), 0)
    col = lax.broadcasted_iota(jnp.int32, (3 * tokens, out_lanes), 1)
    here = col // side == row % tile_cols
    total = jnp.zeros((out_rows, out_lanes), jnp.float32)
    for at in range(PATCH):
        spread = one_hot((values, out_lanes), lambda r, c: r == c % side + at * side)
        wide = jnp.dot(terms, spread, preferred_element_type=jnp.float32)
        wide = jnp.where(here, wide, 0.0).astype(jnp.bfloat16)
        pick = one_hot(
            (out_rows, 3 * tokens), lambda r, c: r == c % tokens // tile_cols * PATCH + at
        )
        total += jnp.dot(pick, wide, preferred_element_type=jnp.float32)
    return total


def final_kernel(
    start,
    index_ref,
    count_ref,
    mixed_ref,
    first_ref,
    rest_ref,
    mod_ref,
    final_ref,
    latent_ref,
    *refs,
):
    velocity_ref, next_ref = refs[-2:]
    tokens = rest_ref.shape[0]
    step = 48
    parts = []
    for at in range(0, tokens, step):
        rows = slice(start + at, start + at + step)
        got = jnp.concatenate([first_ref[rows], rest_ref[at : at + step]], axis=1)
        mixed = mixed_ref[rows] + mod_ref[2:3] * got.astype(jnp.float32)
        mean = jnp.mean(mixed, axis=-1, keepdims=True)
        centered = mixed - mean
        var = jnp.mean(centered * centered, axis=-1, keepdims=True)
        normed = (
            centered * lax.rsqrt(var + EPS) * (1.0 + mod_ref[1:2]) + mod_ref[0:1]
        ).astype(jnp.bfloat16)
        parts.append(
            lax.dot_general(
                normed,
                final_ref[...],
                (((1,), (1,)), ((), ())),
                preferred_element_type=jnp.float32,
            )
        )
    tile_cols = latent_ref.shape[1] // (final_ref.shape[0] // PATCH)
    velocity = to_pixels(jnp.concatenate(parts, axis=0), tile_cols)
    first = start // tile_cols * PATCH
    pixels = slice(first, first + velocity.shape[0])
    index = jnp.full(velocity.shape, index_ref[0], jnp.int32)
    count = jnp.full(velocity.shape, count_ref[0], jnp.int32)
    euler_step = noise_level(index + count) - noise_level(index)
    for before_ref, after_ref in zip(refs[:-2], refs[-2:]):
        after_ref[:first] = before_ref[:first]
    velocity_ref[pixels] = velocity
    next_ref[pixels] = latent_ref[pixels] + euler_step * velocity


def params(limit=VMEM_LIMIT):
    return pltpu.CompilerParams(vmem_limit_bytes=limit)


def shape(dims, dtype=jnp.bfloat16):
    return jax.ShapeDtypeStruct(dims, dtype)


VMEM = pl.BlockSpec(memory_space=pltpu.VMEM)
ANY = pl.BlockSpec(memory_space=pl.ANY)
HBM = pl.BlockSpec(memory_space=pltpu.HBM)
SMEM = pl.BlockSpec(memory_space=pltpu.SMEM)


def on_device(
    image_qkv,
    text_kv,
    gain_query,
    gain_key,
    gain_text,
    out_weight,
    final_weight,
    hidden,
    modulation,
    latent,
    step_index,
    step_count,
):
    tile_rows, tile_cols, _, all_width = image_qkv.shape
    tokens = tile_rows * tile_cols
    words = text_kv.shape[0]
    width = all_width // lax.axis_size("col")
    features = hidden.shape[2]
    gains = [gain.reshape(1, HEAD) for gain in (gain_query, gain_key, gain_text)]
    x = image_qkv.reshape(tokens, 3, all_width)
    weight_half = out_weight.T
    held = pltpu.VMEM((tokens, 3, width), jnp.bfloat16)
    block = shape((tokens, width))

    loads = pltpu.SemaphoreType.DMA((LOADS,))
    k_sent, v_sent, q_sent, gains = pl.pallas_call(
        prep_other_kernel,
        out_shape=(block,) * 3 + (shape((len(gains), HEAD), jnp.float32),),
        in_specs=[HBM] * 4,
        out_specs=(VMEM,) * 4,
        scratch_shapes=[held, loads, pltpu.SemaphoreType.DMA((len(gains),))],
        compiler_params=params(VMEM_MOST),
        name="prep_other",
    )(x, *gains)
    k_got = lax.ppermute(k_sent, "col", SWAP)
    v_got = lax.ppermute(v_sent, "col", SWAP)
    q_got = lax.ppermute(q_sent, "col", SWAP)
    weight_got = lax.ppermute(weight_half, "row", SWAP)
    final_got = lax.ppermute(final_weight, "row", SWAP)
    k_own, v_own, q_own, weight = pl.pallas_call(
        prep_own_kernel,
        out_shape=(
            shape((tokens + words, width)),
            shape((tokens + words, width)),
            block,
            shape((features, width)),
        ),
        in_specs=[HBM, VMEM, VMEM, ANY, ANY],
        out_specs=(VMEM,) * 4,
        scratch_shapes=[held, loads, pltpu.SemaphoreType.DMA((2,))],
        compiler_params=params(),
        name="prep_own",
    )(x, text_kv, gains, weight_half, weight_got)
    keys = [k_own, lax.ppermute(k_own, "row", SWAP), k_got, lax.ppermute(k_got, "row", SWAP)]
    values = [v_own, lax.ppermute(v_own, "row", SWAP), v_got, lax.ppermute(v_got, "row", SWAP)]

    first, attended = pl.pallas_call(
        attend_kernel,
        out_shape=(shape((tokens, FIRST)), block),
        in_specs=[VMEM] * 10,
        out_specs=(VMEM, VMEM),
        compiler_params=params(),
        name="attend",
    )(q_got, *keys, *values, weight)
    first_got = lax.ppermute(first, "col", SWAP)
    cut = tile_rows // 3 * tile_cols
    chunks = [(start, start + cut) for start in range(0, tokens, cut)]
    rests = pl.pallas_call(
        rest_kernel,
        out_shape=tuple(shape((upto - start, features - FIRST)) for start, upto in chunks),
        in_specs=[VMEM] * 2,
        out_specs=(VMEM,) * len(chunks),
        compiler_params=params(),
        name="rest",
    )(attended, weight)
    returned = [lax.ppermute(rest, "col", SWAP) for rest in rests]
    mixed, finals = pl.pallas_call(
        own_kernel,
        out_shape=(shape((tokens, features), jnp.float32), shape((final_weight.shape[0], features))),
        in_specs=[VMEM] * 14,
        out_specs=(VMEM, VMEM),
        scratch_shapes=[pltpu.VMEM((tokens, width), jnp.bfloat16)],
        compiler_params=params(),
        name="own",
    )(q_own, *keys, *values, weight, hidden, modulation, final_weight, final_got)
    results = ()
    for (start, _), got in zip(chunks, returned):
        results = pl.pallas_call(
            functools.partial(final_kernel, start),
            out_shape=(shape(latent.shape, jnp.float32),) * 2,
            in_specs=[SMEM] * 2 + [VMEM] * (6 + len(results)),
            out_specs=(VMEM, VMEM),
            compiler_params=params(),
            name="final",
        )(step_index, step_count, mixed, first_got, got, modulation, finals, latent, *results)
    return results


def solution(mesh):
    placed = (
        P(("req", "row"), "col", None, None),
        P(("req", "row"), None, "col"),
        P(),
        P(),
        P(),
        P("col", "row"),
        P(None, "row"),
        P(("req", "row"), "col", None),
        P("req", None),
        P(("req", "row"), "col"),
        P("req"),
        P("req"),
    )
    return jax.shard_map(
        on_device,
        mesh=mesh,
        in_specs=placed,
        out_specs=(P(("req", "row"), "col"), P(("req", "row"), "col")),
        check_vma=False,
    )
```

```python
import functools
import math

import jax
import jax.numpy as jnp
from jax import lax
from jax.experimental import pallas as pl
from jax.experimental.pallas import tpu as pltpu
from jax.sharding import PartitionSpec as P

HEAD = 64
CH = 16
PATCH = 2
STEPS = 28
SHIFT_FACTOR = 3.0
LANES = 128
EPS = 1e-06
VMEM_LIMIT = 16 * 1024 * 1024
VMEM_MOST = 60 * 1024 * 1024
LOADS = 9
FIRST = 768
SWAP = [(0, 1), (1, 0)]


def noise_level(step_number):
    fraction = 1.0 - step_number.astype(jnp.float32) / STEPS
    return SHIFT_FACTOR * fraction / (1.0 + (SHIFT_FACTOR - 1.0) * fraction)


def same_head(width):
    row = lax.broadcasted_iota(jnp.int32, (width, width), 0) // HEAD
    col = lax.broadcasted_iota(jnp.int32, (width, width), 1) // HEAD
    return (row == col).astype(jnp.bfloat16)


def head_norms(pairs):
    ones = same_head(LANES)
    squares = []
    for x, _ in pairs:
        for at in range(0, x.shape[1], LANES):
            square = x[:, at : at + LANES] * x[:, at : at + LANES]
            high = square.astype(jnp.bfloat16)
            low = (square - high.astype(jnp.float32)).astype(jnp.bfloat16)
            squares.append(jnp.concatenate([high, low], axis=1))
    totals = jnp.dot(
        jnp.concatenate(squares, axis=0),
        jnp.concatenate([ones, ones], axis=0),
        preferred_element_type=jnp.float32,
    )
    inverse = lax.rsqrt(totals * (1.0 / HEAD) + EPS)
    results, start = [], 0
    for x, gain in pairs:
        gain = jnp.concatenate([gain, gain], axis=1)
        pieces = []
        for at in range(0, x.shape[1], LANES):
            factor = inverse[start : start + x.shape[0]]
            pieces.append((x[:, at : at + LANES] * factor * gain).astype(jnp.bfloat16))
            start += x.shape[0]
        results.append(jnp.concatenate(pieces, axis=1))
    return results


def load_half(x_ref, held, sems, column):
    tokens, _, width = held.shape
    at = pl.multiple_of(column * width, LANES)
    step = tokens // sems.shape[0]
    copies = [
        pltpu.make_async_copy(
            x_ref.at[start : start + step, :, pl.ds(at, width)],
            held.at[start : start + step],
            sems.at[start // step],
        )
        for start in range(0, tokens, step)
    ]
    for copy in copies:
        copy.start()
    return [(slice(at * step, at * step + step), copy) for at, copy in enumerate(copies)]


def prep_other_kernel(
    x_ref, gain_q_ref, gain_k_ref, gain_t_ref, q_ref, k_ref, v_ref, gains, held, sems, gain_sems
):
    blocks = load_half(x_ref, held, sems, 1 - lax.axis_index("col"))
    gain_copies = [
        pltpu.make_async_copy(ref, gains.at[at : at + 1], gain_sems.at[at])
        for at, ref in enumerate((gain_q_ref, gain_k_ref, gain_t_ref))
    ]
    for copy in gain_copies:
        copy.start()
    keys = []
    for rows, copy in blocks:
        copy.wait()
        x = held[rows].astype(jnp.float32).transpose(1, 0, 2)
        q_ref[rows] = x[0].astype(jnp.bfloat16)
        v_ref[rows] = x[2].astype(jnp.bfloat16)
        keys.append(x[1])
    for copy in gain_copies:
        copy.wait()
    (k_ref[...],) = head_norms([(jnp.concatenate(keys, axis=0), gains[1:2])])


def norm_kernel(x_ref, gains, out_ref):
    (out_ref[...],) = head_norms([(x_ref[...].astype(jnp.float32), gains[0:1])])


def prep_own_kernel(
    x_ref,
    text_ref,
    gains,
    mine_ref,
    theirs_ref,
    k_ref,
    v_ref,
    q_ref,
    weight_ref,
    held,
    sems,
    stack_sems,
):
    tokens = q_ref.shape[0]
    blocks = load_half(x_ref, held, sems, lax.axis_index("col"))
    rows = mine_ref.shape[0]
    row = lax.axis_index("row")
    stacks = [
        pltpu.make_async_copy(
            ref, weight_ref.at[pl.ds(pl.multiple_of(place * rows, 16), rows)], stack_sems.at[at]
        )
        for at, (ref, place) in enumerate(((mine_ref, row), (theirs_ref, 1 - row)))
    ]
    for stack in stacks:
        stack.start()
    text = text_ref[...].astype(jnp.float32).transpose(1, 0, 2)
    v_ref[tokens:] = text[1].astype(jnp.bfloat16)
    parts = []
    for at, copy in blocks:
        copy.wait()
        parts.append(held[at].astype(jnp.float32).transpose(1, 0, 2))
    q, k, v = (jnp.concatenate([part[kind] for part in parts], axis=0) for kind in range(3))
    v_ref[:tokens] = v.astype(jnp.bfloat16)
    k_ref[:tokens], k_ref[tokens:], q_ref[...] = head_norms(
        [
            (k, gains[1:2]),
            (text[0], gains[2:3]),
            (q, gains[0:1]),
        ]
    )
    for stack in stacks:
        stack.wait()


def attend(q, keys_refs, values_refs, attended_ref):
    tokens, width = q.shape
    first = lax.broadcasted_iota(jnp.int32, (tokens, LANES), 1) < HEAD
    scale = math.log2(math.e) / math.sqrt(HEAD)
    zero = jnp.zeros((tokens, LANES), jnp.bfloat16)
    ones = jnp.ones((sum(ref.shape[0] for ref in keys_refs), LANES), jnp.bfloat16)

    def scores_of(at):
        lanes = slice(at, at + LANES)
        keys = jnp.concatenate([ref[:, lanes] for ref in keys_refs], axis=0)
        block = q[:, lanes]
        both = jnp.concatenate(
            [jnp.where(first, block, zero), jnp.where(first, zero, block)], axis=0
        )
        return lax.dot_general(
            both, keys, (((1,), (1,)), ((), ())), preferred_element_type=jnp.float32
        )

    def finish(at, scores):
        lanes = slice(at, at + LANES)
        values = jnp.concatenate([ref[:, lanes] for ref in values_refs], axis=0)
        weights = jnp.exp2(scores * scale).astype(jnp.bfloat16)
        out = jnp.dot(
            weights,
            jnp.concatenate([values, ones], axis=1),
            preferred_element_type=jnp.float32,
        )
        weighted = jnp.where(first, out[:tokens, :LANES], out[tokens:, :LANES])
        total = jnp.where(first, out[:tokens, LANES:], out[tokens:, LANES:])
        attended_ref[:, lanes] = (weighted / total).astype(jnp.bfloat16)

    ahead = scores_of(0)
    for at in range(0, width, LANES):
        scores = ahead
        if at + LANES < width:
            ahead = scores_of(at + LANES)
        finish(at, scores)


def project(attended, weight_ref, start, upto, store, step):
    for at in range(start, upto, step):
        to = min(at + step, upto)
        product = lax.dot_general(
            attended,
            weight_ref[at:to],
            (((1,), (1,)), ((), ())),
            preferred_element_type=jnp.float32,
        )
        store(at, to, product.astype(jnp.bfloat16))


def attend_kernel(*refs):
    q_ref, keys, values, (w_ref, out_ref, attended) = refs[0], refs[1:5], refs[5:9], refs[9:]
    attend(q_ref[...], keys, values, attended)

    def keep(at, to, product):
        out_ref[:, at:to] = product

    project(attended[...], w_ref, 0, out_ref.shape[1], keep, out_ref.shape[1])


def rest_kernel(attended_ref, w_ref, *out_refs):
    features, start = w_ref.shape[0], w_ref.shape[0] - out_refs[0].shape[1]

    def keep(at, to, product):
        row = 0
        for ref in out_refs:
            ref[:, at - start : to - start] = product[row : row + ref.shape[0]]
            row += ref.shape[0]

    project(attended_ref[...], w_ref, start, features, keep, 640)


def own_kernel(*refs):
    q_ref, keys, values = refs[0], refs[1:5], refs[5:9]
    w_ref, hidden_ref, mod_ref, mine_ref, theirs_ref, out_ref, finals_ref, attended = refs[9:]
    attend(q_ref[...], keys, values, attended)
    tile_rows = hidden_ref.shape[0]

    def keep(at, to, product):
        part = mod_ref[2:3, at:to] * product.astype(jnp.float32)
        held = jnp.concatenate(
            [hidden_ref[row, :, at:to].astype(jnp.float32) for row in range(tile_rows)], axis=0
        )
        out_ref[:, at:to] = held + part

    project(attended[...], w_ref, 0, w_ref.shape[0], keep, 640)
    is_first = lax.axis_index("row") == 0
    mine = mine_ref[...].astype(jnp.float32)
    theirs = theirs_ref[...].astype(jnp.float32)
    finals_ref[...] = jnp.concatenate(
        [jnp.where(is_first, mine, theirs), jnp.where(is_first, theirs, mine)], axis=1
    ).astype(jnp.bfloat16)


def one_hot(dims, condition):
    row = lax.broadcasted_iota(jnp.int32, dims, 0)
    col = lax.broadcasted_iota(jnp.int32, dims, 1)
    return jnp.where(condition(row, col), 1.0, 0.0).astype(jnp.bfloat16)


def to_pixels(velocity, tile_cols):
    tokens, values = velocity.shape
    side = values // PATCH
    out_rows, out_lanes = tokens // tile_cols * PATCH, tile_cols * side
    terms, rest = [], velocity
    for _ in range(3):
        term = rest.astype(jnp.bfloat16)
        rest = rest - term.astype(jnp.float32)
        terms.append(term)
    terms = jnp.concatenate(terms, axis=0)
    row = lax.broadcasted_iota(jnp.int32, (3 * tokens, out_lanes), 0)
    col = lax.broadcasted_iota(jnp.int32, (3 * tokens, out_lanes), 1)
    here = col // side == row % tile_cols
    total = jnp.zeros((out_rows, out_lanes), jnp.float32)
    for at in range(PATCH):
        spread = one_hot((values, out_lanes), lambda r, c: r == c % side + at * side)
        wide = jnp.dot(terms, spread, preferred_element_type=jnp.float32)
        wide = jnp.where(here, wide, 0.0).astype(jnp.bfloat16)
        pick = one_hot(
            (out_rows, 3 * tokens), lambda r, c: r == c % tokens // tile_cols * PATCH + at
        )
        total += jnp.dot(pick, wide, preferred_element_type=jnp.float32)
    return total


def final_kernel(
    start,
    index_ref,
    count_ref,
    mixed_ref,
    first_ref,
    rest_ref,
    mod_ref,
    final_ref,
    latent_ref,
    *refs,
):
    velocity_ref, next_ref = refs[-2:]
    tokens = rest_ref.shape[0]
    step = 48
    parts = []
    for at in range(0, tokens, step):
        rows = slice(start + at, start + at + step)
        got = jnp.concatenate([first_ref[rows], rest_ref[at : at + step]], axis=1)
        mixed = mixed_ref[rows] + mod_ref[2:3] * got.astype(jnp.float32)
        mean = jnp.mean(mixed, axis=-1, keepdims=True)
        centered = mixed - mean
        var = jnp.mean(centered * centered, axis=-1, keepdims=True)
        normed = (
            centered * lax.rsqrt(var + EPS) * (1.0 + mod_ref[1:2]) + mod_ref[0:1]
        ).astype(jnp.bfloat16)
        parts.append(
            lax.dot_general(
                normed,
                final_ref[...],
                (((1,), (1,)), ((), ())),
                preferred_element_type=jnp.float32,
            )
        )
    tile_cols = latent_ref.shape[1] // (final_ref.shape[0] // PATCH)
    velocity = to_pixels(jnp.concatenate(parts, axis=0), tile_cols)
    first = start // tile_cols * PATCH
    pixels = slice(first, first + velocity.shape[0])
    index = jnp.full(velocity.shape, index_ref[0], jnp.int32)
    count = jnp.full(velocity.shape, count_ref[0], jnp.int32)
    euler_step = noise_level(index + count) - noise_level(index)
    for before_ref, after_ref in zip(refs[:-2], refs[-2:]):
        after_ref[:first] = before_ref[:first]
    velocity_ref[pixels] = velocity
    next_ref[pixels] = latent_ref[pixels] + euler_step * velocity


def params(limit=VMEM_LIMIT):
    return pltpu.CompilerParams(vmem_limit_bytes=limit)


def shape(dims, dtype=jnp.bfloat16):
    return jax.ShapeDtypeStruct(dims, dtype)


VMEM = pl.BlockSpec(memory_space=pltpu.VMEM)
ANY = pl.BlockSpec(memory_space=pl.ANY)
HBM = pl.BlockSpec(memory_space=pltpu.HBM)
SMEM = pl.BlockSpec(memory_space=pltpu.SMEM)


def on_device(
    image_qkv,
    text_kv,
    gain_query,
    gain_key,
    gain_text,
    out_weight,
    final_weight,
    hidden,
    modulation,
    latent,
    step_index,
    step_count,
):
    tile_rows, tile_cols, _, all_width = image_qkv.shape
    tokens = tile_rows * tile_cols
    words = text_kv.shape[0]
    width = all_width // lax.axis_size("col")
    features = hidden.shape[2]
    gains = [gain.reshape(1, HEAD) for gain in (gain_query, gain_key, gain_text)]
    x = image_qkv.reshape(tokens, 3, all_width)
    weight_half = out_weight.T
    held = pltpu.VMEM((tokens, 3, width), jnp.bfloat16)
    block = shape((tokens, width))

    loads = pltpu.SemaphoreType.DMA((LOADS,))
    q_raw, k_sent, v_sent, gains = pl.pallas_call(
        prep_other_kernel,
        out_shape=(block,) * 3 + (shape((len(gains), HEAD), jnp.float32),),
        in_specs=[HBM] * 4,
        out_specs=(VMEM,) * 4,
        scratch_shapes=[held, loads, pltpu.SemaphoreType.DMA((len(gains),))],
        compiler_params=params(VMEM_MOST),
        name="prep_other",
    )(x, *gains)
    k_got = lax.ppermute(k_sent, "col", SWAP)
    v_got = lax.ppermute(v_sent, "col", SWAP)
    q_sent = pl.pallas_call(
        norm_kernel,
        out_shape=block,
        in_specs=[VMEM, VMEM],
        out_specs=VMEM,
        compiler_params=params(),
        name="norm",
    )(q_raw, gains)
    q_got = lax.ppermute(q_sent, "col", SWAP)
    weight_got = lax.ppermute(weight_half, "row", SWAP)
    final_got = lax.ppermute(final_weight, "row", SWAP)
    k_own, v_own, q_own, weight = pl.pallas_call(
        prep_own_kernel,
        out_shape=(
            shape((tokens + words, width)),
            shape((tokens + words, width)),
            block,
            shape((features, width)),
        ),
        in_specs=[HBM, VMEM, VMEM, ANY, ANY],
        out_specs=(VMEM,) * 4,
        scratch_shapes=[
            held,
            loads,
            pltpu.SemaphoreType.DMA((2,)),
        ],
        compiler_params=params(),
        name="prep_own",
    )(x, text_kv, gains, weight_half, weight_got)
    keys = [k_own, lax.ppermute(k_own, "row", SWAP), k_got, lax.ppermute(k_got, "row", SWAP)]
    values = [v_own, lax.ppermute(v_own, "row", SWAP), v_got, lax.ppermute(v_got, "row", SWAP)]

    first, attended = pl.pallas_call(
        attend_kernel,
        out_shape=(shape((tokens, FIRST)), block),
        in_specs=[VMEM] * 10,
        out_specs=(VMEM, VMEM),
        compiler_params=params(),
        name="attend",
    )(q_got, *keys, *values, weight)
    first_got = lax.ppermute(first, "col", SWAP)
    cut = tile_rows // 3 * tile_cols
    chunks = [(start, start + cut) for start in range(0, tokens, cut)]
    rests = pl.pallas_call(
        rest_kernel,
        out_shape=tuple(shape((upto - start, features - FIRST)) for start, upto in chunks),
        in_specs=[VMEM] * 2,
        out_specs=(VMEM,) * len(chunks),
        compiler_params=params(),
        name="rest",
    )(attended, weight)
    returned = [lax.ppermute(rest, "col", SWAP) for rest in rests]
    mixed, finals = pl.pallas_call(
        own_kernel,
        out_shape=(shape((tokens, features), jnp.float32), shape((final_weight.shape[0], features))),
        in_specs=[VMEM] * 14,
        out_specs=(VMEM, VMEM),
        scratch_shapes=[pltpu.VMEM((tokens, width), jnp.bfloat16)],
        compiler_params=params(),
        name="own",
    )(q_own, *keys, *values, weight, hidden, modulation, final_weight, final_got)
    results = ()
    for (start, _), got in zip(chunks, returned):
        results = pl.pallas_call(
            functools.partial(final_kernel, start),
            out_shape=(shape(latent.shape, jnp.float32),) * 2,
            in_specs=[SMEM] * 2 + [VMEM] * (6 + len(results)),
            out_specs=(VMEM, VMEM),
            compiler_params=params(),
            name="final",
        )(step_index, step_count, mixed, first_got, got, modulation, finals, latent, *results)
    return results


def solution(mesh):
    placed = (
        P(("req", "row"), "col", None, None),
        P(("req", "row"), None, "col"),
        P(),
        P(),
        P(),
        P("col", "row"),
        P(None, "row"),
        P(("req", "row"), "col", None),
        P("req", None),
        P(("req", "row"), "col"),
        P("req"),
        P("req"),
    )
    return jax.shard_map(
        on_device,
        mesh=mesh,
        in_specs=placed,
        out_specs=(P(("req", "row"), "col"), P(("req", "row"), "col")),
        check_vma=False,
    )
```

```python
import functools
import math

import jax
import jax.numpy as jnp
from jax import lax
from jax.experimental import pallas as pl
from jax.experimental.pallas import tpu as pltpu
from jax.sharding import PartitionSpec as P

HEAD = 64
CH = 16
PATCH = 2
STEPS = 28
SHIFT_FACTOR = 3.0
LANES = 128
EPS = 1e-06
VMEM_LIMIT = 16 * 1024 * 1024
VMEM_MOST = 60 * 1024 * 1024
LOADS = 9
FIRST = 768
SWAP = [(0, 1), (1, 0)]


def noise_level(step_number):
    fraction = 1.0 - step_number.astype(jnp.float32) / STEPS
    return SHIFT_FACTOR * fraction / (1.0 + (SHIFT_FACTOR - 1.0) * fraction)


def same_head(width):
    row = lax.broadcasted_iota(jnp.int32, (width, width), 0) // HEAD
    col = lax.broadcasted_iota(jnp.int32, (width, width), 1) // HEAD
    return (row == col).astype(jnp.bfloat16)


def head_norms(pairs):
    ones = same_head(LANES)
    squares = []
    for x, _ in pairs:
        for at in range(0, x.shape[1], LANES):
            square = x[:, at : at + LANES] * x[:, at : at + LANES]
            high = square.astype(jnp.bfloat16)
            low = (square - high.astype(jnp.float32)).astype(jnp.bfloat16)
            squares.append(jnp.concatenate([high, low], axis=1))
    totals = jnp.dot(
        jnp.concatenate(squares, axis=0),
        jnp.concatenate([ones, ones], axis=0),
        preferred_element_type=jnp.float32,
    )
    inverse = lax.rsqrt(totals * (1.0 / HEAD) + EPS)
    results, start = [], 0
    for x, gain in pairs:
        gain = jnp.concatenate([gain, gain], axis=1)
        pieces = []
        for at in range(0, x.shape[1], LANES):
            factor = inverse[start : start + x.shape[0]]
            pieces.append((x[:, at : at + LANES] * factor * gain).astype(jnp.bfloat16))
            start += x.shape[0]
        results.append(jnp.concatenate(pieces, axis=1))
    return results


def load_half(x_ref, held, sems, column):
    tokens, _, width = held.shape
    at = pl.multiple_of(column * width, LANES)
    step = tokens // sems.shape[0]
    copies = [
        pltpu.make_async_copy(
            x_ref.at[start : start + step, :, pl.ds(at, width)],
            held.at[start : start + step],
            sems.at[start // step],
        )
        for start in range(0, tokens, step)
    ]
    for copy in copies:
        copy.start()
    return [(slice(at * step, at * step + step), copy) for at, copy in enumerate(copies)]


def halves(ref):
    rows = ref.shape[0] // 2
    return ref.at[:rows], ref.at[rows:]


def split_kernel(
    x_ref,
    gain_q_ref,
    gain_k_ref,
    gain_t_ref,
    q_first_ref,
    q_second_ref,
    kv_ref,
    gains,
    held,
    sems,
    gain_sems,
):
    blocks = load_half(x_ref, held, sems, 1 - lax.axis_index("col"))
    gain_copies = [
        pltpu.make_async_copy(ref, gains.at[at : at + 1], gain_sems.at[at])
        for at, ref in enumerate((gain_q_ref, gain_k_ref, gain_t_ref))
    ]
    for copy in gain_copies:
        copy.start()
    cut = q_first_ref.shape[0]
    k_ref, v_ref = halves(kv_ref)
    for rows, copy in blocks:
        copy.wait()
        q, k, v = held[rows].astype(jnp.float32).transpose(1, 0, 2).astype(jnp.bfloat16)
        k_ref[rows] = k
        v_ref[rows] = v
        if rows.stop <= cut:
            q_first_ref[rows] = q
        else:
            q_second_ref[rows.start - cut : rows.stop - cut] = q
    for copy in gain_copies:
        copy.wait()


def q_norm_kernel(x_ref, gains, out_ref):
    (out_ref[...],) = head_norms([(x_ref[...].astype(jnp.float32), gains[0:1])])


def kv_norm_kernel(x_ref, gains, out_ref):
    (k_ref, v_ref), (k_out, v_out) = halves(x_ref), halves(out_ref)
    v_out[...] = v_ref[...]
    (k_out[...],) = head_norms([(k_ref[...].astype(jnp.float32), gains[1:2])])


def keys_and_values(refs):
    pairs = [halves(ref) for ref in refs]
    return [keys for keys, _ in pairs], [values for _, values in pairs]


def prep_own_kernel(
    x_ref,
    text_ref,
    gains,
    mine_ref,
    theirs_ref,
    kv_ref,
    q_ref,
    gains_out,
    weight_ref,
    held,
    sems,
    stack_sems,
):
    tokens = q_ref.shape[0]
    k_ref, v_ref = halves(kv_ref)
    gains_out[...] = gains[...]
    blocks = load_half(x_ref, held, sems, lax.axis_index("col"))
    rows = mine_ref.shape[0]
    row = lax.axis_index("row")
    stacks = [
        pltpu.make_async_copy(
            ref, weight_ref.at[pl.ds(pl.multiple_of(place * rows, 16), rows)], stack_sems.at[at]
        )
        for at, (ref, place) in enumerate(((mine_ref, row), (theirs_ref, 1 - row)))
    ]
    for stack in stacks:
        stack.start()
    text = text_ref[...].astype(jnp.float32).transpose(1, 0, 2)
    v_ref[tokens:] = text[1].astype(jnp.bfloat16)
    for _, copy in blocks:
        copy.wait()
    q, k, v = held[...].transpose(1, 0, 2)
    v_ref[:tokens] = v
    k_ref[:tokens], k_ref[tokens:], q_ref[...] = head_norms(
        [
            (k.astype(jnp.float32), gains[1:2]),
            (text[0], gains[2:3]),
            (q.astype(jnp.float32), gains[0:1]),
        ]
    )
    for stack in stacks:
        stack.wait()


def attend(q, keys_refs, values_refs, attended_ref):
    tokens, width = q.shape
    first = lax.broadcasted_iota(jnp.int32, (tokens, LANES), 1) < HEAD
    scale = math.log2(math.e) / math.sqrt(HEAD)
    zero = jnp.zeros((tokens, LANES), jnp.bfloat16)
    ones = jnp.ones((sum(ref.shape[0] for ref in keys_refs), LANES), jnp.bfloat16)

    def scores_of(at):
        lanes = slice(at, at + LANES)
        keys = jnp.concatenate([ref[:, lanes] for ref in keys_refs], axis=0)
        block = q[:, lanes]
        both = jnp.concatenate(
            [jnp.where(first, block, zero), jnp.where(first, zero, block)], axis=0
        )
        return lax.dot_general(
            both, keys, (((1,), (1,)), ((), ())), preferred_element_type=jnp.float32
        )

    def finish(at, scores):
        lanes = slice(at, at + LANES)
        values = jnp.concatenate([ref[:, lanes] for ref in values_refs], axis=0)
        weights = jnp.exp2(scores * scale).astype(jnp.bfloat16)
        out = jnp.dot(
            weights,
            jnp.concatenate([values, ones], axis=1),
            preferred_element_type=jnp.float32,
        )
        weighted = jnp.where(first, out[:tokens, :LANES], out[tokens:, :LANES])
        total = jnp.where(first, out[:tokens, LANES:], out[tokens:, LANES:])
        attended_ref[:, lanes] = (weighted / total).astype(jnp.bfloat16)

    ahead = scores_of(0)
    for at in range(0, width, LANES):
        scores = ahead
        if at + LANES < width:
            ahead = scores_of(at + LANES)
        finish(at, scores)


def project(attended, weight_ref, start, upto, store, step):
    for at in range(start, upto, step):
        to = min(at + step, upto)
        product = lax.dot_general(
            attended,
            weight_ref[at:to],
            (((1,), (1,)), ((), ())),
            preferred_element_type=jnp.float32,
        )
        store(at, to, product.astype(jnp.bfloat16))


def attend_kernel(*refs):
    q_ref, (w_ref, out_ref, attended) = refs[0], refs[5:]
    attend(q_ref[...], *keys_and_values(refs[1:5]), attended)

    def keep(at, to, product):
        out_ref[:, at:to] = product

    project(attended[...], w_ref, 0, out_ref.shape[1], keep, FIRST)


def rest_kernel(attended_ref, w_ref, out_ref):
    features, start = w_ref.shape[0], w_ref.shape[0] - out_ref.shape[1]

    def keep(at, to, product):
        out_ref[:, at - start : to - start] = product

    project(attended_ref[...], w_ref, start, features, keep, 640)


def own_kernel(*refs):
    q_ref = refs[0]
    w_ref, hidden_ref, mod_ref, got_ref, mine_ref, theirs_ref = refs[5:11]
    out_ref, finals_ref, attended = refs[11:]
    attend(q_ref[...], *keys_and_values(refs[1:5]), attended)
    tile_rows = hidden_ref.shape[0]

    def keep(at, to, product):
        part = mod_ref[2:3, at:to] * product.astype(jnp.float32)
        held = jnp.concatenate(
            [hidden_ref[row, :, at:to].astype(jnp.float32) for row in range(tile_rows)], axis=0
        )
        out_ref[:, at:to] = held + part

    project(attended[...], w_ref, 0, w_ref.shape[0], keep, 640)
    upto, to = got_ref.shape
    out_ref[:upto, :to] += mod_ref[2:3, :to] * got_ref[...].astype(jnp.float32)
    is_first = lax.axis_index("row") == 0
    mine = mine_ref[...].astype(jnp.float32)
    theirs = theirs_ref[...].astype(jnp.float32)
    finals_ref[...] = jnp.concatenate(
        [jnp.where(is_first, mine, theirs), jnp.where(is_first, theirs, mine)], axis=1
    ).astype(jnp.bfloat16)


def one_hot(dims, condition):
    row = lax.broadcasted_iota(jnp.int32, dims, 0)
    col = lax.broadcasted_iota(jnp.int32, dims, 1)
    return jnp.where(condition(row, col), 1.0, 0.0).astype(jnp.bfloat16)


def to_pixels(velocity, tile_cols):
    tokens, values = velocity.shape
    side = values // PATCH
    out_rows, out_lanes = tokens // tile_cols * PATCH, tile_cols * side
    terms, rest = [], velocity
    for _ in range(3):
        term = rest.astype(jnp.bfloat16)
        rest = rest - term.astype(jnp.float32)
        terms.append(term)
    terms = jnp.concatenate(terms, axis=0)
    row = lax.broadcasted_iota(jnp.int32, (3 * tokens, out_lanes), 0)
    col = lax.broadcasted_iota(jnp.int32, (3 * tokens, out_lanes), 1)
    here = col // side == row % tile_cols
    total = jnp.zeros((out_rows, out_lanes), jnp.float32)
    for at in range(PATCH):
        spread = one_hot((values, out_lanes), lambda r, c: r == c % side + at * side)
        wide = jnp.dot(terms, spread, preferred_element_type=jnp.float32)
        wide = jnp.where(here, wide, 0.0).astype(jnp.bfloat16)
        pick = one_hot(
            (out_rows, 3 * tokens), lambda r, c: r == c % tokens // tile_cols * PATCH + at
        )
        total += jnp.dot(pick, wide, preferred_element_type=jnp.float32)
    return total


def final_kernel(
    start,
    index_ref,
    count_ref,
    mixed_ref,
    rest_ref,
    mod_ref,
    final_ref,
    latent_ref,
    *refs,
):
    velocity_ref, next_ref = refs[-2:]
    tokens = rest_ref.shape[0]
    step = 48
    parts = []
    for at in range(0, tokens, step):
        rows = slice(start + at, start + at + step)
        had = mixed_ref.shape[1] - rest_ref.shape[1]
        mixed = mixed_ref[rows]
        got = rest_ref[at : at + step].astype(jnp.float32)
        added = mixed[:, had:] + mod_ref[2:3, had:] * got
        mixed = jnp.concatenate([mixed[:, :had], added], axis=1) if had else added
        mean = jnp.mean(mixed, axis=-1, keepdims=True)
        centered = mixed - mean
        var = jnp.mean(centered * centered, axis=-1, keepdims=True)
        normed = (
            centered * lax.rsqrt(var + EPS) * (1.0 + mod_ref[1:2]) + mod_ref[0:1]
        ).astype(jnp.bfloat16)
        parts.append(
            lax.dot_general(
                normed,
                final_ref[...],
                (((1,), (1,)), ((), ())),
                preferred_element_type=jnp.float32,
            )
        )
    tile_cols = latent_ref.shape[1] // (final_ref.shape[0] // PATCH)
    velocity = to_pixels(jnp.concatenate(parts, axis=0), tile_cols)
    first = start // tile_cols * PATCH
    pixels = slice(first, first + velocity.shape[0])
    index = jnp.full(velocity.shape, index_ref[0], jnp.int32)
    count = jnp.full(velocity.shape, count_ref[0], jnp.int32)
    euler_step = noise_level(index + count) - noise_level(index)
    for before_ref, after_ref in zip(refs[:-2], refs[-2:]):
        after_ref[:first] = before_ref[:first]
    velocity_ref[pixels] = velocity
    next_ref[pixels] = latent_ref[pixels] + euler_step * velocity


def params(limit=VMEM_LIMIT):
    return pltpu.CompilerParams(vmem_limit_bytes=limit)


def lasting(duration):
    return pl.CostEstimate(
        flops=int(duration * 1e9), bytes_accessed=int(duration * 3e6), transcendentals=0
    )


def shape(dims, dtype=jnp.bfloat16):
    return jax.ShapeDtypeStruct(dims, dtype)


VMEM = pl.BlockSpec(memory_space=pltpu.VMEM)
ANY = pl.BlockSpec(memory_space=pl.ANY)
HBM = pl.BlockSpec(memory_space=pltpu.HBM)
SMEM = pl.BlockSpec(memory_space=pltpu.SMEM)


def on_device(
    image_qkv,
    text_kv,
    gain_query,
    gain_key,
    gain_text,
    out_weight,
    final_weight,
    hidden,
    modulation,
    latent,
    step_index,
    step_count,
):
    tile_rows, tile_cols, _, all_width = image_qkv.shape
    tokens = tile_rows * tile_cols
    words = text_kv.shape[0]
    width = all_width // lax.axis_size("col")
    features = hidden.shape[2]
    gains = [gain.reshape(1, HEAD) for gain in (gain_query, gain_key, gain_text)]
    x = image_qkv.reshape(tokens, 3, all_width)
    weight_half = out_weight.T
    held = pltpu.VMEM((tokens, 3, width), jnp.bfloat16)
    block = shape((tokens, width))

    loads = pltpu.SemaphoreType.DMA((LOADS,))
    cut = tile_rows // 3 * 2 * tile_cols
    chunks = ((0, cut), (cut, tokens))
    *q_raw, kv_raw, gains = pl.pallas_call(
        split_kernel,
        out_shape=tuple(shape((upto - start, width)) for start, upto in chunks)
        + (shape((2 * tokens, width)), shape((len(gains), HEAD), jnp.float32)),
        in_specs=[HBM] * 4,
        out_specs=(VMEM,) * 4,
        scratch_shapes=[held, loads, pltpu.SemaphoreType.DMA((len(gains),))],
        compiler_params=params(VMEM_MOST),
        name="split",
    )(x, *gains)

    weight_got = lax.ppermute(weight_half, "row", SWAP)
    final_got = lax.ppermute(final_weight, "row", SWAP)
    kv_own, q_own, gains_on, weight = pl.pallas_call(
        prep_own_kernel,
        out_shape=(
            shape((2 * (tokens + words), width)),
            block,
            shape(gains.shape, jnp.float32),
            shape((features, width)),
        ),
        in_specs=[HBM, VMEM, VMEM, ANY, ANY],
        out_specs=(VMEM,) * 4,
        scratch_shapes=[
            held,
            loads,
            pltpu.SemaphoreType.DMA((2,)),
        ],
        compiler_params=params(),
        name="prep_own",
    )(x, text_kv, gains, weight_half, weight_got)
    def normed(kernel, got, duration):
        return pl.pallas_call(
            kernel,
            out_shape=shape(got.shape),
            in_specs=[VMEM, VMEM],
            out_specs=VMEM,
            compiler_params=params(),
            cost_estimate=lasting(duration),
            name=kernel.__name__,
        )(got, gains_on)

    kv_got = normed(kv_norm_kernel, lax.ppermute(kv_raw, "col", SWAP), 0)
    q_got = [
        normed(q_norm_kernel, lax.ppermute(raw, "col", SWAP), duration)
        for raw, duration in zip(q_raw, (4, 1))
    ]
    pairs = []
    for kv in (kv_own, kv_got):
        pairs += [kv, lax.ppermute(kv, "row", SWAP)]

    def attended(q, projected, scratch):
        rows = q.shape[0]
        out_shape = (shape((rows, projected)),) + (() if scratch else (shape((rows, width)),))
        return pl.pallas_call(
            attend_kernel,
            out_shape=out_shape,
            in_specs=[VMEM] * 6,
            out_specs=(VMEM,) * len(out_shape),
            scratch_shapes=[pltpu.VMEM((rows, width), jnp.bfloat16)] if scratch else (),
            compiler_params=params(),
            name="attend",
        )(q, *pairs, weight)

    first, heads = attended(q_got[0], FIRST, False)
    first_got = lax.ppermute(first, "col", SWAP)
    rest = pl.pallas_call(
        rest_kernel,
        out_shape=shape((cut, features - FIRST)),
        in_specs=[VMEM] * 2,
        out_specs=VMEM,
        compiler_params=params(),
        name="rest",
    )(heads, weight)
    rest_got = lax.ppermute(rest, "col", SWAP)
    second_q, rest = lax.optimization_barrier((q_got[1], rest))
    (second,) = attended(second_q, features, True)
    second_got = lax.ppermute(second, "col", SWAP)
    mixed, finals = pl.pallas_call(
        own_kernel,
        out_shape=(shape((tokens, features), jnp.float32), shape((final_weight.shape[0], features))),
        in_specs=[VMEM] * 11,
        out_specs=(VMEM, VMEM),
        scratch_shapes=[pltpu.VMEM((tokens, width), jnp.bfloat16)],
        compiler_params=params(),
        cost_estimate=lasting(60),
        name="own",
    )(q_own, *pairs, weight, hidden, modulation, first_got, final_weight, final_got)
    results = ()
    for (start, _), got in ((chunks[0], rest_got), (chunks[1], second_got)):
        results = pl.pallas_call(
            functools.partial(final_kernel, start),
            out_shape=(shape(latent.shape, jnp.float32),) * 2,
            in_specs=[SMEM] * 2 + [VMEM] * (5 + len(results)),
            out_specs=(VMEM, VMEM),
            compiler_params=params(),
            name="final",
        )(step_index, step_count, mixed, got, modulation, finals, latent, *results)
    return results


def solution(mesh):
    placed = (
        P(("req", "row"), "col", None, None),
        P(("req", "row"), None, "col"),
        P(),
        P(),
        P(),
        P("col", "row"),
        P(None, "row"),
        P(("req", "row"), "col", None),
        P("req", None),
        P(("req", "row"), "col"),
        P("req"),
        P("req"),
    )
    return jax.shard_map(
        on_device,
        mesh=mesh,
        in_specs=placed,
        out_specs=(P(("req", "row"), "col"), P(("req", "row"), "col")),
        check_vma=False,
    )
```

```python
import functools
import math

import jax
import jax.numpy as jnp
from jax import lax
from jax.experimental import pallas as pl
from jax.experimental.pallas import tpu as pltpu
from jax.sharding import PartitionSpec as P

HEAD = 64
CH = 16
PATCH = 2
STEPS = 28
SHIFT_FACTOR = 3.0
LANES = 128
EPS = 1e-06
VMEM_LIMIT = 16 * 1024 * 1024
VMEM_MOST = 60 * 1024 * 1024
LOADS = 9
FIRST = 768
SWAP = [(0, 1), (1, 0)]


def noise_level(step_number):
    fraction = 1.0 - step_number.astype(jnp.float32) / STEPS
    return SHIFT_FACTOR * fraction / (1.0 + (SHIFT_FACTOR - 1.0) * fraction)


def same_head(width):
    row = lax.broadcasted_iota(jnp.int32, (width, width), 0) // HEAD
    col = lax.broadcasted_iota(jnp.int32, (width, width), 1) // HEAD
    return (row == col).astype(jnp.bfloat16)


def head_norms(pairs):
    ones = same_head(LANES)
    squares = []
    for x, _ in pairs:
        for at in range(0, x.shape[1], LANES):
            square = x[:, at : at + LANES] * x[:, at : at + LANES]
            high = square.astype(jnp.bfloat16)
            low = (square - high.astype(jnp.float32)).astype(jnp.bfloat16)
            squares.append(jnp.concatenate([high, low], axis=1))
    totals = jnp.dot(
        jnp.concatenate(squares, axis=0),
        jnp.concatenate([ones, ones], axis=0),
        preferred_element_type=jnp.float32,
    )
    inverse = lax.rsqrt(totals * (1.0 / HEAD) + EPS)
    results, start = [], 0
    for x, gain in pairs:
        gain = jnp.concatenate([gain, gain], axis=1)
        pieces = []
        for at in range(0, x.shape[1], LANES):
            factor = inverse[start : start + x.shape[0]]
            pieces.append((x[:, at : at + LANES] * factor * gain).astype(jnp.bfloat16))
            start += x.shape[0]
        results.append(jnp.concatenate(pieces, axis=1))
    return results


def load_half(x_ref, held, sems, column):
    tokens, _, width = held.shape
    at = pl.multiple_of(column * width, LANES)
    step = tokens // sems.shape[0]
    copies = [
        pltpu.make_async_copy(
            x_ref.at[start : start + step, :, pl.ds(at, width)],
            held.at[start : start + step],
            sems.at[start // step],
        )
        for start in range(0, tokens, step)
    ]
    for copy in copies:
        copy.start()
    return [(slice(at * step, at * step + step), copy) for at, copy in enumerate(copies)]


def halves(ref):
    rows = ref.shape[0] // 2
    return ref.at[:rows], ref.at[rows:]


def split_kernel(
    x_ref,
    gain_q_ref,
    gain_k_ref,
    gain_t_ref,
    q_first_ref,
    q_second_ref,
    kv_ref,
    gains,
    held,
    sems,
    gain_sems,
):
    blocks = load_half(x_ref, held, sems, 1 - lax.axis_index("col"))
    gain_copies = [
        pltpu.make_async_copy(ref, gains.at[at : at + 1], gain_sems.at[at])
        for at, ref in enumerate((gain_q_ref, gain_k_ref, gain_t_ref))
    ]
    for copy in gain_copies:
        copy.start()
    cut = q_first_ref.shape[0]
    k_ref, v_ref = halves(kv_ref)
    for rows, copy in blocks:
        copy.wait()
        q, k, v = held[rows].astype(jnp.float32).transpose(1, 0, 2).astype(jnp.bfloat16)
        k_ref[rows] = k
        v_ref[rows] = v
        if rows.stop <= cut:
            q_first_ref[rows] = q
        else:
            q_second_ref[rows.start - cut : rows.stop - cut] = q
    for copy in gain_copies:
        copy.wait()


def q_norm_kernel(x_ref, gains, out_ref):
    (out_ref[...],) = head_norms([(x_ref[...].astype(jnp.float32), gains[0:1])])


def kv_norm_kernel(x_ref, gains, out_ref):
    (k_ref, v_ref), (k_out, v_out) = halves(x_ref), halves(out_ref)
    v_out[...] = v_ref[...]
    (k_out[...],) = head_norms([(k_ref[...].astype(jnp.float32), gains[1:2])])


def keys_and_values(refs):
    pairs = [halves(ref) for ref in refs]
    return [keys for keys, _ in pairs], [values for _, values in pairs]


def prep_own_kernel(
    x_ref,
    text_ref,
    gains,
    mine_ref,
    theirs_ref,
    kv_ref,
    q_ref,
    gains_out,
    weight_ref,
    held,
    sems,
    stack_sems,
):
    tokens = q_ref.shape[0]
    k_ref, v_ref = halves(kv_ref)
    gains_out[...] = gains[...]
    blocks = load_half(x_ref, held, sems, lax.axis_index("col"))
    rows = mine_ref.shape[0]
    row = lax.axis_index("row")
    stacks = [
        pltpu.make_async_copy(
            ref, weight_ref.at[pl.ds(pl.multiple_of(place * rows, 16), rows)], stack_sems.at[at]
        )
        for at, (ref, place) in enumerate(((mine_ref, row), (theirs_ref, 1 - row)))
    ]
    for stack in stacks:
        stack.start()
    text = text_ref[...].astype(jnp.float32).transpose(1, 0, 2)
    v_ref[tokens:] = text[1].astype(jnp.bfloat16)
    for _, copy in blocks:
        copy.wait()
    q, k, v = held[...].transpose(1, 0, 2)
    v_ref[:tokens] = v
    k_ref[:tokens], k_ref[tokens:], q_ref[...] = head_norms(
        [
            (k.astype(jnp.float32), gains[1:2]),
            (text[0], gains[2:3]),
            (q.astype(jnp.float32), gains[0:1]),
        ]
    )
    for stack in stacks:
        stack.wait()


def attend(q, keys_refs, values_refs, attended_ref):
    tokens, width = q.shape
    first = lax.broadcasted_iota(jnp.int32, (tokens, LANES), 1) < HEAD
    scale = math.log2(math.e) / math.sqrt(HEAD)
    zero = jnp.zeros((tokens, LANES), jnp.bfloat16)
    ones = jnp.ones((sum(ref.shape[0] for ref in keys_refs), LANES), jnp.bfloat16)

    def scores_of(at):
        lanes = slice(at, at + LANES)
        keys = jnp.concatenate([ref[:, lanes] for ref in keys_refs], axis=0)
        block = q[:, lanes]
        both = jnp.concatenate(
            [jnp.where(first, block, zero), jnp.where(first, zero, block)], axis=0
        )
        return lax.dot_general(
            both, keys, (((1,), (1,)), ((), ())), preferred_element_type=jnp.float32
        )

    def finish(at, scores):
        lanes = slice(at, at + LANES)
        values = jnp.concatenate([ref[:, lanes] for ref in values_refs], axis=0)
        weights = jnp.exp2(scores * scale).astype(jnp.bfloat16)
        out = jnp.dot(
            weights,
            jnp.concatenate([values, ones], axis=1),
            preferred_element_type=jnp.float32,
        )
        weighted = jnp.where(first, out[:tokens, :LANES], out[tokens:, :LANES])
        total = jnp.where(first, out[:tokens, LANES:], out[tokens:, LANES:])
        attended_ref[:, lanes] = (weighted / total).astype(jnp.bfloat16)

    ahead = scores_of(0)
    for at in range(0, width, LANES):
        scores = ahead
        if at + LANES < width:
            ahead = scores_of(at + LANES)
        finish(at, scores)


def project(attended, weight_ref, start, upto, store, step):
    for at in range(start, upto, step):
        to = min(at + step, upto)
        product = lax.dot_general(
            attended,
            weight_ref[at:to],
            (((1,), (1,)), ((), ())),
            preferred_element_type=jnp.float32,
        )
        store(at, to, product.astype(jnp.bfloat16))


def attend_kernel(*refs):
    q_ref, (w_ref, out_ref, attended) = refs[0], refs[5:]
    attend(q_ref[...], *keys_and_values(refs[1:5]), attended)

    def keep(at, to, product):
        out_ref[:, at:to] = product

    project(attended[...], w_ref, 0, out_ref.shape[1], keep, FIRST)


def rest_kernel(attended_ref, w_ref, out_ref):
    features, start = w_ref.shape[0], w_ref.shape[0] - out_ref.shape[1]

    def keep(at, to, product):
        out_ref[:, at - start : to - start] = product

    project(attended_ref[...], w_ref, start, features, keep, 640)


def own_kernel(*refs):
    q_ref = refs[0]
    w_ref, hidden_ref, mod_ref, got_ref, mine_ref, theirs_ref, index_ref, count_ref = refs[5:13]
    out_ref, finals_ref, euler_ref, attended, index, count, sems = refs[13:]
    copies = [
        pltpu.make_async_copy(ref, to, sems.at[at])
        for at, (ref, to) in enumerate(((index_ref, index), (count_ref, count)))
    ]
    for copy in copies:
        copy.start()
    attend(q_ref[...], *keys_and_values(refs[1:5]), attended)
    tile_rows = hidden_ref.shape[0]

    def keep(at, to, product):
        part = mod_ref[2:3, at:to] * product.astype(jnp.float32)
        held = jnp.concatenate(
            [hidden_ref[row, :, at:to].astype(jnp.float32) for row in range(tile_rows)], axis=0
        )
        out_ref[:, at:to] = held + part

    project(attended[...], w_ref, 0, w_ref.shape[0], keep, 640)
    upto, to = got_ref.shape
    out_ref[:upto, :to] += mod_ref[2:3, :to] * got_ref[...].astype(jnp.float32)
    is_first = lax.axis_index("row") == 0
    mine = mine_ref[...].astype(jnp.float32)
    theirs = theirs_ref[...].astype(jnp.float32)
    finals_ref[...] = jnp.concatenate(
        [jnp.where(is_first, mine, theirs), jnp.where(is_first, theirs, mine)], axis=1
    ).astype(jnp.bfloat16)
    for copy in copies:
        copy.wait()
    now = jnp.full(euler_ref.shape, index[0], jnp.int32)
    then = now + jnp.full(euler_ref.shape, count[0], jnp.int32)
    euler_ref[...] = noise_level(then) - noise_level(now)


def one_hot(dims, condition):
    row = lax.broadcasted_iota(jnp.int32, dims, 0)
    col = lax.broadcasted_iota(jnp.int32, dims, 1)
    return jnp.where(condition(row, col), 1.0, 0.0).astype(jnp.bfloat16)


def to_pixels(velocity, tile_cols):
    tokens, values = velocity.shape
    side = values // PATCH
    out_rows, out_lanes = tokens // tile_cols * PATCH, tile_cols * side
    terms, rest = [], velocity
    for _ in range(3):
        term = rest.astype(jnp.bfloat16)
        rest = rest - term.astype(jnp.float32)
        terms.append(term)
    terms = jnp.concatenate(terms, axis=0)
    row = lax.broadcasted_iota(jnp.int32, (3 * tokens, out_lanes), 0)
    col = lax.broadcasted_iota(jnp.int32, (3 * tokens, out_lanes), 1)
    here = col // side == row % tile_cols
    total = jnp.zeros((out_rows, out_lanes), jnp.float32)
    for at in range(PATCH):
        spread = one_hot((values, out_lanes), lambda r, c: r == c % side + at * side)
        wide = jnp.dot(terms, spread, preferred_element_type=jnp.float32)
        wide = jnp.where(here, wide, 0.0).astype(jnp.bfloat16)
        pick = one_hot(
            (out_rows, 3 * tokens), lambda r, c: r == c % tokens // tile_cols * PATCH + at
        )
        total += jnp.dot(pick, wide, preferred_element_type=jnp.float32)
    return total


def final_kernel(
    start,
    euler_ref,
    mixed_ref,
    rest_ref,
    mod_ref,
    final_ref,
    latent_ref,
    *refs,
):
    velocity_ref, next_ref = refs[-2:]
    tokens = rest_ref.shape[0]
    step = 48
    parts = []
    for at in range(0, tokens, step):
        rows = slice(start + at, start + at + step)
        had = mixed_ref.shape[1] - rest_ref.shape[1]
        mixed = mixed_ref[rows]
        got = rest_ref[at : at + step].astype(jnp.float32)
        added = mixed[:, had:] + mod_ref[2:3, had:] * got
        mixed = jnp.concatenate([mixed[:, :had], added], axis=1) if had else added
        mean = jnp.mean(mixed, axis=-1, keepdims=True)
        centered = mixed - mean
        var = jnp.mean(centered * centered, axis=-1, keepdims=True)
        normed = (
            centered * lax.rsqrt(var + EPS) * (1.0 + mod_ref[1:2]) + mod_ref[0:1]
        ).astype(jnp.bfloat16)
        parts.append(
            lax.dot_general(
                normed,
                final_ref[...],
                (((1,), (1,)), ((), ())),
                preferred_element_type=jnp.float32,
            )
        )
    tile_cols = latent_ref.shape[1] // (final_ref.shape[0] // PATCH)
    velocity = to_pixels(jnp.concatenate(parts, axis=0), tile_cols)
    first = start // tile_cols * PATCH
    pixels = slice(first, first + velocity.shape[0])
    for before_ref, after_ref in zip(refs[:-2], refs[-2:]):
        after_ref[:first] = before_ref[:first]
    velocity_ref[pixels] = velocity
    next_ref[pixels] = latent_ref[pixels] + euler_ref[...] * velocity


def params(limit=VMEM_LIMIT):
    return pltpu.CompilerParams(vmem_limit_bytes=limit)


def lasting(duration):
    return pl.CostEstimate(
        flops=int(duration * 1e9), bytes_accessed=int(duration * 3e6), transcendentals=0
    )


def shape(dims, dtype=jnp.bfloat16):
    return jax.ShapeDtypeStruct(dims, dtype)


VMEM = pl.BlockSpec(memory_space=pltpu.VMEM)
ANY = pl.BlockSpec(memory_space=pl.ANY)
HBM = pl.BlockSpec(memory_space=pltpu.HBM)


def on_device(
    image_qkv,
    text_kv,
    gain_query,
    gain_key,
    gain_text,
    out_weight,
    final_weight,
    hidden,
    modulation,
    latent,
    step_index,
    step_count,
):
    tile_rows, tile_cols, _, all_width = image_qkv.shape
    tokens = tile_rows * tile_cols
    words = text_kv.shape[0]
    width = all_width // lax.axis_size("col")
    features = hidden.shape[2]
    gains = [gain.reshape(1, HEAD) for gain in (gain_query, gain_key, gain_text)]
    x = image_qkv.reshape(tokens, 3, all_width)
    weight_half = out_weight.T
    held = pltpu.VMEM((tokens, 3, width), jnp.bfloat16)
    block = shape((tokens, width))

    loads = pltpu.SemaphoreType.DMA((LOADS,))
    cut = tile_rows // 3 * tile_cols
    chunks = ((0, cut), (cut, tokens))
    *q_raw, kv_raw, gains = pl.pallas_call(
        split_kernel,
        out_shape=tuple(shape((upto - start, width)) for start, upto in chunks)
        + (shape((2 * tokens, width)), shape((len(gains), HEAD), jnp.float32)),
        in_specs=[HBM] * 4,
        out_specs=(VMEM,) * 4,
        scratch_shapes=[held, loads, pltpu.SemaphoreType.DMA((len(gains),))],
        compiler_params=params(VMEM_MOST),
        name="split",
    )(x, *gains)

    weight_got = lax.ppermute(weight_half, "row", SWAP)
    final_got = lax.ppermute(final_weight, "row", SWAP)
    kv_own, q_own, gains_on, weight = pl.pallas_call(
        prep_own_kernel,
        out_shape=(
            shape((2 * (tokens + words), width)),
            block,
            shape(gains.shape, jnp.float32),
            shape((features, width)),
        ),
        in_specs=[HBM, VMEM, VMEM, ANY, ANY],
        out_specs=(VMEM,) * 4,
        scratch_shapes=[
            held,
            loads,
            pltpu.SemaphoreType.DMA((2,)),
        ],
        compiler_params=params(),
        name="prep_own",
    )(x, text_kv, gains, weight_half, weight_got)
    def normed(kernel, got, duration):
        return pl.pallas_call(
            kernel,
            out_shape=shape(got.shape),
            in_specs=[VMEM, VMEM],
            out_specs=VMEM,
            compiler_params=params(),
            cost_estimate=lasting(duration),
            name=kernel.__name__,
        )(got, gains_on)

    kv_got = normed(kv_norm_kernel, lax.ppermute(kv_raw, "col", SWAP), 0)
    q_got = [
        normed(q_norm_kernel, lax.ppermute(raw, "col", SWAP), duration)
        for raw, duration in zip(q_raw, (3.5, 1))
    ]
    pairs = []
    for kv in (kv_own, kv_got):
        pairs += [kv, lax.ppermute(kv, "row", SWAP)]

    def attended(q, projected, scratch):
        rows = q.shape[0]
        out_shape = (shape((rows, projected)),) + (() if scratch else (shape((rows, width)),))
        return pl.pallas_call(
            attend_kernel,
            out_shape=out_shape,
            in_specs=[VMEM] * 6,
            out_specs=(VMEM,) * len(out_shape),
            scratch_shapes=[pltpu.VMEM((rows, width), jnp.bfloat16)] if scratch else (),
            compiler_params=params(),
            name="attend",
        )(q, *pairs, weight)

    first, heads = attended(q_got[0], FIRST, False)
    first_got = lax.ppermute(first, "col", SWAP)
    rest = pl.pallas_call(
        rest_kernel,
        out_shape=shape((cut, features - FIRST)),
        in_specs=[VMEM] * 2,
        out_specs=VMEM,
        compiler_params=params(),
        name="rest",
    )(heads, weight)
    rest_got = lax.ppermute(rest, "col", SWAP)
    second_q, rest = lax.optimization_barrier((q_got[1], rest))
    (second,) = attended(second_q, features, True)
    second_got = lax.ppermute(second, "col", SWAP)
    mixed, finals, euler = pl.pallas_call(
        own_kernel,
        out_shape=(
            shape((tokens, features), jnp.float32),
            shape((final_weight.shape[0], features)),
            shape((1, latent.shape[1]), jnp.float32),
        ),
        in_specs=[VMEM] * 11 + [HBM] * 2,
        out_specs=(VMEM,) * 3,
        scratch_shapes=[
            pltpu.VMEM((tokens, width), jnp.bfloat16),
            pltpu.SMEM(step_index.shape, jnp.int32),
            pltpu.SMEM(step_count.shape, jnp.int32),
            pltpu.SemaphoreType.DMA((2,)),
        ],
        compiler_params=params(),
        cost_estimate=lasting(60),
        name="own",
    )(
        q_own,
        *pairs,
        weight,
        hidden,
        modulation,
        first_got,
        final_weight,
        final_got,
        step_index,
        step_count,
    )
    results = ()
    for (start, _), got in ((chunks[0], rest_got), (chunks[1], second_got)):
        results = pl.pallas_call(
            functools.partial(final_kernel, start),
            out_shape=(shape(latent.shape, jnp.float32),) * 2,
            in_specs=[VMEM] * (6 + len(results)),
            out_specs=(VMEM, VMEM),
            compiler_params=params(),
            name="final",
        )(euler, mixed, got, modulation, finals, latent, *results)
    return results


def solution(mesh):
    placed = (
        P(("req", "row"), "col", None, None),
        P(("req", "row"), None, "col"),
        P(),
        P(),
        P(),
        P("col", "row"),
        P(None, "row"),
        P(("req", "row"), "col", None),
        P("req", None),
        P(("req", "row"), "col"),
        P("req"),
        P("req"),
    )
    return jax.shard_map(
        on_device,
        mesh=mesh,
        in_specs=placed,
        out_specs=(P(("req", "row"), "col"), P(("req", "row"), "col")),
        check_vma=False,
    )
```

```python
import functools
import math

import jax
import jax.numpy as jnp
from jax import lax
from jax.experimental import pallas as pl
from jax.experimental.pallas import tpu as pltpu
from jax.sharding import PartitionSpec as P

HEAD = 64
CH = 16
PATCH = 2
STEPS = 28
SHIFT_FACTOR = 3.0
LANES = 128
EPS = 1e-06
VMEM_LIMIT = 16 * 1024 * 1024
VMEM_MOST = 60 * 1024 * 1024
LOADS = 9
FIRST = 768
SWAP = [(0, 1), (1, 0)]


def noise_level(step_number):
    fraction = 1.0 - step_number.astype(jnp.float32) / STEPS
    return SHIFT_FACTOR * fraction / (1.0 + (SHIFT_FACTOR - 1.0) * fraction)


def same_head(width):
    row = lax.broadcasted_iota(jnp.int32, (width, width), 0) // HEAD
    col = lax.broadcasted_iota(jnp.int32, (width, width), 1) // HEAD
    return (row == col).astype(jnp.bfloat16)


def head_norms(pairs):
    ones = same_head(LANES)
    squares = []
    for x, _ in pairs:
        for at in range(0, x.shape[1], LANES):
            square = x[:, at : at + LANES] * x[:, at : at + LANES]
            high = square.astype(jnp.bfloat16)
            low = (square - high.astype(jnp.float32)).astype(jnp.bfloat16)
            squares.append(jnp.concatenate([high, low], axis=1))
    totals = jnp.dot(
        jnp.concatenate(squares, axis=0),
        jnp.concatenate([ones, ones], axis=0),
        preferred_element_type=jnp.float32,
    )
    inverse = lax.rsqrt(totals * (1.0 / HEAD) + EPS)
    results, start = [], 0
    for x, gain in pairs:
        gain = jnp.concatenate([gain, gain], axis=1)
        pieces = []
        for at in range(0, x.shape[1], LANES):
            factor = inverse[start : start + x.shape[0]]
            pieces.append((x[:, at : at + LANES] * factor * gain).astype(jnp.bfloat16))
            start += x.shape[0]
        results.append(jnp.concatenate(pieces, axis=1))
    return results


def load_half(x_ref, held, sems, column):
    tokens, _, width = held.shape
    at = pl.multiple_of(column * width, LANES)
    step = tokens // sems.shape[0]
    copies = [
        pltpu.make_async_copy(
            x_ref.at[start : start + step, :, pl.ds(at, width)],
            held.at[start : start + step],
            sems.at[start // step],
        )
        for start in range(0, tokens, step)
    ]
    for copy in copies:
        copy.start()
    return [(slice(at * step, at * step + step), copy) for at, copy in enumerate(copies)]


def halves(ref):
    rows = ref.shape[0] // 2
    return ref.at[:rows], ref.at[rows:]


def split_kernel(
    x_ref,
    gain_q_ref,
    gain_k_ref,
    gain_t_ref,
    q_first_ref,
    q_second_ref,
    kv_ref,
    gains,
    held,
    sems,
    gain_sems,
):
    blocks = load_half(x_ref, held, sems, 1 - lax.axis_index("col"))
    gain_copies = [
        pltpu.make_async_copy(ref, gains.at[at : at + 1], gain_sems.at[at])
        for at, ref in enumerate((gain_q_ref, gain_k_ref, gain_t_ref))
    ]
    for copy in gain_copies:
        copy.start()
    cut = q_first_ref.shape[0]
    k_ref, v_ref = halves(kv_ref)
    for rows, copy in blocks:
        copy.wait()
        q, k, v = held[rows].astype(jnp.float32).transpose(1, 0, 2).astype(jnp.bfloat16)
        k_ref[rows] = k
        v_ref[rows] = v
        if rows.stop <= cut:
            q_first_ref[rows] = q
        else:
            q_second_ref[rows.start - cut : rows.stop - cut] = q
    for copy in gain_copies:
        copy.wait()


def q_norm_kernel(x_ref, gains, out_ref):
    (out_ref[...],) = head_norms([(x_ref[...].astype(jnp.float32), gains[0:1])])


def kv_norm_kernel(x_ref, gains, out_ref):
    (k_ref, v_ref), (k_out, v_out) = halves(x_ref), halves(out_ref)
    v_out[...] = v_ref[...]
    (k_out[...],) = head_norms([(k_ref[...].astype(jnp.float32), gains[1:2])])


def keys_and_values(refs):
    pairs = [halves(ref) for ref in refs]
    return [keys for keys, _ in pairs], [values for _, values in pairs]


def prep_own_kernel(
    index_ref,
    count_ref,
    x_ref,
    text_ref,
    gains,
    mine_ref,
    theirs_ref,
    kv_ref,
    q_ref,
    gains_out,
    euler_ref,
    weight_ref,
    held,
    sems,
    stack_sems,
):
    tokens = q_ref.shape[0]
    k_ref, v_ref = halves(kv_ref)
    gains_out[...] = gains[...]
    now = jnp.full(euler_ref.shape, index_ref[0], jnp.int32)
    then = now + jnp.full(euler_ref.shape, count_ref[0], jnp.int32)
    euler_ref[...] = noise_level(then) - noise_level(now)
    blocks = load_half(x_ref, held, sems, lax.axis_index("col"))
    rows = mine_ref.shape[0]
    row = lax.axis_index("row")
    stacks = [
        pltpu.make_async_copy(
            ref, weight_ref.at[pl.ds(pl.multiple_of(place * rows, 16), rows)], stack_sems.at[at]
        )
        for at, (ref, place) in enumerate(((mine_ref, row), (theirs_ref, 1 - row)))
    ]
    for stack in stacks:
        stack.start()
    text = text_ref[...].astype(jnp.float32).transpose(1, 0, 2)
    v_ref[tokens:] = text[1].astype(jnp.bfloat16)
    for _, copy in blocks:
        copy.wait()
    q, k, v = held[...].transpose(1, 0, 2)
    v_ref[:tokens] = v
    k_ref[:tokens], k_ref[tokens:], q_ref[...] = head_norms(
        [
            (k.astype(jnp.float32), gains[1:2]),
            (text[0], gains[2:3]),
            (q.astype(jnp.float32), gains[0:1]),
        ]
    )
    for stack in stacks:
        stack.wait()


def attend(q, keys_refs, values_refs, attended_ref):
    tokens, width = q.shape
    first = lax.broadcasted_iota(jnp.int32, (tokens, LANES), 1) < HEAD
    scale = math.log2(math.e) / math.sqrt(HEAD)
    zero = jnp.zeros((tokens, LANES), jnp.bfloat16)
    ones = jnp.ones((sum(ref.shape[0] for ref in keys_refs), LANES), jnp.bfloat16)

    def scores_of(at):
        lanes = slice(at, at + LANES)
        keys = jnp.concatenate([ref[:, lanes] for ref in keys_refs], axis=0)
        block = q[:, lanes]
        both = jnp.concatenate(
            [jnp.where(first, block, zero), jnp.where(first, zero, block)], axis=0
        )
        return lax.dot_general(
            both, keys, (((1,), (1,)), ((), ())), preferred_element_type=jnp.float32
        )

    def finish(at, scores):
        lanes = slice(at, at + LANES)
        values = jnp.concatenate([ref[:, lanes] for ref in values_refs], axis=0)
        weights = jnp.exp2(scores * scale).astype(jnp.bfloat16)
        out = jnp.dot(
            weights,
            jnp.concatenate([values, ones], axis=1),
            preferred_element_type=jnp.float32,
        )
        weighted = jnp.where(first, out[:tokens, :LANES], out[tokens:, :LANES])
        total = jnp.where(first, out[:tokens, LANES:], out[tokens:, LANES:])
        attended_ref[:, lanes] = (weighted / total).astype(jnp.bfloat16)

    ahead = scores_of(0)
    for at in range(0, width, LANES):
        scores = ahead
        if at + LANES < width:
            ahead = scores_of(at + LANES)
        finish(at, scores)


def project(attended, weight_ref, start, upto, store, step):
    for at in range(start, upto, step):
        to = min(at + step, upto)
        product = lax.dot_general(
            attended,
            weight_ref[at:to],
            (((1,), (1,)), ((), ())),
            preferred_element_type=jnp.float32,
        )
        store(at, to, product.astype(jnp.bfloat16))


def attend_kernel(*refs):
    q_ref, (w_ref, out_ref, attended) = refs[0], refs[5:]
    attend(q_ref[...], *keys_and_values(refs[1:5]), attended)

    def keep(at, to, product):
        out_ref[:, at:to] = product

    project(attended[...], w_ref, 0, out_ref.shape[1], keep, FIRST)


def rest_kernel(attended_ref, w_ref, out_ref):
    features, start = w_ref.shape[0], w_ref.shape[0] - out_ref.shape[1]

    def keep(at, to, product):
        out_ref[:, at - start : to - start] = product

    project(attended_ref[...], w_ref, start, features, keep, 640)


def own_kernel(*refs):
    q_ref = refs[0]
    w_ref, hidden_ref, mod_ref, got_ref, mine_ref, theirs_ref = refs[5:11]
    out_ref, finals_ref, attended = refs[11:]
    attend(q_ref[...], *keys_and_values(refs[1:5]), attended)
    tile_rows = hidden_ref.shape[0]

    def keep(at, to, product):
        part = mod_ref[2:3, at:to] * product.astype(jnp.float32)
        held = jnp.concatenate(
            [hidden_ref[row, :, at:to].astype(jnp.float32) for row in range(tile_rows)], axis=0
        )
        out_ref[:, at:to] = held + part

    project(attended[...], w_ref, 0, w_ref.shape[0], keep, 640)
    upto, to = got_ref.shape
    out_ref[:upto, :to] += mod_ref[2:3, :to] * got_ref[...].astype(jnp.float32)
    is_first = lax.axis_index("row") == 0
    mine = mine_ref[...].astype(jnp.float32)
    theirs = theirs_ref[...].astype(jnp.float32)
    finals_ref[...] = jnp.concatenate(
        [jnp.where(is_first, mine, theirs), jnp.where(is_first, theirs, mine)], axis=1
    ).astype(jnp.bfloat16)


def one_hot(dims, condition):
    row = lax.broadcasted_iota(jnp.int32, dims, 0)
    col = lax.broadcasted_iota(jnp.int32, dims, 1)
    return jnp.where(condition(row, col), 1.0, 0.0).astype(jnp.bfloat16)


def to_pixels(velocity, tile_cols):
    tokens, values = velocity.shape
    side = values // PATCH
    out_rows, out_lanes = tokens // tile_cols * PATCH, tile_cols * side
    terms, rest = [], velocity
    for _ in range(3):
        term = rest.astype(jnp.bfloat16)
        rest = rest - term.astype(jnp.float32)
        terms.append(term)
    terms = jnp.concatenate(terms, axis=0)
    row = lax.broadcasted_iota(jnp.int32, (3 * tokens, out_lanes), 0)
    col = lax.broadcasted_iota(jnp.int32, (3 * tokens, out_lanes), 1)
    here = col // side == row % tile_cols
    total = jnp.zeros((out_rows, out_lanes), jnp.float32)
    for at in range(PATCH):
        spread = one_hot((values, out_lanes), lambda r, c: r == c % side + at * side)
        wide = jnp.dot(terms, spread, preferred_element_type=jnp.float32)
        wide = jnp.where(here, wide, 0.0).astype(jnp.bfloat16)
        pick = one_hot(
            (out_rows, 3 * tokens), lambda r, c: r == c % tokens // tile_cols * PATCH + at
        )
        total += jnp.dot(pick, wide, preferred_element_type=jnp.float32)
    return total


def final_kernel(
    start,
    euler_ref,
    mixed_ref,
    rest_ref,
    mod_ref,
    final_ref,
    latent_ref,
    *refs,
):
    velocity_ref, next_ref = refs[-2:]
    tokens = rest_ref.shape[0]
    step = 48
    parts = []
    for at in range(0, tokens, step):
        rows = slice(start + at, start + at + step)
        had = mixed_ref.shape[1] - rest_ref.shape[1]
        mixed = mixed_ref[rows]
        got = rest_ref[at : at + step].astype(jnp.float32)
        added = mixed[:, had:] + mod_ref[2:3, had:] * got
        mixed = jnp.concatenate([mixed[:, :had], added], axis=1) if had else added
        mean = jnp.mean(mixed, axis=-1, keepdims=True)
        centered = mixed - mean
        var = jnp.mean(centered * centered, axis=-1, keepdims=True)
        normed = (
            centered * lax.rsqrt(var + EPS) * (1.0 + mod_ref[1:2]) + mod_ref[0:1]
        ).astype(jnp.bfloat16)
        parts.append(
            lax.dot_general(
                normed,
                final_ref[...],
                (((1,), (1,)), ((), ())),
                preferred_element_type=jnp.float32,
            )
        )
    tile_cols = latent_ref.shape[1] // (final_ref.shape[0] // PATCH)
    velocity = to_pixels(jnp.concatenate(parts, axis=0), tile_cols)
    first = start // tile_cols * PATCH
    pixels = slice(first, first + velocity.shape[0])
    for before_ref, after_ref in zip(refs[:-2], refs[-2:]):
        after_ref[:first] = before_ref[:first]
    velocity_ref[pixels] = velocity
    next_ref[pixels] = latent_ref[pixels] + euler_ref[...] * velocity


def params(limit=VMEM_LIMIT):
    return pltpu.CompilerParams(vmem_limit_bytes=limit)


def lasting(duration):
    return pl.CostEstimate(
        flops=int(duration * 1e9), bytes_accessed=int(duration * 3e6), transcendentals=0
    )


def shape(dims, dtype=jnp.bfloat16):
    return jax.ShapeDtypeStruct(dims, dtype)


VMEM = pl.BlockSpec(memory_space=pltpu.VMEM)
ANY = pl.BlockSpec(memory_space=pl.ANY)
HBM = pl.BlockSpec(memory_space=pltpu.HBM)
SMEM = pl.BlockSpec(memory_space=pltpu.SMEM)


def on_device(
    image_qkv,
    text_kv,
    gain_query,
    gain_key,
    gain_text,
    out_weight,
    final_weight,
    hidden,
    modulation,
    latent,
    step_index,
    step_count,
):
    tile_rows, tile_cols, _, all_width = image_qkv.shape
    tokens = tile_rows * tile_cols
    words = text_kv.shape[0]
    width = all_width // lax.axis_size("col")
    features = hidden.shape[2]
    gains = [gain.reshape(1, HEAD) for gain in (gain_query, gain_key, gain_text)]
    x = image_qkv.reshape(tokens, 3, all_width)
    weight_half = out_weight.T
    held = pltpu.VMEM((tokens, 3, width), jnp.bfloat16)
    block = shape((tokens, width))

    loads = pltpu.SemaphoreType.DMA((LOADS,))
    cut = tile_rows // 3 * tile_cols
    chunks = ((0, cut), (cut, tokens))
    *q_raw, kv_raw, gains = pl.pallas_call(
        split_kernel,
        out_shape=tuple(shape((upto - start, width)) for start, upto in chunks)
        + (shape((2 * tokens, width)), shape((len(gains), HEAD), jnp.float32)),
        in_specs=[HBM] * 4,
        out_specs=(VMEM,) * 4,
        scratch_shapes=[held, loads, pltpu.SemaphoreType.DMA((len(gains),))],
        compiler_params=params(VMEM_MOST),
        name="split",
    )(x, *gains)

    weight_got = lax.ppermute(weight_half, "row", SWAP)
    final_got = lax.ppermute(final_weight, "row", SWAP)
    kv_own, q_own, gains_on, euler, weight = pl.pallas_call(
        prep_own_kernel,
        out_shape=(
            shape((2 * (tokens + words), width)),
            block,
            shape(gains.shape, jnp.float32),
            shape((1, latent.shape[1]), jnp.float32),
            shape((features, width)),
        ),
        in_specs=[SMEM, SMEM, HBM, VMEM, VMEM, ANY, ANY],
        out_specs=(VMEM,) * 5,
        scratch_shapes=[
            held,
            loads,
            pltpu.SemaphoreType.DMA((2,)),
        ],
        compiler_params=params(),
        name="prep_own",
    )(step_index, step_count, x, text_kv, gains, weight_half, weight_got)
    def normed(kernel, got, duration):
        return pl.pallas_call(
            kernel,
            out_shape=shape(got.shape),
            in_specs=[VMEM, VMEM],
            out_specs=VMEM,
            compiler_params=params(),
            cost_estimate=lasting(duration),
            name=kernel.__name__,
        )(got, gains_on)

    kv_got = normed(kv_norm_kernel, lax.ppermute(kv_raw, "col", SWAP), 0)
    q_got = [
        normed(q_norm_kernel, lax.ppermute(raw, "col", SWAP), duration)
        for raw, duration in zip(q_raw, (4.2, 1))
    ]
    pairs = []
    for kv in (kv_own, kv_got):
        pairs += [kv, lax.ppermute(kv, "row", SWAP)]

    def attended(q, projected, scratch):
        rows = q.shape[0]
        out_shape = (shape((rows, projected)),) + (() if scratch else (shape((rows, width)),))
        return pl.pallas_call(
            attend_kernel,
            out_shape=out_shape,
            in_specs=[VMEM] * 6,
            out_specs=(VMEM,) * len(out_shape),
            scratch_shapes=[pltpu.VMEM((rows, width), jnp.bfloat16)] if scratch else (),
            compiler_params=params(),
            name="attend",
        )(q, *pairs, weight)

    first, heads = attended(q_got[0], FIRST, False)
    first_got = lax.ppermute(first, "col", SWAP)
    rest = pl.pallas_call(
        rest_kernel,
        out_shape=shape((cut, features - FIRST)),
        in_specs=[VMEM] * 2,
        out_specs=VMEM,
        compiler_params=params(),
        name="rest",
    )(heads, weight)
    rest_got = lax.ppermute(rest, "col", SWAP)
    second_q, rest = lax.optimization_barrier((q_got[1], rest))
    (second,) = attended(second_q, features, True)
    second_got = lax.ppermute(second, "col", SWAP)
    mixed, finals = pl.pallas_call(
        own_kernel,
        out_shape=(
            shape((tokens, features), jnp.float32),
            shape((final_weight.shape[0], features)),
        ),
        in_specs=[VMEM] * 11,
        out_specs=(VMEM,) * 2,
        scratch_shapes=[pltpu.VMEM((tokens, width), jnp.bfloat16)],
        compiler_params=params(),
        cost_estimate=lasting(60),
        name="own",
    )(
        q_own,
        *pairs,
        weight,
        hidden,
        modulation,
        first_got,
        final_weight,
        final_got,
    )
    results = ()
    for (start, _), got in ((chunks[0], rest_got), (chunks[1], second_got)):
        results = pl.pallas_call(
            functools.partial(final_kernel, start),
            out_shape=(shape(latent.shape, jnp.float32),) * 2,
            in_specs=[VMEM] * (6 + len(results)),
            out_specs=(VMEM, VMEM),
            compiler_params=params(),
            name="final",
        )(euler, mixed, got, modulation, finals, latent, *results)
    return results


def solution(mesh):
    placed = (
        P(("req", "row"), "col", None, None),
        P(("req", "row"), None, "col"),
        P(),
        P(),
        P(),
        P("col", "row"),
        P(None, "row"),
        P(("req", "row"), "col", None),
        P("req", None),
        P(("req", "row"), "col"),
        P("req"),
        P("req"),
    )
    return jax.shard_map(
        on_device,
        mesh=mesh,
        in_specs=placed,
        out_specs=(P(("req", "row"), "col"), P(("req", "row"), "col")),
        check_vma=False,
    )
```

```python
import functools
import math

import jax
import jax.numpy as jnp
from jax import lax
from jax.experimental import pallas as pl
from jax.experimental.pallas import tpu as pltpu
from jax.sharding import PartitionSpec as P

HEAD = 64
CH = 16
PATCH = 2
STEPS = 28
SHIFT_FACTOR = 3.0
LANES = 128
EPS = 1e-06
VMEM_LIMIT = 16 * 1024 * 1024
VMEM_MOST = 60 * 1024 * 1024
LOADS = 9
FIRST = 1280
STEP = 640
SWAP = [(0, 1), (1, 0)]


def noise_level(step_number):
    fraction = 1.0 - step_number.astype(jnp.float32) / STEPS
    return SHIFT_FACTOR * fraction / (1.0 + (SHIFT_FACTOR - 1.0) * fraction)


def same_head(width):
    row = lax.broadcasted_iota(jnp.int32, (width, width), 0) // HEAD
    col = lax.broadcasted_iota(jnp.int32, (width, width), 1) // HEAD
    return (row == col).astype(jnp.bfloat16)


def head_norms(pairs):
    ones = same_head(LANES)
    squares = []
    for x, _ in pairs:
        for at in range(0, x.shape[1], LANES):
            square = x[:, at : at + LANES] * x[:, at : at + LANES]
            high = square.astype(jnp.bfloat16)
            low = (square - high.astype(jnp.float32)).astype(jnp.bfloat16)
            squares.append(jnp.concatenate([high, low], axis=1))
    totals = jnp.dot(
        jnp.concatenate(squares, axis=0),
        jnp.concatenate([ones, ones], axis=0),
        preferred_element_type=jnp.float32,
    )
    inverse = lax.rsqrt(totals * (1.0 / HEAD) + EPS)
    results, start = [], 0
    for x, gain in pairs:
        gain = jnp.concatenate([gain, gain], axis=1)
        pieces = []
        for at in range(0, x.shape[1], LANES):
            factor = inverse[start : start + x.shape[0]]
            pieces.append((x[:, at : at + LANES] * factor * gain).astype(jnp.bfloat16))
            start += x.shape[0]
        results.append(jnp.concatenate(pieces, axis=1))
    return results


def load_half(x_ref, held, sems, column):
    tokens, _, width = held.shape
    at = pl.multiple_of(column * width, LANES)
    step = tokens // sems.shape[0]
    copies = [
        pltpu.make_async_copy(
            x_ref.at[start : start + step, :, pl.ds(at, width)],
            held.at[start : start + step],
            sems.at[start // step],
        )
        for start in range(0, tokens, step)
    ]
    for copy in copies:
        copy.start()
    return [(slice(at * step, at * step + step), copy) for at, copy in enumerate(copies)]


def halves(ref):
    rows = ref.shape[0] // 2
    return ref.at[:rows], ref.at[rows:]


def split_kernel(
    x_ref,
    gain_q_ref,
    gain_k_ref,
    gain_t_ref,
    q_first_ref,
    q_second_ref,
    kv_ref,
    gains,
    held,
    sems,
    gain_sems,
):
    blocks = load_half(x_ref, held, sems, 1 - lax.axis_index("col"))
    gain_copies = [
        pltpu.make_async_copy(ref, gains.at[at : at + 1], gain_sems.at[at])
        for at, ref in enumerate((gain_q_ref, gain_k_ref, gain_t_ref))
    ]
    for copy in gain_copies:
        copy.start()
    cut = q_first_ref.shape[0]
    k_ref, v_ref = halves(kv_ref)
    for rows, copy in blocks:
        copy.wait()
        q, k, v = held[rows].astype(jnp.float32).transpose(1, 0, 2).astype(jnp.bfloat16)
        k_ref[rows] = k
        v_ref[rows] = v
        if rows.stop <= cut:
            q_first_ref[rows] = q
        else:
            q_second_ref[rows.start - cut : rows.stop - cut] = q
    for copy in gain_copies:
        copy.wait()


def q_norm_kernel(x_ref, gains, out_ref):
    (out_ref[...],) = head_norms([(x_ref[...].astype(jnp.float32), gains[0:1])])


def kv_norm_kernel(x_ref, gains, out_ref):
    (k_ref, v_ref), (k_out, v_out) = halves(x_ref), halves(out_ref)
    v_out[...] = v_ref[...]
    (k_out[...],) = head_norms([(k_ref[...].astype(jnp.float32), gains[1:2])])


def keys_and_values(refs):
    pairs = [halves(ref) for ref in refs]
    return [keys for keys, _ in pairs], [values for _, values in pairs]


def prep_own_kernel(
    index_ref, count_ref, x_ref, text_ref, gains, _, kv_ref, q_ref, gains_out, euler_ref, __
):
    tokens, width = q_ref.shape
    k_ref, v_ref = halves(kv_ref)
    gains_out[...] = gains[...]
    now = jnp.full(euler_ref.shape, index_ref[0], jnp.int32)
    then = now + jnp.full(euler_ref.shape, count_ref[0], jnp.int32)
    euler_ref[...] = noise_level(then) - noise_level(now)
    text = text_ref[...].astype(jnp.float32).transpose(1, 0, 2)
    v_ref[tokens:] = text[1].astype(jnp.bfloat16)
    at = pl.multiple_of(lax.axis_index("col") * width, LANES)
    q, k, v = x_ref[:, :, pl.ds(at, width)].transpose(1, 0, 2)
    v_ref[:tokens] = v
    k_ref[:tokens], k_ref[tokens:], q_ref[...] = head_norms(
        [
            (k.astype(jnp.float32), gains[1:2]),
            (text[0], gains[2:3]),
            (q.astype(jnp.float32), gains[0:1]),
        ]
    )


def attend(q, keys_refs, values_refs, attended_ref):
    tokens, width = q.shape
    first = lax.broadcasted_iota(jnp.int32, (tokens, LANES), 1) < HEAD
    scale = math.log2(math.e) / math.sqrt(HEAD)
    zero = jnp.zeros((tokens, LANES), jnp.bfloat16)
    ones = jnp.ones((sum(ref.shape[0] for ref in keys_refs), LANES), jnp.bfloat16)

    def scores_of(at):
        lanes = slice(at, at + LANES)
        keys = jnp.concatenate([ref[:, lanes] for ref in keys_refs], axis=0)
        block = q[:, lanes]
        both = jnp.concatenate(
            [jnp.where(first, block, zero), jnp.where(first, zero, block)], axis=0
        )
        return lax.dot_general(
            both, keys, (((1,), (1,)), ((), ())), preferred_element_type=jnp.float32
        )

    def finish(at, scores):
        lanes = slice(at, at + LANES)
        values = jnp.concatenate([ref[:, lanes] for ref in values_refs], axis=0)
        weights = jnp.exp2(scores * scale).astype(jnp.bfloat16)
        out = jnp.dot(
            weights,
            jnp.concatenate([values, ones], axis=1),
            preferred_element_type=jnp.float32,
        )
        weighted = jnp.where(first, out[:tokens, :LANES], out[tokens:, :LANES])
        total = jnp.where(first, out[:tokens, LANES:], out[tokens:, LANES:])
        attended_ref[:, lanes] = (weighted / total).astype(jnp.bfloat16)

    ahead = scores_of(0)
    for at in range(0, width, LANES):
        scores = ahead
        if at + LANES < width:
            ahead = scores_of(at + LANES)
        finish(at, scores)


def project(attended, halves_refs, start, upto, store):
    half = halves_refs[0].shape[0]
    for at in range(start, upto, STEP):
        to = min(at + STEP, upto)
        parts = []
        for place, ref in enumerate(halves_refs):
            low, high = max(at, place * half), min(to, place * half + half)
            if low < high:
                product = lax.dot_general(
                    attended,
                    ref[low - place * half : high - place * half],
                    (((1,), (1,)), ((), ())),
                    preferred_element_type=jnp.float32,
                )
                parts.append(product.astype(jnp.bfloat16))
        store(at, to, parts[0] if len(parts) == 1 else jnp.concatenate(parts, axis=1))


def attend_kernel(*refs):
    q_ref, weight_refs, (out_ref, attended) = refs[0], refs[5:7], refs[7:]
    attend(q_ref[...], *keys_and_values(refs[1:5]), attended)

    def keep(at, to, product):
        out_ref[:, at:to] = product

    project(attended[...], weight_refs, 0, out_ref.shape[1], keep)


def rest_kernel(attended_ref, mine_ref, theirs_ref, out_ref):
    features = 2 * mine_ref.shape[0]
    start = features - out_ref.shape[1]

    def keep(at, to, product):
        out_ref[:, at - start : to - start] = product

    project(attended_ref[...], (mine_ref, theirs_ref), start, features, keep)


def in_order(x, is_first):
    half = x.shape[1] // 2
    return jnp.where(is_first, x, jnp.concatenate([x[:, half:], x[:, :half]], axis=1))


def own_kernel(*refs):
    q_ref, weight_refs = refs[0], refs[5:7]
    hidden_ref, mod_ref, got_ref, mine_ref, theirs_ref = refs[7:12]
    out_ref, mod_out, finals_ref, attended = refs[12:]
    attend(q_ref[...], *keys_and_values(refs[1:5]), attended)
    is_first = lax.axis_index("row") == 0
    tile_rows, tile_cols, features = hidden_ref.shape
    mod_out[...] = in_order(mod_ref[...], is_first)
    out_ref[...] = in_order(
        jnp.concatenate([hidden_ref[row].astype(jnp.float32) for row in range(tile_rows)], axis=0),
        is_first,
    )

    def keep(at, to, product):
        out_ref[:, at:to] += mod_out[2:3, at:to] * product.astype(jnp.float32)

    project(attended[...], weight_refs, 0, features, keep)
    upto, to = got_ref.shape
    out_ref[:upto, :to] += mod_out[2:3, :to] * got_ref[...].astype(jnp.float32)
    finals_ref[...] = jnp.concatenate(
        [mine_ref[...].astype(jnp.float32), theirs_ref[...].astype(jnp.float32)], axis=1
    ).astype(jnp.bfloat16)


def one_hot(dims, condition):
    row = lax.broadcasted_iota(jnp.int32, dims, 0)
    col = lax.broadcasted_iota(jnp.int32, dims, 1)
    return jnp.where(condition(row, col), 1.0, 0.0).astype(jnp.bfloat16)


def to_pixels(velocity, tile_cols):
    tokens, values = velocity.shape
    side = values // PATCH
    out_rows, out_lanes = tokens // tile_cols * PATCH, tile_cols * side
    terms, rest = [], velocity
    for _ in range(3):
        term = rest.astype(jnp.bfloat16)
        rest = rest - term.astype(jnp.float32)
        terms.append(term)
    terms = jnp.concatenate(terms, axis=0)
    row = lax.broadcasted_iota(jnp.int32, (3 * tokens, out_lanes), 0)
    col = lax.broadcasted_iota(jnp.int32, (3 * tokens, out_lanes), 1)
    here = col // side == row % tile_cols
    total = jnp.zeros((out_rows, out_lanes), jnp.float32)
    for at in range(PATCH):
        spread = one_hot((values, out_lanes), lambda r, c: r == c % side + at * side)
        wide = jnp.dot(terms, spread, preferred_element_type=jnp.float32)
        wide = jnp.where(here, wide, 0.0).astype(jnp.bfloat16)
        pick = one_hot(
            (out_rows, 3 * tokens), lambda r, c: r == c % tokens // tile_cols * PATCH + at
        )
        total += jnp.dot(pick, wide, preferred_element_type=jnp.float32)
    return total


def final_kernel(
    start,
    euler_ref,
    mixed_ref,
    rest_ref,
    mod_ref,
    final_ref,
    latent_ref,
    *refs,
):
    velocity_ref, next_ref = refs[-2:]
    tokens = rest_ref.shape[0]
    step = 48
    parts = []
    for at in range(0, tokens, step):
        rows = slice(start + at, start + at + step)
        had = mixed_ref.shape[1] - rest_ref.shape[1]
        mixed = mixed_ref[rows]
        got = rest_ref[at : at + step].astype(jnp.float32)
        added = mixed[:, had:] + mod_ref[2:3, had:] * got
        mixed = jnp.concatenate([mixed[:, :had], added], axis=1) if had else added
        mean = jnp.mean(mixed, axis=-1, keepdims=True)
        centered = mixed - mean
        var = jnp.mean(centered * centered, axis=-1, keepdims=True)
        normed = (
            centered * lax.rsqrt(var + EPS) * (1.0 + mod_ref[1:2]) + mod_ref[0:1]
        ).astype(jnp.bfloat16)
        parts.append(
            lax.dot_general(
                normed,
                final_ref[...],
                (((1,), (1,)), ((), ())),
                preferred_element_type=jnp.float32,
            )
        )
    tile_cols = latent_ref.shape[1] // (final_ref.shape[0] // PATCH)
    velocity = to_pixels(jnp.concatenate(parts, axis=0), tile_cols)
    first = start // tile_cols * PATCH
    pixels = slice(first, first + velocity.shape[0])
    for before_ref, after_ref in zip(refs[:-2], refs[-2:]):
        after_ref[:first] = before_ref[:first]
    velocity_ref[pixels] = velocity
    next_ref[pixels] = latent_ref[pixels] + euler_ref[...] * velocity


def params(limit=VMEM_LIMIT):
    return pltpu.CompilerParams(vmem_limit_bytes=limit)


def lasting(duration):
    return pl.CostEstimate(
        flops=int(duration * 1e9), bytes_accessed=int(duration * 3e6), transcendentals=0
    )


def shape(dims, dtype=jnp.bfloat16):
    return jax.ShapeDtypeStruct(dims, dtype)


VMEM = pl.BlockSpec(memory_space=pltpu.VMEM)
ANY = pl.BlockSpec(memory_space=pl.ANY)
HBM = pl.BlockSpec(memory_space=pltpu.HBM)
SMEM = pl.BlockSpec(memory_space=pltpu.SMEM)


def on_device(
    image_qkv,
    text_kv,
    gain_query,
    gain_key,
    gain_text,
    out_weight,
    final_weight,
    hidden,
    modulation,
    latent,
    step_index,
    step_count,
):
    tile_rows, tile_cols, _, all_width = image_qkv.shape
    tokens = tile_rows * tile_cols
    words = text_kv.shape[0]
    width = all_width // lax.axis_size("col")
    features = hidden.shape[2]
    gains = [gain.reshape(1, HEAD) for gain in (gain_query, gain_key, gain_text)]
    x = image_qkv.reshape(tokens, 3, all_width)
    weight_half = out_weight.T
    held = pltpu.VMEM((tokens, 3, width), jnp.bfloat16)
    block = shape((tokens, width))

    loads = pltpu.SemaphoreType.DMA((LOADS,))
    cut = tile_rows // 3 * tile_cols
    chunks = ((0, cut), (cut, tokens))
    *q_raw, kv_raw, gains = pl.pallas_call(
        split_kernel,
        out_shape=tuple(shape((upto - start, width)) for start, upto in chunks)
        + (shape((2 * tokens, width)), shape((len(gains), HEAD), jnp.float32)),
        in_specs=[HBM] * 4,
        out_specs=(VMEM,) * 4,
        scratch_shapes=[held, loads, pltpu.SemaphoreType.DMA((len(gains),))],
        compiler_params=params(VMEM_MOST),
        name="split",
    )(x, *gains)

    weight_got = lax.ppermute(weight_half, "row", SWAP)
    final_got = lax.ppermute(final_weight, "row", SWAP)
    kv_own, q_own, gains_on, euler, weight_theirs = pl.pallas_call(
        prep_own_kernel,
        out_shape=(
            shape((2 * (tokens + words), width)),
            block,
            shape(gains.shape, jnp.float32),
            shape((1, latent.shape[1]), jnp.float32),
            shape(weight_got.shape),
        ),
        in_specs=[SMEM, SMEM, VMEM, VMEM, VMEM, ANY],
        out_specs=(VMEM,) * 4 + (ANY,),
        input_output_aliases={5: 4},
        compiler_params=params(),
        name="prep_own",
    )(step_index, step_count, x, text_kv, gains, weight_got)
    weights = (weight_half, weight_theirs)

    def normed(kernel, got, duration):
        return pl.pallas_call(
            kernel,
            out_shape=shape(got.shape),
            in_specs=[VMEM, VMEM],
            out_specs=VMEM,
            compiler_params=params(),
            cost_estimate=lasting(duration),
            name=kernel.__name__,
        )(got, gains_on)

    kv_got = normed(kv_norm_kernel, lax.ppermute(kv_raw, "col", SWAP), 0)
    q_got = [
        normed(q_norm_kernel, lax.ppermute(raw, "col", SWAP), duration)
        for raw, duration in zip(q_raw, (4.2, 1))
    ]
    pairs = []
    for kv in (kv_own, kv_got):
        pairs += [kv, lax.ppermute(kv, "row", SWAP)]

    def attended(q, projected, scratch):
        rows = q.shape[0]
        out_shape = (shape((rows, projected)),) + (() if scratch else (shape((rows, width)),))
        return pl.pallas_call(
            attend_kernel,
            out_shape=out_shape,
            in_specs=[VMEM] * 7,
            out_specs=(VMEM,) * len(out_shape),
            scratch_shapes=[pltpu.VMEM((rows, width), jnp.bfloat16)] if scratch else (),
            compiler_params=params(),
            name="attend",
        )(q, *pairs, *weights)

    first, heads = attended(q_got[0], FIRST, False)
    first_got = lax.ppermute(first, "col", SWAP)
    rest = pl.pallas_call(
        rest_kernel,
        out_shape=shape((cut, features - FIRST)),
        in_specs=[VMEM] * 3,
        out_specs=VMEM,
        compiler_params=params(),
        name="rest",
    )(heads, *weights)
    rest_got = lax.ppermute(rest, "col", SWAP)
    second_q, rest = lax.optimization_barrier((q_got[1], rest))
    (second,) = attended(second_q, features, True)
    second_got = lax.ppermute(second, "col", SWAP)
    mixed, mods, finals = pl.pallas_call(
        own_kernel,
        out_shape=(
            shape((tokens, features), jnp.float32),
            shape(modulation.shape, jnp.float32),
            shape((final_weight.shape[0], features)),
        ),
        in_specs=[VMEM] * 12,
        out_specs=(VMEM,) * 3,
        scratch_shapes=[pltpu.VMEM((tokens, width), jnp.bfloat16)],
        compiler_params=params(),
        cost_estimate=lasting(60),
        name="own",
    )(
        q_own,
        *pairs,
        *weights,
        hidden,
        modulation,
        first_got,
        final_weight,
        final_got,
    )
    results = ()
    for (start, _), got in ((chunks[0], rest_got), (chunks[1], second_got)):
        results = pl.pallas_call(
            functools.partial(final_kernel, start),
            out_shape=(shape(latent.shape, jnp.float32),) * 2,
            in_specs=[VMEM] * (6 + len(results)),
            out_specs=(VMEM, VMEM),
            compiler_params=params(),
            name="final",
        )(euler, mixed, got, mods, finals, latent, *results)
    return results


def solution(mesh):
    placed = (
        P(("req", "row"), "col", None, None),
        P(("req", "row"), None, "col"),
        P(),
        P(),
        P(),
        P("col", "row"),
        P(None, "row"),
        P(("req", "row"), "col", None),
        P("req", None),
        P(("req", "row"), "col"),
        P("req"),
        P("req"),
    )
    return jax.shard_map(
        on_device,
        mesh=mesh,
        in_specs=placed,
        out_specs=(P(("req", "row"), "col"), P(("req", "row"), "col")),
        check_vma=False,
    )
```

```python
import functools
import math

import jax
import jax.numpy as jnp
from jax import lax
from jax.experimental import pallas as pl
from jax.experimental.pallas import tpu as pltpu
from jax.sharding import PartitionSpec as P

HEAD = 64
CH = 16
PATCH = 2
STEPS = 28
SHIFT_FACTOR = 3.0
LANES = 128
EPS = 1e-06
VMEM_LIMIT = 16 * 1024 * 1024
VMEM_MOST = 60 * 1024 * 1024
LOADS = 3
FIRST = 1280
STEP = 640
SWAP = [(0, 1), (1, 0)]


def noise_level(step_number):
    fraction = 1.0 - step_number.astype(jnp.float32) / STEPS
    return SHIFT_FACTOR * fraction / (1.0 + (SHIFT_FACTOR - 1.0) * fraction)


def same_head(width):
    row = lax.broadcasted_iota(jnp.int32, (width, width), 0) // HEAD
    col = lax.broadcasted_iota(jnp.int32, (width, width), 1) // HEAD
    return (row == col).astype(jnp.bfloat16)


def head_norms(pairs):
    ones = same_head(LANES)
    squares = []
    for x, _ in pairs:
        for at in range(0, x.shape[1], LANES):
            square = x[:, at : at + LANES] * x[:, at : at + LANES]
            high = square.astype(jnp.bfloat16)
            low = (square - high.astype(jnp.float32)).astype(jnp.bfloat16)
            squares.append(jnp.concatenate([high, low], axis=1))
    totals = jnp.dot(
        jnp.concatenate(squares, axis=0),
        jnp.concatenate([ones, ones], axis=0),
        preferred_element_type=jnp.float32,
    )
    inverse = lax.rsqrt(totals * (1.0 / HEAD) + EPS)
    results, start = [], 0
    for x, gain in pairs:
        gain = jnp.concatenate([gain, gain], axis=1)
        pieces = []
        for at in range(0, x.shape[1], LANES):
            factor = inverse[start : start + x.shape[0]]
            pieces.append((x[:, at : at + LANES] * factor * gain).astype(jnp.bfloat16))
            start += x.shape[0]
        results.append(jnp.concatenate(pieces, axis=1))
    return results


def load_half(x_ref, held, sems, column):
    tokens, _, width = held.shape
    at = pl.multiple_of(column * width, LANES)
    step = tokens // sems.shape[0]
    copies = [
        pltpu.make_async_copy(
            x_ref.at[start : start + step, :, pl.ds(at, width)],
            held.at[start : start + step],
            sems.at[start // step],
        )
        for start in range(0, tokens, step)
    ]
    for copy in copies:
        copy.start()
    return [(slice(at * step, at * step + step), copy) for at, copy in enumerate(copies)]


def halves(ref):
    rows = ref.shape[0] // 2
    return ref.at[:rows], ref.at[rows:]


def three(ref, tokens):
    return ref.at[:tokens], ref.at[tokens : 2 * tokens], ref.at[2 * tokens :]


def split_kernel(
    x_ref,
    gain_q_ref,
    gain_k_ref,
    gain_t_ref,
    first_ref,
    q_second_ref,
    gains,
    held,
    sems,
    gain_sems,
):
    blocks = load_half(x_ref, held, sems, 1 - lax.axis_index("col"))
    gain_copies = [
        pltpu.make_async_copy(ref, gains.at[at : at + 1], gain_sems.at[at])
        for at, ref in enumerate((gain_q_ref, gain_k_ref, gain_t_ref))
    ]
    for copy in gain_copies:
        copy.start()
    tokens = held.shape[0]
    k_ref, v_ref, q_first_ref = three(first_ref, tokens)
    cut = q_first_ref.shape[0]
    for rows, copy in blocks:
        copy.wait()
        q, k, v = held[rows].transpose(1, 0, 2)
        k_ref[rows] = k
        v_ref[rows] = v
        if rows.stop <= cut:
            q_first_ref[rows] = q
        else:
            q_second_ref[rows.start - cut : rows.stop - cut] = q
    for copy in gain_copies:
        copy.wait()


def q_norm(x_ref, gains):
    (q,) = head_norms([(x_ref[...].astype(jnp.float32), gains[0:1])])
    return q


def norm_kernel(x_ref, gains, kv_ref, q_ref):
    k, v, q = three(x_ref, kv_ref.shape[0] // 2)
    k_out, v_out = halves(kv_ref)
    v_out[...] = v[...]
    k_out[...], q_ref[...] = head_norms(
        [(k[...].astype(jnp.float32), gains[1:2]), (q[...].astype(jnp.float32), gains[0:1])]
    )


def keys_and_values(refs):
    k_own, v_own, k_row, v_row, *joined = refs
    pairs = [(k_own, v_own), (k_row, v_row)] + [halves(ref) for ref in joined]
    return [keys for keys, _ in pairs], [values for _, values in pairs]


def prep_own_kernel(
    index_ref, count_ref, x_ref, text_ref, gains, _, k_ref, v_ref, q_ref, gains_out, euler_ref, __
):
    tokens, width = q_ref.shape
    gains_out[...] = gains[...]
    now = jnp.full(euler_ref.shape, index_ref[0], jnp.int32)
    then = now + jnp.full(euler_ref.shape, count_ref[0], jnp.int32)
    euler_ref[...] = noise_level(then) - noise_level(now)
    text = text_ref[...].astype(jnp.float32).transpose(1, 0, 2)
    v_ref[tokens:] = text[1].astype(jnp.bfloat16)
    at = pl.multiple_of(lax.axis_index("col") * width, LANES)
    q, k, v = x_ref[:, :, pl.ds(at, width)].transpose(1, 0, 2)
    v_ref[:tokens] = v
    k_ref[:tokens], k_ref[tokens:], q_ref[...] = head_norms(
        [
            (k.astype(jnp.float32), gains[1:2]),
            (text[0], gains[2:3]),
            (q.astype(jnp.float32), gains[0:1]),
        ]
    )


def attend(q, keys_refs, values_refs, store):
    tokens, width = q.shape
    first = lax.broadcasted_iota(jnp.int32, (tokens, LANES), 1) < HEAD
    scale = math.log2(math.e) / math.sqrt(HEAD)
    zero = jnp.zeros((tokens, LANES), jnp.bfloat16)
    ones = jnp.ones((sum(ref.shape[0] for ref in keys_refs), LANES), jnp.bfloat16)

    def scores_of(at):
        lanes = slice(at, at + LANES)
        keys = jnp.concatenate([ref[:, lanes] for ref in keys_refs], axis=0)
        block = q[:, lanes]
        both = jnp.concatenate(
            [jnp.where(first, block, zero), jnp.where(first, zero, block)], axis=0
        )
        return lax.dot_general(
            both, keys, (((1,), (1,)), ((), ())), preferred_element_type=jnp.float32
        )

    def finish(at, scores):
        lanes = slice(at, at + LANES)
        values = jnp.concatenate([ref[:, lanes] for ref in values_refs], axis=0)
        weights = jnp.exp2(scores * scale).astype(jnp.bfloat16)
        out = jnp.dot(
            weights,
            jnp.concatenate([values, ones], axis=1),
            preferred_element_type=jnp.float32,
        )
        weighted = jnp.where(first, out[:tokens, :LANES], out[tokens:, :LANES])
        total = jnp.where(first, out[:tokens, LANES:], out[tokens:, LANES:])
        store(lanes, weighted, total)

    ahead = scores_of(0)
    for at in range(0, width, LANES):
        scores = ahead
        if at + LANES < width:
            ahead = scores_of(at + LANES)
        finish(at, scores)


def project(attended, halves_refs, start, upto, store):
    half = halves_refs[0].shape[0]
    for at in range(start, upto, STEP):
        to = min(at + STEP, upto)
        parts = []
        for place, ref in enumerate(halves_refs):
            low, high = max(at, place * half), min(to, place * half + half)
            if low < high:
                product = lax.dot_general(
                    attended,
                    ref[low - place * half : high - place * half],
                    (((1,), (1,)), ((), ())),
                    preferred_element_type=jnp.float32,
                )
                parts.append(product.astype(jnp.bfloat16))
        store(at, to, parts[0] if len(parts) == 1 else jnp.concatenate(parts, axis=1))


def divide_into(ref):
    def store(lanes, weighted, total):
        ref[:, lanes] = (weighted / total).astype(jnp.bfloat16)

    return store


def part_kernel(q_ref, *refs):
    sum_ref, total_ref = refs[5:]

    def store(lanes, weighted, total):
        sum_ref[:, lanes] = weighted
        total_ref[:, lanes] = total

    attend(q_ref[...], *keys_and_values(refs[:5]), store)


def first_kernel(
    q_ref, last_ref, sum_ref, total_ref, mine_ref, theirs_ref, out_ref, attended
):
    finish = divide_into(attended)

    def store(lanes, weighted, total):
        finish(lanes, weighted + sum_ref[:, lanes], total + total_ref[:, lanes])

    keys, values = halves(last_ref)
    attend(q_ref[...], [keys], [values], store)

    def keep(at, to, product):
        out_ref[:, at:to] = product

    project(attended[...], (mine_ref, theirs_ref), 0, out_ref.shape[1], keep)


def second_kernel(*refs):
    x_ref, gains, weight_refs, (out_ref, attended) = refs[0], refs[1], refs[8:10], refs[10:]
    attend(q_norm(x_ref, gains), *keys_and_values(refs[2:8]), divide_into(attended))

    def keep(at, to, product):
        out_ref[:, at:to] = product

    project(attended[...], weight_refs, 0, out_ref.shape[1], keep)


def rest_kernel(attended_ref, mine_ref, theirs_ref, out_ref):
    features = 2 * mine_ref.shape[0]
    start = features - out_ref.shape[1]

    def keep(at, to, product):
        out_ref[:, at - start : to - start] = product

    project(attended_ref[...], (mine_ref, theirs_ref), start, features, keep)


def in_order(x, is_first):
    half = x.shape[1] // 2
    return jnp.where(is_first, x, jnp.concatenate([x[:, half:], x[:, :half]], axis=1))


def own_kernel(*refs):
    q_ref, weight_refs = refs[0], refs[7:9]
    hidden_ref, mod_ref, got_ref, mine_ref, theirs_ref = refs[9:14]
    out_ref, mod_out, finals_ref, attended = refs[14:]
    attend(q_ref[...], *keys_and_values(refs[1:7]), divide_into(attended))
    is_first = lax.axis_index("row") == 0
    tile_rows, tile_cols, features = hidden_ref.shape
    mod_out[...] = in_order(mod_ref[...], is_first)
    out_ref[...] = in_order(
        jnp.concatenate([hidden_ref[row].astype(jnp.float32) for row in range(tile_rows)], axis=0),
        is_first,
    )

    def keep(at, to, product):
        out_ref[:, at:to] += mod_out[2:3, at:to] * product.astype(jnp.float32)

    project(attended[...], weight_refs, 0, features, keep)
    upto, to = got_ref.shape
    out_ref[:upto, :to] += mod_out[2:3, :to] * got_ref[...].astype(jnp.float32)
    finals_ref[...] = jnp.concatenate(
        [mine_ref[...].astype(jnp.float32), theirs_ref[...].astype(jnp.float32)], axis=1
    ).astype(jnp.bfloat16)


def one_hot(dims, condition):
    row = lax.broadcasted_iota(jnp.int32, dims, 0)
    col = lax.broadcasted_iota(jnp.int32, dims, 1)
    return jnp.where(condition(row, col), 1.0, 0.0).astype(jnp.bfloat16)


def to_pixels(velocity, tile_cols):
    tokens, values = velocity.shape
    side = values // PATCH
    out_rows, out_lanes = tokens // tile_cols * PATCH, tile_cols * side
    terms, rest = [], velocity
    for _ in range(3):
        term = rest.astype(jnp.bfloat16)
        rest = rest - term.astype(jnp.float32)
        terms.append(term)
    terms = jnp.concatenate(terms, axis=0)
    row = lax.broadcasted_iota(jnp.int32, (3 * tokens, out_lanes), 0)
    col = lax.broadcasted_iota(jnp.int32, (3 * tokens, out_lanes), 1)
    here = col // side == row % tile_cols
    total = jnp.zeros((out_rows, out_lanes), jnp.float32)
    for at in range(PATCH):
        spread = one_hot((values, out_lanes), lambda r, c: r == c % side + at * side)
        wide = jnp.dot(terms, spread, preferred_element_type=jnp.float32)
        wide = jnp.where(here, wide, 0.0).astype(jnp.bfloat16)
        pick = one_hot(
            (out_rows, 3 * tokens), lambda r, c: r == c % tokens // tile_cols * PATCH + at
        )
        total += jnp.dot(pick, wide, preferred_element_type=jnp.float32)
    return total


def final_kernel(
    start,
    euler_ref,
    mixed_ref,
    rest_ref,
    mod_ref,
    final_ref,
    latent_ref,
    *refs,
):
    velocity_ref, next_ref = refs[-2:]
    tokens = rest_ref.shape[0]
    step = 48
    parts = []
    for at in range(0, tokens, step):
        rows = slice(start + at, start + at + step)
        had = mixed_ref.shape[1] - rest_ref.shape[1]
        mixed = mixed_ref[rows]
        got = rest_ref[at : at + step].astype(jnp.float32)
        added = mixed[:, had:] + mod_ref[2:3, had:] * got
        mixed = jnp.concatenate([mixed[:, :had], added], axis=1) if had else added
        mean = jnp.mean(mixed, axis=-1, keepdims=True)
        centered = mixed - mean
        var = jnp.mean(centered * centered, axis=-1, keepdims=True)
        normed = (
            centered * lax.rsqrt(var + EPS) * (1.0 + mod_ref[1:2]) + mod_ref[0:1]
        ).astype(jnp.bfloat16)
        parts.append(
            lax.dot_general(
                normed,
                final_ref[...],
                (((1,), (1,)), ((), ())),
                preferred_element_type=jnp.float32,
            )
        )
    tile_cols = latent_ref.shape[1] // (final_ref.shape[0] // PATCH)
    velocity = to_pixels(jnp.concatenate(parts, axis=0), tile_cols)
    first = start // tile_cols * PATCH
    pixels = slice(first, first + velocity.shape[0])
    for before_ref, after_ref in zip(refs[:-2], refs[-2:]):
        after_ref[:first] = before_ref[:first]
    velocity_ref[pixels] = velocity
    next_ref[pixels] = latent_ref[pixels] + euler_ref[...] * velocity


def params(limit=VMEM_LIMIT):
    return pltpu.CompilerParams(vmem_limit_bytes=limit)


def lasting(duration):
    return pl.CostEstimate(
        flops=int(duration * 1e9), bytes_accessed=int(duration * 3e6), transcendentals=0
    )


def shape(dims, dtype=jnp.bfloat16):
    return jax.ShapeDtypeStruct(dims, dtype)


VMEM = pl.BlockSpec(memory_space=pltpu.VMEM)
ANY = pl.BlockSpec(memory_space=pl.ANY)
HBM = pl.BlockSpec(memory_space=pltpu.HBM)
SMEM = pl.BlockSpec(memory_space=pltpu.SMEM)


def on_device(
    image_qkv,
    text_kv,
    gain_query,
    gain_key,
    gain_text,
    out_weight,
    final_weight,
    hidden,
    modulation,
    latent,
    step_index,
    step_count,
):
    tile_rows, tile_cols, _, all_width = image_qkv.shape
    tokens = tile_rows * tile_cols
    words = text_kv.shape[0]
    width = all_width // lax.axis_size("col")
    features = hidden.shape[2]
    gains = [gain.reshape(1, HEAD) for gain in (gain_query, gain_key, gain_text)]
    x = image_qkv.reshape(tokens, 3, all_width)
    weight_half = out_weight.T
    held = pltpu.VMEM((tokens, 3, width), jnp.bfloat16)
    block = shape((tokens, width))

    loads = pltpu.SemaphoreType.DMA((LOADS,))
    cut = tile_rows // 3 * tile_cols
    chunks = ((0, cut), (cut, tokens))
    first_raw, second_raw, gains = pl.pallas_call(
        split_kernel,
        out_shape=(
            shape((2 * tokens + cut, width)),
            shape((tokens - cut, width)),
            shape((len(gains), HEAD), jnp.float32),
        ),
        in_specs=[HBM] * 4,
        out_specs=(VMEM,) * 3,
        scratch_shapes=[held, loads, pltpu.SemaphoreType.DMA((len(gains),))],
        compiler_params=params(VMEM_MOST),
        name="split",
    )(x, *gains)

    weight_got = lax.ppermute(weight_half, "row", SWAP)
    final_got = lax.ppermute(final_weight, "row", SWAP)
    k_own, v_own, q_own, gains_on, euler, weight_theirs = pl.pallas_call(
        prep_own_kernel,
        out_shape=(
            shape((tokens + words, width)),
            shape((tokens + words, width)),
            block,
            shape(gains.shape, jnp.float32),
            shape((1, latent.shape[1]), jnp.float32),
            shape(weight_got.shape),
        ),
        in_specs=[SMEM, SMEM, VMEM, VMEM, VMEM, ANY],
        out_specs=(VMEM,) * 5 + (ANY,),
        input_output_aliases={5: 5},
        compiler_params=params(),
        name="prep_own",
    )(step_index, step_count, x, text_kv, gains, weight_got)
    weights = (weight_half, weight_theirs)

    kv_got, q_first = pl.pallas_call(
        norm_kernel,
        out_shape=(shape((2 * tokens, width)), shape((cut, width))),
        in_specs=[VMEM] * 2,
        out_specs=(VMEM,) * 2,
        compiler_params=params(),
        name="norm",
    )(lax.ppermute(first_raw, "col", SWAP), gains_on)
    q_second = lax.ppermute(second_raw, "col", SWAP)
    k_row, v_row, kv_last = (lax.ppermute(x, "row", SWAP) for x in (k_own, v_own, kv_got))
    pairs = (k_own, v_own, k_row, v_row, kv_got, kv_last)
    sums = pl.pallas_call(
        part_kernel,
        out_shape=(shape((cut, width), jnp.float32),) * 2,
        in_specs=[VMEM] * 6,
        out_specs=(VMEM,) * 2,
        compiler_params=params(),
        cost_estimate=lasting(4.5),
        name="part",
    )(q_first, *pairs[:5])
    first, heads = pl.pallas_call(
        first_kernel,
        out_shape=(shape((cut, FIRST)), shape((cut, width))),
        in_specs=[VMEM] * 6,
        out_specs=(VMEM,) * 2,
        compiler_params=params(),
        name="first",
    )(q_first, kv_last, *sums, *weights)
    first_got = lax.ppermute(first, "col", SWAP)
    rest = pl.pallas_call(
        rest_kernel,
        out_shape=shape((cut, features - FIRST)),
        in_specs=[VMEM] * 3,
        out_specs=VMEM,
        compiler_params=params(),
        name="rest",
    )(heads, *weights)
    rest_got = lax.ppermute(rest, "col", SWAP)
    q_second, rest = lax.optimization_barrier((q_second, rest))
    second = pl.pallas_call(
        second_kernel,
        out_shape=shape((tokens - cut, features)),
        in_specs=[VMEM] * 10,
        out_specs=VMEM,
        scratch_shapes=[pltpu.VMEM((tokens - cut, width), jnp.bfloat16)],
        compiler_params=params(),
        name="second",
    )(q_second, gains_on, *pairs, *weights)
    second_got = lax.ppermute(second, "col", SWAP)
    mixed, mods, finals = pl.pallas_call(
        own_kernel,
        out_shape=(
            shape((tokens, features), jnp.float32),
            shape(modulation.shape, jnp.float32),
            shape((final_weight.shape[0], features)),
        ),
        in_specs=[VMEM] * 14,
        out_specs=(VMEM,) * 3,
        scratch_shapes=[pltpu.VMEM((tokens, width), jnp.bfloat16)],
        compiler_params=params(),
        cost_estimate=lasting(60),
        name="own",
    )(
        q_own,
        *pairs,
        *weights,
        hidden,
        modulation,
        first_got,
        final_weight,
        final_got,
    )
    results = ()
    for (start, _), got in ((chunks[0], rest_got), (chunks[1], second_got)):
        results = pl.pallas_call(
            functools.partial(final_kernel, start),
            out_shape=(shape(latent.shape, jnp.float32),) * 2,
            in_specs=[VMEM] * (6 + len(results)),
            out_specs=(VMEM, VMEM),
            compiler_params=params(),
            name="final",
        )(euler, mixed, got, mods, finals, latent, *results)
    return results


def solution(mesh):
    placed = (
        P(("req", "row"), "col", None, None),
        P(("req", "row"), None, "col"),
        P(),
        P(),
        P(),
        P("col", "row"),
        P(None, "row"),
        P(("req", "row"), "col", None),
        P("req", None),
        P(("req", "row"), "col"),
        P("req"),
        P("req"),
    )
    return jax.shard_map(
        on_device,
        mesh=mesh,
        in_specs=placed,
        out_specs=(P(("req", "row"), "col"), P(("req", "row"), "col")),
        check_vma=False,
    )
```

```python
import functools
import math

import jax
import jax.numpy as jnp
from jax import lax
from jax.experimental import pallas as pl
from jax.experimental.pallas import tpu as pltpu
from jax.sharding import PartitionSpec as P

HEAD = 64
CH = 16
PATCH = 2
STEPS = 28
SHIFT_FACTOR = 3.0
LANES = 128
EPS = 1e-06
VMEM_LIMIT = 16 * 1024 * 1024
VMEM_MOST = 52 * 1024 * 1024
LOADS = 3
STEP = 640
SWAP = [(0, 1), (1, 0)]


def noise_level(step_number):
    fraction = 1.0 - step_number.astype(jnp.float32) / STEPS
    return SHIFT_FACTOR * fraction / (1.0 + (SHIFT_FACTOR - 1.0) * fraction)


def same_head(width):
    row = lax.broadcasted_iota(jnp.int32, (width, width), 0) // HEAD
    col = lax.broadcasted_iota(jnp.int32, (width, width), 1) // HEAD
    return (row == col).astype(jnp.bfloat16)


def head_norms(pairs):
    ones = same_head(LANES)
    squares = []
    for x, _ in pairs:
        for at in range(0, x.shape[1], LANES):
            square = x[:, at : at + LANES] * x[:, at : at + LANES]
            high = square.astype(jnp.bfloat16)
            low = (square - high.astype(jnp.float32)).astype(jnp.bfloat16)
            squares.append(jnp.concatenate([high, low], axis=1))
    totals = jnp.dot(
        jnp.concatenate(squares, axis=0),
        jnp.concatenate([ones, ones], axis=0),
        preferred_element_type=jnp.float32,
    )
    inverse = lax.rsqrt(totals * (1.0 / HEAD) + EPS)
    results, start = [], 0
    for x, gain in pairs:
        gain = jnp.concatenate([gain, gain], axis=1)
        pieces = []
        for at in range(0, x.shape[1], LANES):
            factor = inverse[start : start + x.shape[0]]
            pieces.append((x[:, at : at + LANES] * factor * gain).astype(jnp.bfloat16))
            start += x.shape[0]
        results.append(jnp.concatenate(pieces, axis=1))
    return results


def load_half(x_ref, held, sems, column):
    tokens, _, width = held.shape
    at = pl.multiple_of(column * width, LANES)
    step = tokens // sems.shape[0]
    copies = [
        pltpu.make_async_copy(
            x_ref.at[start : start + step, :, pl.ds(at, width)],
            held.at[start : start + step],
            sems.at[start // step],
        )
        for start in range(0, tokens, step)
    ]
    for copy in copies:
        copy.start()
    return [(slice(at * step, at * step + step), copy) for at, copy in enumerate(copies)]


def halves(ref):
    rows = ref.shape[0] // 2
    return ref.at[:rows], ref.at[rows:]


def split_kernel(
    x_ref,
    q_first_ref,
    q_second_ref,
    kv_ref,
    own_ref,
    held,
    sems,
    own_sems,
):
    column = lax.axis_index("col")
    blocks = load_half(x_ref, held, sems, 1 - column)
    own_blocks = load_half(x_ref, own_ref, own_sems, column)
    cut = q_first_ref.shape[0]
    k_ref, v_ref = halves(kv_ref)
    for rows, copy in blocks:
        copy.wait()
        q, k, v = held[rows].transpose(1, 0, 2)
        k_ref[rows] = k
        v_ref[rows] = v
        if rows.stop <= cut:
            q_first_ref[rows] = q
        else:
            q_second_ref[rows.start - cut : rows.stop - cut] = q
    for _, copy in own_blocks:
        copy.wait()


def q_norm_kernel(x_ref, gains, out_ref):
    (out_ref[...],) = head_norms([(x_ref[...].astype(jnp.float32), gains[0:1])])


def kv_norm_kernel(x_ref, gains, out_ref):
    (k_ref, v_ref), (k_out, v_out) = halves(x_ref), halves(out_ref)
    v_out[...] = v_ref[...]
    (k_out[...],) = head_norms([(k_ref[...].astype(jnp.float32), gains[1:2])])


def keys_and_values(refs):
    pairs = [halves(ref) for ref in refs]
    return [keys for keys, _ in pairs], [values for _, values in pairs]


def prep_own_kernel(
    index_ref,
    count_ref,
    x_ref,
    text_ref,
    gain_q_ref,
    gain_k_ref,
    gain_t_ref,
    _,
    kv_ref,
    q_ref,
    gains,
    euler_ref,
    __,
):
    tokens, width = q_ref.shape
    k_ref, v_ref = halves(kv_ref)
    for at, ref in enumerate((gain_q_ref, gain_k_ref, gain_t_ref)):
        gains[at : at + 1] = ref[...]
    now = jnp.full(euler_ref.shape, index_ref[0], jnp.int32)
    then = now + jnp.full(euler_ref.shape, count_ref[0], jnp.int32)
    euler_ref[...] = noise_level(then) - noise_level(now)
    text = text_ref[...].astype(jnp.float32).transpose(1, 0, 2)
    v_ref[tokens:] = text[1].astype(jnp.bfloat16)
    q, k, v = x_ref[...].transpose(1, 0, 2)
    v_ref[:tokens] = v
    k_ref[:tokens], k_ref[tokens:], q_ref[...] = head_norms(
        [
            (k.astype(jnp.float32), gains[1:2]),
            (text[0], gains[2:3]),
            (q.astype(jnp.float32), gains[0:1]),
        ]
    )


def attend(q, keys_refs, values_refs, attended_ref):
    tokens, width = q.shape
    first = lax.broadcasted_iota(jnp.int32, (tokens, LANES), 1) < HEAD
    scale = math.log2(math.e) / math.sqrt(HEAD)
    zero = jnp.zeros((tokens, LANES), jnp.bfloat16)
    ones = jnp.ones((sum(ref.shape[0] for ref in keys_refs), LANES), jnp.bfloat16)

    def scores_of(at):
        lanes = slice(at, at + LANES)
        keys = jnp.concatenate([ref[:, lanes] for ref in keys_refs], axis=0)
        block = q[:, lanes]
        both = jnp.concatenate(
            [jnp.where(first, block, zero), jnp.where(first, zero, block)], axis=0
        )
        return lax.dot_general(
            both, keys, (((1,), (1,)), ((), ())), preferred_element_type=jnp.float32
        )

    def finish(at, scores):
        lanes = slice(at, at + LANES)
        values = jnp.concatenate([ref[:, lanes] for ref in values_refs], axis=0)
        weights = jnp.exp2(scores * scale).astype(jnp.bfloat16)
        out = jnp.dot(
            weights,
            jnp.concatenate([values, ones], axis=1),
            preferred_element_type=jnp.float32,
        )
        weighted = jnp.where(first, out[:tokens, :LANES], out[tokens:, :LANES])
        total = jnp.where(first, out[:tokens, LANES:], out[tokens:, LANES:])
        attended_ref[:, lanes] = (weighted / total).astype(jnp.bfloat16)

    ahead = scores_of(0)
    for at in range(0, width, LANES):
        scores = ahead
        if at + LANES < width:
            ahead = scores_of(at + LANES)
        finish(at, scores)


def project(attended, halves_refs, start, upto, store):
    half = halves_refs[0].shape[0]
    for at in range(start, upto, STEP):
        to = min(at + STEP, upto)
        parts = []
        for place, ref in enumerate(halves_refs):
            low, high = max(at, place * half), min(to, place * half + half)
            if low < high:
                product = lax.dot_general(
                    attended,
                    ref[low - place * half : high - place * half],
                    (((1,), (1,)), ((), ())),
                    preferred_element_type=jnp.float32,
                )
                parts.append(product.astype(jnp.bfloat16))
        store(at, to, parts[0] if len(parts) == 1 else jnp.concatenate(parts, axis=1))


def attend_kernel(*refs):
    q_ref, weight_refs, (out_ref, attended) = refs[0], refs[5:7], refs[7:]
    attend(q_ref[...], *keys_and_values(refs[1:5]), attended)

    def keep(at, to, product):
        out_ref[:, at:to] = product

    project(attended[...], weight_refs, 0, out_ref.shape[1], keep)


def in_order(x, is_first):
    half = x.shape[1] // 2
    return jnp.where(is_first, x, jnp.concatenate([x[:, half:], x[:, :half]], axis=1))


def own_kernel(*refs):
    q_ref, weight_refs = refs[0], refs[5:7]
    hidden_ref, mod_ref, got_ref, mine_ref, theirs_ref = refs[7:12]
    out_ref, mod_out, finals_ref, attended = refs[12:]
    attend(q_ref[...], *keys_and_values(refs[1:5]), attended)
    is_first = lax.axis_index("row") == 0
    tile_rows, tile_cols, features = hidden_ref.shape
    mod_out[...] = in_order(mod_ref[...], is_first)
    out_ref[...] = in_order(
        jnp.concatenate([hidden_ref[row].astype(jnp.float32) for row in range(tile_rows)], axis=0),
        is_first,
    )

    def keep(at, to, product):
        out_ref[:, at:to] += mod_out[2:3, at:to] * product.astype(jnp.float32)

    project(attended[...], weight_refs, 0, features, keep)
    upto = got_ref.shape[0]
    out_ref[:upto] += mod_out[2:3] * got_ref[...].astype(jnp.float32)
    finals_ref[...] = jnp.concatenate(
        [mine_ref[...].astype(jnp.float32), theirs_ref[...].astype(jnp.float32)], axis=1
    ).astype(jnp.bfloat16)


def one_hot(dims, condition):
    row = lax.broadcasted_iota(jnp.int32, dims, 0)
    col = lax.broadcasted_iota(jnp.int32, dims, 1)
    return jnp.where(condition(row, col), 1.0, 0.0).astype(jnp.bfloat16)


def to_pixels(velocity, tile_cols):
    tokens, values = velocity.shape
    side = values // PATCH
    out_rows, out_lanes = tokens // tile_cols * PATCH, tile_cols * side
    terms, rest = [], velocity
    for _ in range(3):
        term = rest.astype(jnp.bfloat16)
        rest = rest - term.astype(jnp.float32)
        terms.append(term)
    terms = jnp.concatenate(terms, axis=0)
    row = lax.broadcasted_iota(jnp.int32, (3 * tokens, out_lanes), 0)
    col = lax.broadcasted_iota(jnp.int32, (3 * tokens, out_lanes), 1)
    here = col // side == row % tile_cols
    total = jnp.zeros((out_rows, out_lanes), jnp.float32)
    for at in range(PATCH):
        spread = one_hot((values, out_lanes), lambda r, c: r == c % side + at * side)
        wide = jnp.dot(terms, spread, preferred_element_type=jnp.float32)
        wide = jnp.where(here, wide, 0.0).astype(jnp.bfloat16)
        pick = one_hot(
            (out_rows, 3 * tokens), lambda r, c: r == c % tokens // tile_cols * PATCH + at
        )
        total += jnp.dot(pick, wide, preferred_element_type=jnp.float32)
    return total


def final_kernel(start, upto, euler_ref, mixed_ref, mod_ref, final_ref, latent_ref, *refs):
    velocity_ref, next_ref = refs[-2:]
    got_ref = refs[0] if len(refs) > 2 else None
    tokens = upto - start
    step = 48
    parts = []
    for at in range(0, tokens, step):
        rows = slice(start + at, start + at + step)
        mixed = mixed_ref[rows]
        if got_ref is not None:
            mixed += mod_ref[2:3] * got_ref[at : at + step].astype(jnp.float32)
        mean = jnp.mean(mixed, axis=-1, keepdims=True)
        centered = mixed - mean
        var = jnp.mean(centered * centered, axis=-1, keepdims=True)
        normed = (
            centered * lax.rsqrt(var + EPS) * (1.0 + mod_ref[1:2]) + mod_ref[0:1]
        ).astype(jnp.bfloat16)
        parts.append(
            lax.dot_general(
                normed,
                final_ref[...],
                (((1,), (1,)), ((), ())),
                preferred_element_type=jnp.float32,
            )
        )
    tile_cols = latent_ref.shape[1] // (final_ref.shape[0] // PATCH)
    velocity = to_pixels(jnp.concatenate(parts, axis=0), tile_cols)
    first = start // tile_cols * PATCH
    pixels = slice(first, first + velocity.shape[0])
    if got_ref is not None:
        for before_ref, after_ref in zip(refs[1:3], refs[3:]):
            after_ref[:first] = before_ref[:first]
    velocity_ref[pixels] = velocity
    next_ref[pixels] = latent_ref[pixels] + euler_ref[...] * velocity


def params(limit=VMEM_LIMIT):
    return pltpu.CompilerParams(vmem_limit_bytes=limit)


def lasting(duration):
    return pl.CostEstimate(
        flops=int(duration * 1e9), bytes_accessed=int(duration * 3e6), transcendentals=0
    )


def shape(dims, dtype=jnp.bfloat16):
    return jax.ShapeDtypeStruct(dims, dtype)


VMEM = pl.BlockSpec(memory_space=pltpu.VMEM)
ANY = pl.BlockSpec(memory_space=pl.ANY)
HBM = pl.BlockSpec(memory_space=pltpu.HBM)
SMEM = pl.BlockSpec(memory_space=pltpu.SMEM)


def on_device(
    image_qkv,
    text_kv,
    gain_query,
    gain_key,
    gain_text,
    out_weight,
    final_weight,
    hidden,
    modulation,
    latent,
    step_index,
    step_count,
):
    tile_rows, tile_cols, _, all_width = image_qkv.shape
    tokens = tile_rows * tile_cols
    words = text_kv.shape[0]
    width = all_width // lax.axis_size("col")
    features = hidden.shape[2]
    gains = [gain.reshape(1, HEAD) for gain in (gain_query, gain_key, gain_text)]
    x = image_qkv.reshape(tokens, 3, all_width)
    weight_half = out_weight.T
    held = pltpu.VMEM((tokens, 3, width), jnp.bfloat16)
    block = shape((tokens, width))

    loads = pltpu.SemaphoreType.DMA((LOADS,))
    cut = tile_rows // 3 * tile_cols
    chunks = ((0, cut), (cut, tokens))
    *q_raw, kv_raw, own_raw = pl.pallas_call(
        split_kernel,
        out_shape=tuple(shape((upto - start, width)) for start, upto in chunks)
        + (
            shape((2 * tokens, width)),
            shape((tokens, 3, width)),
        ),
        in_specs=[HBM],
        out_specs=(VMEM,) * 4,
        scratch_shapes=[held, loads, loads],
        compiler_params=params(VMEM_MOST),
        name="split",
    )(x)

    weight_got = lax.ppermute(weight_half, "row", SWAP)
    final_got = lax.ppermute(final_weight, "row", SWAP)
    kv_own, q_own, gains_on, euler, weight_theirs = pl.pallas_call(
        prep_own_kernel,
        out_shape=(
            shape((2 * (tokens + words), width)),
            block,
            shape((len(gains), HEAD), jnp.float32),
            shape((1, latent.shape[1]), jnp.float32),
            shape(weight_got.shape),
        ),
        in_specs=[SMEM] * 2 + [VMEM] * 5 + [ANY],
        out_specs=(VMEM,) * 4 + (ANY,),
        input_output_aliases={7: 4},
        compiler_params=params(),
        name="prep_own",
    )(step_index, step_count, own_raw, text_kv, *gains, weight_got)
    weights = (weight_half, weight_theirs)

    def normed(kernel, got, duration):
        return pl.pallas_call(
            kernel,
            out_shape=shape(got.shape),
            in_specs=[VMEM, VMEM],
            out_specs=VMEM,
            compiler_params=params(),
            cost_estimate=lasting(duration),
            name=kernel.__name__,
        )(got, gains_on)

    kv_got = normed(kv_norm_kernel, lax.ppermute(kv_raw, "col", SWAP), 0)
    q_got = [
        normed(q_norm_kernel, lax.ppermute(raw, "col", SWAP), duration)
        for raw, duration in zip(q_raw, (4.2, 4))
    ]
    pairs = []
    for kv in (kv_own, kv_got):
        pairs += [kv, lax.ppermute(kv, "row", SWAP)]

    def group(q):
        rows = q.shape[0]
        return pl.pallas_call(
            attend_kernel,
            out_shape=shape((rows, features)),
            in_specs=[VMEM] * 7,
            out_specs=VMEM,
            scratch_shapes=[pltpu.VMEM((rows, width), jnp.bfloat16)],
            compiler_params=params(),
            name="group",
        )(q, *pairs, *weights)

    first_got, second_got = (lax.ppermute(group(q), "col", SWAP) for q in q_got)
    mixed, mods, finals = pl.pallas_call(
        own_kernel,
        out_shape=(
            shape((tokens, features), jnp.float32),
            shape(modulation.shape, jnp.float32),
            shape((final_weight.shape[0], features)),
        ),
        in_specs=[VMEM] * 12,
        out_specs=(VMEM,) * 3,
        scratch_shapes=[pltpu.VMEM((tokens, width), jnp.bfloat16)],
        compiler_params=params(),
        cost_estimate=lasting(60),
        name="own",
    )(
        q_own,
        *pairs,
        *weights,
        hidden,
        modulation,
        first_got,
        final_weight,
        final_got,
    )
    results = ()
    for (start, upto), got in zip(chunks, ((), (second_got,))):
        results = pl.pallas_call(
            functools.partial(final_kernel, start, upto),
            out_shape=(shape(latent.shape, jnp.float32),) * 2,
            in_specs=[VMEM] * (5 + len(got) + len(results)),
            out_specs=(VMEM, VMEM),
            compiler_params=params(),
            name="final",
        )(euler, mixed, mods, finals, latent, *got, *results)
    return results


def solution(mesh):
    placed = (
        P(("req", "row"), "col", None, None),
        P(("req", "row"), None, "col"),
        P(),
        P(),
        P(),
        P("col", "row"),
        P(None, "row"),
        P(("req", "row"), "col", None),
        P("req", None),
        P(("req", "row"), "col"),
        P("req"),
        P("req"),
    )
    return jax.shard_map(
        on_device,
        mesh=mesh,
        in_specs=placed,
        out_specs=(P(("req", "row"), "col"), P(("req", "row"), "col")),
        check_vma=False,
    )
```

```python
import functools
import math

import jax
import jax.numpy as jnp
from jax import lax
from jax.experimental import pallas as pl
from jax.experimental.pallas import tpu as pltpu
from jax.sharding import PartitionSpec as P

HEAD = 64
CH = 16
PATCH = 2
STEPS = 28
SHIFT_FACTOR = 3.0
LANES = 128
EPS = 1e-06
VMEM_LIMIT = 16 * 1024 * 1024
VMEM_MOST = 52 * 1024 * 1024
LOADS = 3
FIRST = 1280
STEP = 640
SWAP = [(0, 1), (1, 0)]


def noise_level(step_number):
    fraction = 1.0 - step_number.astype(jnp.float32) / STEPS
    return SHIFT_FACTOR * fraction / (1.0 + (SHIFT_FACTOR - 1.0) * fraction)


def same_head(width):
    row = lax.broadcasted_iota(jnp.int32, (width, width), 0) // HEAD
    col = lax.broadcasted_iota(jnp.int32, (width, width), 1) // HEAD
    return (row == col).astype(jnp.bfloat16)


def head_norms(pairs):
    ones = same_head(LANES)
    squares = []
    for x, _ in pairs:
        for at in range(0, x.shape[1], LANES):
            square = x[:, at : at + LANES] * x[:, at : at + LANES]
            high = square.astype(jnp.bfloat16)
            low = (square - high.astype(jnp.float32)).astype(jnp.bfloat16)
            squares.append(jnp.concatenate([high, low], axis=1))
    totals = jnp.dot(
        jnp.concatenate(squares, axis=0),
        jnp.concatenate([ones, ones], axis=0),
        preferred_element_type=jnp.float32,
    )
    inverse = lax.rsqrt(totals * (1.0 / HEAD) + EPS)
    results, start = [], 0
    for x, gain in pairs:
        gain = jnp.concatenate([gain, gain], axis=1)
        pieces = []
        for at in range(0, x.shape[1], LANES):
            factor = inverse[start : start + x.shape[0]]
            pieces.append((x[:, at : at + LANES] * factor * gain).astype(jnp.bfloat16))
            start += x.shape[0]
        results.append(jnp.concatenate(pieces, axis=1))
    return results


def load_half(x_ref, held, sems, column):
    tokens, _, width = held.shape
    at = pl.multiple_of(column * width, LANES)
    step = tokens // sems.shape[0]
    copies = [
        pltpu.make_async_copy(
            x_ref.at[start : start + step, :, pl.ds(at, width)],
            held.at[start : start + step],
            sems.at[start // step],
        )
        for start in range(0, tokens, step)
    ]
    for copy in copies:
        copy.start()
    return [(slice(at * step, at * step + step), copy) for at, copy in enumerate(copies)]


def halves(ref):
    rows = ref.shape[0] // 2
    return ref.at[:rows], ref.at[rows:]


def split_kernel(
    x_ref,
    q_first_ref,
    q_second_ref,
    kv_ref,
    own_ref,
    held,
    sems,
    own_sems,
):
    column = lax.axis_index("col")
    blocks = load_half(x_ref, held, sems, 1 - column)
    own_blocks = load_half(x_ref, own_ref, own_sems, column)
    cut = q_first_ref.shape[0]
    k_ref, v_ref = halves(kv_ref)
    for rows, copy in blocks:
        copy.wait()
        q, k, v = held[rows].transpose(1, 0, 2)
        k_ref[rows] = k
        v_ref[rows] = v
        if rows.stop <= cut:
            q_first_ref[rows] = q
        else:
            q_second_ref[rows.start - cut : rows.stop - cut] = q
    for _, copy in own_blocks:
        copy.wait()


def q_norm_kernel(x_ref, gains, out_ref):
    (out_ref[...],) = head_norms([(x_ref[...].astype(jnp.float32), gains[0:1])])


def kv_norm_kernel(x_ref, gains, out_ref):
    (k_ref, v_ref), (k_out, v_out) = halves(x_ref), halves(out_ref)
    v_out[...] = v_ref[...]
    (k_out[...],) = head_norms([(k_ref[...].astype(jnp.float32), gains[1:2])])


def keys_and_values(refs):
    pairs = [halves(ref) for ref in refs]
    return [keys for keys, _ in pairs], [values for _, values in pairs]


def prep_own_kernel(
    index_ref,
    count_ref,
    x_ref,
    text_ref,
    gain_q_ref,
    gain_k_ref,
    gain_t_ref,
    _,
    kv_ref,
    q_ref,
    gains,
    euler_ref,
    __,
):
    tokens, width = q_ref.shape
    k_ref, v_ref = halves(kv_ref)
    for at, ref in enumerate((gain_q_ref, gain_k_ref, gain_t_ref)):
        gains[at : at + 1] = ref[...]
    now = jnp.full(euler_ref.shape, index_ref[0], jnp.int32)
    then = now + jnp.full(euler_ref.shape, count_ref[0], jnp.int32)
    euler_ref[...] = noise_level(then) - noise_level(now)
    text = text_ref[...].astype(jnp.float32).transpose(1, 0, 2)
    v_ref[tokens:] = text[1].astype(jnp.bfloat16)
    q, k, v = x_ref[...].transpose(1, 0, 2)
    v_ref[:tokens] = v
    k_ref[:tokens], k_ref[tokens:], q_ref[...] = head_norms(
        [
            (k.astype(jnp.float32), gains[1:2]),
            (text[0], gains[2:3]),
            (q.astype(jnp.float32), gains[0:1]),
        ]
    )


def attend(q, keys_refs, values_refs, attended_ref):
    tokens, width = q.shape
    first = lax.broadcasted_iota(jnp.int32, (tokens, LANES), 1) < HEAD
    scale = math.log2(math.e) / math.sqrt(HEAD)
    zero = jnp.zeros((tokens, LANES), jnp.bfloat16)
    ones = jnp.ones((sum(ref.shape[0] for ref in keys_refs), LANES), jnp.bfloat16)

    def scores_of(at):
        lanes = slice(at, at + LANES)
        keys = jnp.concatenate([ref[:, lanes] for ref in keys_refs], axis=0)
        block = q[:, lanes]
        both = jnp.concatenate(
            [jnp.where(first, block, zero), jnp.where(first, zero, block)], axis=0
        )
        return lax.dot_general(
            both, keys, (((1,), (1,)), ((), ())), preferred_element_type=jnp.float32
        )

    def finish(at, scores):
        lanes = slice(at, at + LANES)
        values = jnp.concatenate([ref[:, lanes] for ref in values_refs], axis=0)
        weights = jnp.exp2(scores * scale).astype(jnp.bfloat16)
        out = jnp.dot(
            weights,
            jnp.concatenate([values, ones], axis=1),
            preferred_element_type=jnp.float32,
        )
        weighted = jnp.where(first, out[:tokens, :LANES], out[tokens:, :LANES])
        total = jnp.where(first, out[:tokens, LANES:], out[tokens:, LANES:])
        attended_ref[:, lanes] = (weighted / total).astype(jnp.bfloat16)

    ahead = scores_of(0)
    for at in range(0, width, LANES):
        scores = ahead
        if at + LANES < width:
            ahead = scores_of(at + LANES)
        finish(at, scores)


def project(attended, halves_refs, start, upto, store):
    half = halves_refs[0].shape[0]
    for at in range(start, upto, STEP):
        to = min(at + STEP, upto)
        parts = []
        for place, ref in enumerate(halves_refs):
            low, high = max(at, place * half), min(to, place * half + half)
            if low < high:
                product = lax.dot_general(
                    attended,
                    ref[low - place * half : high - place * half],
                    (((1,), (1,)), ((), ())),
                    preferred_element_type=jnp.float32,
                )
                parts.append(product.astype(jnp.bfloat16))
        store(at, to, parts[0] if len(parts) == 1 else jnp.concatenate(parts, axis=1))


def attend_kernel(*refs):
    q_ref, weight_refs, (out_ref, attended) = refs[0], refs[5:7], refs[7:]
    attend(q_ref[...], *keys_and_values(refs[1:5]), attended)

    def keep(at, to, product):
        out_ref[:, at:to] = product

    project(attended[...], weight_refs, 0, out_ref.shape[1], keep)


def rest_kernel(attended_ref, mine_ref, theirs_ref, out_ref):
    features = 2 * mine_ref.shape[0]
    start = features - out_ref.shape[1]

    def keep(at, to, product):
        out_ref[:, at - start : to - start] = product

    project(attended_ref[...], (mine_ref, theirs_ref), start, features, keep)


def in_order(x, is_first):
    half = x.shape[1] // 2
    return jnp.where(is_first, x, jnp.concatenate([x[:, half:], x[:, :half]], axis=1))


def own_kernel(*refs):
    q_ref, weight_refs = refs[0], refs[5:7]
    hidden_ref, mod_ref, got_ref, mine_ref, theirs_ref = refs[7:12]
    out_ref, mod_out, finals_ref, attended = refs[12:]
    attend(q_ref[...], *keys_and_values(refs[1:5]), attended)
    is_first = lax.axis_index("row") == 0
    tile_rows, tile_cols, features = hidden_ref.shape
    mod_out[...] = in_order(mod_ref[...], is_first)
    out_ref[...] = in_order(
        jnp.concatenate([hidden_ref[row].astype(jnp.float32) for row in range(tile_rows)], axis=0),
        is_first,
    )

    def keep(at, to, product):
        out_ref[:, at:to] += mod_out[2:3, at:to] * product.astype(jnp.float32)

    project(attended[...], weight_refs, 0, features, keep)
    upto, to = got_ref.shape
    out_ref[:upto, :to] += mod_out[2:3, :to] * got_ref[...].astype(jnp.float32)
    finals_ref[...] = jnp.concatenate(
        [mine_ref[...].astype(jnp.float32), theirs_ref[...].astype(jnp.float32)], axis=1
    ).astype(jnp.bfloat16)


def one_hot(dims, condition):
    row = lax.broadcasted_iota(jnp.int32, dims, 0)
    col = lax.broadcasted_iota(jnp.int32, dims, 1)
    return jnp.where(condition(row, col), 1.0, 0.0).astype(jnp.bfloat16)


def to_pixels(velocity, tile_cols):
    tokens, values = velocity.shape
    side = values // PATCH
    out_rows, out_lanes = tokens // tile_cols * PATCH, tile_cols * side
    terms, rest = [], velocity
    for _ in range(3):
        term = rest.astype(jnp.bfloat16)
        rest = rest - term.astype(jnp.float32)
        terms.append(term)
    terms = jnp.concatenate(terms, axis=0)
    row = lax.broadcasted_iota(jnp.int32, (3 * tokens, out_lanes), 0)
    col = lax.broadcasted_iota(jnp.int32, (3 * tokens, out_lanes), 1)
    here = col // side == row % tile_cols
    total = jnp.zeros((out_rows, out_lanes), jnp.float32)
    for at in range(PATCH):
        spread = one_hot((values, out_lanes), lambda r, c: r == c % side + at * side)
        wide = jnp.dot(terms, spread, preferred_element_type=jnp.float32)
        wide = jnp.where(here, wide, 0.0).astype(jnp.bfloat16)
        pick = one_hot(
            (out_rows, 3 * tokens), lambda r, c: r == c % tokens // tile_cols * PATCH + at
        )
        total += jnp.dot(pick, wide, preferred_element_type=jnp.float32)
    return total


def final_kernel(start, euler_ref, mixed_ref, got_ref, mod_ref, final_ref, latent_ref, *refs):
    velocity_ref, next_ref = refs[-2:]
    tokens = got_ref.shape[0]
    step = 48
    had = mixed_ref.shape[1] - got_ref.shape[1]
    parts = []
    for at in range(0, tokens, step):
        rows = slice(start + at, start + at + step)
        got = got_ref[at : at + step].astype(jnp.float32)
        mixed = mixed_ref[rows, had:] + mod_ref[2:3, had:] * got
        if had:
            mixed = jnp.concatenate([mixed_ref[rows, :had], mixed], axis=1)
        mean = jnp.mean(mixed, axis=-1, keepdims=True)
        centered = mixed - mean
        var = jnp.mean(centered * centered, axis=-1, keepdims=True)
        normed = (
            centered * lax.rsqrt(var + EPS) * (1.0 + mod_ref[1:2]) + mod_ref[0:1]
        ).astype(jnp.bfloat16)
        parts.append(
            lax.dot_general(
                normed,
                final_ref[...],
                (((1,), (1,)), ((), ())),
                preferred_element_type=jnp.float32,
            )
        )
    tile_cols = latent_ref.shape[1] // (final_ref.shape[0] // PATCH)
    velocity = to_pixels(jnp.concatenate(parts, axis=0), tile_cols)
    first = start // tile_cols * PATCH
    pixels = slice(first, first + velocity.shape[0])
    for before_ref, after_ref in zip(refs[:-2], refs[-2:]):
        after_ref[:first] = before_ref[:first]
    velocity_ref[pixels] = velocity
    next_ref[pixels] = latent_ref[pixels] + euler_ref[...] * velocity


def params(limit=VMEM_LIMIT):
    return pltpu.CompilerParams(vmem_limit_bytes=limit)


def lasting(duration):
    return pl.CostEstimate(
        flops=int(duration * 1e9), bytes_accessed=int(duration * 3e6), transcendentals=0
    )


def shape(dims, dtype=jnp.bfloat16):
    return jax.ShapeDtypeStruct(dims, dtype)


VMEM = pl.BlockSpec(memory_space=pltpu.VMEM)
ANY = pl.BlockSpec(memory_space=pl.ANY)
HBM = pl.BlockSpec(memory_space=pltpu.HBM)
SMEM = pl.BlockSpec(memory_space=pltpu.SMEM)


def on_device(
    image_qkv,
    text_kv,
    gain_query,
    gain_key,
    gain_text,
    out_weight,
    final_weight,
    hidden,
    modulation,
    latent,
    step_index,
    step_count,
):
    tile_rows, tile_cols, _, all_width = image_qkv.shape
    tokens = tile_rows * tile_cols
    words = text_kv.shape[0]
    width = all_width // lax.axis_size("col")
    features = hidden.shape[2]
    gains = [gain.reshape(1, HEAD) for gain in (gain_query, gain_key, gain_text)]
    x = image_qkv.reshape(tokens, 3, all_width)
    weight_half = out_weight.T
    held = pltpu.VMEM((tokens, 3, width), jnp.bfloat16)
    block = shape((tokens, width))

    loads = pltpu.SemaphoreType.DMA((LOADS,))
    cut = tile_rows // 3 * tile_cols
    chunks = ((0, cut), (cut, tokens))
    *q_raw, kv_raw, own_raw = pl.pallas_call(
        split_kernel,
        out_shape=tuple(shape((upto - start, width)) for start, upto in chunks)
        + (
            shape((2 * tokens, width)),
            shape((tokens, 3, width)),
        ),
        in_specs=[HBM],
        out_specs=(VMEM,) * 4,
        scratch_shapes=[held, loads, loads],
        compiler_params=params(VMEM_MOST),
        name="split",
    )(x)

    weight_got = lax.ppermute(weight_half, "row", SWAP)
    final_got = lax.ppermute(final_weight, "row", SWAP)
    kv_own, q_own, gains_on, euler, weight_theirs = pl.pallas_call(
        prep_own_kernel,
        out_shape=(
            shape((2 * (tokens + words), width)),
            block,
            shape((len(gains), HEAD), jnp.float32),
            shape((1, latent.shape[1]), jnp.float32),
            shape(weight_got.shape),
        ),
        in_specs=[SMEM] * 2 + [VMEM] * 5 + [ANY],
        out_specs=(VMEM,) * 4 + (ANY,),
        input_output_aliases={7: 4},
        compiler_params=params(),
        name="prep_own",
    )(step_index, step_count, own_raw, text_kv, *gains, weight_got)
    weights = (weight_half, weight_theirs)

    def normed(kernel, got, duration):
        return pl.pallas_call(
            kernel,
            out_shape=shape(got.shape),
            in_specs=[VMEM, VMEM],
            out_specs=VMEM,
            compiler_params=params(),
            cost_estimate=lasting(duration),
            name=kernel.__name__,
        )(got, gains_on)

    kv_got = normed(kv_norm_kernel, lax.ppermute(kv_raw, "col", SWAP), 0)
    q_got = [
        normed(q_norm_kernel, lax.ppermute(raw, "col", SWAP), duration)
        for raw, duration in zip(q_raw, (4.2, 4))
    ]
    pairs = []
    for kv in (kv_own, kv_got):
        pairs += [kv, lax.ppermute(kv, "row", SWAP)]

    def group(q, sent):
        rows = q.shape[0]
        return pl.pallas_call(
            attend_kernel,
            out_shape=(shape((rows, sent)), shape((rows, width))),
            in_specs=[VMEM] * 7,
            out_specs=(VMEM, VMEM),
            compiler_params=params(),
            name="group",
        )(q, *pairs, *weights)

    first, heads = group(q_got[0], FIRST)
    first_got = lax.ppermute(first, "col", SWAP)
    rest = pl.pallas_call(
        rest_kernel,
        out_shape=shape((cut, features - FIRST)),
        in_specs=[VMEM] * 3,
        out_specs=VMEM,
        compiler_params=params(),
        name="rest",
    )(heads, *weights)
    rest_got = lax.ppermute(rest, "col", SWAP)
    second_q, rest = lax.optimization_barrier((q_got[1], rest))
    second, _ = group(second_q, features)
    second_got = lax.ppermute(second, "col", SWAP)
    mixed, mods, finals = pl.pallas_call(
        own_kernel,
        out_shape=(
            shape((tokens, features), jnp.float32),
            shape(modulation.shape, jnp.float32),
            shape((final_weight.shape[0], features)),
        ),
        in_specs=[VMEM] * 12,
        out_specs=(VMEM,) * 3,
        scratch_shapes=[pltpu.VMEM((tokens, width), jnp.bfloat16)],
        compiler_params=params(),
        cost_estimate=lasting(60),
        name="own",
    )(
        q_own,
        *pairs,
        *weights,
        hidden,
        modulation,
        first_got,
        final_weight,
        final_got,
    )
    results = ()
    for (start, _), got in zip(chunks, (rest_got, second_got)):
        results = pl.pallas_call(
            functools.partial(final_kernel, start),
            out_shape=(shape(latent.shape, jnp.float32),) * 2,
            in_specs=[VMEM] * (6 + len(results)),
            out_specs=(VMEM, VMEM),
            compiler_params=params(),
            name="final",
        )(euler, mixed, got, mods, finals, latent, *results)
    return results


def solution(mesh):
    placed = (
        P(("req", "row"), "col", None, None),
        P(("req", "row"), None, "col"),
        P(),
        P(),
        P(),
        P("col", "row"),
        P(None, "row"),
        P(("req", "row"), "col", None),
        P("req", None),
        P(("req", "row"), "col"),
        P("req"),
        P("req"),
    )
    return jax.shard_map(
        on_device,
        mesh=mesh,
        in_specs=placed,
        out_specs=(P(("req", "row"), "col"), P(("req", "row"), "col")),
        check_vma=False,
    )
```

```python
import functools
import math

import jax
import jax.numpy as jnp
from jax import lax
from jax.experimental import pallas as pl
from jax.experimental.pallas import tpu as pltpu
from jax.sharding import PartitionSpec as P

HEAD = 64
CH = 16
PATCH = 2
STEPS = 28
SHIFT_FACTOR = 3.0
LANES = 128
EPS = 1e-06
VMEM_LIMIT = 16 * 1024 * 1024
VMEM_MOST = 52 * 1024 * 1024
LOADS = 3
FIRST = 1280
STEP = 640
SWAP = [(0, 1), (1, 0)]


def noise_level(step_number):
    fraction = 1.0 - step_number.astype(jnp.float32) / STEPS
    return SHIFT_FACTOR * fraction / (1.0 + (SHIFT_FACTOR - 1.0) * fraction)


def same_head(width):
    row = lax.broadcasted_iota(jnp.int32, (width, width), 0) // HEAD
    col = lax.broadcasted_iota(jnp.int32, (width, width), 1) // HEAD
    return (row == col).astype(jnp.bfloat16)


def head_norms(pairs):
    ones = same_head(LANES)
    squares = []
    for x, _ in pairs:
        for at in range(0, x.shape[1], LANES):
            square = x[:, at : at + LANES] * x[:, at : at + LANES]
            high = square.astype(jnp.bfloat16)
            low = (square - high.astype(jnp.float32)).astype(jnp.bfloat16)
            squares.append(jnp.concatenate([high, low], axis=1))
    totals = jnp.dot(
        jnp.concatenate(squares, axis=0),
        jnp.concatenate([ones, ones], axis=0),
        preferred_element_type=jnp.float32,
    )
    inverse = lax.rsqrt(totals * (1.0 / HEAD) + EPS)
    results, start = [], 0
    for x, gain in pairs:
        gain = jnp.concatenate([gain, gain], axis=1)
        pieces = []
        for at in range(0, x.shape[1], LANES):
            factor = inverse[start : start + x.shape[0]]
            pieces.append((x[:, at : at + LANES] * factor * gain).astype(jnp.bfloat16))
            start += x.shape[0]
        results.append(jnp.concatenate(pieces, axis=1))
    return results


def load_half(x_ref, held, sems, column):
    tokens, _, width = held.shape
    at = pl.multiple_of(column * width, LANES)
    step = tokens // sems.shape[0]
    copies = [
        pltpu.make_async_copy(
            x_ref.at[start : start + step, :, pl.ds(at, width)],
            held.at[start : start + step],
            sems.at[start // step],
        )
        for start in range(0, tokens, step)
    ]
    for copy in copies:
        copy.start()
    return [(slice(at * step, at * step + step), copy) for at, copy in enumerate(copies)]


def halves(ref):
    rows = ref.shape[0] // 2
    return ref.at[:rows], ref.at[rows:]


def three(ref, tokens):
    return ref.at[:tokens], ref.at[tokens : 2 * tokens], ref.at[2 * tokens :]


def split_kernel(
    x_ref,
    first_ref,
    q_second_ref,
    own_ref,
    held,
    sems,
    own_sems,
):
    column = lax.axis_index("col")
    blocks = load_half(x_ref, held, sems, 1 - column)
    own_blocks = load_half(x_ref, own_ref, own_sems, column)
    tokens = held.shape[0]
    k_ref, v_ref, q_first_ref = three(first_ref, tokens)
    cut = q_first_ref.shape[0]
    for rows, copy in blocks:
        copy.wait()
        q, k, v = held[rows].transpose(1, 0, 2)
        k_ref[rows] = k
        v_ref[rows] = v
        if rows.stop <= cut:
            q_first_ref[rows] = q
        else:
            q_second_ref[rows.start - cut : rows.stop - cut] = q
    for _, copy in own_blocks:
        copy.wait()


def q_norm(x_ref, gains):
    (q,) = head_norms([(x_ref[...].astype(jnp.float32), gains[0:1])])
    return q


def norm_kernel(x_ref, gains, kv_ref, q_ref):
    k, v, q = three(x_ref, kv_ref.shape[0] // 2)
    k_out, v_out = halves(kv_ref)
    v_out[...] = v[...]
    k_out[...], q_ref[...] = head_norms(
        [(k[...].astype(jnp.float32), gains[1:2]), (q[...].astype(jnp.float32), gains[0:1])]
    )


def keys_and_values(refs):
    k_own, v_own, k_row, v_row, *joined = refs
    pairs = [(k_own, v_own), (k_row, v_row)] + [halves(ref) for ref in joined]
    return [keys for keys, _ in pairs], [values for _, values in pairs]


def prep_own_kernel(
    index_ref,
    count_ref,
    x_ref,
    text_ref,
    gain_q_ref,
    gain_k_ref,
    gain_t_ref,
    _,
    k_ref,
    v_ref,
    q_ref,
    gains,
    euler_ref,
    __,
):
    tokens, width = q_ref.shape
    for at, ref in enumerate((gain_q_ref, gain_k_ref, gain_t_ref)):
        gains[at : at + 1] = ref[...]
    now = jnp.full(euler_ref.shape, index_ref[0], jnp.int32)
    then = now + jnp.full(euler_ref.shape, count_ref[0], jnp.int32)
    euler_ref[...] = noise_level(then) - noise_level(now)
    text = text_ref[...].astype(jnp.float32).transpose(1, 0, 2)
    v_ref[tokens:] = text[1].astype(jnp.bfloat16)
    q, k, v = x_ref[...].transpose(1, 0, 2)
    v_ref[:tokens] = v
    k_ref[:tokens], k_ref[tokens:], q_ref[...] = head_norms(
        [
            (k.astype(jnp.float32), gains[1:2]),
            (text[0], gains[2:3]),
            (q.astype(jnp.float32), gains[0:1]),
        ]
    )


def attend(q, keys_refs, values_refs, store):
    tokens, width = q.shape
    first = lax.broadcasted_iota(jnp.int32, (tokens, LANES), 1) < HEAD
    scale = math.log2(math.e) / math.sqrt(HEAD)
    zero = jnp.zeros((tokens, LANES), jnp.bfloat16)
    ones = jnp.ones((sum(ref.shape[0] for ref in keys_refs), LANES), jnp.bfloat16)

    def scores_of(at):
        lanes = slice(at, at + LANES)
        keys = jnp.concatenate([ref[:, lanes] for ref in keys_refs], axis=0)
        block = q[:, lanes]
        both = jnp.concatenate(
            [jnp.where(first, block, zero), jnp.where(first, zero, block)], axis=0
        )
        return lax.dot_general(
            both, keys, (((1,), (1,)), ((), ())), preferred_element_type=jnp.float32
        )

    def finish(at, scores):
        lanes = slice(at, at + LANES)
        values = jnp.concatenate([ref[:, lanes] for ref in values_refs], axis=0)
        weights = jnp.exp2(scores * scale).astype(jnp.bfloat16)
        out = jnp.dot(
            weights,
            jnp.concatenate([values, ones], axis=1),
            preferred_element_type=jnp.float32,
        )
        weighted = jnp.where(first, out[:tokens, :LANES], out[tokens:, :LANES])
        total = jnp.where(first, out[:tokens, LANES:], out[tokens:, LANES:])
        store(lanes, weighted, total)

    ahead = scores_of(0)
    for at in range(0, width, LANES):
        scores = ahead
        if at + LANES < width:
            ahead = scores_of(at + LANES)
        finish(at, scores)


def project(attended, halves_refs, start, upto, store):
    half = halves_refs[0].shape[0]
    for at in range(start, upto, STEP):
        to = min(at + STEP, upto)
        parts = []
        for place, ref in enumerate(halves_refs):
            low, high = max(at, place * half), min(to, place * half + half)
            if low < high:
                product = lax.dot_general(
                    attended,
                    ref[low - place * half : high - place * half],
                    (((1,), (1,)), ((), ())),
                    preferred_element_type=jnp.float32,
                )
                parts.append(product.astype(jnp.bfloat16))
        store(at, to, parts[0] if len(parts) == 1 else jnp.concatenate(parts, axis=1))


def divide_into(ref):
    def store(lanes, weighted, total):
        ref[:, lanes] = (weighted / total).astype(jnp.bfloat16)

    return store


def keep_sums(sum_ref, total_ref):
    def store(lanes, weighted, total):
        sum_ref[:, lanes] = weighted
        total_ref[:, lanes] = total

    return store


def part_kernel(q_ref, *refs):
    attend(q_ref[...], *keys_and_values(refs[:5]), keep_sums(*refs[5:]))


def first_kernel(
    q_ref, last_ref, sum_ref, total_ref, mine_ref, theirs_ref, out_ref, attended
):
    finish = divide_into(attended)

    def store(lanes, weighted, total):
        finish(lanes, weighted + sum_ref[:, lanes], total + total_ref[:, lanes])

    keys, values = halves(last_ref)
    attend(q_ref[...], [keys], [values], store)

    def keep(at, to, product):
        out_ref[:, at:to] = product

    project(attended[...], (mine_ref, theirs_ref), 0, out_ref.shape[1], keep)


def second_kernel(*refs):
    x_ref, gains, weight_refs, (out_ref, attended) = refs[0], refs[1], refs[8:10], refs[10:]
    attend(q_norm(x_ref, gains), *keys_and_values(refs[2:8]), divide_into(attended))

    def keep(at, to, product):
        out_ref[:, at:to] = product

    project(attended[...], weight_refs, 0, out_ref.shape[1], keep)


def rest_kernel(attended_ref, mine_ref, theirs_ref, out_ref):
    features = 2 * mine_ref.shape[0]
    start = features - out_ref.shape[1]

    def keep(at, to, product):
        out_ref[:, at - start : to - start] = product

    project(attended_ref[...], (mine_ref, theirs_ref), start, features, keep)


def in_order(x, is_first):
    half = x.shape[1] // 2
    return jnp.where(is_first, x, jnp.concatenate([x[:, half:], x[:, :half]], axis=1))


def early_kernel(*refs):
    q_ref, gains, hidden_ref, mod_ref, mine_ref, theirs_ref = refs[0], *refs[5:10]
    sum_ref, total_ref, mixed_ref, gains_out, mod_out, finals_ref, _ = refs[11:]
    attend(q_ref[...], *keys_and_values(refs[1:5]), keep_sums(sum_ref, total_ref))
    gains_out[...] = gains[...]
    is_first = lax.axis_index("row") == 0
    mod_out[...] = in_order(mod_ref[...], is_first)
    mixed_ref[...] = in_order(
        jnp.concatenate(
            [hidden_ref[row].astype(jnp.float32) for row in range(hidden_ref.shape[0])], axis=0
        ),
        is_first,
    )
    finals_ref[...] = jnp.concatenate(
        [mine_ref[...].astype(jnp.float32), theirs_ref[...].astype(jnp.float32)], axis=1
    ).astype(jnp.bfloat16)


def own_kernel(
    q_ref,
    got_ref,
    last_ref,
    sum_ref,
    total_ref,
    mine_ref,
    theirs_ref,
    mixed_ref,
    mod_ref,
    first_ref,
    out_ref,
    attended,
):
    finish = divide_into(attended)

    def store(lanes, weighted, total):
        finish(lanes, weighted + sum_ref[:, lanes], total + total_ref[:, lanes])

    pairs = [halves(got_ref), halves(last_ref)]
    attend(q_ref[...], [keys for keys, _ in pairs], [values for _, values in pairs], store)

    def keep(at, to, product):
        out_ref[:, at:to] = mixed_ref[:, at:to] + mod_ref[2:3, at:to] * product.astype(jnp.float32)

    project(attended[...], (mine_ref, theirs_ref), 0, out_ref.shape[1], keep)
    upto, to = first_ref.shape
    out_ref[:upto, :to] += mod_ref[2:3, :to] * first_ref[...].astype(jnp.float32)


def one_hot(dims, condition):
    row = lax.broadcasted_iota(jnp.int32, dims, 0)
    col = lax.broadcasted_iota(jnp.int32, dims, 1)
    return jnp.where(condition(row, col), 1.0, 0.0).astype(jnp.bfloat16)


def to_pixels(velocity, tile_cols):
    tokens, values = velocity.shape
    side = values // PATCH
    out_rows, out_lanes = tokens // tile_cols * PATCH, tile_cols * side
    terms, rest = [], velocity
    for _ in range(3):
        term = rest.astype(jnp.bfloat16)
        rest = rest - term.astype(jnp.float32)
        terms.append(term)
    terms = jnp.concatenate(terms, axis=0)
    row = lax.broadcasted_iota(jnp.int32, (3 * tokens, out_lanes), 0)
    col = lax.broadcasted_iota(jnp.int32, (3 * tokens, out_lanes), 1)
    here = col // side == row % tile_cols
    total = jnp.zeros((out_rows, out_lanes), jnp.float32)
    for at in range(PATCH):
        spread = one_hot((values, out_lanes), lambda r, c: r == c % side + at * side)
        wide = jnp.dot(terms, spread, preferred_element_type=jnp.float32)
        wide = jnp.where(here, wide, 0.0).astype(jnp.bfloat16)
        pick = one_hot(
            (out_rows, 3 * tokens), lambda r, c: r == c % tokens // tile_cols * PATCH + at
        )
        total += jnp.dot(pick, wide, preferred_element_type=jnp.float32)
    return total


def final_kernel(
    start,
    euler_ref,
    mixed_ref,
    rest_ref,
    mod_ref,
    final_ref,
    latent_ref,
    *refs,
):
    velocity_ref, next_ref = refs[-2:]
    tokens = rest_ref.shape[0]
    step = 48
    parts = []
    for at in range(0, tokens, step):
        rows = slice(start + at, start + at + step)
        had = mixed_ref.shape[1] - rest_ref.shape[1]
        mixed = mixed_ref[rows]
        got = rest_ref[at : at + step].astype(jnp.float32)
        added = mixed[:, had:] + mod_ref[2:3, had:] * got
        mixed = jnp.concatenate([mixed[:, :had], added], axis=1) if had else added
        mean = jnp.mean(mixed, axis=-1, keepdims=True)
        centered = mixed - mean
        var = jnp.mean(centered * centered, axis=-1, keepdims=True)
        normed = (
            centered * lax.rsqrt(var + EPS) * (1.0 + mod_ref[1:2]) + mod_ref[0:1]
        ).astype(jnp.bfloat16)
        parts.append(
            lax.dot_general(
                normed,
                final_ref[...],
                (((1,), (1,)), ((), ())),
                preferred_element_type=jnp.float32,
            )
        )
    tile_cols = latent_ref.shape[1] // (final_ref.shape[0] // PATCH)
    velocity = to_pixels(jnp.concatenate(parts, axis=0), tile_cols)
    first = start // tile_cols * PATCH
    pixels = slice(first, first + velocity.shape[0])
    for before_ref, after_ref in zip(refs[:-2], refs[-2:]):
        after_ref[:first] = before_ref[:first]
    velocity_ref[pixels] = velocity
    next_ref[pixels] = latent_ref[pixels] + euler_ref[...] * velocity


def params(limit=VMEM_LIMIT):
    return pltpu.CompilerParams(vmem_limit_bytes=limit)


def lasting(duration):
    return pl.CostEstimate(
        flops=int(duration * 1e9), bytes_accessed=int(duration * 3e6), transcendentals=0
    )


def shape(dims, dtype=jnp.bfloat16):
    return jax.ShapeDtypeStruct(dims, dtype)


VMEM = pl.BlockSpec(memory_space=pltpu.VMEM)
ANY = pl.BlockSpec(memory_space=pl.ANY)
HBM = pl.BlockSpec(memory_space=pltpu.HBM)
SMEM = pl.BlockSpec(memory_space=pltpu.SMEM)


def on_device(
    image_qkv,
    text_kv,
    gain_query,
    gain_key,
    gain_text,
    out_weight,
    final_weight,
    hidden,
    modulation,
    latent,
    step_index,
    step_count,
):
    tile_rows, tile_cols, _, all_width = image_qkv.shape
    tokens = tile_rows * tile_cols
    words = text_kv.shape[0]
    width = all_width // lax.axis_size("col")
    features = hidden.shape[2]
    gains = [gain.reshape(1, HEAD) for gain in (gain_query, gain_key, gain_text)]
    x = image_qkv.reshape(tokens, 3, all_width)
    weight_half = out_weight.T
    held = pltpu.VMEM((tokens, 3, width), jnp.bfloat16)
    block = shape((tokens, width))

    loads = pltpu.SemaphoreType.DMA((LOADS,))
    cut = tile_rows // 3 * tile_cols
    chunks = ((0, cut), (cut, tokens))
    first_raw, second_raw, own_raw = pl.pallas_call(
        split_kernel,
        out_shape=(
            shape((2 * tokens + cut, width)),
            shape((tokens - cut, width)),
            shape((tokens, 3, width)),
        ),
        in_specs=[HBM],
        out_specs=(VMEM,) * 3,
        scratch_shapes=[held, loads, loads],
        compiler_params=params(VMEM_MOST),
        name="split",
    )(x)
    weight_got = lax.ppermute(weight_half, "row", SWAP)
    final_got = lax.ppermute(final_weight, "row", SWAP)
    k_own, v_own, q_own, gains, euler, weight_theirs = pl.pallas_call(
        prep_own_kernel,
        out_shape=(
            shape((tokens + words, width)),
            shape((tokens + words, width)),
            block,
            shape((len(gains), HEAD), jnp.float32),
            shape((1, latent.shape[1]), jnp.float32),
            shape(weight_got.shape),
        ),
        in_specs=[SMEM] * 2 + [VMEM] * 5 + [ANY],
        out_specs=(VMEM,) * 5 + (ANY,),
        input_output_aliases={7: 5},
        compiler_params=params(),
        name="prep_own",
    )(step_index, step_count, own_raw, text_kv, *gains, weight_got)
    weights = (weight_half, weight_theirs)
    k_row, v_row = (lax.ppermute(x, "row", SWAP) for x in (k_own, v_own))
    nearby = (k_own, v_own, k_row, v_row)
    own_sum, own_total, mixed, gains, mods, finals, second_raw = pl.pallas_call(
        early_kernel,
        out_shape=(
            shape((tokens, width), jnp.float32),
            shape((tokens, width), jnp.float32),
            shape((tokens, features), jnp.float32),
            shape(gains.shape, jnp.float32),
            shape(modulation.shape, jnp.float32),
            shape((final_weight.shape[0], features)),
            shape(second_raw.shape),
        ),
        in_specs=[VMEM] * 10 + [ANY],
        out_specs=(VMEM,) * 6 + (ANY,),
        input_output_aliases={10: 6},
        compiler_params=params(),
        name="early",
    )(q_own, *nearby, gains, hidden, modulation, final_weight, final_got, second_raw)
    q_second = lax.ppermute(second_raw, "col", SWAP)
    kv_got, q_first = pl.pallas_call(
        norm_kernel,
        out_shape=(shape((2 * tokens, width)), shape((cut, width))),
        in_specs=[VMEM] * 2,
        out_specs=(VMEM,) * 2,
        compiler_params=params(),
        name="norm",
    )(lax.ppermute(first_raw, "col", SWAP), gains)
    kv_last = lax.ppermute(kv_got, "row", SWAP)
    sums = pl.pallas_call(
        part_kernel,
        out_shape=(shape((cut, width), jnp.float32),) * 2,
        in_specs=[VMEM] * 6,
        out_specs=(VMEM,) * 2,
        compiler_params=params(),
        cost_estimate=lasting(4.5),
        name="part",
    )(q_first, *nearby, kv_got)
    first, heads = pl.pallas_call(
        first_kernel,
        out_shape=(shape((cut, FIRST)), shape((cut, width))),
        in_specs=[VMEM] * 6,
        out_specs=(VMEM,) * 2,
        compiler_params=params(),
        name="first",
    )(q_first, kv_last, *sums, *weights)
    first_got = lax.ppermute(first, "col", SWAP)
    rest = pl.pallas_call(
        rest_kernel,
        out_shape=shape((cut, features - FIRST)),
        in_specs=[VMEM] * 3,
        out_specs=VMEM,
        compiler_params=params(),
        name="rest",
    )(heads, *weights)
    rest_got = lax.ppermute(rest, "col", SWAP)
    q_second, rest = lax.optimization_barrier((q_second, rest))
    second = pl.pallas_call(
        second_kernel,
        out_shape=shape((tokens - cut, features)),
        in_specs=[VMEM] * 10,
        out_specs=VMEM,
        scratch_shapes=[pltpu.VMEM((tokens - cut, width), jnp.bfloat16)],
        compiler_params=params(),
        name="second",
    )(q_second, gains, *nearby, kv_got, kv_last, *weights)
    second_got = lax.ppermute(second, "col", SWAP)
    mixed = pl.pallas_call(
        own_kernel,
        out_shape=shape(mixed.shape, jnp.float32),
        in_specs=[VMEM] * 10,
        out_specs=VMEM,
        scratch_shapes=[pltpu.VMEM((tokens, width), jnp.bfloat16)],
        compiler_params=params(),
        cost_estimate=lasting(60),
        name="own",
    )(q_own, kv_got, kv_last, own_sum, own_total, *weights, mixed, mods, first_got)
    results = ()
    for (start, _), got in ((chunks[0], rest_got), (chunks[1], second_got)):
        results = pl.pallas_call(
            functools.partial(final_kernel, start),
            out_shape=(shape(latent.shape, jnp.float32),) * 2,
            in_specs=[VMEM] * (6 + len(results)),
            out_specs=(VMEM, VMEM),
            compiler_params=params(),
            name="final",
        )(euler, mixed, got, mods, finals, latent, *results)
    return results


def solution(mesh):
    placed = (
        P(("req", "row"), "col", None, None),
        P(("req", "row"), None, "col"),
        P(),
        P(),
        P(),
        P("col", "row"),
        P(None, "row"),
        P(("req", "row"), "col", None),
        P("req", None),
        P(("req", "row"), "col"),
        P("req"),
        P("req"),
    )
    return jax.shard_map(
        on_device,
        mesh=mesh,
        in_specs=placed,
        out_specs=(P(("req", "row"), "col"), P(("req", "row"), "col")),
        check_vma=False,
    )
```

```python
import functools
import math

import jax
import jax.numpy as jnp
from jax import lax
from jax.experimental import pallas as pl
from jax.experimental.pallas import tpu as pltpu
from jax.sharding import PartitionSpec as P

HEAD = 64
CH = 16
PATCH = 2
STEPS = 28
SHIFT_FACTOR = 3.0
LANES = 128
EPS = 1e-06
VMEM_LIMIT = 16 * 1024 * 1024
VMEM_MOST = 52 * 1024 * 1024
LOADS = 3
FIRST = 1280
STEP = 640
SWAP = [(0, 1), (1, 0)]


def noise_level(step_number):
    fraction = 1.0 - step_number.astype(jnp.float32) / STEPS
    return SHIFT_FACTOR * fraction / (1.0 + (SHIFT_FACTOR - 1.0) * fraction)


def same_head(width):
    row = lax.broadcasted_iota(jnp.int32, (width, width), 0) // HEAD
    col = lax.broadcasted_iota(jnp.int32, (width, width), 1) // HEAD
    return (row == col).astype(jnp.bfloat16)


def head_norms(pairs):
    ones = same_head(LANES)
    squares = []
    for x, _ in pairs:
        for at in range(0, x.shape[1], LANES):
            square = x[:, at : at + LANES] * x[:, at : at + LANES]
            high = square.astype(jnp.bfloat16)
            low = (square - high.astype(jnp.float32)).astype(jnp.bfloat16)
            squares.append(jnp.concatenate([high, low], axis=1))
    totals = jnp.dot(
        jnp.concatenate(squares, axis=0),
        jnp.concatenate([ones, ones], axis=0),
        preferred_element_type=jnp.float32,
    )
    inverse = lax.rsqrt(totals * (1.0 / HEAD) + EPS)
    results, start = [], 0
    for x, gain in pairs:
        gain = jnp.concatenate([gain, gain], axis=1)
        pieces = []
        for at in range(0, x.shape[1], LANES):
            factor = inverse[start : start + x.shape[0]]
            pieces.append((x[:, at : at + LANES] * factor * gain).astype(jnp.bfloat16))
            start += x.shape[0]
        results.append(jnp.concatenate(pieces, axis=1))
    return results


def load_half(x_ref, held, sems, column):
    tokens, _, width = held.shape
    at = pl.multiple_of(column * width, LANES)
    step = tokens // sems.shape[0]
    copies = [
        pltpu.make_async_copy(
            x_ref.at[start : start + step, :, pl.ds(at, width)],
            held.at[start : start + step],
            sems.at[start // step],
        )
        for start in range(0, tokens, step)
    ]
    for copy in copies:
        copy.start()
    return [(slice(at * step, at * step + step), copy) for at, copy in enumerate(copies)]


def halves(ref):
    rows = ref.shape[0] // 2
    return ref.at[:rows], ref.at[rows:]


def split_kernel(
    x_ref,
    kv_ref,
    q_first_ref,
    q_second_ref,
    own_ref,
    held,
    sems,
    own_sems,
):
    column = lax.axis_index("col")
    blocks = load_half(x_ref, held, sems, 1 - column)
    own_blocks = load_half(x_ref, own_ref, own_sems, column)
    k_ref, v_ref = halves(kv_ref)
    cut = q_first_ref.shape[0]
    for rows, copy in blocks:
        copy.wait()
        q, k, v = held[rows].transpose(1, 0, 2)
        k_ref[rows] = k
        v_ref[rows] = v
        if rows.stop <= cut:
            q_first_ref[rows] = q
        else:
            q_second_ref[rows.start - cut : rows.stop - cut] = q
    for _, copy in own_blocks:
        copy.wait()


def q_norm(x_ref, gains):
    (q,) = head_norms([(x_ref[...].astype(jnp.float32), gains[0:1])])
    return q


def norm_kernel(x_ref, gains, kv_ref):
    (k, v), (k_out, v_out) = halves(x_ref), halves(kv_ref)
    v_out[...] = v[...]
    (k_out[...],) = head_norms([(k[...].astype(jnp.float32), gains[1:2])])


def keys_and_values(refs):
    k_own, v_own, k_row, v_row, *joined = refs
    pairs = [(k_own, v_own), (k_row, v_row)] + [halves(ref) for ref in joined]
    return [keys for keys, _ in pairs], [values for _, values in pairs]


def prep_own_kernel(
    index_ref,
    count_ref,
    x_ref,
    text_ref,
    gain_q_ref,
    gain_k_ref,
    gain_t_ref,
    _,
    k_ref,
    v_ref,
    q_ref,
    gains,
    euler_ref,
    __,
):
    tokens, width = q_ref.shape
    for at, ref in enumerate((gain_q_ref, gain_k_ref, gain_t_ref)):
        gains[at : at + 1] = ref[...]
    now = jnp.full(euler_ref.shape, index_ref[0], jnp.int32)
    then = now + jnp.full(euler_ref.shape, count_ref[0], jnp.int32)
    euler_ref[...] = noise_level(then) - noise_level(now)
    text = text_ref[...].astype(jnp.float32).transpose(1, 0, 2)
    v_ref[tokens:] = text[1].astype(jnp.bfloat16)
    q, k, v = x_ref[...].transpose(1, 0, 2)
    v_ref[:tokens] = v
    k_ref[:tokens], k_ref[tokens:], q_ref[...] = head_norms(
        [
            (k.astype(jnp.float32), gains[1:2]),
            (text[0], gains[2:3]),
            (q.astype(jnp.float32), gains[0:1]),
        ]
    )


def attend(q, keys_refs, values_refs, store):
    tokens, width = q.shape
    first = lax.broadcasted_iota(jnp.int32, (tokens, LANES), 1) < HEAD
    scale = math.log2(math.e) / math.sqrt(HEAD)
    zero = jnp.zeros((tokens, LANES), jnp.bfloat16)
    ones = jnp.ones((sum(ref.shape[0] for ref in keys_refs), LANES), jnp.bfloat16)

    def scores_of(at):
        lanes = slice(at, at + LANES)
        keys = jnp.concatenate([ref[:, lanes] for ref in keys_refs], axis=0)
        block = q[:, lanes]
        both = jnp.concatenate(
            [jnp.where(first, block, zero), jnp.where(first, zero, block)], axis=0
        )
        return lax.dot_general(
            both, keys, (((1,), (1,)), ((), ())), preferred_element_type=jnp.float32
        )

    def finish(at, scores):
        lanes = slice(at, at + LANES)
        values = jnp.concatenate([ref[:, lanes] for ref in values_refs], axis=0)
        weights = jnp.exp2(scores * scale).astype(jnp.bfloat16)
        out = jnp.dot(
            weights,
            jnp.concatenate([values, ones], axis=1),
            preferred_element_type=jnp.float32,
        )
        weighted = jnp.where(first, out[:tokens, :LANES], out[tokens:, :LANES])
        total = jnp.where(first, out[:tokens, LANES:], out[tokens:, LANES:])
        store(lanes, weighted, total)

    ahead = scores_of(0)
    for at in range(0, width, LANES):
        scores = ahead
        if at + LANES < width:
            ahead = scores_of(at + LANES)
        finish(at, scores)


def project(attended, halves_refs, start, upto, store):
    half = halves_refs[0].shape[0]
    for at in range(start, upto, STEP):
        to = min(at + STEP, upto)
        parts = []
        for place, ref in enumerate(halves_refs):
            low, high = max(at, place * half), min(to, place * half + half)
            if low < high:
                product = lax.dot_general(
                    attended,
                    ref[low - place * half : high - place * half],
                    (((1,), (1,)), ((), ())),
                    preferred_element_type=jnp.float32,
                )
                parts.append(product.astype(jnp.bfloat16))
        store(at, to, parts[0] if len(parts) == 1 else jnp.concatenate(parts, axis=1))


def divide_into(ref):
    def store(lanes, weighted, total):
        ref[:, lanes] = (weighted / total).astype(jnp.bfloat16)

    return store


def keep_sums(sum_ref, total_ref):
    def store(lanes, weighted, total):
        sum_ref[:, lanes] = weighted
        total_ref[:, lanes] = total

    return store


def part_kernel(x_ref, gains, *refs):
    q_ref, sum_ref, total_ref = refs[5:]
    q_ref[...] = q_norm(x_ref, gains)
    attend(q_ref[...], *keys_and_values(refs[:5]), keep_sums(sum_ref, total_ref))


def first_kernel(
    q_ref, last_ref, sum_ref, total_ref, mine_ref, theirs_ref, out_ref, attended
):
    finish = divide_into(attended)

    def store(lanes, weighted, total):
        finish(lanes, weighted + sum_ref[:, lanes], total + total_ref[:, lanes])

    keys, values = halves(last_ref)
    attend(q_ref[...], [keys], [values], store)

    def keep(at, to, product):
        out_ref[:, at:to] = product

    project(attended[...], (mine_ref, theirs_ref), 0, out_ref.shape[1], keep)


def second_kernel(*refs):
    x_ref, gains, weight_refs, (out_ref, attended) = refs[0], refs[1], refs[8:10], refs[10:]
    attend(q_norm(x_ref, gains), *keys_and_values(refs[2:8]), divide_into(attended))

    def keep(at, to, product):
        out_ref[:, at:to] = product

    project(attended[...], weight_refs, 0, out_ref.shape[1], keep)


def rest_kernel(attended_ref, mine_ref, theirs_ref, out_ref):
    features = 2 * mine_ref.shape[0]
    start = features - out_ref.shape[1]

    def keep(at, to, product):
        out_ref[:, at - start : to - start] = product

    project(attended_ref[...], (mine_ref, theirs_ref), start, features, keep)


def in_order(x, is_first):
    half = x.shape[1] // 2
    return jnp.where(is_first, x, jnp.concatenate([x[:, half:], x[:, :half]], axis=1))


def early_kernel(*refs):
    q_ref, gains, hidden_ref, mod_ref, mine_ref, theirs_ref = refs[0], *refs[5:10]
    sum_ref, total_ref, mixed_ref, gains_out, mod_out, finals_ref = refs[12:18]
    attend(q_ref[...], *keys_and_values(refs[1:5]), keep_sums(sum_ref, total_ref))
    gains_out[...] = gains[...]
    is_first = lax.axis_index("row") == 0
    mod_out[...] = in_order(mod_ref[...], is_first)
    mixed_ref[...] = in_order(
        jnp.concatenate(
            [hidden_ref[row].astype(jnp.float32) for row in range(hidden_ref.shape[0])], axis=0
        ),
        is_first,
    )
    finals_ref[...] = jnp.concatenate(
        [mine_ref[...].astype(jnp.float32), theirs_ref[...].astype(jnp.float32)], axis=1
    ).astype(jnp.bfloat16)


def own_kernel(
    q_ref,
    got_ref,
    last_ref,
    sum_ref,
    total_ref,
    mine_ref,
    theirs_ref,
    mixed_ref,
    mod_ref,
    first_ref,
    out_ref,
    attended,
):
    finish = divide_into(attended)

    def store(lanes, weighted, total):
        finish(lanes, weighted + sum_ref[:, lanes], total + total_ref[:, lanes])

    pairs = [halves(got_ref), halves(last_ref)]
    attend(q_ref[...], [keys for keys, _ in pairs], [values for _, values in pairs], store)

    def keep(at, to, product):
        out_ref[:, at:to] = mixed_ref[:, at:to] + mod_ref[2:3, at:to] * product.astype(jnp.float32)

    project(attended[...], (mine_ref, theirs_ref), 0, out_ref.shape[1], keep)
    upto, to = first_ref.shape
    out_ref[:upto, :to] += mod_ref[2:3, :to] * first_ref[...].astype(jnp.float32)


def one_hot(dims, condition):
    row = lax.broadcasted_iota(jnp.int32, dims, 0)
    col = lax.broadcasted_iota(jnp.int32, dims, 1)
    return jnp.where(condition(row, col), 1.0, 0.0).astype(jnp.bfloat16)


def to_pixels(velocity, tile_cols):
    tokens, values = velocity.shape
    side = values // PATCH
    out_rows, out_lanes = tokens // tile_cols * PATCH, tile_cols * side
    terms, rest = [], velocity
    for _ in range(3):
        term = rest.astype(jnp.bfloat16)
        rest = rest - term.astype(jnp.float32)
        terms.append(term)
    terms = jnp.concatenate(terms, axis=0)
    row = lax.broadcasted_iota(jnp.int32, (3 * tokens, out_lanes), 0)
    col = lax.broadcasted_iota(jnp.int32, (3 * tokens, out_lanes), 1)
    here = col // side == row % tile_cols
    total = jnp.zeros((out_rows, out_lanes), jnp.float32)
    for at in range(PATCH):
        spread = one_hot((values, out_lanes), lambda r, c: r == c % side + at * side)
        wide = jnp.dot(terms, spread, preferred_element_type=jnp.float32)
        wide = jnp.where(here, wide, 0.0).astype(jnp.bfloat16)
        pick = one_hot(
            (out_rows, 3 * tokens), lambda r, c: r == c % tokens // tile_cols * PATCH + at
        )
        total += jnp.dot(pick, wide, preferred_element_type=jnp.float32)
    return total


def final_kernel(
    start,
    euler_ref,
    mixed_ref,
    rest_ref,
    mod_ref,
    final_ref,
    latent_ref,
    *refs,
):
    velocity_ref, next_ref = refs[-2:]
    tokens = rest_ref.shape[0]
    step = 48
    parts = []
    for at in range(0, tokens, step):
        rows = slice(start + at, start + at + step)
        had = mixed_ref.shape[1] - rest_ref.shape[1]
        mixed = mixed_ref[rows]
        got = rest_ref[at : at + step].astype(jnp.float32)
        added = mixed[:, had:] + mod_ref[2:3, had:] * got
        mixed = jnp.concatenate([mixed[:, :had], added], axis=1) if had else added
        mean = jnp.mean(mixed, axis=-1, keepdims=True)
        centered = mixed - mean
        var = jnp.mean(centered * centered, axis=-1, keepdims=True)
        normed = (
            centered * lax.rsqrt(var + EPS) * (1.0 + mod_ref[1:2]) + mod_ref[0:1]
        ).astype(jnp.bfloat16)
        parts.append(
            lax.dot_general(
                normed,
                final_ref[...],
                (((1,), (1,)), ((), ())),
                preferred_element_type=jnp.float32,
            )
        )
    tile_cols = latent_ref.shape[1] // (final_ref.shape[0] // PATCH)
    velocity = to_pixels(jnp.concatenate(parts, axis=0), tile_cols)
    first = start // tile_cols * PATCH
    pixels = slice(first, first + velocity.shape[0])
    for before_ref, after_ref in zip(refs[:-2], refs[-2:]):
        after_ref[:first] = before_ref[:first]
    velocity_ref[pixels] = velocity
    next_ref[pixels] = latent_ref[pixels] + euler_ref[...] * velocity


def params(limit=VMEM_LIMIT):
    return pltpu.CompilerParams(vmem_limit_bytes=limit)


def lasting(duration):
    return pl.CostEstimate(
        flops=int(duration * 1e9), bytes_accessed=int(duration * 3e6), transcendentals=0
    )


def shape(dims, dtype=jnp.bfloat16):
    return jax.ShapeDtypeStruct(dims, dtype)


VMEM = pl.BlockSpec(memory_space=pltpu.VMEM)
ANY = pl.BlockSpec(memory_space=pl.ANY)
HBM = pl.BlockSpec(memory_space=pltpu.HBM)
SMEM = pl.BlockSpec(memory_space=pltpu.SMEM)


def on_device(
    image_qkv,
    text_kv,
    gain_query,
    gain_key,
    gain_text,
    out_weight,
    final_weight,
    hidden,
    modulation,
    latent,
    step_index,
    step_count,
):
    tile_rows, tile_cols, _, all_width = image_qkv.shape
    tokens = tile_rows * tile_cols
    words = text_kv.shape[0]
    width = all_width // lax.axis_size("col")
    features = hidden.shape[2]
    gains = [gain.reshape(1, HEAD) for gain in (gain_query, gain_key, gain_text)]
    x = image_qkv.reshape(tokens, 3, all_width)
    weight_half = out_weight.T
    held = pltpu.VMEM((tokens, 3, width), jnp.bfloat16)
    block = shape((tokens, width))

    loads = pltpu.SemaphoreType.DMA((LOADS,))
    cut = tile_rows // 3 * tile_cols
    chunks = ((0, cut), (cut, tokens))
    kv_raw, first_raw, second_raw, own_raw = pl.pallas_call(
        split_kernel,
        out_shape=(
            shape((2 * tokens, width)),
            shape((cut, width)),
            shape((tokens - cut, width)),
            shape((tokens, 3, width)),
        ),
        in_specs=[HBM],
        out_specs=(VMEM,) * 4,
        scratch_shapes=[held, loads, loads],
        compiler_params=params(VMEM_MOST),
        name="split",
    )(x)
    weight_got = lax.ppermute(weight_half, "row", SWAP)
    final_got = lax.ppermute(final_weight, "row", SWAP)
    k_own, v_own, q_own, gains, euler, weight_theirs = pl.pallas_call(
        prep_own_kernel,
        out_shape=(
            shape((tokens + words, width)),
            shape((tokens + words, width)),
            block,
            shape((len(gains), HEAD), jnp.float32),
            shape((1, latent.shape[1]), jnp.float32),
            shape(weight_got.shape),
        ),
        in_specs=[SMEM] * 2 + [VMEM] * 5 + [ANY],
        out_specs=(VMEM,) * 5 + (ANY,),
        input_output_aliases={7: 5},
        compiler_params=params(),
        name="prep_own",
    )(step_index, step_count, own_raw, text_kv, *gains, weight_got)
    weights = (weight_half, weight_theirs)
    k_row, v_row = (lax.ppermute(x, "row", SWAP) for x in (k_own, v_own))
    nearby = (k_own, v_own, k_row, v_row)
    own_sum, own_total, mixed, gains, mods, finals, *q_raw = pl.pallas_call(
        early_kernel,
        out_shape=(
            shape((tokens, width), jnp.float32),
            shape((tokens, width), jnp.float32),
            shape((tokens, features), jnp.float32),
            shape(gains.shape, jnp.float32),
            shape(modulation.shape, jnp.float32),
            shape((final_weight.shape[0], features)),
            shape(first_raw.shape),
            shape(second_raw.shape),
        ),
        in_specs=[VMEM] * 10 + [ANY] * 2,
        out_specs=(VMEM,) * 6 + (ANY,) * 2,
        input_output_aliases={10: 6, 11: 7},
        compiler_params=params(),
        name="early",
    )(q_own, *nearby, gains, hidden, modulation, final_weight, final_got, first_raw, second_raw)
    q_first, q_second = (lax.ppermute(raw, "col", SWAP) for raw in q_raw)
    kv_got = pl.pallas_call(
        norm_kernel,
        out_shape=shape((2 * tokens, width)),
        in_specs=[VMEM] * 2,
        out_specs=VMEM,
        compiler_params=params(),
        name="norm",
    )(lax.ppermute(kv_raw, "col", SWAP), gains)
    kv_last = lax.ppermute(kv_got, "row", SWAP)
    q_first, *sums = pl.pallas_call(
        part_kernel,
        out_shape=(shape((cut, width)),) + (shape((cut, width), jnp.float32),) * 2,
        in_specs=[VMEM] * 7,
        out_specs=(VMEM,) * 3,
        compiler_params=params(),
        cost_estimate=lasting(4.5),
        name="part",
    )(q_first, gains, *nearby, kv_got)
    first, heads = pl.pallas_call(
        first_kernel,
        out_shape=(shape((cut, FIRST)), shape((cut, width))),
        in_specs=[VMEM] * 6,
        out_specs=(VMEM,) * 2,
        compiler_params=params(),
        name="first",
    )(q_first, kv_last, *sums, *weights)
    first_got = lax.ppermute(first, "col", SWAP)
    rest = pl.pallas_call(
        rest_kernel,
        out_shape=shape((cut, features - FIRST)),
        in_specs=[VMEM] * 3,
        out_specs=VMEM,
        compiler_params=params(),
        name="rest",
    )(heads, *weights)
    rest_got = lax.ppermute(rest, "col", SWAP)
    q_second, rest = lax.optimization_barrier((q_second, rest))
    second = pl.pallas_call(
        second_kernel,
        out_shape=shape((tokens - cut, features)),
        in_specs=[VMEM] * 10,
        out_specs=VMEM,
        scratch_shapes=[pltpu.VMEM((tokens - cut, width), jnp.bfloat16)],
        compiler_params=params(),
        name="second",
    )(q_second, gains, *nearby, kv_got, kv_last, *weights)
    second_got = lax.ppermute(second, "col", SWAP)
    mixed = pl.pallas_call(
        own_kernel,
        out_shape=shape(mixed.shape, jnp.float32),
        in_specs=[VMEM] * 10,
        out_specs=VMEM,
        scratch_shapes=[pltpu.VMEM((tokens, width), jnp.bfloat16)],
        compiler_params=params(),
        cost_estimate=lasting(60),
        name="own",
    )(q_own, kv_got, kv_last, own_sum, own_total, *weights, mixed, mods, first_got)
    results = ()
    for (start, _), got in ((chunks[0], rest_got), (chunks[1], second_got)):
        results = pl.pallas_call(
            functools.partial(final_kernel, start),
            out_shape=(shape(latent.shape, jnp.float32),) * 2,
            in_specs=[VMEM] * (6 + len(results)),
            out_specs=(VMEM, VMEM),
            compiler_params=params(),
            name="final",
        )(euler, mixed, got, mods, finals, latent, *results)
    return results


def solution(mesh):
    placed = (
        P(("req", "row"), "col", None, None),
        P(("req", "row"), None, "col"),
        P(),
        P(),
        P(),
        P("col", "row"),
        P(None, "row"),
        P(("req", "row"), "col", None),
        P("req", None),
        P(("req", "row"), "col"),
        P("req"),
        P("req"),
    )
    return jax.shard_map(
        on_device,
        mesh=mesh,
        in_specs=placed,
        out_specs=(P(("req", "row"), "col"), P(("req", "row"), "col")),
        check_vma=False,
    )
```

```python
import functools
import math

import jax
import jax.numpy as jnp
from jax import lax
from jax.experimental import pallas as pl
from jax.experimental.pallas import tpu as pltpu
from jax.sharding import PartitionSpec as P

HEAD = 64
CH = 16
PATCH = 2
STEPS = 28
SHIFT_FACTOR = 3.0
LANES = 128
EPS = 1e-06
VMEM_LIMIT = 16 * 1024 * 1024
VMEM_MOST = 52 * 1024 * 1024
LOADS = 3
FIRST = 1280
STEP = 640
SWAP = [(0, 1), (1, 0)]


def noise_level(step_number):
    fraction = 1.0 - step_number.astype(jnp.float32) / STEPS
    return SHIFT_FACTOR * fraction / (1.0 + (SHIFT_FACTOR - 1.0) * fraction)


def same_head(width):
    row = lax.broadcasted_iota(jnp.int32, (width, width), 0) // HEAD
    col = lax.broadcasted_iota(jnp.int32, (width, width), 1) // HEAD
    return (row == col).astype(jnp.bfloat16)


def head_norms(pairs):
    ones = same_head(LANES)
    squares = []
    for x, _ in pairs:
        for at in range(0, x.shape[1], LANES):
            square = x[:, at : at + LANES] * x[:, at : at + LANES]
            high = square.astype(jnp.bfloat16)
            low = (square - high.astype(jnp.float32)).astype(jnp.bfloat16)
            squares.append(jnp.concatenate([high, low], axis=1))
    totals = jnp.dot(
        jnp.concatenate(squares, axis=0),
        jnp.concatenate([ones, ones], axis=0),
        preferred_element_type=jnp.float32,
    )
    inverse = lax.rsqrt(totals * (1.0 / HEAD) + EPS)
    results, start = [], 0
    for x, gain in pairs:
        gain = jnp.concatenate([gain, gain], axis=1)
        pieces = []
        for at in range(0, x.shape[1], LANES):
            factor = inverse[start : start + x.shape[0]]
            pieces.append((x[:, at : at + LANES] * factor * gain).astype(jnp.bfloat16))
            start += x.shape[0]
        results.append(jnp.concatenate(pieces, axis=1))
    return results


def load_half(x_ref, held, sems, column):
    tokens, _, width = held.shape
    at = pl.multiple_of(column * width, LANES)
    step = tokens // sems.shape[0]
    copies = [
        pltpu.make_async_copy(
            x_ref.at[start : start + step, :, pl.ds(at, width)],
            held.at[start : start + step],
            sems.at[start // step],
        )
        for start in range(0, tokens, step)
    ]
    for copy in copies:
        copy.start()
    return [(slice(at * step, at * step + step), copy) for at, copy in enumerate(copies)]


def halves(ref):
    rows = ref.shape[0] // 2
    return ref.at[:rows], ref.at[rows:]


def split_kernel(
    x_ref,
    kv_ref,
    q_first_ref,
    q_second_ref,
    own_ref,
    held,
    sems,
    own_sems,
):
    column = lax.axis_index("col")
    blocks = load_half(x_ref, held, sems, 1 - column)
    own_blocks = load_half(x_ref, own_ref, own_sems, column)
    k_ref, v_ref = halves(kv_ref)
    cut = q_first_ref.shape[0]
    for rows, copy in blocks:
        copy.wait()
        q, k, v = held[rows].transpose(1, 0, 2)
        k_ref[rows] = k
        v_ref[rows] = v
        if rows.stop <= cut:
            q_first_ref[rows] = q
        else:
            q_second_ref[rows.start - cut : rows.stop - cut] = q
    for _, copy in own_blocks:
        copy.wait()


def q_norm(x_ref, gains):
    (q,) = head_norms([(x_ref[...].astype(jnp.float32), gains[0:1])])
    return q


def norm_kernel(x_ref, gains, kv_ref):
    (k, v), (k_out, v_out) = halves(x_ref), halves(kv_ref)
    v_out[...] = v[...]
    (k_out[...],) = head_norms([(k[...].astype(jnp.float32), gains[1:2])])


def keys_and_values(refs):
    k_own, v_own, k_row, v_row, *joined = refs
    pairs = [(k_own, v_own), (k_row, v_row)] + [halves(ref) for ref in joined]
    return [keys for keys, _ in pairs], [values for _, values in pairs]


def prep_own_kernel(
    index_ref,
    count_ref,
    x_ref,
    text_ref,
    gain_q_ref,
    gain_k_ref,
    gain_t_ref,
    _,
    k_ref,
    v_ref,
    q_ref,
    gains,
    euler_ref,
    __,
):
    tokens, width = q_ref.shape
    for at, ref in enumerate((gain_q_ref, gain_k_ref, gain_t_ref)):
        gains[at : at + 1] = ref[...]
    now = jnp.full(euler_ref.shape, index_ref[0], jnp.int32)
    then = now + jnp.full(euler_ref.shape, count_ref[0], jnp.int32)
    euler_ref[...] = noise_level(then) - noise_level(now)
    text = text_ref[...].astype(jnp.float32).transpose(1, 0, 2)
    v_ref[tokens:] = text[1].astype(jnp.bfloat16)
    q, k, v = x_ref[...].transpose(1, 0, 2)
    v_ref[:tokens] = v
    k_ref[:tokens], k_ref[tokens:], q_ref[...] = head_norms(
        [
            (k.astype(jnp.float32), gains[1:2]),
            (text[0], gains[2:3]),
            (q.astype(jnp.float32), gains[0:1]),
        ]
    )


def attend(q, keys_refs, values_refs, store):
    tokens, width = q.shape
    first = lax.broadcasted_iota(jnp.int32, (tokens, LANES), 1) < HEAD
    scale = math.log2(math.e) / math.sqrt(HEAD)
    zero = jnp.zeros((tokens, LANES), jnp.bfloat16)
    ones = jnp.ones((sum(ref.shape[0] for ref in keys_refs), LANES), jnp.bfloat16)

    def scores_of(at):
        lanes = slice(at, at + LANES)
        keys = jnp.concatenate([ref[:, lanes] for ref in keys_refs], axis=0)
        block = q[:, lanes]
        both = jnp.concatenate(
            [jnp.where(first, block, zero), jnp.where(first, zero, block)], axis=0
        )
        return lax.dot_general(
            both, keys, (((1,), (1,)), ((), ())), preferred_element_type=jnp.float32
        )

    def finish(at, scores):
        lanes = slice(at, at + LANES)
        values = jnp.concatenate([ref[:, lanes] for ref in values_refs], axis=0)
        weights = jnp.exp2(scores * scale).astype(jnp.bfloat16)
        out = jnp.dot(
            weights,
            jnp.concatenate([values, ones], axis=1),
            preferred_element_type=jnp.float32,
        )
        weighted = jnp.where(first, out[:tokens, :LANES], out[tokens:, :LANES])
        total = jnp.where(first, out[:tokens, LANES:], out[tokens:, LANES:])
        store(lanes, weighted, total)

    ahead = scores_of(0)
    for at in range(0, width, LANES):
        scores = ahead
        if at + LANES < width:
            ahead = scores_of(at + LANES)
        finish(at, scores)


def project(attended, halves_refs, start, upto, store):
    half = halves_refs[0].shape[0]
    for at in range(start, upto, STEP):
        to = min(at + STEP, upto)
        parts = []
        for place, ref in enumerate(halves_refs):
            low, high = max(at, place * half), min(to, place * half + half)
            if low < high:
                product = lax.dot_general(
                    attended,
                    ref[low - place * half : high - place * half],
                    (((1,), (1,)), ((), ())),
                    preferred_element_type=jnp.float32,
                )
                parts.append(product.astype(jnp.bfloat16))
        store(at, to, parts[0] if len(parts) == 1 else jnp.concatenate(parts, axis=1))


def divide_into(ref):
    def store(lanes, weighted, total):
        ref[:, lanes] = (weighted / total).astype(jnp.bfloat16)

    return store


def keep_sums(sum_ref, total_ref):
    def store(lanes, weighted, total):
        sum_ref[:, lanes] = weighted
        total_ref[:, lanes] = total

    return store


def part_kernel(x_ref, gains, *refs):
    q_ref, sum_ref, total_ref = refs[5:]
    q_ref[...] = q_norm(x_ref, gains)
    attend(q_ref[...], *keys_and_values(refs[:5]), keep_sums(sum_ref, total_ref))


def first_kernel(
    q_ref, last_ref, sum_ref, total_ref, mine_ref, theirs_ref, out_ref, attended
):
    finish = divide_into(attended)

    def store(lanes, weighted, total):
        finish(lanes, weighted + sum_ref[:, lanes], total + total_ref[:, lanes])

    keys, values = halves(last_ref)
    attend(q_ref[...], [keys], [values], store)

    def keep(at, to, product):
        out_ref[:, at:to] = product

    project(attended[...], (mine_ref, theirs_ref), 0, out_ref.shape[1], keep)


def second_kernel(*refs):
    x_ref, gains, weight_refs, (out_ref, attended) = refs[0], refs[1], refs[8:10], refs[10:]
    attend(q_norm(x_ref, gains), *keys_and_values(refs[2:8]), divide_into(attended))

    def keep(at, to, product):
        out_ref[:, at:to] = product

    project(attended[...], weight_refs, 0, out_ref.shape[1], keep)


def rest_kernel(attended_ref, mine_ref, theirs_ref, out_ref):
    features = 2 * mine_ref.shape[0]
    start = features - out_ref.shape[1]

    def keep(at, to, product):
        out_ref[:, at - start : to - start] = product

    project(attended_ref[...], (mine_ref, theirs_ref), start, features, keep)


def in_order(x, is_first):
    half = x.shape[1] // 2
    return jnp.where(is_first, x, jnp.concatenate([x[:, half:], x[:, :half]], axis=1))


def early_kernel(*refs):
    q_ref, gains, hidden_ref, mod_ref, mine_ref, theirs_ref = refs[0], *refs[5:10]
    sum_ref, total_ref, mixed_ref, gains_out, mod_out, finals_ref = refs[11:17]
    attend(q_ref[...], *keys_and_values(refs[1:5]), keep_sums(sum_ref, total_ref))
    gains_out[...] = gains[...]
    is_first = lax.axis_index("row") == 0
    mod_out[...] = in_order(mod_ref[...], is_first)
    mixed_ref[...] = in_order(
        jnp.concatenate(
            [hidden_ref[row].astype(jnp.float32) for row in range(hidden_ref.shape[0])], axis=0
        ),
        is_first,
    )
    finals_ref[...] = jnp.concatenate(
        [mine_ref[...].astype(jnp.float32), theirs_ref[...].astype(jnp.float32)], axis=1
    ).astype(jnp.bfloat16)


def own_kernel(
    q_ref,
    got_ref,
    last_ref,
    sum_ref,
    total_ref,
    mine_ref,
    theirs_ref,
    mixed_ref,
    mod_ref,
    first_ref,
    out_ref,
    attended,
):
    finish = divide_into(attended)

    def store(lanes, weighted, total):
        finish(lanes, weighted + sum_ref[:, lanes], total + total_ref[:, lanes])

    pairs = [halves(got_ref), halves(last_ref)]
    attend(q_ref[...], [keys for keys, _ in pairs], [values for _, values in pairs], store)

    def keep(at, to, product):
        out_ref[:, at:to] = mixed_ref[:, at:to] + mod_ref[2:3, at:to] * product.astype(jnp.float32)

    project(attended[...], (mine_ref, theirs_ref), 0, out_ref.shape[1], keep)
    upto, to = first_ref.shape
    out_ref[:upto, :to] += mod_ref[2:3, :to] * first_ref[...].astype(jnp.float32)


def one_hot(dims, condition):
    row = lax.broadcasted_iota(jnp.int32, dims, 0)
    col = lax.broadcasted_iota(jnp.int32, dims, 1)
    return jnp.where(condition(row, col), 1.0, 0.0).astype(jnp.bfloat16)


def to_pixels(velocity, tile_cols):
    tokens, values = velocity.shape
    side = values // PATCH
    out_rows, out_lanes = tokens // tile_cols * PATCH, tile_cols * side
    terms, rest = [], velocity
    for _ in range(3):
        term = rest.astype(jnp.bfloat16)
        rest = rest - term.astype(jnp.float32)
        terms.append(term)
    terms = jnp.concatenate(terms, axis=0)
    row = lax.broadcasted_iota(jnp.int32, (3 * tokens, out_lanes), 0)
    col = lax.broadcasted_iota(jnp.int32, (3 * tokens, out_lanes), 1)
    here = col // side == row % tile_cols
    total = jnp.zeros((out_rows, out_lanes), jnp.float32)
    for at in range(PATCH):
        spread = one_hot((values, out_lanes), lambda r, c: r == c % side + at * side)
        wide = jnp.dot(terms, spread, preferred_element_type=jnp.float32)
        wide = jnp.where(here, wide, 0.0).astype(jnp.bfloat16)
        pick = one_hot(
            (out_rows, 3 * tokens), lambda r, c: r == c % tokens // tile_cols * PATCH + at
        )
        total += jnp.dot(pick, wide, preferred_element_type=jnp.float32)
    return total


def final_kernel(
    start,
    euler_ref,
    mixed_ref,
    rest_ref,
    mod_ref,
    final_ref,
    latent_ref,
    *refs,
):
    velocity_ref, next_ref = refs[-2:]
    tokens = rest_ref.shape[0]
    step = 48
    parts = []
    for at in range(0, tokens, step):
        rows = slice(start + at, start + at + step)
        had = mixed_ref.shape[1] - rest_ref.shape[1]
        mixed = mixed_ref[rows]
        got = rest_ref[at : at + step].astype(jnp.float32)
        added = mixed[:, had:] + mod_ref[2:3, had:] * got
        mixed = jnp.concatenate([mixed[:, :had], added], axis=1) if had else added
        mean = jnp.mean(mixed, axis=-1, keepdims=True)
        centered = mixed - mean
        var = jnp.mean(centered * centered, axis=-1, keepdims=True)
        normed = (
            centered * lax.rsqrt(var + EPS) * (1.0 + mod_ref[1:2]) + mod_ref[0:1]
        ).astype(jnp.bfloat16)
        parts.append(
            lax.dot_general(
                normed,
                final_ref[...],
                (((1,), (1,)), ((), ())),
                preferred_element_type=jnp.float32,
            )
        )
    tile_cols = latent_ref.shape[1] // (final_ref.shape[0] // PATCH)
    velocity = to_pixels(jnp.concatenate(parts, axis=0), tile_cols)
    first = start // tile_cols * PATCH
    pixels = slice(first, first + velocity.shape[0])
    for before_ref, after_ref in zip(refs[:-2], refs[-2:]):
        after_ref[:first] = before_ref[:first]
    velocity_ref[pixels] = velocity
    next_ref[pixels] = latent_ref[pixels] + euler_ref[...] * velocity


def params(limit=VMEM_LIMIT):
    return pltpu.CompilerParams(vmem_limit_bytes=limit)


def lasting(duration):
    return pl.CostEstimate(
        flops=int(duration * 1e9), bytes_accessed=int(duration * 3e6), transcendentals=0
    )


def shape(dims, dtype=jnp.bfloat16):
    return jax.ShapeDtypeStruct(dims, dtype)


VMEM = pl.BlockSpec(memory_space=pltpu.VMEM)
ANY = pl.BlockSpec(memory_space=pl.ANY)
HBM = pl.BlockSpec(memory_space=pltpu.HBM)
SMEM = pl.BlockSpec(memory_space=pltpu.SMEM)


def on_device(
    image_qkv,
    text_kv,
    gain_query,
    gain_key,
    gain_text,
    out_weight,
    final_weight,
    hidden,
    modulation,
    latent,
    step_index,
    step_count,
):
    tile_rows, tile_cols, _, all_width = image_qkv.shape
    tokens = tile_rows * tile_cols
    words = text_kv.shape[0]
    width = all_width // lax.axis_size("col")
    features = hidden.shape[2]
    gains = [gain.reshape(1, HEAD) for gain in (gain_query, gain_key, gain_text)]
    x = image_qkv.reshape(tokens, 3, all_width)
    weight_half = out_weight.T
    held = pltpu.VMEM((tokens, 3, width), jnp.bfloat16)
    block = shape((tokens, width))

    loads = pltpu.SemaphoreType.DMA((LOADS,))
    cut = tile_rows // 3 * tile_cols
    chunks = ((0, cut), (cut, tokens))
    kv_raw, first_raw, second_raw, own_raw = pl.pallas_call(
        split_kernel,
        out_shape=(
            shape((2 * tokens, width)),
            shape((cut, width)),
            shape((tokens - cut, width)),
            shape((tokens, 3, width)),
        ),
        in_specs=[HBM],
        out_specs=(VMEM,) * 4,
        scratch_shapes=[held, loads, loads],
        compiler_params=params(VMEM_MOST),
        name="split",
    )(x)
    weight_got = lax.ppermute(weight_half, "row", SWAP)
    final_got = lax.ppermute(final_weight, "row", SWAP)
    k_own, v_own, q_own, gains, euler, weight_theirs = pl.pallas_call(
        prep_own_kernel,
        out_shape=(
            shape((tokens + words, width)),
            shape((tokens + words, width)),
            block,
            shape((len(gains), HEAD), jnp.float32),
            shape((1, latent.shape[1]), jnp.float32),
            shape(weight_got.shape),
        ),
        in_specs=[SMEM] * 2 + [VMEM] * 5 + [ANY],
        out_specs=(VMEM,) * 5 + (ANY,),
        input_output_aliases={7: 5},
        compiler_params=params(),
        name="prep_own",
    )(step_index, step_count, own_raw, text_kv, *gains, weight_got)
    weights = (weight_half, weight_theirs)
    k_row, v_row = (lax.ppermute(x, "row", SWAP) for x in (k_own, v_own))
    nearby = (k_own, v_own, k_row, v_row)
    own_sum, own_total, mixed, gains, mods, finals, second_raw = pl.pallas_call(
        early_kernel,
        out_shape=(
            shape((tokens, width), jnp.float32),
            shape((tokens, width), jnp.float32),
            shape((tokens, features), jnp.float32),
            shape(gains.shape, jnp.float32),
            shape(modulation.shape, jnp.float32),
            shape((final_weight.shape[0], features)),
            shape(second_raw.shape),
        ),
        in_specs=[VMEM] * 10 + [ANY],
        out_specs=(VMEM,) * 6 + (ANY,),
        input_output_aliases={10: 6},
        compiler_params=params(),
        name="early",
    )(q_own, *nearby, gains, hidden, modulation, final_weight, final_got, second_raw)
    q_first, q_second = (lax.ppermute(raw, "col", SWAP) for raw in (first_raw, second_raw))
    kv_got = pl.pallas_call(
        norm_kernel,
        out_shape=shape((2 * tokens, width)),
        in_specs=[VMEM] * 2,
        out_specs=VMEM,
        compiler_params=params(),
        name="norm",
    )(lax.ppermute(kv_raw, "col", SWAP), gains)
    kv_last = lax.ppermute(kv_got, "row", SWAP)
    q_first, *sums = pl.pallas_call(
        part_kernel,
        out_shape=(shape((cut, width)),) + (shape((cut, width), jnp.float32),) * 2,
        in_specs=[VMEM] * 7,
        out_specs=(VMEM,) * 3,
        compiler_params=params(),
        cost_estimate=lasting(4.5),
        name="part",
    )(q_first, gains, *nearby, kv_got)
    first, heads = pl.pallas_call(
        first_kernel,
        out_shape=(shape((cut, FIRST)), shape((cut, width))),
        in_specs=[VMEM] * 6,
        out_specs=(VMEM,) * 2,
        compiler_params=params(),
        name="first",
    )(q_first, kv_last, *sums, *weights)
    first_got = lax.ppermute(first, "col", SWAP)
    rest = pl.pallas_call(
        rest_kernel,
        out_shape=shape((cut, features - FIRST)),
        in_specs=[VMEM] * 3,
        out_specs=VMEM,
        compiler_params=params(),
        name="rest",
    )(heads, *weights)
    rest_got = lax.ppermute(rest, "col", SWAP)
    q_second, rest = lax.optimization_barrier((q_second, rest))
    second = pl.pallas_call(
        second_kernel,
        out_shape=shape((tokens - cut, features)),
        in_specs=[VMEM] * 10,
        out_specs=VMEM,
        scratch_shapes=[pltpu.VMEM((tokens - cut, width), jnp.bfloat16)],
        compiler_params=params(),
        name="second",
    )(q_second, gains, *nearby, kv_got, kv_last, *weights)
    second_got = lax.ppermute(second, "col", SWAP)
    mixed = pl.pallas_call(
        own_kernel,
        out_shape=shape(mixed.shape, jnp.float32),
        in_specs=[VMEM] * 10,
        out_specs=VMEM,
        scratch_shapes=[pltpu.VMEM((tokens, width), jnp.bfloat16)],
        compiler_params=params(),
        cost_estimate=lasting(60),
        name="own",
    )(q_own, kv_got, kv_last, own_sum, own_total, *weights, mixed, mods, first_got)
    results = ()
    for (start, _), got in ((chunks[0], rest_got), (chunks[1], second_got)):
        results = pl.pallas_call(
            functools.partial(final_kernel, start),
            out_shape=(shape(latent.shape, jnp.float32),) * 2,
            in_specs=[VMEM] * (6 + len(results)),
            out_specs=(VMEM, VMEM),
            compiler_params=params(),
            name="final",
        )(euler, mixed, got, mods, finals, latent, *results)
    return results


def solution(mesh):
    placed = (
        P(("req", "row"), "col", None, None),
        P(("req", "row"), None, "col"),
        P(),
        P(),
        P(),
        P("col", "row"),
        P(None, "row"),
        P(("req", "row"), "col", None),
        P("req", None),
        P(("req", "row"), "col"),
        P("req"),
        P("req"),
    )
    return jax.shard_map(
        on_device,
        mesh=mesh,
        in_specs=placed,
        out_specs=(P(("req", "row"), "col"), P(("req", "row"), "col")),
        check_vma=False,
    )
```

```python
import functools
import math

import jax
import jax.numpy as jnp
from jax import lax
from jax.experimental import pallas as pl
from jax.experimental.pallas import tpu as pltpu
from jax.sharding import PartitionSpec as P

HEAD = 64
CH = 16
PATCH = 2
STEPS = 28
SHIFT_FACTOR = 3.0
LANES = 128
EPS = 1e-06
VMEM_LIMIT = 16 * 1024 * 1024
VMEM_MOST = 52 * 1024 * 1024
LOADS = 3
FIRST = 1280
STEP = 640
SWAP = [(0, 1), (1, 0)]


def noise_level(step_number):
    fraction = 1.0 - step_number.astype(jnp.float32) / STEPS
    return SHIFT_FACTOR * fraction / (1.0 + (SHIFT_FACTOR - 1.0) * fraction)


def same_head(width):
    row = lax.broadcasted_iota(jnp.int32, (width, width), 0) // HEAD
    col = lax.broadcasted_iota(jnp.int32, (width, width), 1) // HEAD
    return (row == col).astype(jnp.bfloat16)


def head_norms(pairs):
    ones = same_head(LANES)
    squares = []
    for x, _ in pairs:
        for at in range(0, x.shape[1], LANES):
            square = x[:, at : at + LANES] * x[:, at : at + LANES]
            high = square.astype(jnp.bfloat16)
            low = (square - high.astype(jnp.float32)).astype(jnp.bfloat16)
            squares.append(jnp.concatenate([high, low], axis=1))
    totals = jnp.dot(
        jnp.concatenate(squares, axis=0),
        jnp.concatenate([ones, ones], axis=0),
        preferred_element_type=jnp.float32,
    )
    inverse = lax.rsqrt(totals * (1.0 / HEAD) + EPS)
    results, start = [], 0
    for x, gain in pairs:
        gain = jnp.concatenate([gain, gain], axis=1)
        pieces = []
        for at in range(0, x.shape[1], LANES):
            factor = inverse[start : start + x.shape[0]]
            pieces.append((x[:, at : at + LANES] * factor * gain).astype(jnp.bfloat16))
            start += x.shape[0]
        results.append(jnp.concatenate(pieces, axis=1))
    return results


def load_half(x_ref, held, sems, column):
    tokens, _, width = held.shape
    at = pl.multiple_of(column * width, LANES)
    step = tokens // sems.shape[0]
    copies = [
        pltpu.make_async_copy(
            x_ref.at[start : start + step, :, pl.ds(at, width)],
            held.at[start : start + step],
            sems.at[start // step],
        )
        for start in range(0, tokens, step)
    ]
    for copy in copies:
        copy.start()
    return [(slice(at * step, at * step + step), copy) for at, copy in enumerate(copies)]


def halves(ref):
    rows = ref.shape[0] // 2
    return ref.at[:rows], ref.at[rows:]


def split_kernel(
    x_ref,
    kv_ref,
    q_first_ref,
    q_second_ref,
    own_ref,
    held,
    sems,
    own_sems,
):
    column = lax.axis_index("col")
    blocks = load_half(x_ref, held, sems, 1 - column)
    own_blocks = load_half(x_ref, own_ref, own_sems, column)
    k_ref, v_ref = halves(kv_ref)
    cut = q_first_ref.shape[0]
    for rows, copy in blocks:
        copy.wait()
        q, k, v = held[rows].transpose(1, 0, 2)
        k_ref[rows] = k
        v_ref[rows] = v
        if rows.stop <= cut:
            q_first_ref[rows] = q
        else:
            q_second_ref[rows.start - cut : rows.stop - cut] = q
    for _, copy in own_blocks:
        copy.wait()


def q_norm(x_ref, gains):
    (q,) = head_norms([(x_ref[...].astype(jnp.float32), gains[0:1])])
    return q


def norm_kernel(x_ref, gains, kv_ref):
    (k, v), (k_out, v_out) = halves(x_ref), halves(kv_ref)
    v_out[...] = v[...]
    (k_out[...],) = head_norms([(k[...].astype(jnp.float32), gains[1:2])])


def keys_and_values(refs):
    k_own, v_own, k_row, v_row, *joined = refs
    pairs = [(k_own, v_own), (k_row, v_row)] + [halves(ref) for ref in joined]
    return [keys for keys, _ in pairs], [values for _, values in pairs]


def prep_own_kernel(
    index_ref,
    count_ref,
    x_ref,
    text_ref,
    gain_q_ref,
    gain_k_ref,
    gain_t_ref,
    _,
    k_ref,
    v_ref,
    q_ref,
    gains,
    euler_ref,
    __,
):
    tokens, width = q_ref.shape
    for at, ref in enumerate((gain_q_ref, gain_k_ref, gain_t_ref)):
        gains[at : at + 1] = ref[...]
    now = jnp.full(euler_ref.shape, index_ref[0], jnp.int32)
    then = now + jnp.full(euler_ref.shape, count_ref[0], jnp.int32)
    euler_ref[...] = noise_level(then) - noise_level(now)
    text = text_ref[...].astype(jnp.float32).transpose(1, 0, 2)
    v_ref[tokens:] = text[1].astype(jnp.bfloat16)
    q, k, v = x_ref[...].transpose(1, 0, 2)
    v_ref[:tokens] = v
    k_ref[:tokens], k_ref[tokens:], q_ref[...] = head_norms(
        [
            (k.astype(jnp.float32), gains[1:2]),
            (text[0], gains[2:3]),
            (q.astype(jnp.float32), gains[0:1]),
        ]
    )


def attend(q, keys_refs, values_refs, store):
    tokens, width = q.shape
    first = lax.broadcasted_iota(jnp.int32, (tokens, LANES), 1) < HEAD
    scale = math.log2(math.e) / math.sqrt(HEAD)
    zero = jnp.zeros((tokens, LANES), jnp.bfloat16)
    ones = jnp.ones((sum(ref.shape[0] for ref in keys_refs), LANES), jnp.bfloat16)

    def scores_of(at):
        lanes = slice(at, at + LANES)
        keys = jnp.concatenate([ref[:, lanes] for ref in keys_refs], axis=0)
        block = q[:, lanes]
        both = jnp.concatenate(
            [jnp.where(first, block, zero), jnp.where(first, zero, block)], axis=0
        )
        return lax.dot_general(
            both, keys, (((1,), (1,)), ((), ())), preferred_element_type=jnp.float32
        )

    def finish(at, scores):
        lanes = slice(at, at + LANES)
        values = jnp.concatenate([ref[:, lanes] for ref in values_refs], axis=0)
        weights = jnp.exp2(scores * scale).astype(jnp.bfloat16)
        out = jnp.dot(
            weights,
            jnp.concatenate([values, ones], axis=1),
            preferred_element_type=jnp.float32,
        )
        weighted = jnp.where(first, out[:tokens, :LANES], out[tokens:, :LANES])
        total = jnp.where(first, out[:tokens, LANES:], out[tokens:, LANES:])
        store(lanes, weighted, total)

    ahead = scores_of(0)
    for at in range(0, width, LANES):
        scores = ahead
        if at + LANES < width:
            ahead = scores_of(at + LANES)
        finish(at, scores)


def project(attended, halves_refs, start, upto, store):
    half = halves_refs[0].shape[0]
    for at in range(start, upto, STEP):
        to = min(at + STEP, upto)
        parts = []
        for place, ref in enumerate(halves_refs):
            low, high = max(at, place * half), min(to, place * half + half)
            if low < high:
                product = lax.dot_general(
                    attended,
                    ref[low - place * half : high - place * half],
                    (((1,), (1,)), ((), ())),
                    preferred_element_type=jnp.float32,
                )
                parts.append(product.astype(jnp.bfloat16))
        store(at, to, parts[0] if len(parts) == 1 else jnp.concatenate(parts, axis=1))


def divide_into(ref):
    def store(lanes, weighted, total):
        ref[:, lanes] = (weighted / total).astype(jnp.bfloat16)

    return store


def keep_sums(sum_ref, total_ref):
    def store(lanes, weighted, total):
        sum_ref[:, lanes] = weighted
        total_ref[:, lanes] = total

    return store


def part_kernel(x_ref, gains, *refs):
    q_ref, sum_ref, total_ref = refs[5:]
    q_ref[...] = q_norm(x_ref, gains)
    attend(q_ref[...], *keys_and_values(refs[:5]), keep_sums(sum_ref, total_ref))


def first_kernel(
    q_ref, last_ref, sum_ref, total_ref, mine_ref, theirs_ref, out_ref, attended
):
    finish = divide_into(attended)

    def store(lanes, weighted, total):
        finish(lanes, weighted + sum_ref[:, lanes], total + total_ref[:, lanes])

    keys, values = halves(last_ref)
    attend(q_ref[...], [keys], [values], store)

    def keep(at, to, product):
        out_ref[:, at:to] = product

    project(attended[...], (mine_ref, theirs_ref), 0, out_ref.shape[1], keep)


def second_kernel(*refs):
    x_ref, gains, weight_refs, (out_ref, attended) = refs[0], refs[1], refs[8:10], refs[10:]
    attend(q_norm(x_ref, gains), *keys_and_values(refs[2:8]), divide_into(attended))

    def keep(at, to, product):
        out_ref[:, at:to] = product

    project(attended[...], weight_refs, 0, out_ref.shape[1], keep)


def rest_kernel(attended_ref, mine_ref, theirs_ref, out_ref):
    features = 2 * mine_ref.shape[0]
    start = features - out_ref.shape[1]

    def keep(at, to, product):
        out_ref[:, at - start : to - start] = product

    project(attended_ref[...], (mine_ref, theirs_ref), start, features, keep)


def in_order(x, is_first):
    half = x.shape[1] // 2
    return jnp.where(is_first, x, jnp.concatenate([x[:, half:], x[:, :half]], axis=1))


def early_kernel(*refs):
    q_ref, gains, hidden_ref, mod_ref, mine_ref, theirs_ref = refs[0], *refs[5:10]
    sum_ref, total_ref, mixed_ref, gains_out, mod_out, finals_ref = refs[11:17]
    attend(q_ref[...], *keys_and_values(refs[1:5]), keep_sums(sum_ref, total_ref))
    gains_out[...] = gains[...]
    is_first = lax.axis_index("row") == 0
    mod_out[...] = in_order(mod_ref[...], is_first)
    mixed_ref[...] = in_order(
        jnp.concatenate(
            [hidden_ref[row].astype(jnp.float32) for row in range(hidden_ref.shape[0])], axis=0
        ),
        is_first,
    )
    finals_ref[...] = jnp.concatenate(
        [mine_ref[...].astype(jnp.float32), theirs_ref[...].astype(jnp.float32)], axis=1
    ).astype(jnp.bfloat16)


def own_kernel(
    q_ref,
    got_ref,
    last_ref,
    sum_ref,
    total_ref,
    mine_ref,
    theirs_ref,
    mixed_ref,
    mod_ref,
    first_ref,
    out_ref,
    attended,
):
    finish = divide_into(attended)

    def store(lanes, weighted, total):
        finish(lanes, weighted + sum_ref[:, lanes], total + total_ref[:, lanes])

    pairs = [halves(got_ref), halves(last_ref)]
    attend(q_ref[...], [keys for keys, _ in pairs], [values for _, values in pairs], store)

    def keep(at, to, product):
        out_ref[:, at:to] = mixed_ref[:, at:to] + mod_ref[2:3, at:to] * product.astype(jnp.float32)

    project(attended[...], (mine_ref, theirs_ref), 0, out_ref.shape[1], keep)
    upto, to = first_ref.shape
    out_ref[:upto, :to] += mod_ref[2:3, :to] * first_ref[...].astype(jnp.float32)


def final_kernel(
    start,
    euler_ref,
    mixed_ref,
    rest_ref,
    mod_ref,
    final_ref,
    latent_ref,
    *refs,
):
    velocity_ref, next_ref, values_ref, pixels_ref = refs[-4:]
    tokens = rest_ref.shape[0]
    step = 48
    parts = []
    for at in range(0, tokens, step):
        rows = slice(start + at, start + at + step)
        had = mixed_ref.shape[1] - rest_ref.shape[1]
        mixed = mixed_ref[rows]
        got = rest_ref[at : at + step].astype(jnp.float32)
        added = mixed[:, had:] + mod_ref[2:3, had:] * got
        mixed = jnp.concatenate([mixed[:, :had], added], axis=1) if had else added
        mean = jnp.mean(mixed, axis=-1, keepdims=True)
        centered = mixed - mean
        var = jnp.mean(centered * centered, axis=-1, keepdims=True)
        normed = (
            centered * lax.rsqrt(var + EPS) * (1.0 + mod_ref[1:2]) + mod_ref[0:1]
        ).astype(jnp.bfloat16)
        parts.append(
            lax.dot_general(
                normed,
                final_ref[...],
                (((1,), (1,)), ((), ())),
                preferred_element_type=jnp.float32,
            )
        )
    values = final_ref.shape[0]
    values_ref[:tokens, :values] = jnp.concatenate(parts, axis=0)
    side = values // PATCH
    tile_cols = latent_ref.shape[1] // side
    rows = tokens // tile_cols
    columns = [values_ref[pl.ds(at, rows, stride=tile_cols), :] for at in range(tile_cols)]
    for at in range(PATCH):
        wide = jnp.concatenate([column[:, at * side : (at + 1) * side] for column in columns], axis=1)
        for tile in range(pixels_ref.shape[0]):
            lanes = slice(tile * LANES, (tile + 1) * LANES)
            pixels_ref[tile, pl.ds(at, rows, stride=PATCH), :] = wide[:, lanes]
    first = start // tile_cols * PATCH
    pixels = slice(first, first + rows * PATCH)
    for before_ref, after_ref in zip(refs[:-4], refs[-4:-2]):
        after_ref[:first] = before_ref[:first]
    for tile in range(pixels_ref.shape[0]):
        lanes = slice(tile * LANES, (tile + 1) * LANES)
        velocity = pixels_ref[tile, : rows * PATCH]
        velocity_ref[pixels, lanes] = velocity
        next_ref[pixels, lanes] = latent_ref[pixels, lanes] + euler_ref[:, lanes] * velocity


def params(limit=VMEM_LIMIT):
    return pltpu.CompilerParams(vmem_limit_bytes=limit)


def lasting(duration):
    return pl.CostEstimate(
        flops=int(duration * 1e9), bytes_accessed=int(duration * 3e6), transcendentals=0
    )


def shape(dims, dtype=jnp.bfloat16):
    return jax.ShapeDtypeStruct(dims, dtype)


VMEM = pl.BlockSpec(memory_space=pltpu.VMEM)
ANY = pl.BlockSpec(memory_space=pl.ANY)
HBM = pl.BlockSpec(memory_space=pltpu.HBM)
SMEM = pl.BlockSpec(memory_space=pltpu.SMEM)


def on_device(
    image_qkv,
    text_kv,
    gain_query,
    gain_key,
    gain_text,
    out_weight,
    final_weight,
    hidden,
    modulation,
    latent,
    step_index,
    step_count,
):
    tile_rows, tile_cols, _, all_width = image_qkv.shape
    tokens = tile_rows * tile_cols
    words = text_kv.shape[0]
    width = all_width // lax.axis_size("col")
    features = hidden.shape[2]
    gains = [gain.reshape(1, HEAD) for gain in (gain_query, gain_key, gain_text)]
    x = image_qkv.reshape(tokens, 3, all_width)
    weight_half = out_weight.T
    held = pltpu.VMEM((tokens, 3, width), jnp.bfloat16)
    block = shape((tokens, width))

    loads = pltpu.SemaphoreType.DMA((LOADS,))
    cut = tile_rows // 3 * tile_cols
    chunks = ((0, cut), (cut, tokens))
    kv_raw, first_raw, second_raw, own_raw = pl.pallas_call(
        split_kernel,
        out_shape=(
            shape((2 * tokens, width)),
            shape((cut, width)),
            shape((tokens - cut, width)),
            shape((tokens, 3, width)),
        ),
        in_specs=[HBM],
        out_specs=(VMEM,) * 4,
        scratch_shapes=[held, loads, loads],
        compiler_params=params(VMEM_MOST),
        name="split",
    )(x)
    weight_got = lax.ppermute(weight_half, "row", SWAP)
    final_got = lax.ppermute(final_weight, "row", SWAP)
    k_own, v_own, q_own, gains, euler, weight_theirs = pl.pallas_call(
        prep_own_kernel,
        out_shape=(
            shape((tokens + words, width)),
            shape((tokens + words, width)),
            block,
            shape((len(gains), HEAD), jnp.float32),
            shape((1, latent.shape[1]), jnp.float32),
            shape(weight_got.shape),
        ),
        in_specs=[SMEM] * 2 + [VMEM] * 5 + [ANY],
        out_specs=(VMEM,) * 5 + (ANY,),
        input_output_aliases={7: 5},
        compiler_params=params(),
        name="prep_own",
    )(step_index, step_count, own_raw, text_kv, *gains, weight_got)
    weights = (weight_half, weight_theirs)
    k_row, v_row = (lax.ppermute(x, "row", SWAP) for x in (k_own, v_own))
    nearby = (k_own, v_own, k_row, v_row)
    own_sum, own_total, mixed, gains, mods, finals, second_raw = pl.pallas_call(
        early_kernel,
        out_shape=(
            shape((tokens, width), jnp.float32),
            shape((tokens, width), jnp.float32),
            shape((tokens, features), jnp.float32),
            shape(gains.shape, jnp.float32),
            shape(modulation.shape, jnp.float32),
            shape((final_weight.shape[0], features)),
            shape(second_raw.shape),
        ),
        in_specs=[VMEM] * 10 + [ANY],
        out_specs=(VMEM,) * 6 + (ANY,),
        input_output_aliases={10: 6},
        compiler_params=params(),
        name="early",
    )(q_own, *nearby, gains, hidden, modulation, final_weight, final_got, second_raw)
    q_first, q_second = (lax.ppermute(raw, "col", SWAP) for raw in (first_raw, second_raw))
    kv_got = pl.pallas_call(
        norm_kernel,
        out_shape=shape((2 * tokens, width)),
        in_specs=[VMEM] * 2,
        out_specs=VMEM,
        compiler_params=params(),
        name="norm",
    )(lax.ppermute(kv_raw, "col", SWAP), gains)
    kv_last = lax.ppermute(kv_got, "row", SWAP)
    q_first, *sums = pl.pallas_call(
        part_kernel,
        out_shape=(shape((cut, width)),) + (shape((cut, width), jnp.float32),) * 2,
        in_specs=[VMEM] * 7,
        out_specs=(VMEM,) * 3,
        compiler_params=params(),
        cost_estimate=lasting(4.5),
        name="part",
    )(q_first, gains, *nearby, kv_got)
    first, heads = pl.pallas_call(
        first_kernel,
        out_shape=(shape((cut, FIRST)), shape((cut, width))),
        in_specs=[VMEM] * 6,
        out_specs=(VMEM,) * 2,
        compiler_params=params(),
        name="first",
    )(q_first, kv_last, *sums, *weights)
    first_got = lax.ppermute(first, "col", SWAP)
    rest = pl.pallas_call(
        rest_kernel,
        out_shape=shape((cut, features - FIRST)),
        in_specs=[VMEM] * 3,
        out_specs=VMEM,
        compiler_params=params(),
        name="rest",
    )(heads, *weights)
    rest_got = lax.ppermute(rest, "col", SWAP)
    q_second, rest = lax.optimization_barrier((q_second, rest))
    second = pl.pallas_call(
        second_kernel,
        out_shape=shape((tokens - cut, features)),
        in_specs=[VMEM] * 10,
        out_specs=VMEM,
        scratch_shapes=[pltpu.VMEM((tokens - cut, width), jnp.bfloat16)],
        compiler_params=params(),
        name="second",
    )(q_second, gains, *nearby, kv_got, kv_last, *weights)
    second_got = lax.ppermute(second, "col", SWAP)
    mixed = pl.pallas_call(
        own_kernel,
        out_shape=shape(mixed.shape, jnp.float32),
        in_specs=[VMEM] * 10,
        out_specs=VMEM,
        scratch_shapes=[pltpu.VMEM((tokens, width), jnp.bfloat16)],
        compiler_params=params(),
        cost_estimate=lasting(60),
        name="own",
    )(q_own, kv_got, kv_last, own_sum, own_total, *weights, mixed, mods, first_got)
    room = -(-tile_rows // 8) * 8 + 8
    results = ()
    for (start, _), got in ((chunks[0], rest_got), (chunks[1], second_got)):
        results = pl.pallas_call(
            functools.partial(final_kernel, start),
            out_shape=(shape(latent.shape, jnp.float32),) * 2,
            in_specs=[VMEM] * (6 + len(results)),
            out_specs=(VMEM, VMEM),
            scratch_shapes=[
                pltpu.VMEM((room * tile_cols, LANES), jnp.float32),
                pltpu.VMEM((latent.shape[1] // LANES, room * PATCH, LANES), jnp.float32),
            ],
            compiler_params=params(),
            name="final",
        )(euler, mixed, got, mods, finals, latent, *results)
    return results


def solution(mesh):
    placed = (
        P(("req", "row"), "col", None, None),
        P(("req", "row"), None, "col"),
        P(),
        P(),
        P(),
        P("col", "row"),
        P(None, "row"),
        P(("req", "row"), "col", None),
        P("req", None),
        P(("req", "row"), "col"),
        P("req"),
        P("req"),
    )
    return jax.shard_map(
        on_device,
        mesh=mesh,
        in_specs=placed,
        out_specs=(P(("req", "row"), "col"), P(("req", "row"), "col")),
        check_vma=False,
    )
```

```python
import functools
import math

import jax
import jax.numpy as jnp
from jax import lax
from jax.experimental import pallas as pl
from jax.experimental.pallas import tpu as pltpu
from jax.sharding import PartitionSpec as P

HEAD = 64
CH = 16
PATCH = 2
STEPS = 28
SHIFT_FACTOR = 3.0
LANES = 128
EPS = 1e-06
VMEM_LIMIT = 16 * 1024 * 1024
VMEM_MOST = 53 * 1024 * 1024
VMEM_OWN = 52 * 1024 * 1024
LOADS = 3
FIRST = 1280
STEP = 640
SWAP = [(0, 1), (1, 0)]


def noise_level(step_number):
    fraction = 1.0 - step_number.astype(jnp.float32) / STEPS
    return SHIFT_FACTOR * fraction / (1.0 + (SHIFT_FACTOR - 1.0) * fraction)


def same_head(width):
    row = lax.broadcasted_iota(jnp.int32, (width, width), 0) // HEAD
    col = lax.broadcasted_iota(jnp.int32, (width, width), 1) // HEAD
    return (row == col).astype(jnp.bfloat16)


def head_norms(pairs):
    ones = same_head(LANES)
    squares = []
    for x, _ in pairs:
        for at in range(0, x.shape[1], LANES):
            square = x[:, at : at + LANES] * x[:, at : at + LANES]
            high = square.astype(jnp.bfloat16)
            low = (square - high.astype(jnp.float32)).astype(jnp.bfloat16)
            squares.append(jnp.concatenate([high, low], axis=1))
    totals = jnp.dot(
        jnp.concatenate(squares, axis=0),
        jnp.concatenate([ones, ones], axis=0),
        preferred_element_type=jnp.float32,
    )
    inverse = lax.rsqrt(totals * (1.0 / HEAD) + EPS)
    results, start = [], 0
    for x, gain in pairs:
        gain = jnp.concatenate([gain, gain], axis=1)
        pieces = []
        for at in range(0, x.shape[1], LANES):
            factor = inverse[start : start + x.shape[0]]
            pieces.append((x[:, at : at + LANES] * factor * gain).astype(jnp.bfloat16))
            start += x.shape[0]
        results.append(jnp.concatenate(pieces, axis=1))
    return results


def load_half(x_ref, held, sems, column):
    tokens, _, width = held.shape
    at = pl.multiple_of(column * width, LANES)
    step = tokens // sems.shape[0]
    copies = [
        pltpu.make_async_copy(
            x_ref.at[start : start + step, :, pl.ds(at, width)],
            held.at[start : start + step],
            sems.at[start // step],
        )
        for start in range(0, tokens, step)
    ]
    for copy in copies:
        copy.start()
    return [(slice(at * step, at * step + step), copy) for at, copy in enumerate(copies)]


def halves(ref):
    rows = ref.shape[0] // 2
    return ref.at[:rows], ref.at[rows:]


def split_kernel(
    x_ref,
    kv_ref,
    q_first_ref,
    q_second_ref,
    held,
    sems,
):
    blocks = load_half(x_ref, held, sems, 1 - lax.axis_index("col"))
    k_ref, v_ref = halves(kv_ref)
    cut = q_first_ref.shape[0]
    for rows, copy in blocks:
        copy.wait()
        q, k, v = held[rows].transpose(1, 0, 2)
        k_ref[rows] = k
        v_ref[rows] = v
        if rows.stop <= cut:
            q_first_ref[rows] = q
        else:
            q_second_ref[rows.start - cut : rows.stop - cut] = q


def q_norm(x_ref, gains):
    (q,) = head_norms([(x_ref[...].astype(jnp.float32), gains[0:1])])
    return q


def norm_kernel(x_ref, gains, kv_ref):
    (k, v), (k_out, v_out) = halves(x_ref), halves(kv_ref)
    v_out[...] = v[...]
    (k_out[...],) = head_norms([(k[...].astype(jnp.float32), gains[1:2])])


def keys_and_values(refs):
    k_own, v_own, k_row, v_row, *joined = refs
    pairs = [(k_own, v_own), (k_row, v_row)] + [halves(ref) for ref in joined]
    return [keys for keys, _ in pairs], [values for _, values in pairs]


def prep_own_kernel(
    index_ref,
    count_ref,
    x_ref,
    text_ref,
    gains_in,
    k_ref,
    v_ref,
    q_ref,
    gains,
    euler_ref,
    held,
    sems,
):
    blocks = load_half(x_ref, held, sems, lax.axis_index("col"))
    tokens, width = q_ref.shape
    gains[...] = gains_in[...]
    now = jnp.full(euler_ref.shape, index_ref[0], jnp.int32)
    then = now + jnp.full(euler_ref.shape, count_ref[0], jnp.int32)
    euler_ref[...] = noise_level(then) - noise_level(now)
    text = text_ref[...].astype(jnp.float32).transpose(1, 0, 2)
    v_ref[tokens:] = text[1].astype(jnp.bfloat16)
    for _, copy in blocks:
        copy.wait()
    q, k, v = held[...].transpose(1, 0, 2)
    v_ref[:tokens] = v
    k_ref[:tokens], k_ref[tokens:], q_ref[...] = head_norms(
        [
            (k.astype(jnp.float32), gains[1:2]),
            (text[0], gains[2:3]),
            (q.astype(jnp.float32), gains[0:1]),
        ]
    )


def attend(q, keys_refs, values_refs, store):
    tokens, width = q.shape
    first = lax.broadcasted_iota(jnp.int32, (tokens, LANES), 1) < HEAD
    scale = math.log2(math.e) / math.sqrt(HEAD)
    zero = jnp.zeros((tokens, LANES), jnp.bfloat16)
    ones = jnp.ones((sum(ref.shape[0] for ref in keys_refs), LANES), jnp.bfloat16)

    def scores_of(at):
        lanes = slice(at, at + LANES)
        keys = jnp.concatenate([ref[:, lanes] for ref in keys_refs], axis=0)
        block = q[:, lanes]
        both = jnp.concatenate(
            [jnp.where(first, block, zero), jnp.where(first, zero, block)], axis=0
        )
        return lax.dot_general(
            both, keys, (((1,), (1,)), ((), ())), preferred_element_type=jnp.float32
        )

    def finish(at, scores):
        lanes = slice(at, at + LANES)
        values = jnp.concatenate([ref[:, lanes] for ref in values_refs], axis=0)
        weights = jnp.exp2(scores * scale).astype(jnp.bfloat16)
        out = jnp.dot(
            weights,
            jnp.concatenate([values, ones], axis=1),
            preferred_element_type=jnp.float32,
        )
        weighted = jnp.where(first, out[:tokens, :LANES], out[tokens:, :LANES])
        total = jnp.where(first, out[:tokens, LANES:], out[tokens:, LANES:])
        store(lanes, weighted, total)

    ahead = scores_of(0)
    for at in range(0, width, LANES):
        scores = ahead
        if at + LANES < width:
            ahead = scores_of(at + LANES)
        finish(at, scores)


def project(attended, halves_refs, start, upto, store):
    half = halves_refs[0].shape[0]
    for at in range(start, upto, STEP):
        to = min(at + STEP, upto)
        parts = []
        for place, ref in enumerate(halves_refs):
            low, high = max(at, place * half), min(to, place * half + half)
            if low < high:
                product = lax.dot_general(
                    attended,
                    ref[low - place * half : high - place * half],
                    (((1,), (1,)), ((), ())),
                    preferred_element_type=jnp.float32,
                )
                parts.append(product.astype(jnp.bfloat16))
        store(at, to, parts[0] if len(parts) == 1 else jnp.concatenate(parts, axis=1))


def divide_into(ref):
    def store(lanes, weighted, total):
        ref[:, lanes] = (weighted / total).astype(jnp.bfloat16)

    return store


def keep_sums(sum_ref, total_ref):
    def store(lanes, weighted, total):
        sum_ref[:, lanes] = weighted
        total_ref[:, lanes] = total

    return store


def part_kernel(x_ref, gains, *refs):
    q_ref, sum_ref, total_ref = refs[5:]
    q_ref[...] = q_norm(x_ref, gains)
    attend(q_ref[...], *keys_and_values(refs[:5]), keep_sums(sum_ref, total_ref))


def first_kernel(
    q_ref, last_ref, sum_ref, total_ref, mine_ref, theirs_ref, out_ref, attended
):
    finish = divide_into(attended)

    def store(lanes, weighted, total):
        finish(lanes, weighted + sum_ref[:, lanes], total + total_ref[:, lanes])

    keys, values = halves(last_ref)
    attend(q_ref[...], [keys], [values], store)

    def keep(at, to, product):
        out_ref[:, at:to] = product

    project(attended[...], (mine_ref, theirs_ref), 0, out_ref.shape[1], keep)


def second_kernel(*refs):
    x_ref, gains, weight_refs, (out_ref, attended) = refs[0], refs[1], refs[8:10], refs[10:]
    attend(q_norm(x_ref, gains), *keys_and_values(refs[2:8]), divide_into(attended))

    def keep(at, to, product):
        out_ref[:, at:to] = product

    project(attended[...], weight_refs, 0, out_ref.shape[1], keep)


def rest_kernel(attended_ref, mine_ref, theirs_ref, out_ref):
    features = 2 * mine_ref.shape[0]
    start = features - out_ref.shape[1]

    def keep(at, to, product):
        out_ref[:, at - start : to - start] = product

    project(attended_ref[...], (mine_ref, theirs_ref), start, features, keep)


def in_order(x, is_first):
    half = x.shape[1] // 2
    return jnp.where(is_first, x, jnp.concatenate([x[:, half:], x[:, :half]], axis=1))


def early_kernel(*refs):
    q_ref, gains, hidden_ref, mod_ref, mine_ref, theirs_ref = refs[0], *refs[5:10]
    sum_ref, total_ref, mixed_ref, gains_out, mod_out, finals_ref = refs[11:17]
    attend(q_ref[...], *keys_and_values(refs[1:5]), keep_sums(sum_ref, total_ref))
    gains_out[...] = gains[...]
    is_first = lax.axis_index("row") == 0
    mod_out[...] = in_order(mod_ref[...], is_first)
    mixed_ref[...] = in_order(
        jnp.concatenate(
            [hidden_ref[row].astype(jnp.float32) for row in range(hidden_ref.shape[0])], axis=0
        ),
        is_first,
    )
    finals_ref[...] = jnp.concatenate(
        [mine_ref[...].astype(jnp.float32), theirs_ref[...].astype(jnp.float32)], axis=1
    ).astype(jnp.bfloat16)


def own_kernel(
    q_ref,
    got_ref,
    last_ref,
    sum_ref,
    total_ref,
    mine_ref,
    theirs_ref,
    mixed_ref,
    mod_ref,
    first_ref,
    out_ref,
    attended,
):
    finish = divide_into(attended)

    def store(lanes, weighted, total):
        finish(lanes, weighted + sum_ref[:, lanes], total + total_ref[:, lanes])

    pairs = [halves(got_ref), halves(last_ref)]
    attend(q_ref[...], [keys for keys, _ in pairs], [values for _, values in pairs], store)

    def keep(at, to, product):
        out_ref[:, at:to] = mixed_ref[:, at:to] + mod_ref[2:3, at:to] * product.astype(jnp.float32)

    project(attended[...], (mine_ref, theirs_ref), 0, out_ref.shape[1], keep)
    upto, to = first_ref.shape
    out_ref[:upto, :to] += mod_ref[2:3, :to] * first_ref[...].astype(jnp.float32)


def final_kernel(
    start,
    euler_ref,
    mixed_ref,
    rest_ref,
    mod_ref,
    final_ref,
    latent_ref,
    *refs,
):
    velocity_ref, next_ref, values_ref, pixels_ref = refs[-4:]
    tokens = rest_ref.shape[0]
    step = 48
    parts = []
    for at in range(0, tokens, step):
        rows = slice(start + at, start + at + step)
        had = mixed_ref.shape[1] - rest_ref.shape[1]
        mixed = mixed_ref[rows]
        got = rest_ref[at : at + step].astype(jnp.float32)
        added = mixed[:, had:] + mod_ref[2:3, had:] * got
        mixed = jnp.concatenate([mixed[:, :had], added], axis=1) if had else added
        mean = jnp.mean(mixed, axis=-1, keepdims=True)
        centered = mixed - mean
        var = jnp.mean(centered * centered, axis=-1, keepdims=True)
        normed = (
            centered * lax.rsqrt(var + EPS) * (1.0 + mod_ref[1:2]) + mod_ref[0:1]
        ).astype(jnp.bfloat16)
        parts.append(
            lax.dot_general(
                normed,
                final_ref[...],
                (((1,), (1,)), ((), ())),
                preferred_element_type=jnp.float32,
            )
        )
    values = final_ref.shape[0]
    values_ref[:tokens, :values] = jnp.concatenate(parts, axis=0)
    side = values // PATCH
    tile_cols = latent_ref.shape[1] // side
    rows = tokens // tile_cols
    columns = [values_ref[pl.ds(at, rows, stride=tile_cols), :] for at in range(tile_cols)]
    for at in range(PATCH):
        wide = jnp.concatenate([column[:, at * side : (at + 1) * side] for column in columns], axis=1)
        for tile in range(pixels_ref.shape[0]):
            lanes = slice(tile * LANES, (tile + 1) * LANES)
            pixels_ref[tile, pl.ds(at, rows, stride=PATCH), :] = wide[:, lanes]
    first = start // tile_cols * PATCH
    pixels = slice(first, first + rows * PATCH)
    for before_ref, after_ref in zip(refs[:-4], refs[-4:-2]):
        after_ref[:first] = before_ref[:first]
    for tile in range(pixels_ref.shape[0]):
        lanes = slice(tile * LANES, (tile + 1) * LANES)
        velocity = pixels_ref[tile, : rows * PATCH]
        velocity_ref[pixels, lanes] = velocity
        next_ref[pixels, lanes] = latent_ref[pixels, lanes] + euler_ref[:, lanes] * velocity


def params(limit=VMEM_LIMIT):
    return pltpu.CompilerParams(vmem_limit_bytes=limit)


def lasting(duration):
    return pl.CostEstimate(
        flops=int(duration * 1e9), bytes_accessed=int(duration * 3e6), transcendentals=0
    )


def shape(dims, dtype=jnp.bfloat16):
    return jax.ShapeDtypeStruct(dims, dtype)


VMEM = pl.BlockSpec(memory_space=pltpu.VMEM)
ANY = pl.BlockSpec(memory_space=pl.ANY)
HBM = pl.BlockSpec(memory_space=pltpu.HBM)
SMEM = pl.BlockSpec(memory_space=pltpu.SMEM)


def on_device(
    image_qkv,
    text_kv,
    gain_query,
    gain_key,
    gain_text,
    out_weight,
    final_weight,
    hidden,
    modulation,
    latent,
    step_index,
    step_count,
):
    tile_rows, tile_cols, _, all_width = image_qkv.shape
    tokens = tile_rows * tile_cols
    words = text_kv.shape[0]
    width = all_width // lax.axis_size("col")
    features = hidden.shape[2]
    gains = jnp.stack([gain_query, gain_key, gain_text])
    x = image_qkv.reshape(tokens, 3, all_width)
    weight_half = out_weight.T
    held = pltpu.VMEM((tokens, 3, width), jnp.bfloat16)
    block = shape((tokens, width))

    loads = pltpu.SemaphoreType.DMA((LOADS,))
    cut = tile_rows // 3 * tile_cols
    chunks = ((0, cut), (cut, tokens))
    kv_raw, first_raw, second_raw = pl.pallas_call(
        split_kernel,
        out_shape=(
            shape((2 * tokens, width)),
            shape((cut, width)),
            shape((tokens - cut, width)),
        ),
        in_specs=[HBM],
        out_specs=(VMEM,) * 3,
        scratch_shapes=[held, loads],
        compiler_params=params(VMEM_MOST),
        name="split",
    )(x)
    weight_got = lax.ppermute(weight_half, "row", SWAP)
    final_got = lax.ppermute(final_weight, "row", SWAP)
    k_own, v_own, q_own, gains, euler = pl.pallas_call(
        prep_own_kernel,
        out_shape=(
            shape((tokens + words, width)),
            shape((tokens + words, width)),
            block,
            shape(gains.shape, jnp.float32),
            shape((1, latent.shape[1]), jnp.float32),
        ),
        in_specs=[SMEM] * 2 + [HBM] + [VMEM] * 2,
        out_specs=(VMEM,) * 5,
        scratch_shapes=[held, loads],
        compiler_params=params(VMEM_OWN),
        name="prep_own",
    )(step_index, step_count, x, text_kv, gains)
    weights = (weight_half, weight_got)
    k_row, v_row = (lax.ppermute(x, "row", SWAP) for x in (k_own, v_own))
    nearby = (k_own, v_own, k_row, v_row)
    own_sum, own_total, mixed, gains, mods, finals, second_raw = pl.pallas_call(
        early_kernel,
        out_shape=(
            shape((tokens, width), jnp.float32),
            shape((tokens, width), jnp.float32),
            shape((tokens, features), jnp.float32),
            shape(gains.shape, jnp.float32),
            shape(modulation.shape, jnp.float32),
            shape((final_weight.shape[0], features)),
            shape(second_raw.shape),
        ),
        in_specs=[VMEM] * 10 + [ANY],
        out_specs=(VMEM,) * 6 + (ANY,),
        input_output_aliases={10: 6},
        compiler_params=params(),
        name="early",
    )(q_own, *nearby, gains, hidden, modulation, final_weight, final_got, second_raw)
    q_first, q_second = (lax.ppermute(raw, "col", SWAP) for raw in (first_raw, second_raw))
    kv_got = pl.pallas_call(
        norm_kernel,
        out_shape=shape((2 * tokens, width)),
        in_specs=[VMEM] * 2,
        out_specs=VMEM,
        compiler_params=params(),
        name="norm",
    )(lax.ppermute(kv_raw, "col", SWAP), gains)
    kv_last = lax.ppermute(kv_got, "row", SWAP)
    q_first, *sums = pl.pallas_call(
        part_kernel,
        out_shape=(shape((cut, width)),) + (shape((cut, width), jnp.float32),) * 2,
        in_specs=[VMEM] * 7,
        out_specs=(VMEM,) * 3,
        compiler_params=params(),
        cost_estimate=lasting(4.5),
        name="part",
    )(q_first, gains, *nearby, kv_got)
    first, heads = pl.pallas_call(
        first_kernel,
        out_shape=(shape((cut, FIRST)), shape((cut, width))),
        in_specs=[VMEM] * 6,
        out_specs=(VMEM,) * 2,
        compiler_params=params(),
        name="first",
    )(q_first, kv_last, *sums, *weights)
    first_got = lax.ppermute(first, "col", SWAP)
    rest = pl.pallas_call(
        rest_kernel,
        out_shape=shape((cut, features - FIRST)),
        in_specs=[VMEM] * 3,
        out_specs=VMEM,
        compiler_params=params(),
        name="rest",
    )(heads, *weights)
    rest_got = lax.ppermute(rest, "col", SWAP)
    q_second, rest = lax.optimization_barrier((q_second, rest))
    second = pl.pallas_call(
        second_kernel,
        out_shape=shape((tokens - cut, features)),
        in_specs=[VMEM] * 10,
        out_specs=VMEM,
        scratch_shapes=[pltpu.VMEM((tokens - cut, width), jnp.bfloat16)],
        compiler_params=params(),
        name="second",
    )(q_second, gains, *nearby, kv_got, kv_last, *weights)
    second_got = lax.ppermute(second, "col", SWAP)
    mixed = pl.pallas_call(
        own_kernel,
        out_shape=shape(mixed.shape, jnp.float32),
        in_specs=[VMEM] * 10,
        out_specs=VMEM,
        scratch_shapes=[pltpu.VMEM((tokens, width), jnp.bfloat16)],
        compiler_params=params(),
        cost_estimate=lasting(60),
        name="own",
    )(q_own, kv_got, kv_last, own_sum, own_total, *weights, mixed, mods, first_got)
    room = -(-tile_rows // 8) * 8 + 8
    results = ()
    for (start, _), got in ((chunks[0], rest_got), (chunks[1], second_got)):
        results = pl.pallas_call(
            functools.partial(final_kernel, start),
            out_shape=(shape(latent.shape, jnp.float32),) * 2,
            in_specs=[VMEM] * (6 + len(results)),
            out_specs=(VMEM, VMEM),
            scratch_shapes=[
                pltpu.VMEM((room * tile_cols, LANES), jnp.float32),
                pltpu.VMEM((latent.shape[1] // LANES, room * PATCH, LANES), jnp.float32),
            ],
            compiler_params=params(),
            name="final",
        )(euler, mixed, got, mods, finals, latent, *results)
    return results


def solution(mesh):
    placed = (
        P(("req", "row"), "col", None, None),
        P(("req", "row"), None, "col"),
        P(),
        P(),
        P(),
        P("col", "row"),
        P(None, "row"),
        P(("req", "row"), "col", None),
        P("req", None),
        P(("req", "row"), "col"),
        P("req"),
        P("req"),
    )
    return jax.shard_map(
        on_device,
        mesh=mesh,
        in_specs=placed,
        out_specs=(P(("req", "row"), "col"), P(("req", "row"), "col")),
        check_vma=False,
    )
```

```python
import functools
import math

import jax
import jax.numpy as jnp
from jax import lax
from jax.experimental import pallas as pl
from jax.experimental.pallas import tpu as pltpu
from jax.sharding import PartitionSpec as P

HEAD = 64
CH = 16
PATCH = 2
STEPS = 28
SHIFT_FACTOR = 3.0
LANES = 128
EPS = 1e-06
VMEM_LIMIT = 16 * 1024 * 1024
VMEM_MOST = 53 * 1024 * 1024
VMEM_OWN = 52 * 1024 * 1024
LOADS = 3
FIRST = 1280
STEP = 640
SWAP = [(0, 1), (1, 0)]


def noise_level(step_number):
    fraction = 1.0 - step_number.astype(jnp.float32) / STEPS
    return SHIFT_FACTOR * fraction / (1.0 + (SHIFT_FACTOR - 1.0) * fraction)


def same_head(width):
    row = lax.broadcasted_iota(jnp.int32, (width, width), 0) // HEAD
    col = lax.broadcasted_iota(jnp.int32, (width, width), 1) // HEAD
    return (row == col).astype(jnp.bfloat16)


def head_norms(pairs):
    ones = same_head(LANES)
    squares = []
    for x, _ in pairs:
        for at in range(0, x.shape[1], LANES):
            square = x[:, at : at + LANES] * x[:, at : at + LANES]
            high = square.astype(jnp.bfloat16)
            low = (square - high.astype(jnp.float32)).astype(jnp.bfloat16)
            squares.append(jnp.concatenate([high, low], axis=1))
    totals = jnp.dot(
        jnp.concatenate(squares, axis=0),
        jnp.concatenate([ones, ones], axis=0),
        preferred_element_type=jnp.float32,
    )
    inverse = lax.rsqrt(totals * (1.0 / HEAD) + EPS)
    results, start = [], 0
    for x, gain in pairs:
        gain = jnp.concatenate([gain, gain], axis=1)
        pieces = []
        for at in range(0, x.shape[1], LANES):
            factor = inverse[start : start + x.shape[0]]
            pieces.append((x[:, at : at + LANES] * factor * gain).astype(jnp.bfloat16))
            start += x.shape[0]
        results.append(jnp.concatenate(pieces, axis=1))
    return results


def load_half(x_ref, held, sems, column):
    tokens, _, width = held.shape
    at = pl.multiple_of(column * width, LANES)
    step = tokens // sems.shape[0]
    copies = [
        pltpu.make_async_copy(
            x_ref.at[start : start + step, :, pl.ds(at, width)],
            held.at[start : start + step],
            sems.at[start // step],
        )
        for start in range(0, tokens, step)
    ]
    for copy in copies:
        copy.start()
    return [(slice(at * step, at * step + step), copy) for at, copy in enumerate(copies)]


def halves(ref):
    rows = ref.shape[0] // 2
    return ref.at[:rows], ref.at[rows:]


def split_kernel(
    x_ref,
    kv_ref,
    q_first_ref,
    q_second_ref,
    held,
    sems,
):
    blocks = load_half(x_ref, held, sems, 1 - lax.axis_index("col"))
    k_ref, v_ref = halves(kv_ref)
    cut = q_first_ref.shape[0]
    for rows, copy in blocks:
        copy.wait()
        q, k, v = held[rows].transpose(1, 0, 2)
        k_ref[rows] = k
        v_ref[rows] = v
        if rows.stop <= cut:
            q_first_ref[rows] = q
        else:
            q_second_ref[rows.start - cut : rows.stop - cut] = q


def q_norm(x_ref, gains):
    (q,) = head_norms([(x_ref[...].astype(jnp.float32), gains[0:1])])
    return q


def norm_kernel(x_ref, gains, kv_ref):
    (k, v), (k_out, v_out) = halves(x_ref), halves(kv_ref)
    v_out[...] = v[...]
    (k_out[...],) = head_norms([(k[...].astype(jnp.float32), gains[1:2])])


def keys_and_values(refs):
    k_own, v_own, k_row, v_row, *joined = refs
    pairs = [(k_own, v_own), (k_row, v_row)] + [halves(ref) for ref in joined]
    return [keys for keys, _ in pairs], [values for _, values in pairs]


def prep_own_kernel(
    index_ref,
    count_ref,
    x_ref,
    text_ref,
    gains_in,
    k_ref,
    v_ref,
    q_ref,
    gains,
    euler_ref,
    held,
    sems,
):
    blocks = load_half(x_ref, held, sems, lax.axis_index("col"))
    tokens, width = q_ref.shape
    gains[...] = gains_in[...]
    now = jnp.full(euler_ref.shape, index_ref[0], jnp.int32)
    then = now + jnp.full(euler_ref.shape, count_ref[0], jnp.int32)
    euler_ref[...] = noise_level(then) - noise_level(now)
    text = text_ref[...].astype(jnp.float32).transpose(1, 0, 2)
    v_ref[tokens:] = text[1].astype(jnp.bfloat16)
    for _, copy in blocks:
        copy.wait()
    q, k, v = held[...].transpose(1, 0, 2)
    v_ref[:tokens] = v
    k_ref[:tokens], k_ref[tokens:], q_ref[...] = head_norms(
        [
            (k.astype(jnp.float32), gains[1:2]),
            (text[0], gains[2:3]),
            (q.astype(jnp.float32), gains[0:1]),
        ]
    )


def attend(q, keys_refs, values_refs, store):
    tokens, width = q.shape
    first = lax.broadcasted_iota(jnp.int32, (tokens, LANES), 1) < HEAD
    scale = math.log2(math.e) / math.sqrt(HEAD)
    zero = jnp.zeros((tokens, LANES), jnp.bfloat16)
    ones = jnp.ones((sum(ref.shape[0] for ref in keys_refs), LANES), jnp.bfloat16)

    def scores_of(at):
        lanes = slice(at, at + LANES)
        keys = jnp.concatenate([ref[:, lanes] for ref in keys_refs], axis=0)
        block = q[:, lanes]
        both = jnp.concatenate(
            [jnp.where(first, block, zero), jnp.where(first, zero, block)], axis=0
        )
        return lax.dot_general(
            both, keys, (((1,), (1,)), ((), ())), preferred_element_type=jnp.float32
        )

    def finish(at, scores):
        lanes = slice(at, at + LANES)
        values = jnp.concatenate([ref[:, lanes] for ref in values_refs], axis=0)
        weights = jnp.exp2(scores * scale).astype(jnp.bfloat16)
        out = jnp.dot(
            weights,
            jnp.concatenate([values, ones], axis=1),
            preferred_element_type=jnp.float32,
        )
        weighted = jnp.where(first, out[:tokens, :LANES], out[tokens:, :LANES])
        total = jnp.where(first, out[:tokens, LANES:], out[tokens:, LANES:])
        store(lanes, weighted, total)

    ahead = scores_of(0)
    for at in range(0, width, LANES):
        scores = ahead
        if at + LANES < width:
            ahead = scores_of(at + LANES)
        finish(at, scores)


def project(attended, halves_refs, start, upto, store):
    half = halves_refs[0].shape[0]
    for at in range(start, upto, STEP):
        to = min(at + STEP, upto)
        parts = []
        for place, ref in enumerate(halves_refs):
            low, high = max(at, place * half), min(to, place * half + half)
            if low < high:
                product = lax.dot_general(
                    attended,
                    ref[low - place * half : high - place * half],
                    (((1,), (1,)), ((), ())),
                    preferred_element_type=jnp.float32,
                )
                parts.append(product.astype(jnp.bfloat16))
        store(at, to, parts[0] if len(parts) == 1 else jnp.concatenate(parts, axis=1))


def divide_into(ref):
    def store(lanes, weighted, total):
        ref[:, lanes] = (weighted / total).astype(jnp.bfloat16)

    return store


def keep_sums(sum_ref, total_ref):
    def store(lanes, weighted, total):
        sum_ref[:, lanes] = weighted
        total_ref[:, lanes] = total

    return store


def part_kernel(x_ref, gains, *refs):
    q_ref, sum_ref, total_ref = refs[5:]
    q_ref[...] = q_norm(x_ref, gains)
    attend(q_ref[...], *keys_and_values(refs[:5]), keep_sums(sum_ref, total_ref))


def first_kernel(
    q_ref, last_ref, sum_ref, total_ref, mine_ref, theirs_ref, out_ref, attended
):
    finish = divide_into(attended)

    def store(lanes, weighted, total):
        finish(lanes, weighted + sum_ref[:, lanes], total + total_ref[:, lanes])

    keys, values = halves(last_ref)
    attend(q_ref[...], [keys], [values], store)

    def keep(at, to, product):
        out_ref[:, at:to] = product

    project(attended[...], (mine_ref, theirs_ref), 0, out_ref.shape[1], keep)


def second_kernel(*refs):
    x_ref, gains, weight_refs, (out_ref, attended) = refs[0], refs[1], refs[8:10], refs[10:]
    attend(q_norm(x_ref, gains), *keys_and_values(refs[2:8]), divide_into(attended))

    def keep(at, to, product):
        out_ref[:, at:to] = product

    project(attended[...], weight_refs, 0, out_ref.shape[1], keep)


def rest_kernel(attended_ref, mine_ref, theirs_ref, out_ref):
    features = 2 * mine_ref.shape[0]
    start = features - out_ref.shape[1]

    def keep(at, to, product):
        out_ref[:, at - start : to - start] = product

    project(attended_ref[...], (mine_ref, theirs_ref), start, features, keep)


def in_order(x, is_first):
    half = x.shape[1] // 2
    return jnp.where(is_first, x, jnp.concatenate([x[:, half:], x[:, :half]], axis=1))


def early_kernel(*refs):
    q_ref, gains, hidden_ref, mod_ref, mine_ref, theirs_ref = refs[0], *refs[5:10]
    sum_ref, total_ref, mixed_ref, gains_out, mod_out, finals_ref = refs[11:17]
    attend(q_ref[...], *keys_and_values(refs[1:5]), keep_sums(sum_ref, total_ref))
    gains_out[...] = gains[...]
    is_first = lax.axis_index("row") == 0
    mod_out[...] = in_order(mod_ref[...], is_first)
    mixed_ref[...] = in_order(
        jnp.concatenate(
            [hidden_ref[row].astype(jnp.float32) for row in range(hidden_ref.shape[0])], axis=0
        ),
        is_first,
    )
    finals_ref[...] = jnp.concatenate(
        [mine_ref[...].astype(jnp.float32), theirs_ref[...].astype(jnp.float32)], axis=1
    ).astype(jnp.bfloat16)


def own_kernel(
    q_ref,
    got_ref,
    last_ref,
    sum_ref,
    total_ref,
    mine_ref,
    theirs_ref,
    mixed_ref,
    mod_ref,
    first_ref,
    out_ref,
    attended,
):
    finish = divide_into(attended)

    def store(lanes, weighted, total):
        finish(lanes, weighted + sum_ref[:, lanes], total + total_ref[:, lanes])

    pairs = [halves(got_ref), halves(last_ref)]
    attend(q_ref[...], [keys for keys, _ in pairs], [values for _, values in pairs], store)

    def keep(at, to, product):
        out_ref[:, at:to] = mixed_ref[:, at:to] + mod_ref[2:3, at:to] * product.astype(jnp.float32)

    project(attended[...], (mine_ref, theirs_ref), 0, out_ref.shape[1], keep)
    upto, to = first_ref.shape
    out_ref[:upto, :to] += mod_ref[2:3, :to] * first_ref[...].astype(jnp.float32)


def final_kernel(
    start,
    euler_ref,
    mixed_ref,
    rest_ref,
    mod_ref,
    final_ref,
    latent_ref,
    *refs,
):
    velocity_ref, next_ref, values_ref, pixels_ref = refs[-4:]
    tokens = rest_ref.shape[0]
    step = 16
    parts = []
    for at in range(0, tokens, step):
        rows = slice(start + at, start + at + step)
        had = mixed_ref.shape[1] - rest_ref.shape[1]
        mixed = mixed_ref[rows]
        got = rest_ref[at : at + step].astype(jnp.float32)
        added = mixed[:, had:] + mod_ref[2:3, had:] * got
        mixed = jnp.concatenate([mixed[:, :had], added], axis=1) if had else added
        mean = jnp.mean(mixed, axis=-1, keepdims=True)
        centered = mixed - mean
        var = jnp.mean(centered * centered, axis=-1, keepdims=True)
        normed = (
            centered * lax.rsqrt(var + EPS) * (1.0 + mod_ref[1:2]) + mod_ref[0:1]
        ).astype(jnp.bfloat16)
        parts.append(normed)
    velocity = lax.dot_general(
        jnp.concatenate(parts, axis=0),
        final_ref[...],
        (((1,), (1,)), ((), ())),
        preferred_element_type=jnp.float32,
    )
    values = final_ref.shape[0]
    values_ref[:tokens, :values] = velocity
    side = values // PATCH
    tile_cols = latent_ref.shape[1] // side
    rows = tokens // tile_cols
    columns = [values_ref[pl.ds(at, rows, stride=tile_cols), :] for at in range(tile_cols)]
    for at in range(PATCH):
        wide = jnp.concatenate([column[:, at * side : (at + 1) * side] for column in columns], axis=1)
        for tile in range(pixels_ref.shape[0]):
            lanes = slice(tile * LANES, (tile + 1) * LANES)
            pixels_ref[tile, pl.ds(at, rows, stride=PATCH), :] = wide[:, lanes]
    first = start // tile_cols * PATCH
    pixels = slice(first, first + rows * PATCH)
    for before_ref, after_ref in zip(refs[:-4], refs[-4:-2]):
        after_ref[:first] = before_ref[:first]
    for tile in range(pixels_ref.shape[0]):
        lanes = slice(tile * LANES, (tile + 1) * LANES)
        placed = pixels_ref[tile, : rows * PATCH]
        velocity_ref[pixels, lanes] = placed
        next_ref[pixels, lanes] = latent_ref[pixels, lanes] + euler_ref[:, lanes] * placed


def params(limit=VMEM_LIMIT):
    return pltpu.CompilerParams(vmem_limit_bytes=limit)


def lasting(duration):
    return pl.CostEstimate(
        flops=int(duration * 1e9), bytes_accessed=int(duration * 3e6), transcendentals=0
    )


def shape(dims, dtype=jnp.bfloat16):
    return jax.ShapeDtypeStruct(dims, dtype)


VMEM = pl.BlockSpec(memory_space=pltpu.VMEM)
ANY = pl.BlockSpec(memory_space=pl.ANY)
HBM = pl.BlockSpec(memory_space=pltpu.HBM)
SMEM = pl.BlockSpec(memory_space=pltpu.SMEM)


def on_device(
    image_qkv,
    text_kv,
    gain_query,
    gain_key,
    gain_text,
    out_weight,
    final_weight,
    hidden,
    modulation,
    latent,
    step_index,
    step_count,
):
    tile_rows, tile_cols, _, all_width = image_qkv.shape
    tokens = tile_rows * tile_cols
    words = text_kv.shape[0]
    width = all_width // lax.axis_size("col")
    features = hidden.shape[2]
    gains = jnp.stack([gain_query, gain_key, gain_text])
    x = image_qkv.reshape(tokens, 3, all_width)
    weight_half = out_weight.T
    held = pltpu.VMEM((tokens, 3, width), jnp.bfloat16)
    block = shape((tokens, width))

    loads = pltpu.SemaphoreType.DMA((LOADS,))
    cut = tile_rows // 3 * tile_cols
    chunks = ((0, cut), (cut, tokens))
    kv_raw, first_raw, second_raw = pl.pallas_call(
        split_kernel,
        out_shape=(
            shape((2 * tokens, width)),
            shape((cut, width)),
            shape((tokens - cut, width)),
        ),
        in_specs=[HBM],
        out_specs=(VMEM,) * 3,
        scratch_shapes=[held, loads],
        compiler_params=params(VMEM_MOST),
        name="split",
    )(x)
    weight_got = lax.ppermute(weight_half, "row", SWAP)
    final_got = lax.ppermute(final_weight, "row", SWAP)
    k_own, v_own, q_own, gains, euler = pl.pallas_call(
        prep_own_kernel,
        out_shape=(
            shape((tokens + words, width)),
            shape((tokens + words, width)),
            block,
            shape(gains.shape, jnp.float32),
            shape((1, latent.shape[1]), jnp.float32),
        ),
        in_specs=[SMEM] * 2 + [HBM] + [VMEM] * 2,
        out_specs=(VMEM,) * 5,
        scratch_shapes=[held, loads],
        compiler_params=params(VMEM_OWN),
        name="prep_own",
    )(step_index, step_count, x, text_kv, gains)
    weights = (weight_half, weight_got)
    k_row, v_row = (lax.ppermute(x, "row", SWAP) for x in (k_own, v_own))
    nearby = (k_own, v_own, k_row, v_row)
    own_sum, own_total, mixed, gains, mods, finals, second_raw = pl.pallas_call(
        early_kernel,
        out_shape=(
            shape((tokens, width), jnp.float32),
            shape((tokens, width), jnp.float32),
            shape((tokens, features), jnp.float32),
            shape(gains.shape, jnp.float32),
            shape(modulation.shape, jnp.float32),
            shape((final_weight.shape[0], features)),
            shape(second_raw.shape),
        ),
        in_specs=[VMEM] * 10 + [ANY],
        out_specs=(VMEM,) * 6 + (ANY,),
        input_output_aliases={10: 6},
        compiler_params=params(),
        name="early",
    )(q_own, *nearby, gains, hidden, modulation, final_weight, final_got, second_raw)
    q_first, q_second = (lax.ppermute(raw, "col", SWAP) for raw in (first_raw, second_raw))
    kv_got = pl.pallas_call(
        norm_kernel,
        out_shape=shape((2 * tokens, width)),
        in_specs=[VMEM] * 2,
        out_specs=VMEM,
        compiler_params=params(),
        name="norm",
    )(lax.ppermute(kv_raw, "col", SWAP), gains)
    kv_last = lax.ppermute(kv_got, "row", SWAP)
    q_first, *sums = pl.pallas_call(
        part_kernel,
        out_shape=(shape((cut, width)),) + (shape((cut, width), jnp.float32),) * 2,
        in_specs=[VMEM] * 7,
        out_specs=(VMEM,) * 3,
        compiler_params=params(),
        cost_estimate=lasting(4.5),
        name="part",
    )(q_first, gains, *nearby, kv_got)
    first, heads = pl.pallas_call(
        first_kernel,
        out_shape=(shape((cut, FIRST)), shape((cut, width))),
        in_specs=[VMEM] * 6,
        out_specs=(VMEM,) * 2,
        compiler_params=params(),
        name="first",
    )(q_first, kv_last, *sums, *weights)
    first_got = lax.ppermute(first, "col", SWAP)
    rest = pl.pallas_call(
        rest_kernel,
        out_shape=shape((cut, features - FIRST)),
        in_specs=[VMEM] * 3,
        out_specs=VMEM,
        compiler_params=params(),
        name="rest",
    )(heads, *weights)
    rest_got = lax.ppermute(rest, "col", SWAP)
    q_second, rest = lax.optimization_barrier((q_second, rest))
    second = pl.pallas_call(
        second_kernel,
        out_shape=shape((tokens - cut, features)),
        in_specs=[VMEM] * 10,
        out_specs=VMEM,
        scratch_shapes=[pltpu.VMEM((tokens - cut, width), jnp.bfloat16)],
        compiler_params=params(),
        name="second",
    )(q_second, gains, *nearby, kv_got, kv_last, *weights)
    second_got = lax.ppermute(second, "col", SWAP)
    mixed = pl.pallas_call(
        own_kernel,
        out_shape=shape(mixed.shape, jnp.float32),
        in_specs=[VMEM] * 10,
        out_specs=VMEM,
        scratch_shapes=[pltpu.VMEM((tokens, width), jnp.bfloat16)],
        compiler_params=params(),
        cost_estimate=lasting(60),
        name="own",
    )(q_own, kv_got, kv_last, own_sum, own_total, *weights, mixed, mods, first_got)
    room = -(-tile_rows // 8) * 8 + 8
    results = ()
    for (start, _), got in ((chunks[0], rest_got), (chunks[1], second_got)):
        results = pl.pallas_call(
            functools.partial(final_kernel, start),
            out_shape=(shape(latent.shape, jnp.float32),) * 2,
            in_specs=[VMEM] * (6 + len(results)),
            out_specs=(VMEM, VMEM),
            scratch_shapes=[
                pltpu.VMEM((room * tile_cols, LANES), jnp.float32),
                pltpu.VMEM((latent.shape[1] // LANES, room * PATCH, LANES), jnp.float32),
            ],
            compiler_params=params(),
            name="final",
        )(euler, mixed, got, mods, finals, latent, *results)
    return results


def solution(mesh):
    placed = (
        P(("req", "row"), "col", None, None),
        P(("req", "row"), None, "col"),
        P(),
        P(),
        P(),
        P("col", "row"),
        P(None, "row"),
        P(("req", "row"), "col", None),
        P("req", None),
        P(("req", "row"), "col"),
        P("req"),
        P("req"),
    )
    return jax.shard_map(
        on_device,
        mesh=mesh,
        in_specs=placed,
        out_specs=(P(("req", "row"), "col"), P(("req", "row"), "col")),
        check_vma=False,
    )
```

```python
import functools
import math

import jax
import jax.numpy as jnp
from jax import lax
from jax.experimental import pallas as pl
from jax.experimental.pallas import tpu as pltpu
from jax.sharding import PartitionSpec as P

HEAD = 64
CH = 16
PATCH = 2
STEPS = 28
SHIFT_FACTOR = 3.0
LANES = 128
EPS = 1e-06
VMEM_LIMIT = 16 * 1024 * 1024
VMEM_MOST = 53 * 1024 * 1024
VMEM_OWN = 52 * 1024 * 1024
LOADS = 3
FIRST = 1536
STEP = 640
SWAP = [(0, 1), (1, 0)]


def noise_level(step_number):
    fraction = 1.0 - step_number.astype(jnp.float32) / STEPS
    return SHIFT_FACTOR * fraction / (1.0 + (SHIFT_FACTOR - 1.0) * fraction)


def same_head(width):
    row = lax.broadcasted_iota(jnp.int32, (width, width), 0) // HEAD
    col = lax.broadcasted_iota(jnp.int32, (width, width), 1) // HEAD
    return (row == col).astype(jnp.bfloat16)


def head_norms(pairs):
    ones = same_head(LANES)
    squares = []
    for x, _ in pairs:
        for at in range(0, x.shape[1], LANES):
            square = x[:, at : at + LANES] * x[:, at : at + LANES]
            high = square.astype(jnp.bfloat16)
            low = (square - high.astype(jnp.float32)).astype(jnp.bfloat16)
            squares.append(jnp.concatenate([high, low], axis=1))
    totals = jnp.dot(
        jnp.concatenate(squares, axis=0),
        jnp.concatenate([ones, ones], axis=0),
        preferred_element_type=jnp.float32,
    )
    inverse = lax.rsqrt(totals * (1.0 / HEAD) + EPS)
    results, start = [], 0
    for x, gain in pairs:
        gain = jnp.concatenate([gain, gain], axis=1)
        pieces = []
        for at in range(0, x.shape[1], LANES):
            factor = inverse[start : start + x.shape[0]]
            pieces.append((x[:, at : at + LANES] * factor * gain).astype(jnp.bfloat16))
            start += x.shape[0]
        results.append(jnp.concatenate(pieces, axis=1))
    return results


def load_half(x_ref, held, sems, column):
    tokens, _, width = held.shape
    at = pl.multiple_of(column * width, LANES)
    step = tokens // sems.shape[0]
    copies = [
        pltpu.make_async_copy(
            x_ref.at[start : start + step, :, pl.ds(at, width)],
            held.at[start : start + step],
            sems.at[start // step],
        )
        for start in range(0, tokens, step)
    ]
    for copy in copies:
        copy.start()
    return [(slice(at * step, at * step + step), copy) for at, copy in enumerate(copies)]


def halves(ref):
    rows = ref.shape[0] // 2
    return ref.at[:rows], ref.at[rows:]


def split_kernel(
    x_ref,
    kv_ref,
    q_first_ref,
    q_second_ref,
    held,
    sems,
):
    blocks = load_half(x_ref, held, sems, 1 - lax.axis_index("col"))
    k_ref, v_ref = halves(kv_ref)
    cut = q_first_ref.shape[0]
    for rows, copy in blocks:
        copy.wait()
        q, k, v = held[rows].transpose(1, 0, 2)
        k_ref[rows] = k
        v_ref[rows] = v
        if rows.stop <= cut:
            q_first_ref[rows] = q
        else:
            q_second_ref[rows.start - cut : rows.stop - cut] = q


def q_norm(x_ref, gains):
    (q,) = head_norms([(x_ref[...].astype(jnp.float32), gains[0:1])])
    return q


def norm_kernel(x_ref, gains, kv_ref):
    (k, v), (k_out, v_out) = halves(x_ref), halves(kv_ref)
    v_out[...] = v[...]
    (k_out[...],) = head_norms([(k[...].astype(jnp.float32), gains[1:2])])


def keys_and_values(refs):
    k_own, v_own, k_row, v_row, *joined = refs
    pairs = [(k_own, v_own), (k_row, v_row)] + [halves(ref) for ref in joined]
    return [keys for keys, _ in pairs], [values for _, values in pairs]


def prep_own_kernel(
    index_ref,
    count_ref,
    x_ref,
    text_ref,
    gains_in,
    k_ref,
    v_ref,
    q_ref,
    gains,
    euler_ref,
    held,
    sems,
):
    blocks = load_half(x_ref, held, sems, lax.axis_index("col"))
    tokens, width = q_ref.shape
    gains[...] = gains_in[...]
    now = jnp.full(euler_ref.shape, index_ref[0], jnp.int32)
    then = now + jnp.full(euler_ref.shape, count_ref[0], jnp.int32)
    euler_ref[...] = noise_level(then) - noise_level(now)
    text = text_ref[...].astype(jnp.float32).transpose(1, 0, 2)
    v_ref[tokens:] = text[1].astype(jnp.bfloat16)
    for _, copy in blocks:
        copy.wait()
    q, k, v = held[...].transpose(1, 0, 2)
    v_ref[:tokens] = v
    k_ref[:tokens], k_ref[tokens:], q_ref[...] = head_norms(
        [
            (k.astype(jnp.float32), gains[1:2]),
            (text[0], gains[2:3]),
            (q.astype(jnp.float32), gains[0:1]),
        ]
    )


def attend(q, keys_refs, values_refs, store):
    tokens, width = q.shape
    first = lax.broadcasted_iota(jnp.int32, (tokens, LANES), 1) < HEAD
    scale = math.log2(math.e) / math.sqrt(HEAD)
    zero = jnp.zeros((tokens, LANES), jnp.bfloat16)
    ones = jnp.ones((sum(ref.shape[0] for ref in keys_refs), LANES), jnp.bfloat16)

    def scores_of(at):
        lanes = slice(at, at + LANES)
        keys = jnp.concatenate([ref[:, lanes] for ref in keys_refs], axis=0)
        block = q[:, lanes]
        both = jnp.concatenate(
            [jnp.where(first, block, zero), jnp.where(first, zero, block)], axis=0
        )
        return lax.dot_general(
            both, keys, (((1,), (1,)), ((), ())), preferred_element_type=jnp.float32
        )

    def finish(at, scores):
        lanes = slice(at, at + LANES)
        values = jnp.concatenate([ref[:, lanes] for ref in values_refs], axis=0)
        weights = jnp.exp2(scores * scale).astype(jnp.bfloat16)
        out = jnp.dot(
            weights,
            jnp.concatenate([values, ones], axis=1),
            preferred_element_type=jnp.float32,
        )
        weighted = jnp.where(first, out[:tokens, :LANES], out[tokens:, :LANES])
        total = jnp.where(first, out[:tokens, LANES:], out[tokens:, LANES:])
        store(lanes, weighted, total)

    ahead = scores_of(0)
    for at in range(0, width, LANES):
        scores = ahead
        if at + LANES < width:
            ahead = scores_of(at + LANES)
        finish(at, scores)


def project(attended, halves_refs, start, upto, store):
    half = halves_refs[0].shape[0]
    for at in range(start, upto, STEP):
        to = min(at + STEP, upto)
        parts = []
        for place, ref in enumerate(halves_refs):
            low, high = max(at, place * half), min(to, place * half + half)
            if low < high:
                product = lax.dot_general(
                    attended,
                    ref[low - place * half : high - place * half],
                    (((1,), (1,)), ((), ())),
                    preferred_element_type=jnp.float32,
                )
                parts.append(product.astype(jnp.bfloat16))
        store(at, to, parts[0] if len(parts) == 1 else jnp.concatenate(parts, axis=1))


def divide_into(ref):
    def store(lanes, weighted, total):
        ref[:, lanes] = (weighted / total).astype(jnp.bfloat16)

    return store


def keep_sums(sum_ref, total_ref):
    def store(lanes, weighted, total):
        sum_ref[:, lanes] = weighted
        total_ref[:, lanes] = total

    return store


def part_kernel(x_ref, gains, *refs):
    q_ref, sum_ref, total_ref = refs[5:]
    q_ref[...] = q_norm(x_ref, gains)
    attend(q_ref[...], *keys_and_values(refs[:5]), keep_sums(sum_ref, total_ref))


def first_kernel(
    q_ref, last_ref, sum_ref, total_ref, mine_ref, theirs_ref, out_ref, attended
):
    finish = divide_into(attended)

    def store(lanes, weighted, total):
        finish(lanes, weighted + sum_ref[:, lanes], total + total_ref[:, lanes])

    keys, values = halves(last_ref)
    attend(q_ref[...], [keys], [values], store)

    def keep(at, to, product):
        out_ref[:, at:to] = product

    project(attended[...], (mine_ref, theirs_ref), 0, out_ref.shape[1], keep)


def second_kernel(*refs):
    x_ref, gains, weight_refs, (out_ref, attended) = refs[0], refs[1], refs[8:10], refs[10:]
    attend(q_norm(x_ref, gains), *keys_and_values(refs[2:8]), divide_into(attended))

    def keep(at, to, product):
        out_ref[:, at:to] = product

    project(attended[...], weight_refs, 0, out_ref.shape[1], keep)


def rest_kernel(attended_ref, mine_ref, theirs_ref, out_ref):
    features = 2 * mine_ref.shape[0]
    start = features - out_ref.shape[1]

    def keep(at, to, product):
        out_ref[:, at - start : to - start] = product

    project(attended_ref[...], (mine_ref, theirs_ref), start, features, keep)


def in_order(x, is_first):
    half = x.shape[1] // 2
    return jnp.where(is_first, x, jnp.concatenate([x[:, half:], x[:, :half]], axis=1))


def early_kernel(*refs):
    q_ref, gains, hidden_ref, mod_ref, mine_ref, theirs_ref = refs[0], *refs[5:10]
    sum_ref, total_ref, mixed_ref, gains_out, mod_out, finals_ref = refs[11:17]
    attend(q_ref[...], *keys_and_values(refs[1:5]), keep_sums(sum_ref, total_ref))
    gains_out[...] = gains[...]
    is_first = lax.axis_index("row") == 0
    mod_out[...] = in_order(mod_ref[...], is_first)
    mixed_ref[...] = in_order(
        jnp.concatenate(
            [hidden_ref[row].astype(jnp.float32) for row in range(hidden_ref.shape[0])], axis=0
        ),
        is_first,
    )
    finals_ref[...] = jnp.concatenate(
        [mine_ref[...].astype(jnp.float32), theirs_ref[...].astype(jnp.float32)], axis=1
    ).astype(jnp.bfloat16)


def own_kernel(
    q_ref,
    got_ref,
    last_ref,
    sum_ref,
    total_ref,
    mine_ref,
    theirs_ref,
    mixed_ref,
    mod_ref,
    first_ref,
    out_ref,
    attended,
):
    finish = divide_into(attended)

    def store(lanes, weighted, total):
        finish(lanes, weighted + sum_ref[:, lanes], total + total_ref[:, lanes])

    pairs = [halves(got_ref), halves(last_ref)]
    attend(q_ref[...], [keys for keys, _ in pairs], [values for _, values in pairs], store)

    def keep(at, to, product):
        out_ref[:, at:to] = mixed_ref[:, at:to] + mod_ref[2:3, at:to] * product.astype(jnp.float32)

    project(attended[...], (mine_ref, theirs_ref), 0, out_ref.shape[1], keep)
    upto, to = first_ref.shape
    out_ref[:upto, :to] += mod_ref[2:3, :to] * first_ref[...].astype(jnp.float32)


def final_kernel(
    start,
    euler_ref,
    mixed_ref,
    rest_ref,
    mod_ref,
    final_ref,
    latent_ref,
    *refs,
):
    velocity_ref, next_ref, values_ref, pixels_ref = refs[-4:]
    tokens = rest_ref.shape[0]
    step = 16
    parts = []
    for at in range(0, tokens, step):
        rows = slice(start + at, start + at + step)
        had = mixed_ref.shape[1] - rest_ref.shape[1]
        mixed = mixed_ref[rows]
        got = rest_ref[at : at + step].astype(jnp.float32)
        added = mixed[:, had:] + mod_ref[2:3, had:] * got
        mixed = jnp.concatenate([mixed[:, :had], added], axis=1) if had else added
        mean = jnp.mean(mixed, axis=-1, keepdims=True)
        centered = mixed - mean
        var = jnp.mean(centered * centered, axis=-1, keepdims=True)
        normed = (
            centered * lax.rsqrt(var + EPS) * (1.0 + mod_ref[1:2]) + mod_ref[0:1]
        ).astype(jnp.bfloat16)
        parts.append(normed)
    velocity = lax.dot_general(
        jnp.concatenate(parts, axis=0),
        final_ref[...],
        (((1,), (1,)), ((), ())),
        preferred_element_type=jnp.float32,
    )
    values = final_ref.shape[0]
    values_ref[:tokens, :values] = velocity
    side = values // PATCH
    tile_cols = latent_ref.shape[1] // side
    rows = tokens // tile_cols
    columns = [values_ref[pl.ds(at, rows, stride=tile_cols), :] for at in range(tile_cols)]
    for at in range(PATCH):
        wide = jnp.concatenate([column[:, at * side : (at + 1) * side] for column in columns], axis=1)
        for tile in range(pixels_ref.shape[0]):
            lanes = slice(tile * LANES, (tile + 1) * LANES)
            pixels_ref[tile, pl.ds(at, rows, stride=PATCH), :] = wide[:, lanes]
    first = start // tile_cols * PATCH
    pixels = slice(first, first + rows * PATCH)
    for before_ref, after_ref in zip(refs[:-4], refs[-4:-2]):
        after_ref[:first] = before_ref[:first]
    for tile in range(pixels_ref.shape[0]):
        lanes = slice(tile * LANES, (tile + 1) * LANES)
        placed = pixels_ref[tile, : rows * PATCH]
        velocity_ref[pixels, lanes] = placed
        next_ref[pixels, lanes] = latent_ref[pixels, lanes] + euler_ref[:, lanes] * placed


def params(limit=VMEM_LIMIT):
    return pltpu.CompilerParams(vmem_limit_bytes=limit)


def lasting(duration):
    return pl.CostEstimate(
        flops=int(duration * 1e9), bytes_accessed=int(duration * 3e6), transcendentals=0
    )


def shape(dims, dtype=jnp.bfloat16):
    return jax.ShapeDtypeStruct(dims, dtype)


VMEM = pl.BlockSpec(memory_space=pltpu.VMEM)
ANY = pl.BlockSpec(memory_space=pl.ANY)
HBM = pl.BlockSpec(memory_space=pltpu.HBM)
SMEM = pl.BlockSpec(memory_space=pltpu.SMEM)


def on_device(
    image_qkv,
    text_kv,
    gain_query,
    gain_key,
    gain_text,
    out_weight,
    final_weight,
    hidden,
    modulation,
    latent,
    step_index,
    step_count,
):
    tile_rows, tile_cols, _, all_width = image_qkv.shape
    tokens = tile_rows * tile_cols
    words = text_kv.shape[0]
    width = all_width // lax.axis_size("col")
    features = hidden.shape[2]
    gains = jnp.stack([gain_query, gain_key, gain_text])
    x = image_qkv.reshape(tokens, 3, all_width)
    weight_half = out_weight.T
    held = pltpu.VMEM((tokens, 3, width), jnp.bfloat16)
    block = shape((tokens, width))

    loads = pltpu.SemaphoreType.DMA((LOADS,))
    cut = tile_rows // 3 * tile_cols
    chunks = ((0, cut), (cut, tokens))
    kv_raw, first_raw, second_raw = pl.pallas_call(
        split_kernel,
        out_shape=(
            shape((2 * tokens, width)),
            shape((cut, width)),
            shape((tokens - cut, width)),
        ),
        in_specs=[HBM],
        out_specs=(VMEM,) * 3,
        scratch_shapes=[held, loads],
        compiler_params=params(VMEM_MOST),
        name="split",
    )(x)
    weight_got = lax.ppermute(weight_half, "row", SWAP)
    final_got = lax.ppermute(final_weight, "row", SWAP)
    k_own, v_own, q_own, gains, euler = pl.pallas_call(
        prep_own_kernel,
        out_shape=(
            shape((tokens + words, width)),
            shape((tokens + words, width)),
            block,
            shape(gains.shape, jnp.float32),
            shape((1, latent.shape[1]), jnp.float32),
        ),
        in_specs=[SMEM] * 2 + [HBM] + [VMEM] * 2,
        out_specs=(VMEM,) * 5,
        scratch_shapes=[held, loads],
        compiler_params=params(VMEM_OWN),
        name="prep_own",
    )(step_index, step_count, x, text_kv, gains)
    weights = (weight_half, weight_got)
    k_row, v_row = (lax.ppermute(x, "row", SWAP) for x in (k_own, v_own))
    nearby = (k_own, v_own, k_row, v_row)
    own_sum, own_total, mixed, gains, mods, finals, second_raw = pl.pallas_call(
        early_kernel,
        out_shape=(
            shape((tokens, width), jnp.float32),
            shape((tokens, width), jnp.float32),
            shape((tokens, features), jnp.float32),
            shape(gains.shape, jnp.float32),
            shape(modulation.shape, jnp.float32),
            shape((final_weight.shape[0], features)),
            shape(second_raw.shape),
        ),
        in_specs=[VMEM] * 10 + [ANY],
        out_specs=(VMEM,) * 6 + (ANY,),
        input_output_aliases={10: 6},
        compiler_params=params(),
        name="early",
    )(q_own, *nearby, gains, hidden, modulation, final_weight, final_got, second_raw)
    q_first, q_second = (lax.ppermute(raw, "col", SWAP) for raw in (first_raw, second_raw))
    kv_got = pl.pallas_call(
        norm_kernel,
        out_shape=shape((2 * tokens, width)),
        in_specs=[VMEM] * 2,
        out_specs=VMEM,
        compiler_params=params(),
        name="norm",
    )(lax.ppermute(kv_raw, "col", SWAP), gains)
    kv_last = lax.ppermute(kv_got, "row", SWAP)
    q_first, *sums = pl.pallas_call(
        part_kernel,
        out_shape=(shape((cut, width)),) + (shape((cut, width), jnp.float32),) * 2,
        in_specs=[VMEM] * 7,
        out_specs=(VMEM,) * 3,
        compiler_params=params(),
        cost_estimate=lasting(4.5),
        name="part",
    )(q_first, gains, *nearby, kv_got)
    first, heads = pl.pallas_call(
        first_kernel,
        out_shape=(shape((cut, FIRST)), shape((cut, width))),
        in_specs=[VMEM] * 6,
        out_specs=(VMEM,) * 2,
        compiler_params=params(),
        name="first",
    )(q_first, kv_last, *sums, *weights)
    first_got = lax.ppermute(first, "col", SWAP)
    rest = pl.pallas_call(
        rest_kernel,
        out_shape=shape((cut, features - FIRST)),
        in_specs=[VMEM] * 3,
        out_specs=VMEM,
        compiler_params=params(),
        name="rest",
    )(heads, *weights)
    rest_got = lax.ppermute(rest, "col", SWAP)
    q_second, rest = lax.optimization_barrier((q_second, rest))
    second = pl.pallas_call(
        second_kernel,
        out_shape=shape((tokens - cut, features)),
        in_specs=[VMEM] * 10,
        out_specs=VMEM,
        scratch_shapes=[pltpu.VMEM((tokens - cut, width), jnp.bfloat16)],
        compiler_params=params(),
        name="second",
    )(q_second, gains, *nearby, kv_got, kv_last, *weights)
    second_got = lax.ppermute(second, "col", SWAP)
    mixed = pl.pallas_call(
        own_kernel,
        out_shape=shape(mixed.shape, jnp.float32),
        in_specs=[VMEM] * 10,
        out_specs=VMEM,
        scratch_shapes=[pltpu.VMEM((tokens, width), jnp.bfloat16)],
        compiler_params=params(),
        cost_estimate=lasting(60),
        name="own",
    )(q_own, kv_got, kv_last, own_sum, own_total, *weights, mixed, mods, first_got)
    room = -(-tile_rows // 8) * 8 + 8
    results = ()
    for (start, _), got in ((chunks[0], rest_got), (chunks[1], second_got)):
        results = pl.pallas_call(
            functools.partial(final_kernel, start),
            out_shape=(shape(latent.shape, jnp.float32),) * 2,
            in_specs=[VMEM] * (6 + len(results)),
            out_specs=(VMEM, VMEM),
            scratch_shapes=[
                pltpu.VMEM((room * tile_cols, LANES), jnp.float32),
                pltpu.VMEM((latent.shape[1] // LANES, room * PATCH, LANES), jnp.float32),
            ],
            compiler_params=params(),
            name="final",
        )(euler, mixed, got, mods, finals, latent, *results)
    return results


def solution(mesh):
    placed = (
        P(("req", "row"), "col", None, None),
        P(("req", "row"), None, "col"),
        P(),
        P(),
        P(),
        P("col", "row"),
        P(None, "row"),
        P(("req", "row"), "col", None),
        P("req", None),
        P(("req", "row"), "col"),
        P("req"),
        P("req"),
    )
    return jax.shard_map(
        on_device,
        mesh=mesh,
        in_specs=placed,
        out_specs=(P(("req", "row"), "col"), P(("req", "row"), "col")),
        check_vma=False,
    )
```

```python
import functools
import math

import jax
import jax.numpy as jnp
from jax import lax
from jax.experimental import pallas as pl
from jax.experimental.pallas import tpu as pltpu
from jax.sharding import PartitionSpec as P

HEAD = 64
CH = 16
PATCH = 2
STEPS = 28
SHIFT_FACTOR = 3.0
LANES = 128
EPS = 1e-06
VMEM_LIMIT = 16 * 1024 * 1024
VMEM_MOST = 53 * 1024 * 1024
VMEM_OWN = 52 * 1024 * 1024
LOADS = 3
FIRST = 1280
STEP = 640
SWAP = [(0, 1), (1, 0)]


def noise_level(step_number):
    fraction = 1.0 - step_number.astype(jnp.float32) / STEPS
    return SHIFT_FACTOR * fraction / (1.0 + (SHIFT_FACTOR - 1.0) * fraction)


def same_head(width):
    row = lax.broadcasted_iota(jnp.int32, (width, width), 0) // HEAD
    col = lax.broadcasted_iota(jnp.int32, (width, width), 1) // HEAD
    return (row == col).astype(jnp.bfloat16)


def head_norms(pairs):
    ones = same_head(LANES)
    squares = []
    for x, _ in pairs:
        for at in range(0, x.shape[1], LANES):
            square = x[:, at : at + LANES] * x[:, at : at + LANES]
            high = square.astype(jnp.bfloat16)
            low = (square - high.astype(jnp.float32)).astype(jnp.bfloat16)
            squares.append(jnp.concatenate([high, low], axis=1))
    totals = jnp.dot(
        jnp.concatenate(squares, axis=0),
        jnp.concatenate([ones, ones], axis=0),
        preferred_element_type=jnp.float32,
    )
    inverse = lax.rsqrt(totals * (1.0 / HEAD) + EPS)
    results, start = [], 0
    for x, gain in pairs:
        gain = jnp.concatenate([gain, gain], axis=1)
        pieces = []
        for at in range(0, x.shape[1], LANES):
            factor = inverse[start : start + x.shape[0]]
            pieces.append((x[:, at : at + LANES] * factor * gain).astype(jnp.bfloat16))
            start += x.shape[0]
        results.append(jnp.concatenate(pieces, axis=1))
    return results


def load_half(x_ref, held, sems, column):
    tokens, _, width = held.shape
    at = pl.multiple_of(column * width, LANES)
    step = tokens // sems.shape[0]
    copies = [
        pltpu.make_async_copy(
            x_ref.at[start : start + step, :, pl.ds(at, width)],
            held.at[start : start + step],
            sems.at[start // step],
        )
        for start in range(0, tokens, step)
    ]
    for copy in copies:
        copy.start()
    return [(slice(at * step, at * step + step), copy) for at, copy in enumerate(copies)]


def halves(ref):
    rows = ref.shape[0] // 2
    return ref.at[:rows], ref.at[rows:]


def split_kernel(
    x_ref,
    kv_ref,
    q_first_ref,
    q_second_ref,
    held,
    sems,
):
    blocks = load_half(x_ref, held, sems, 1 - lax.axis_index("col"))
    k_ref, v_ref = halves(kv_ref)
    cut = q_first_ref.shape[0]
    for rows, copy in blocks:
        copy.wait()
        q, k, v = held[rows].transpose(1, 0, 2)
        k_ref[rows] = k
        v_ref[rows] = v
        if rows.stop <= cut:
            q_first_ref[rows] = q
        else:
            q_second_ref[rows.start - cut : rows.stop - cut] = q


def q_norm(x_ref, gains):
    (q,) = head_norms([(x_ref[...].astype(jnp.float32), gains[0:1])])
    return q


def norm_kernel(x_ref, gains, kv_ref):
    (k, v), (k_out, v_out) = halves(x_ref), halves(kv_ref)
    v_out[...] = v[...]
    (k_out[...],) = head_norms([(k[...].astype(jnp.float32), gains[1:2])])


def keys_and_values(refs):
    k_own, v_own, k_row, v_row, *joined = refs
    pairs = [(k_own, v_own), (k_row, v_row)] + [halves(ref) for ref in joined]
    return [keys for keys, _ in pairs], [values for _, values in pairs]


def prep_own_kernel(
    index_ref,
    count_ref,
    x_ref,
    text_ref,
    gains_in,
    k_ref,
    v_ref,
    q_ref,
    gains,
    euler_ref,
    held,
    sems,
):
    blocks = load_half(x_ref, held, sems, lax.axis_index("col"))
    tokens, width = q_ref.shape
    gains[...] = gains_in[...]
    now = jnp.full(euler_ref.shape, index_ref[0], jnp.int32)
    then = now + jnp.full(euler_ref.shape, count_ref[0], jnp.int32)
    euler_ref[...] = noise_level(then) - noise_level(now)
    text = text_ref[...].astype(jnp.float32).transpose(1, 0, 2)
    v_ref[tokens:] = text[1].astype(jnp.bfloat16)
    for _, copy in blocks:
        copy.wait()
    q, k, v = held[...].transpose(1, 0, 2)
    v_ref[:tokens] = v
    k_ref[:tokens], k_ref[tokens:], q_ref[...] = head_norms(
        [
            (k.astype(jnp.float32), gains[1:2]),
            (text[0], gains[2:3]),
            (q.astype(jnp.float32), gains[0:1]),
        ]
    )


def attend(q, keys_refs, values_refs, store):
    tokens, width = q.shape
    first = lax.broadcasted_iota(jnp.int32, (tokens, LANES), 1) < HEAD
    scale = math.log2(math.e) / math.sqrt(HEAD)
    zero = jnp.zeros((tokens, LANES), jnp.bfloat16)
    ones = jnp.ones((sum(ref.shape[0] for ref in keys_refs), LANES), jnp.bfloat16)

    def scores_of(at):
        lanes = slice(at, at + LANES)
        keys = jnp.concatenate([ref[:, lanes] for ref in keys_refs], axis=0)
        block = q[:, lanes]
        both = jnp.concatenate(
            [jnp.where(first, block, zero), jnp.where(first, zero, block)], axis=0
        )
        return lax.dot_general(
            both, keys, (((1,), (1,)), ((), ())), preferred_element_type=jnp.float32
        )

    def finish(at, scores):
        lanes = slice(at, at + LANES)
        values = jnp.concatenate([ref[:, lanes] for ref in values_refs], axis=0)
        weights = jnp.exp2(scores * scale).astype(jnp.bfloat16)
        out = jnp.dot(
            weights,
            jnp.concatenate([values, ones], axis=1),
            preferred_element_type=jnp.float32,
        )
        weighted = jnp.where(first, out[:tokens, :LANES], out[tokens:, :LANES])
        total = jnp.where(first, out[:tokens, LANES:], out[tokens:, LANES:])
        store(lanes, weighted, total)

    ahead = scores_of(0)
    for at in range(0, width, LANES):
        scores = ahead
        if at + LANES < width:
            ahead = scores_of(at + LANES)
        finish(at, scores)


def project(attended, halves_refs, start, upto, store):
    half = halves_refs[0].shape[0]
    for at in range(start, upto, STEP):
        to = min(at + STEP, upto)
        parts = []
        for place, ref in enumerate(halves_refs):
            low, high = max(at, place * half), min(to, place * half + half)
            if low < high:
                product = lax.dot_general(
                    attended,
                    ref[low - place * half : high - place * half],
                    (((1,), (1,)), ((), ())),
                    preferred_element_type=jnp.float32,
                )
                parts.append(product.astype(jnp.bfloat16))
        store(at, to, parts[0] if len(parts) == 1 else jnp.concatenate(parts, axis=1))


def divide_into(ref):
    def store(lanes, weighted, total):
        ref[:, lanes] = (weighted / total).astype(jnp.bfloat16)

    return store


def keep_sums(sum_ref, total_ref):
    def store(lanes, weighted, total):
        sum_ref[:, lanes] = weighted
        total_ref[:, lanes] = total

    return store


def part_kernel(x_ref, gains, *refs):
    q_ref, sum_ref, total_ref = refs[5:]
    q_ref[...] = q_norm(x_ref, gains)
    attend(q_ref[...], *keys_and_values(refs[:5]), keep_sums(sum_ref, total_ref))


def first_kernel(
    q_ref, last_ref, sum_ref, total_ref, mine_ref, theirs_ref, out_ref, attended
):
    finish = divide_into(attended)

    def store(lanes, weighted, total):
        finish(lanes, weighted + sum_ref[:, lanes], total + total_ref[:, lanes])

    keys, values = halves(last_ref)
    attend(q_ref[...], [keys], [values], store)

    def keep(at, to, product):
        out_ref[:, at:to] = product

    project(attended[...], (mine_ref, theirs_ref), 0, out_ref.shape[1], keep)


def second_kernel(*refs):
    x_ref, gains, weight_refs, (out_ref, attended) = refs[0], refs[1], refs[8:10], refs[10:]
    attend(q_norm(x_ref, gains), *keys_and_values(refs[2:8]), divide_into(attended))

    def keep(at, to, product):
        out_ref[:, at:to] = product

    project(attended[: out_ref.shape[0]], weight_refs, 0, out_ref.shape[1], keep)


def rest_kernel(attended_ref, mine_ref, theirs_ref, out_ref):
    features = 2 * mine_ref.shape[0]
    start = features - out_ref.shape[1]

    def keep(at, to, product):
        out_ref[:, at - start : to - start] = product

    last = attended_ref[attended_ref.shape[0] - out_ref.shape[0] :]
    project(last, (mine_ref, theirs_ref), start, features, keep)


def in_order(x, is_first):
    half = x.shape[1] // 2
    return jnp.where(is_first, x, jnp.concatenate([x[:, half:], x[:, :half]], axis=1))


def early_kernel(*refs):
    q_ref, gains, hidden_ref, mod_ref, mine_ref, theirs_ref = refs[0], *refs[5:10]
    sum_ref, total_ref, mixed_ref, gains_out, mod_out, finals_ref = refs[11:17]
    attend(q_ref[...], *keys_and_values(refs[1:5]), keep_sums(sum_ref, total_ref))
    gains_out[...] = gains[...]
    is_first = lax.axis_index("row") == 0
    mod_out[...] = in_order(mod_ref[...], is_first)
    mixed_ref[...] = in_order(
        jnp.concatenate(
            [hidden_ref[row].astype(jnp.float32) for row in range(hidden_ref.shape[0])], axis=0
        ),
        is_first,
    )
    finals_ref[...] = jnp.concatenate(
        [mine_ref[...].astype(jnp.float32), theirs_ref[...].astype(jnp.float32)], axis=1
    ).astype(jnp.bfloat16)


def own_kernel(
    q_ref,
    got_ref,
    last_ref,
    sum_ref,
    total_ref,
    mine_ref,
    theirs_ref,
    mixed_ref,
    mod_ref,
    first_ref,
    out_ref,
    attended,
):
    finish = divide_into(attended)

    def store(lanes, weighted, total):
        finish(lanes, weighted + sum_ref[:, lanes], total + total_ref[:, lanes])

    pairs = [halves(got_ref), halves(last_ref)]
    attend(q_ref[...], [keys for keys, _ in pairs], [values for _, values in pairs], store)

    def keep(at, to, product):
        out_ref[:, at:to] = mixed_ref[:, at:to] + mod_ref[2:3, at:to] * product.astype(jnp.float32)

    project(attended[...], (mine_ref, theirs_ref), 0, out_ref.shape[1], keep)
    upto, to = first_ref.shape
    out_ref[:upto, :to] += mod_ref[2:3, :to] * first_ref[...].astype(jnp.float32)


def final_kernel(
    start,
    euler_ref,
    mixed_ref,
    rest_ref,
    mod_ref,
    final_ref,
    latent_ref,
    *refs,
):
    velocity_ref, next_ref, values_ref, pixels_ref = refs[-4:]
    tokens = rest_ref.shape[0]
    step = 16
    parts = []
    for at in range(0, tokens, step):
        rows = slice(start + at, start + at + step)
        had = mixed_ref.shape[1] - rest_ref.shape[1]
        mixed = mixed_ref[rows]
        got = rest_ref[at : at + step].astype(jnp.float32)
        added = mixed[:, had:] + mod_ref[2:3, had:] * got
        mixed = jnp.concatenate([mixed[:, :had], added], axis=1) if had else added
        mean = jnp.mean(mixed, axis=-1, keepdims=True)
        centered = mixed - mean
        var = jnp.mean(centered * centered, axis=-1, keepdims=True)
        normed = (
            centered * lax.rsqrt(var + EPS) * (1.0 + mod_ref[1:2]) + mod_ref[0:1]
        ).astype(jnp.bfloat16)
        parts.append(normed)
    velocity = lax.dot_general(
        jnp.concatenate(parts, axis=0),
        final_ref[...],
        (((1,), (1,)), ((), ())),
        preferred_element_type=jnp.float32,
    )
    values = final_ref.shape[0]
    values_ref[:tokens, :values] = velocity
    side = values // PATCH
    tile_cols = latent_ref.shape[1] // side
    rows = tokens // tile_cols
    columns = [values_ref[pl.ds(at, rows, stride=tile_cols), :] for at in range(tile_cols)]
    for at in range(PATCH):
        wide = jnp.concatenate([column[:, at * side : (at + 1) * side] for column in columns], axis=1)
        for tile in range(pixels_ref.shape[0]):
            lanes = slice(tile * LANES, (tile + 1) * LANES)
            pixels_ref[tile, pl.ds(at, rows, stride=PATCH), :] = wide[:, lanes]
    first = start // tile_cols * PATCH
    pixels = slice(first, first + rows * PATCH)
    for before_ref, after_ref in zip(refs[:-4], refs[-4:-2]):
        after_ref[:first] = before_ref[:first]
    for tile in range(pixels_ref.shape[0]):
        lanes = slice(tile * LANES, (tile + 1) * LANES)
        placed = pixels_ref[tile, : rows * PATCH]
        velocity_ref[pixels, lanes] = placed
        next_ref[pixels, lanes] = latent_ref[pixels, lanes] + euler_ref[:, lanes] * placed


def params(limit=VMEM_LIMIT):
    return pltpu.CompilerParams(vmem_limit_bytes=limit)


def lasting(duration):
    return pl.CostEstimate(
        flops=int(duration * 1e9), bytes_accessed=int(duration * 3e6), transcendentals=0
    )


def shape(dims, dtype=jnp.bfloat16):
    return jax.ShapeDtypeStruct(dims, dtype)


VMEM = pl.BlockSpec(memory_space=pltpu.VMEM)
ANY = pl.BlockSpec(memory_space=pl.ANY)
HBM = pl.BlockSpec(memory_space=pltpu.HBM)
SMEM = pl.BlockSpec(memory_space=pltpu.SMEM)


def on_device(
    image_qkv,
    text_kv,
    gain_query,
    gain_key,
    gain_text,
    out_weight,
    final_weight,
    hidden,
    modulation,
    latent,
    step_index,
    step_count,
):
    tile_rows, tile_cols, _, all_width = image_qkv.shape
    tokens = tile_rows * tile_cols
    words = text_kv.shape[0]
    width = all_width // lax.axis_size("col")
    features = hidden.shape[2]
    gains = jnp.stack([gain_query, gain_key, gain_text])
    x = image_qkv.reshape(tokens, 3, all_width)
    weight_half = out_weight.T
    held = pltpu.VMEM((tokens, 3, width), jnp.bfloat16)
    block = shape((tokens, width))

    loads = pltpu.SemaphoreType.DMA((LOADS,))
    cut = tile_rows // 3 * tile_cols
    chunks = ((0, cut), (cut, tokens))
    kv_raw, first_raw, second_raw = pl.pallas_call(
        split_kernel,
        out_shape=(
            shape((2 * tokens, width)),
            shape((cut, width)),
            shape((tokens - cut, width)),
        ),
        in_specs=[HBM],
        out_specs=(VMEM,) * 3,
        scratch_shapes=[held, loads],
        compiler_params=params(VMEM_MOST),
        name="split",
    )(x)
    weight_got = lax.ppermute(weight_half, "row", SWAP)
    final_got = lax.ppermute(final_weight, "row", SWAP)
    k_own, v_own, q_own, gains, euler = pl.pallas_call(
        prep_own_kernel,
        out_shape=(
            shape((tokens + words, width)),
            shape((tokens + words, width)),
            block,
            shape(gains.shape, jnp.float32),
            shape((1, latent.shape[1]), jnp.float32),
        ),
        in_specs=[SMEM] * 2 + [HBM] + [VMEM] * 2,
        out_specs=(VMEM,) * 5,
        scratch_shapes=[held, loads],
        compiler_params=params(VMEM_OWN),
        name="prep_own",
    )(step_index, step_count, x, text_kv, gains)
    weights = (weight_half, weight_got)
    k_row, v_row = (lax.ppermute(x, "row", SWAP) for x in (k_own, v_own))
    nearby = (k_own, v_own, k_row, v_row)
    own_sum, own_total, mixed, gains, mods, finals, second_raw = pl.pallas_call(
        early_kernel,
        out_shape=(
            shape((tokens, width), jnp.float32),
            shape((tokens, width), jnp.float32),
            shape((tokens, features), jnp.float32),
            shape(gains.shape, jnp.float32),
            shape(modulation.shape, jnp.float32),
            shape((final_weight.shape[0], features)),
            shape(second_raw.shape),
        ),
        in_specs=[VMEM] * 10 + [ANY],
        out_specs=(VMEM,) * 6 + (ANY,),
        input_output_aliases={10: 6},
        compiler_params=params(),
        name="early",
    )(q_own, *nearby, gains, hidden, modulation, final_weight, final_got, second_raw)
    q_first, q_second = (lax.ppermute(raw, "col", SWAP) for raw in (first_raw, second_raw))
    kv_got = pl.pallas_call(
        norm_kernel,
        out_shape=shape((2 * tokens, width)),
        in_specs=[VMEM] * 2,
        out_specs=VMEM,
        compiler_params=params(),
        name="norm",
    )(lax.ppermute(kv_raw, "col", SWAP), gains)
    kv_last = lax.ppermute(kv_got, "row", SWAP)
    q_first, *sums = pl.pallas_call(
        part_kernel,
        out_shape=(shape((cut, width)),) + (shape((cut, width), jnp.float32),) * 2,
        in_specs=[VMEM] * 7,
        out_specs=(VMEM,) * 3,
        compiler_params=params(),
        cost_estimate=lasting(4.5),
        name="part",
    )(q_first, gains, *nearby, kv_got)
    first, heads = pl.pallas_call(
        first_kernel,
        out_shape=(shape((cut, FIRST)), shape((cut, width))),
        in_specs=[VMEM] * 6,
        out_specs=(VMEM,) * 2,
        compiler_params=params(),
        name="first",
    )(q_first, kv_last, *sums, *weights)
    first_got = lax.ppermute(first, "col", SWAP)
    rest = pl.pallas_call(
        rest_kernel,
        out_shape=shape((cut, features - FIRST)),
        in_specs=[VMEM] * 3,
        out_specs=VMEM,
        compiler_params=params(),
        name="rest",
    )(heads, *weights)
    rest_got = lax.ppermute(rest, "col", SWAP)
    q_second, rest = lax.optimization_barrier((q_second, rest))
    second, heads = pl.pallas_call(
        second_kernel,
        out_shape=(shape((cut, features)), shape((tokens - cut, width))),
        in_specs=[VMEM] * 10,
        out_specs=(VMEM, VMEM),
        compiler_params=params(),
        name="second",
    )(q_second, gains, *nearby, kv_got, kv_last, *weights)
    third = pl.pallas_call(
        rest_kernel,
        out_shape=shape((tokens - 2 * cut, features)),
        in_specs=[VMEM] * 3,
        out_specs=VMEM,
        compiler_params=params(),
        name="third",
    )(heads, *weights)
    second_got, third_got = (lax.ppermute(x, "col", SWAP) for x in (second, third))
    mixed = pl.pallas_call(
        own_kernel,
        out_shape=shape(mixed.shape, jnp.float32),
        in_specs=[VMEM] * 10,
        out_specs=VMEM,
        scratch_shapes=[pltpu.VMEM((tokens, width), jnp.bfloat16)],
        compiler_params=params(),
        cost_estimate=lasting(0),
        name="own",
    )(q_own, kv_got, kv_last, own_sum, own_total, *weights, mixed, mods, first_got)
    room = -(-tile_rows // 8) * 8 + 8
    results = ()
    for start, got in zip(range(0, tokens, cut), (rest_got, second_got, third_got)):
        results = pl.pallas_call(
            functools.partial(final_kernel, start),
            out_shape=(shape(latent.shape, jnp.float32),) * 2,
            in_specs=[VMEM] * (6 + len(results)),
            out_specs=(VMEM, VMEM),
            scratch_shapes=[
                pltpu.VMEM((room * tile_cols, LANES), jnp.float32),
                pltpu.VMEM((latent.shape[1] // LANES, room * PATCH, LANES), jnp.float32),
            ],
            compiler_params=params(),
            cost_estimate=lasting(30 if start == cut else 2 if start == 0 else 0),
            name="final",
        )(euler, mixed, got, mods, finals, latent, *results)
    return results


def solution(mesh):
    placed = (
        P(("req", "row"), "col", None, None),
        P(("req", "row"), None, "col"),
        P(),
        P(),
        P(),
        P("col", "row"),
        P(None, "row"),
        P(("req", "row"), "col", None),
        P("req", None),
        P(("req", "row"), "col"),
        P("req"),
        P("req"),
    )
    return jax.shard_map(
        on_device,
        mesh=mesh,
        in_specs=placed,
        out_specs=(P(("req", "row"), "col"), P(("req", "row"), "col")),
        check_vma=False,
    )
```

```python
import functools
import math

import jax
import jax.numpy as jnp
from jax import lax
from jax.experimental import pallas as pl
from jax.experimental.pallas import tpu as pltpu
from jax.sharding import PartitionSpec as P

HEAD = 64
CH = 16
PATCH = 2
STEPS = 28
SHIFT_FACTOR = 3.0
LANES = 128
EPS = 1e-06
VMEM_LIMIT = 16 * 1024 * 1024
VMEM_MOST = 53 * 1024 * 1024
VMEM_OWN = 52 * 1024 * 1024
LOADS = 3
FIRST = 1280
STEP = 1280
SWAP = [(0, 1), (1, 0)]


def noise_level(step_number):
    fraction = 1.0 - step_number.astype(jnp.float32) / STEPS
    return SHIFT_FACTOR * fraction / (1.0 + (SHIFT_FACTOR - 1.0) * fraction)


def same_head(width):
    row = lax.broadcasted_iota(jnp.int32, (width, width), 0) // HEAD
    col = lax.broadcasted_iota(jnp.int32, (width, width), 1) // HEAD
    return (row == col).astype(jnp.bfloat16)


def head_norms(pairs):
    ones = same_head(LANES)
    squares = []
    for x, _ in pairs:
        for at in range(0, x.shape[1], LANES):
            square = x[:, at : at + LANES] * x[:, at : at + LANES]
            high = square.astype(jnp.bfloat16)
            low = (square - high.astype(jnp.float32)).astype(jnp.bfloat16)
            squares.append(jnp.concatenate([high, low], axis=1))
    totals = jnp.dot(
        jnp.concatenate(squares, axis=0),
        jnp.concatenate([ones, ones], axis=0),
        preferred_element_type=jnp.float32,
    )
    inverse = lax.rsqrt(totals * (1.0 / HEAD) + EPS)
    results, start = [], 0
    for x, gain in pairs:
        gain = jnp.concatenate([gain, gain], axis=1)
        pieces = []
        for at in range(0, x.shape[1], LANES):
            factor = inverse[start : start + x.shape[0]]
            pieces.append((x[:, at : at + LANES] * factor * gain).astype(jnp.bfloat16))
            start += x.shape[0]
        results.append(jnp.concatenate(pieces, axis=1))
    return results


def load_half(x_ref, held, sems, column):
    tokens, _, width = held.shape
    at = pl.multiple_of(column * width, LANES)
    step = tokens // sems.shape[0]
    copies = [
        pltpu.make_async_copy(
            x_ref.at[start : start + step, :, pl.ds(at, width)],
            held.at[start : start + step],
            sems.at[start // step],
        )
        for start in range(0, tokens, step)
    ]
    for copy in copies:
        copy.start()
    return [(slice(at * step, at * step + step), copy) for at, copy in enumerate(copies)]


def halves(ref):
    rows = ref.shape[0] // 2
    return ref.at[:rows], ref.at[rows:]


def split_kernel(
    x_ref,
    kv_ref,
    q_first_ref,
    q_second_ref,
    held,
    sems,
):
    blocks = load_half(x_ref, held, sems, 1 - lax.axis_index("col"))
    k_ref, v_ref = halves(kv_ref)
    cut = q_first_ref.shape[0]
    for rows, copy in blocks:
        copy.wait()
        q, k, v = held[rows].transpose(1, 0, 2)
        k_ref[rows] = k
        v_ref[rows] = v
        if rows.stop <= cut:
            q_first_ref[rows] = q
        else:
            q_second_ref[rows.start - cut : rows.stop - cut] = q


def q_norm(x_ref, gains):
    (q,) = head_norms([(x_ref[...].astype(jnp.float32), gains[0:1])])
    return q


def norm_kernel(x_ref, gains, kv_ref):
    (k, v), (k_out, v_out) = halves(x_ref), halves(kv_ref)
    v_out[...] = v[...]
    (k_out[...],) = head_norms([(k[...].astype(jnp.float32), gains[1:2])])


def keys_and_values(refs):
    k_own, v_own, k_row, v_row, *joined = refs
    pairs = [(k_own, v_own), (k_row, v_row)] + [halves(ref) for ref in joined]
    return [keys for keys, _ in pairs], [values for _, values in pairs]


def prep_own_kernel(
    index_ref,
    count_ref,
    x_ref,
    text_ref,
    gains_in,
    k_ref,
    v_ref,
    q_ref,
    gains,
    euler_ref,
    held,
    sems,
):
    blocks = load_half(x_ref, held, sems, lax.axis_index("col"))
    tokens, width = q_ref.shape
    gains[...] = gains_in[...]
    now = jnp.full(euler_ref.shape, index_ref[0], jnp.int32)
    then = now + jnp.full(euler_ref.shape, count_ref[0], jnp.int32)
    euler_ref[...] = noise_level(then) - noise_level(now)
    text = text_ref[...].astype(jnp.float32).transpose(1, 0, 2)
    v_ref[tokens:] = text[1].astype(jnp.bfloat16)
    for _, copy in blocks:
        copy.wait()
    q, k, v = held[...].transpose(1, 0, 2)
    v_ref[:tokens] = v
    k_ref[:tokens], k_ref[tokens:], q_ref[...] = head_norms(
        [
            (k.astype(jnp.float32), gains[1:2]),
            (text[0], gains[2:3]),
            (q.astype(jnp.float32), gains[0:1]),
        ]
    )


def attend(q, keys_refs, values_refs, store):
    tokens, width = q.shape
    first = lax.broadcasted_iota(jnp.int32, (tokens, LANES), 1) < HEAD
    scale = math.log2(math.e) / math.sqrt(HEAD)
    zero = jnp.zeros((tokens, LANES), jnp.bfloat16)
    ones = jnp.ones((sum(ref.shape[0] for ref in keys_refs), LANES), jnp.bfloat16)

    def scores_of(at):
        lanes = slice(at, at + LANES)
        keys = jnp.concatenate([ref[:, lanes] for ref in keys_refs], axis=0)
        block = q[:, lanes]
        both = jnp.concatenate(
            [jnp.where(first, block, zero), jnp.where(first, zero, block)], axis=0
        )
        return lax.dot_general(
            both, keys, (((1,), (1,)), ((), ())), preferred_element_type=jnp.float32
        )

    def finish(at, scores):
        lanes = slice(at, at + LANES)
        values = jnp.concatenate([ref[:, lanes] for ref in values_refs], axis=0)
        weights = jnp.exp2(scores * scale).astype(jnp.bfloat16)
        out = jnp.dot(
            weights,
            jnp.concatenate([values, ones], axis=1),
            preferred_element_type=jnp.float32,
        )
        weighted = jnp.where(first, out[:tokens, :LANES], out[tokens:, :LANES])
        total = jnp.where(first, out[:tokens, LANES:], out[tokens:, LANES:])
        store(lanes, weighted, total)

    ahead = scores_of(0)
    for at in range(0, width, LANES):
        scores = ahead
        if at + LANES < width:
            ahead = scores_of(at + LANES)
        finish(at, scores)


def project(attended, halves_refs, start, upto, store):
    half = halves_refs[0].shape[0]
    for at in range(start, upto, STEP):
        to = min(at + STEP, upto)
        parts = []
        for place, ref in enumerate(halves_refs):
            low, high = max(at, place * half), min(to, place * half + half)
            if low < high:
                product = lax.dot_general(
                    attended,
                    ref[low - place * half : high - place * half],
                    (((1,), (1,)), ((), ())),
                    preferred_element_type=jnp.float32,
                )
                parts.append(product.astype(jnp.bfloat16))
        store(at, to, parts[0] if len(parts) == 1 else jnp.concatenate(parts, axis=1))


def divide_into(ref):
    def store(lanes, weighted, total):
        ref[:, lanes] = (weighted / total).astype(jnp.bfloat16)

    return store


def keep_sums(sum_ref, total_ref):
    def store(lanes, weighted, total):
        sum_ref[:, lanes] = weighted
        total_ref[:, lanes] = total

    return store


def part_kernel(x_ref, gains, *refs):
    q_ref, sum_ref, total_ref = refs[5:]
    q_ref[...] = q_norm(x_ref, gains)
    attend(q_ref[...], *keys_and_values(refs[:5]), keep_sums(sum_ref, total_ref))


def first_kernel(
    q_ref, last_ref, sum_ref, total_ref, mine_ref, theirs_ref, out_ref, attended
):
    finish = divide_into(attended)

    def store(lanes, weighted, total):
        finish(lanes, weighted + sum_ref[:, lanes], total + total_ref[:, lanes])

    keys, values = halves(last_ref)
    attend(q_ref[...], [keys], [values], store)

    def keep(at, to, product):
        out_ref[:, at:to] = product

    project(attended[...], (mine_ref, theirs_ref), 0, out_ref.shape[1], keep)


def second_kernel(*refs):
    x_ref, gains, weight_refs, (out_ref, attended) = refs[0], refs[1], refs[8:10], refs[10:]
    attend(q_norm(x_ref, gains), *keys_and_values(refs[2:8]), divide_into(attended))

    def keep(at, to, product):
        out_ref[:, at:to] = product

    project(attended[: out_ref.shape[0]], weight_refs, 0, out_ref.shape[1], keep)


def rest_kernel(attended_ref, mine_ref, theirs_ref, out_ref):
    features = 2 * mine_ref.shape[0]
    start = features - out_ref.shape[1]

    def keep(at, to, product):
        out_ref[:, at - start : to - start] = product

    last = attended_ref[attended_ref.shape[0] - out_ref.shape[0] :]
    project(last, (mine_ref, theirs_ref), start, features, keep)


def in_order(x, is_first):
    half = x.shape[1] // 2
    return jnp.where(is_first, x, jnp.concatenate([x[:, half:], x[:, :half]], axis=1))


def early_kernel(*refs):
    q_ref, gains, hidden_ref, mod_ref, mine_ref, theirs_ref = refs[0], *refs[5:10]
    sum_ref, total_ref, mixed_ref, gains_out, mod_out, finals_ref = refs[11:17]
    attend(q_ref[...], *keys_and_values(refs[1:5]), keep_sums(sum_ref, total_ref))
    gains_out[...] = gains[...]
    is_first = lax.axis_index("row") == 0
    mod_out[...] = in_order(mod_ref[...], is_first)
    mixed_ref[...] = in_order(
        jnp.concatenate(
            [hidden_ref[row].astype(jnp.float32) for row in range(hidden_ref.shape[0])], axis=0
        ),
        is_first,
    )
    finals_ref[...] = jnp.concatenate(
        [mine_ref[...].astype(jnp.float32), theirs_ref[...].astype(jnp.float32)], axis=1
    ).astype(jnp.bfloat16)


def own_kernel(
    q_ref,
    got_ref,
    last_ref,
    sum_ref,
    total_ref,
    mine_ref,
    theirs_ref,
    mixed_ref,
    mod_ref,
    first_ref,
    out_ref,
    attended,
):
    finish = divide_into(attended)

    def store(lanes, weighted, total):
        finish(lanes, weighted + sum_ref[:, lanes], total + total_ref[:, lanes])

    pairs = [halves(got_ref), halves(last_ref)]
    attend(q_ref[...], [keys for keys, _ in pairs], [values for _, values in pairs], store)

    def keep(at, to, product):
        out_ref[:, at:to] = mixed_ref[:, at:to] + mod_ref[2:3, at:to] * product.astype(jnp.float32)

    project(attended[...], (mine_ref, theirs_ref), 0, out_ref.shape[1], keep)
    upto, to = first_ref.shape
    out_ref[:upto, :to] += mod_ref[2:3, :to] * first_ref[...].astype(jnp.float32)


def final_kernel(
    start,
    euler_ref,
    mixed_ref,
    rest_ref,
    mod_ref,
    final_ref,
    latent_ref,
    *refs,
):
    velocity_ref, next_ref, values_ref, pixels_ref = refs[-4:]
    tokens = rest_ref.shape[0]
    step = 16
    parts = []
    for at in range(0, tokens, step):
        rows = slice(start + at, start + at + step)
        had = mixed_ref.shape[1] - rest_ref.shape[1]
        mixed = mixed_ref[rows]
        got = rest_ref[at : at + step].astype(jnp.float32)
        added = mixed[:, had:] + mod_ref[2:3, had:] * got
        mixed = jnp.concatenate([mixed[:, :had], added], axis=1) if had else added
        mean = jnp.mean(mixed, axis=-1, keepdims=True)
        centered = mixed - mean
        var = jnp.mean(centered * centered, axis=-1, keepdims=True)
        normed = (
            centered * lax.rsqrt(var + EPS) * (1.0 + mod_ref[1:2]) + mod_ref[0:1]
        ).astype(jnp.bfloat16)
        parts.append(normed)
    velocity = lax.dot_general(
        jnp.concatenate(parts, axis=0),
        final_ref[...],
        (((1,), (1,)), ((), ())),
        preferred_element_type=jnp.float32,
    )
    values = final_ref.shape[0]
    values_ref[:tokens, :values] = velocity
    side = values // PATCH
    tile_cols = latent_ref.shape[1] // side
    rows = tokens // tile_cols
    columns = [values_ref[pl.ds(at, rows, stride=tile_cols), :] for at in range(tile_cols)]
    for at in range(PATCH):
        wide = jnp.concatenate([column[:, at * side : (at + 1) * side] for column in columns], axis=1)
        for tile in range(pixels_ref.shape[0]):
            lanes = slice(tile * LANES, (tile + 1) * LANES)
            pixels_ref[tile, pl.ds(at, rows, stride=PATCH), :] = wide[:, lanes]
    first = start // tile_cols * PATCH
    pixels = slice(first, first + rows * PATCH)
    for before_ref, after_ref in zip(refs[:-4], refs[-4:-2]):
        after_ref[:first] = before_ref[:first]
    for tile in range(pixels_ref.shape[0]):
        lanes = slice(tile * LANES, (tile + 1) * LANES)
        placed = pixels_ref[tile, : rows * PATCH]
        velocity_ref[pixels, lanes] = placed
        next_ref[pixels, lanes] = latent_ref[pixels, lanes] + euler_ref[:, lanes] * placed


def params(limit=VMEM_LIMIT):
    return pltpu.CompilerParams(vmem_limit_bytes=limit)


def lasting(duration):
    return pl.CostEstimate(
        flops=int(duration * 1e9), bytes_accessed=int(duration * 3e6), transcendentals=0
    )


def shape(dims, dtype=jnp.bfloat16):
    return jax.ShapeDtypeStruct(dims, dtype)


VMEM = pl.BlockSpec(memory_space=pltpu.VMEM)
ANY = pl.BlockSpec(memory_space=pl.ANY)
HBM = pl.BlockSpec(memory_space=pltpu.HBM)
SMEM = pl.BlockSpec(memory_space=pltpu.SMEM)


def on_device(
    image_qkv,
    text_kv,
    gain_query,
    gain_key,
    gain_text,
    out_weight,
    final_weight,
    hidden,
    modulation,
    latent,
    step_index,
    step_count,
):
    tile_rows, tile_cols, _, all_width = image_qkv.shape
    tokens = tile_rows * tile_cols
    words = text_kv.shape[0]
    width = all_width // lax.axis_size("col")
    features = hidden.shape[2]
    gains = jnp.stack([gain_query, gain_key, gain_text])
    x = image_qkv.reshape(tokens, 3, all_width)
    weight_half = out_weight.T
    held = pltpu.VMEM((tokens, 3, width), jnp.bfloat16)
    block = shape((tokens, width))

    loads = pltpu.SemaphoreType.DMA((LOADS,))
    cut = tile_rows // 3 * tile_cols
    chunks = ((0, cut), (cut, tokens))
    kv_raw, first_raw, second_raw = pl.pallas_call(
        split_kernel,
        out_shape=(
            shape((2 * tokens, width)),
            shape((cut, width)),
            shape((tokens - cut, width)),
        ),
        in_specs=[HBM],
        out_specs=(VMEM,) * 3,
        scratch_shapes=[held, loads],
        compiler_params=params(VMEM_MOST),
        name="split",
    )(x)
    weight_got = lax.ppermute(weight_half, "row", SWAP)
    final_got = lax.ppermute(final_weight, "row", SWAP)
    k_own, v_own, q_own, gains, euler = pl.pallas_call(
        prep_own_kernel,
        out_shape=(
            shape((tokens + words, width)),
            shape((tokens + words, width)),
            block,
            shape(gains.shape, jnp.float32),
            shape((1, latent.shape[1]), jnp.float32),
        ),
        in_specs=[SMEM] * 2 + [HBM] + [VMEM] * 2,
        out_specs=(VMEM,) * 5,
        scratch_shapes=[held, loads],
        compiler_params=params(VMEM_OWN),
        name="prep_own",
    )(step_index, step_count, x, text_kv, gains)
    weights = (weight_half, weight_got)
    k_row, v_row = (lax.ppermute(x, "row", SWAP) for x in (k_own, v_own))
    nearby = (k_own, v_own, k_row, v_row)
    own_sum, own_total, mixed, gains, mods, finals, second_raw = pl.pallas_call(
        early_kernel,
        out_shape=(
            shape((tokens, width), jnp.float32),
            shape((tokens, width), jnp.float32),
            shape((tokens, features), jnp.float32),
            shape(gains.shape, jnp.float32),
            shape(modulation.shape, jnp.float32),
            shape((final_weight.shape[0], features)),
            shape(second_raw.shape),
        ),
        in_specs=[VMEM] * 10 + [ANY],
        out_specs=(VMEM,) * 6 + (ANY,),
        input_output_aliases={10: 6},
        compiler_params=params(),
        name="early",
    )(q_own, *nearby, gains, hidden, modulation, final_weight, final_got, second_raw)
    q_first, q_second = (lax.ppermute(raw, "col", SWAP) for raw in (first_raw, second_raw))
    kv_got = pl.pallas_call(
        norm_kernel,
        out_shape=shape((2 * tokens, width)),
        in_specs=[VMEM] * 2,
        out_specs=VMEM,
        compiler_params=params(),
        name="norm",
    )(lax.ppermute(kv_raw, "col", SWAP), gains)
    kv_last = lax.ppermute(kv_got, "row", SWAP)
    q_first, *sums = pl.pallas_call(
        part_kernel,
        out_shape=(shape((cut, width)),) + (shape((cut, width), jnp.float32),) * 2,
        in_specs=[VMEM] * 7,
        out_specs=(VMEM,) * 3,
        compiler_params=params(),
        cost_estimate=lasting(4.5),
        name="part",
    )(q_first, gains, *nearby, kv_got)
    first, heads = pl.pallas_call(
        first_kernel,
        out_shape=(shape((cut, FIRST)), shape((cut, width))),
        in_specs=[VMEM] * 6,
        out_specs=(VMEM,) * 2,
        compiler_params=params(),
        name="first",
    )(q_first, kv_last, *sums, *weights)
    first_got = lax.ppermute(first, "col", SWAP)
    rest = pl.pallas_call(
        rest_kernel,
        out_shape=shape((cut, features - FIRST)),
        in_specs=[VMEM] * 3,
        out_specs=VMEM,
        compiler_params=params(),
        name="rest",
    )(heads, *weights)
    rest_got = lax.ppermute(rest, "col", SWAP)
    q_second, rest = lax.optimization_barrier((q_second, rest))
    second, heads = pl.pallas_call(
        second_kernel,
        out_shape=(shape((cut, features)), shape((tokens - cut, width))),
        in_specs=[VMEM] * 10,
        out_specs=(VMEM, VMEM),
        compiler_params=params(),
        name="second",
    )(q_second, gains, *nearby, kv_got, kv_last, *weights)
    third = pl.pallas_call(
        rest_kernel,
        out_shape=shape((tokens - 2 * cut, features)),
        in_specs=[VMEM] * 3,
        out_specs=VMEM,
        compiler_params=params(),
        name="third",
    )(heads, *weights)
    second_got, third_got = (lax.ppermute(x, "col", SWAP) for x in (second, third))
    mixed = pl.pallas_call(
        own_kernel,
        out_shape=shape(mixed.shape, jnp.float32),
        in_specs=[VMEM] * 10,
        out_specs=VMEM,
        scratch_shapes=[pltpu.VMEM((tokens, width), jnp.bfloat16)],
        compiler_params=params(),
        cost_estimate=lasting(0),
        name="own",
    )(q_own, kv_got, kv_last, own_sum, own_total, *weights, mixed, mods, first_got)
    room = -(-tile_rows // 8) * 8 + 8
    results = ()
    for start, got in zip(range(0, tokens, cut), (rest_got, second_got, third_got)):
        results = pl.pallas_call(
            functools.partial(final_kernel, start),
            out_shape=(shape(latent.shape, jnp.float32),) * 2,
            in_specs=[VMEM] * (6 + len(results)),
            out_specs=(VMEM, VMEM),
            scratch_shapes=[
                pltpu.VMEM((room * tile_cols, LANES), jnp.float32),
                pltpu.VMEM((latent.shape[1] // LANES, room * PATCH, LANES), jnp.float32),
            ],
            compiler_params=params(),
            cost_estimate=lasting(30 if start == cut else 2 if start == 0 else 0),
            name="final",
        )(euler, mixed, got, mods, finals, latent, *results)
    return results


def solution(mesh):
    placed = (
        P(("req", "row"), "col", None, None),
        P(("req", "row"), None, "col"),
        P(),
        P(),
        P(),
        P("col", "row"),
        P(None, "row"),
        P(("req", "row"), "col", None),
        P("req", None),
        P(("req", "row"), "col"),
        P("req"),
        P("req"),
    )
    return jax.shard_map(
        on_device,
        mesh=mesh,
        in_specs=placed,
        out_specs=(P(("req", "row"), "col"), P(("req", "row"), "col")),
        check_vma=False,
    )
```
